32 devices in a mesh: section: 4 (over y, x), dp: 8 (over z, core).
Axes of the slice: x: 2, y: 2, z: 4, core: 2. Of those that a mesh axis runs over, the one named last changes fastest.
Arguments:
- images: bfloat16 [16, 32, 32, 512], P('dp', None, None, 'section'), may hold values from -6 to 6
- cotangent: bfloat16 [16, 16, 16, 1024], P('dp', None, None, 'section'), may hold values from -6 to 6
- res_codes: int32 [16], P('dp'), may hold values from 0 to 2, as said below
- section_weights: float32 [4, 1351680], P('section', 'dp'), may hold values from -2 to 2
Outputs:
- block_out: bfloat16 [16, 16, 16, 1024], P('dp', None, None, 'section')
- input_grad: bfloat16 [16, 32, 32, 512], P('dp', None, None, 'section')
- section_grads: float32 [4, 1351680], P('section', 'dp')
The draws below stay inside these ranges and needn't reach their ends.
Inputs may be any that keep to these rules, and one draw needn't show every extreme that they name: `res_codes`: image 0 has code 2 and image 1 code 0.
All inputs are finite; a program needn't handle non-finite values.
Results may differ from the reference program's by a relative error of at most 0.019.
The reference program's roundings to bfloat16 on the way count: a program that leaves them out, or rounds other values in their place, can miss the bound.
Values may be sent and summed in bfloat16 or wider, within the bound.
A program may use at most 128 MiB of HBM per device.

```python
import math
import jax
import jax.numpy as jnp
from jax import lax

CIN = 512
COUT = 1024
CMID = 256
CSQ = 128
RES_MAX = 16
IMG_DEV = 1
MICRO = 2
WSLOTS = 1351680
IMAGES = 16
N_DP = 8


def weight_layouts_drawn():
    group_width = CMID // 2
    radix_width = 2 * CMID
    first_section = (('w_in', (CIN, CMID)), ('g_in', (CMID,)), ('b_in', (CMID,)), ('w_mid', (9, group_width, radix_width)), ('g_mid', (radix_width,)), ('b_mid', (radix_width,)), ('w_squeeze', (CMID, CSQ)), ('g_squeeze', (CSQ,)), ('b_squeeze', (CSQ,)), ('w_excite', (CSQ, radix_width)), ('b_excite', (radix_width,)), ('w_short', (CIN, COUT)), ('g_short', (COUT,)), ('b_short', (COUT,)))
    second_section = (('w_out', (CMID, COUT)), ('g_out', (COUT,)), ('b_out', (COUT,)), ('w_in', (COUT, CMID)), ('g_in', (CMID,)), ('b_in', (CMID,)))
    return (first_section, second_section, first_section[3:11], second_section[:3])


def draw_section_weights(key, part):
    key = jax.random.fold_in(key, 11)
    section_rows = []
    for section_number, layout in enumerate(weight_layouts_drawn()):
        pieces = []
        used_size = 0
        for entry_number, (entry_name, entry_shape) in enumerate(layout):
            entry_key = jax.random.fold_in(key, 100 * section_number + entry_number)
            entry_size = math.prod(entry_shape)
            gaussian = jnp.clip(jax.random.normal(entry_key, (entry_size,), jnp.float32), -3.0, 3.0)
            prefix = entry_name[:2]
            if prefix == 'g_':
                pieces.append(1.0 + 0.15 * gaussian)
            elif prefix == 'b_':
                pieces.append(0.3 * gaussian)
            else:
                fan_in = entry_size // entry_shape[-1]
                pieces.append(gaussian * (1.0 / math.sqrt(fan_in)))
            used_size = used_size + entry_size
        filler_key = jax.random.fold_in(key, 1000 + section_number)
        pieces.append(0.02 * jax.random.normal(filler_key, (WSLOTS - used_size,), jnp.float32))
        section_rows.append(jnp.concatenate(pieces))
    return jnp.stack(section_rows)


def draw_res_codes(key, part):
    key = jax.random.fold_in(key, 5)
    code_values = jax.random.randint(key, (IMAGES,), 0, 3)
    return code_values.at[0].set(2).at[1].set(0)


def draw_cotangent(key, part):
    key = jax.random.fold_in(key, 7)
    noise_key = jax.random.fold_in(key, 1)
    offset_key = jax.random.fold_in(key, 2)
    full_shape = (IMAGES, RES_MAX, RES_MAX, COUT)
    channel_shift = jnp.clip(jax.random.normal(offset_key, (COUT,), jnp.float32), -3.0, 3.0)
    noise = jnp.clip(jax.random.normal(noise_key, full_shape, jnp.float32), -5.0, 5.0)
    channel_shift = 0.1 * channel_shift
    return (noise + channel_shift).astype(jnp.bfloat16)


def shard_levels(stream_key, dims, split, low, largest):
    gain, own = 1.0, jax.random.fold_in(stream_key, 6)
    for position, blocks in split:
        heights = jnp.exp(jax.random.uniform(jax.random.fold_in(own, position), (blocks,), jnp.float32, low / len(split), largest / len(split)))
        gain = gain * jnp.repeat(heights, dims[position] // blocks).reshape([-1 if axis == position else 1 for axis in range(len(dims))])
    return gain


def bell_draw(own_key, shape, deviation, limit, split=(), kind=jnp.bfloat16):
    array = jax.random.normal(own_key, shape, jnp.float32) * deviation
    if len(split) > 0:
        array = shard_levels(own_key, shape, split, -0.22, 0.18) * array
    return jnp.clip(array, min=-limit, max=limit).astype(kind)


def setup_inputs(seed: int = 0) -> dict:
    seeds = jax.random.split(jax.random.key(seed), 5)
    images = bell_draw(seeds[0], (IMAGES, 2 * RES_MAX, 2 * RES_MAX, CIN), 1.0, 6.0, ((0, 8), (3, 4)))
    cotangent = draw_cotangent(jax.random.fold_in(seeds[4], 71), 0)
    res_codes = draw_res_codes(jax.random.fold_in(seeds[4], 71), 0)
    section_weights = draw_section_weights(jax.random.fold_in(seeds[4], 71), 0)
    return dict(images=images, cotangent=cotangent, res_codes=res_codes, section_weights=section_weights)


EPS = 1e-05
HIGH = lax.Precision.HIGHEST

@jax.custom_vjp
def low(v):
    return lax.optimization_barrier(v.astype(jnp.bfloat16)).astype(jnp.float32)

@jax.custom_vjp
def low_back(v):
    return v

def low_keep(v):
    return (low(v), None)

def low_pass(kept, grad):
    return (grad,)

def back_keep(v):
    return (v, None)

def back_low(kept, grad):
    return (low(grad),)
low.defvjp(low_keep, low_pass)
low_back.defvjp(back_keep, back_low)

def weight_layouts():
    group_width = CMID // 2
    radix_width = 2 * CMID
    first_section = (('w_in', (CIN, CMID)), ('g_in', (CMID,)), ('b_in', (CMID,)), ('w_mid', (9, group_width, radix_width)), ('g_mid', (radix_width,)), ('b_mid', (radix_width,)), ('w_squeeze', (CMID, CSQ)), ('g_squeeze', (CSQ,)), ('b_squeeze', (CSQ,)), ('w_excite', (CSQ, radix_width)), ('b_excite', (radix_width,)), ('w_short', (CIN, COUT)), ('g_short', (COUT,)), ('b_short', (COUT,)))
    second_section = (('w_out', (CMID, COUT)), ('g_out', (COUT,)), ('b_out', (COUT,)), ('w_in', (COUT, CMID)), ('g_in', (CMID,)), ('b_in', (CMID,)))
    return (first_section, second_section, first_section[3:11], second_section[:3])

def unpack(section_flat, layout):
    pieces = {}
    offset = 0
    for entry_name, entry_shape in layout:
        length = math.prod(entry_shape)
        pieces[entry_name] = section_flat[offset:offset + length].reshape(entry_shape)
        offset = offset + length
    return pieces

def send(values):
    return low_back(low(values))

def pixel_norm(values, valid_mask, gain_vec, bias_vec):
    counted = jnp.sum(valid_mask)
    average = lax.optimization_barrier(jnp.sum(values * valid_mask, axis=(0, 1, 2))) / counted
    second = lax.optimization_barrier(jnp.sum(values * values * valid_mask, axis=(0, 1, 2))) / counted
    return (values - average) * lax.rsqrt(second - average * average + EPS) * gain_vec + bias_vec

def one_by_one(values, weight):
    return jnp.einsum('ghwc,co->ghwo', values, weight, precision=HIGH)

def radix_conv(values, weight, stride):
    kernel = weight.reshape(3, 3, CMID // 2, 2 * CMID)
    return lax.conv_general_dilated(values, kernel, (stride, stride), ((1, 1), (1, 1)), dimension_numbers=('NHWC', 'HWIO', 'NHWC'), feature_group_count=2, precision=HIGH)

def split_attention(pre_mid, valid_mask, pixel_area, params):
    radix_out = jax.nn.silu(pixel_norm(pre_mid, valid_mask, params['g_mid'], params['b_mid'])) * valid_mask
    first_half = radix_out[..., :CMID]
    second_half = radix_out[..., CMID:]
    pooled = lax.optimization_barrier(jnp.sum(first_half + second_half, axis=(1, 2))) / pixel_area[:, None]
    squeezed = jnp.dot(pooled, params['w_squeeze'], precision=HIGH)
    average = lax.optimization_barrier(jnp.mean(squeezed, axis=0))
    second = lax.optimization_barrier(jnp.mean(squeezed * squeezed, axis=0))
    gate_in = jax.nn.silu((squeezed - average) * lax.rsqrt(second - average * average + EPS) * params['g_squeeze'] + params['b_squeeze'])
    logits = jnp.dot(gate_in, params['w_excite'], precision=HIGH) + params['b_excite']
    shares = jax.nn.softmax(logits.reshape(-1, 2, CMID), axis=1)
    return first_half * shares[:, None, None, 0, :] + second_half * shares[:, None, None, 1, :]

def micro_forward(images, code_values, weights):
    res_step = max(RES_MAX // 8, 1)
    side_len = (RES_MAX - code_values * res_step).astype(jnp.float32)
    out_pos = jnp.arange(RES_MAX, dtype=jnp.float32)
    in_pos = jnp.arange(2 * RES_MAX, dtype=jnp.float32)
    out_mask = ((out_pos[None, :, None] < side_len[:, None, None]) & (out_pos[None, None, :] < side_len[:, None, None])).astype(jnp.float32)[..., None]
    in_mask = ((in_pos[None, :, None] < 2 * side_len[:, None, None]) & (in_pos[None, None, :] < 2 * side_len[:, None, None])).astype(jnp.float32)[..., None]
    pixel_area = side_len * side_len
    layouts = weight_layouts()
    first = unpack(weights[0], layouts[0])
    second = unpack(weights[1], layouts[1])
    third = unpack(weights[2], layouts[2])
    fourth = unpack(weights[3], layouts[3])
    group_count = images.shape[0]
    inputs = images * in_mask
    pre_in = low_back(one_by_one(inputs, first['w_in']))
    hidden = low(jax.nn.silu(pixel_norm(pre_in, in_mask, first['g_in'], first['b_in'])) * in_mask)
    pooled_in = low(lax.optimization_barrier(jnp.mean(inputs.reshape(group_count, RES_MAX, 2, RES_MAX, 2, CIN), axis=(2, 4))))
    pre_short = low_back(one_by_one(pooled_in, first['w_short']))
    pre_mid = low_back(radix_conv(hidden, first['w_mid'], 2))
    attended = send(split_attention(pre_mid, out_mask, pixel_area, first))
    shortcut = send(pixel_norm(pre_short, out_mask, first['g_short'], first['b_short']))
    pre_out = low_back(one_by_one(attended, second['w_out']))
    block_one = low(jax.nn.silu(pixel_norm(pre_out, out_mask, second['g_out'], second['b_out']) + shortcut) * out_mask)
    pre_next = low_back(one_by_one(block_one, second['w_in']))
    hidden_next = send(jax.nn.silu(pixel_norm(pre_next, out_mask, second['g_in'], second['b_in'])) * out_mask)
    carried = low_back(block_one)
    pre_mid_next = low_back(radix_conv(hidden_next, third['w_mid'], 1))
    attended_next = send(split_attention(pre_mid_next, out_mask, pixel_area, third))
    carried = low_back(carried)
    pre_last = low_back(one_by_one(attended_next, fourth['w_out']))
    return jax.nn.silu(pixel_norm(pre_last, out_mask, fourth['g_out'], fourth['b_out']) + carried) * out_mask

def regroup(values):
    tail_shape = values.shape[1:]
    grouped = values.reshape((N_DP, MICRO, IMG_DEV) + tail_shape)
    grouped = jnp.swapaxes(grouped, 0, 1)
    return grouped.reshape((MICRO, N_DP * IMG_DEV) + tail_shape)

def ungroup(values):
    tail_shape = values.shape[2:]
    grouped = values.reshape((MICRO, N_DP, IMG_DEV) + tail_shape)
    grouped = jnp.swapaxes(grouped, 0, 1)
    return grouped.reshape((N_DP * MICRO * IMG_DEV,) + tail_shape)

def reference(images, cotangent, res_codes, section_weights):
    grouped_images = regroup(images.astype(jnp.float32))
    grouped_codes = regroup(res_codes)
    grouped_cot = regroup(cotangent.astype(jnp.float32))

    def whole(all_images, all_weights):
        weights_low = low(all_weights)
        step_fn = jax.checkpoint(lambda pair: micro_forward(pair[0], pair[1], weights_low))
        return lax.map(step_fn, (all_images, grouped_codes))
    outputs, back_fn = jax.vjp(whole, grouped_images, section_weights)
    grad_images, grad_weights = back_fn(grouped_cot)
    return (ungroup(outputs).astype(jnp.bfloat16), ungroup(grad_images).astype(jnp.bfloat16), grad_weights)
```

```python
import math

import jax
import jax.numpy as jnp
from jax import lax
from jax.experimental import pallas as pl
from jax.experimental.pallas import tpu as pltpu
from jax.sharding import PartitionSpec as P

CIN = 512
COUT = 1024
CMID = 256
CSQ = 128
SIDE = 16
PX = SIDE * SIDE
HALF = 128
WSLOTS = 1351680
EPS = 1e-05
HIGH = lax.Precision.HIGHEST
MESH = pl.DeviceIdType.MESH
F32 = jnp.float32
BF16 = jnp.bfloat16
PHASES = 14


def layouts():
    first = (
        ("w_in", (CIN, CMID)),
        ("g_in", (CMID,)),
        ("b_in", (CMID,)),
        ("w_mid", (9, HALF, 2 * CMID)),
        ("g_mid", (2 * CMID,)),
        ("b_mid", (2 * CMID,)),
        ("w_sq", (CMID, CSQ)),
        ("g_sq", (CSQ,)),
        ("b_sq", (CSQ,)),
        ("w_ex", (CSQ, 2 * CMID)),
        ("b_ex", (2 * CMID,)),
        ("w_sc", (CIN, COUT)),
        ("g_sc", (COUT,)),
        ("b_sc", (COUT,)),
    )
    second = (
        ("w_out", (CMID, COUT)),
        ("g_out", (COUT,)),
        ("b_out", (COUT,)),
        ("w_in", (COUT, CMID)),
        ("g_in", (CMID,)),
        ("b_in", (CMID,)),
    )
    return (first, second, first[3:11], second[:3])


VECTORS = (
    (0, "g_in", True),
    (0, "b_in", True),
    (0, "g_mid", True),
    (0, "b_mid", True),
    (0, "g_sq", False),
    (0, "b_sq", False),
    (0, "b_ex", False),
    (0, "g_sc", True),
    (0, "b_sc", True),
    (1, "g_out", True),
    (1, "b_out", True),
    (1, "g_in", True),
    (1, "b_in", True),
    (2, "g_mid", True),
    (2, "b_mid", True),
    (2, "g_sq", False),
    (2, "b_sq", False),
    (2, "b_ex", False),
    (3, "g_out", True),
    (3, "b_out", True),
)
VROW = {(s, name): i for i, (s, name, _) in enumerate(VECTORS)}
VROWS = 24
VCOLS = 512


def dot(a, b):
    return lax.dot_general(a, b, (((1,), (0,)), ((), ())), preferred_element_type=F32)


def dot_rt(a, b):
    return lax.dot_general(a, b, (((1,), (1,)), ((), ())), preferred_element_type=F32)


def dot_lt(a, b):
    return lax.dot_general(a, b, (((0,), (0,)), ((), ())), preferred_element_type=F32)


def dot_hi(a, b, dims=((1,), (0,))):
    return lax.dot_general(a, b, (dims, ((), ())), precision=HIGH, preferred_element_type=F32)


def sigmoid(v):
    return 0.5 + 0.5 * jnp.tanh(0.5 * v)


def fold8(x):
    return jnp.sum(x.reshape(x.shape[0] // 8, 8, x.shape[1]), axis=0)


def lanes(x, count):
    return jnp.concatenate([x] * count, axis=1) if count > 1 else x


def make_kernel(n):
    chips = n // 2

    def kernel(
        img,
        cot,
        codes,
        w_in0,
        w_mid0,
        w_sq0,
        w_ex0,
        w_sc,
        w_out1,
        w_in1,
        w_mid2,
        w_sq2,
        w_ex2,
        w_out3,
        vec,
        out_o,
        out_i,
        gw_in0,
        gw_mid0,
        gw_sq0,
        gw_ex0,
        gw_sc,
        gw_out1,
        gw_in1,
        gw_mid2,
        gw_sq2,
        gw_ex2,
        gw_out3,
        gvec,
        snd,
        rcv,
        side_t,
        u,
        um,
        pool,
        ctb,
        mref,
        z1,
        z2,
        zs,
        z3,
        z4,
        z5,
        z6,
        v3,
        cols1,
        cols2,
        rr1,
        rr2,
        a1,
        a2,
        y1,
        dv6,
        dbuf,
        spb,
        pz,
        pda,
        pdp,
        dz4,
        dz1,
        dz3,
        dzs,
        ep,
        dh,
        obuf,
        ibuf,
        ssem,
        rsem,
        bs,
        br,
        img_s,
        img_r,
        ct_s,
        ct_r,
        oo_s,
        oo_r,
        oi_s,
        oi_r,
    ):
        s = lax.axis_index("section")
        d = lax.axis_index("dp")
        c = d // 2
        k = d % 2
        m = s % 2
        g = (s // 2) * chips + c

        def peer(o, kk):
            gg = lax.rem(g + o, n)
            return ((gg // chips) * 2 + m, 2 * (gg % chips) + kk)

        barrier = pltpu.get_barrier_semaphore()

        def greet(o, _):
            pl.semaphore_signal(barrier, inc=1, device_id=peer(o, 0), device_id_type=MESH)
            pl.semaphore_signal(barrier, inc=1, device_id=peer(o, 1), device_id_type=MESH)
            return 0

        lax.fori_loop(1, n, greet, 0)
        pl.semaphore_signal(barrier, inc=1, device_id=(s, 2 * c + 1 - k), device_id_type=MESH)
        for i in range(2):
            for kk in range(2):
                pl.semaphore_signal(
                    barrier,
                    inc=1,
                    device_id=(2 * i + 1 - m, 2 * c + kk),
                    device_id_type=MESH,
                )
        pl.semaphore_wait(barrier, 2 * n - 1 + 4)

        def to_twin(i, src, dst):
            return pltpu.make_async_remote_copy(
                src, dst, bs.at[i], br.at[i], device_id=(s, 2 * c + 1 - k), device_id_type=MESH
            )

        def move(src, dst, s_sem, r_sem, dev):
            own = (dev[0] == s) & (dev[1] == d)

            @pl.when(own)
            def _():
                pltpu.make_async_copy(src, dst, r_sem).start()

            @pl.when(jnp.logical_not(own))
            def _():
                pltpu.make_async_remote_copy(
                    src, dst, s_sem, r_sem, device_id=dev, device_id_type=MESH
                ).start()

        def end_move(src, s_sem, dev):
            own = (dev[0] == s) & (dev[1] == d)

            @pl.when(jnp.logical_not(own))
            def _():
                pltpu.make_async_copy(src, src, s_sem).wait()

        for slot in range(2):
            for kk in range(2):
                move(
                    img.at[slot, pl.ds(2 * kk, 2)],
                    u.at[s, pl.ds(2 * kk, 2)],
                    img_s.at[slot, kk],
                    img_r.at[s],
                    (2 * k + slot, 2 * c + kk),
                )
        for slot in range(2):
            move(
                cot.at[slot],
                ctb.at[lax.rem(s, 2)],
                ct_s.at[slot],
                ct_r.at[lax.rem(s, 2)],
                (2 * k + slot, 2 * c + s // 2),
            )
        for slot in range(2):
            width = (SIDE - 2 * codes[slot]).astype(F32)
            side_t[k, slot] = jnp.full((8, 128), width, F32)
        side_copy = to_twin(0, side_t.at[k], side_t.at[k])
        side_copy.start()
        snd[...] = jnp.zeros(snd.shape, F32)

        def put(ph, base, value):
            for j in range(value.shape[1] // 128):
                snd[ph, base + j : base + j + 1, :] = value[:, 128 * j : 128 * (j + 1)]

        def send(ph, rows, both=False):
            def one(o, _):
                pltpu.make_async_remote_copy(
                    snd.at[ph, pl.ds(0, rows)],
                    rcv.at[ph, k, o, pl.ds(0, rows)],
                    ssem.at[ph],
                    rsem.at[ph, k],
                    device_id=peer(o, k),
                    device_id_type=MESH,
                ).start()
                return 0

            def other(o, _):
                pltpu.make_async_remote_copy(
                    snd.at[ph, pl.ds(0, rows)],
                    rcv.at[ph, k, o, pl.ds(0, rows)],
                    ssem.at[ph],
                    rsem.at[ph, k],
                    device_id=peer(o, 1 - k),
                    device_id_type=MESH,
                ).start()
                return 0

            lax.fori_loop(1, n, one, 0)
            if both:
                lax.fori_loop(0, n, other, 0)
            rcv[ph, k, 0, 0:rows] = snd[ph, 0:rows]

        def receive(ph, rows, both=False):
            mine = rcv.at[ph, k, pl.ds(1, n - 1), pl.ds(0, rows)]
            pltpu.make_async_copy(mine, mine, rsem.at[ph, k]).wait()
            if both:
                theirs = rcv.at[ph, 1 - k, :, pl.ds(0, rows)]
                pltpu.make_async_copy(theirs, theirs, rsem.at[ph, 1 - k]).wait()

        def end_send(ph, rows, both=False):
            mine = rcv.at[ph, k, pl.ds(1, n - 1), pl.ds(0, rows)]
            pltpu.make_async_copy(mine, mine, ssem.at[ph]).wait()
            if both:
                theirs = rcv.at[ph, 1 - k, :, pl.ds(0, rows)]
                pltpu.make_async_copy(theirs, theirs, ssem.at[ph]).wait()

        def totals(ph, rows):
            return jnp.sum(rcv[ph, k, :, 0:rows, :], axis=0)

        def row(total, base, width):
            return jnp.concatenate(
                [total[base + j : base + j + 1, :] for j in range(width // 128)], axis=1
            )

        def across(ph, h, base, width):
            return jnp.concatenate(
                [rcv[ph, h, :, base + j, :] for j in range(width // 128)], axis=1
            )

        def vrow(key, width):
            i = VROW[key]
            return vec[i : i + 1, 0:width]

        def set_gvec(key, value):
            i = VROW[key]
            gvec[i : i + 1, 0 : value.shape[1]] = value

        def mean_rstd(total, base, width, count):
            mu = row(total, base, width) / count
            second = row(total, base + width // 128, width) / count
            return mu, lax.rsqrt(jnp.maximum(second - mu * mu, 0.0) + EPS)

        gvec[...] = jnp.zeros(gvec.shape, F32)

        side_copy.wait()
        side_row = jnp.where(
            m == 0, side_t[s // 2, 0, 0:1, :], side_t[s // 2, 1, 0:1, :]
        )
        pixel = lax.broadcasted_iota(jnp.int32, (PX, 128), 0)
        prow = (pixel // SIDE).astype(F32)
        pcol = (pixel % SIDE).astype(F32)
        mref[...] = jnp.where((prow < side_row) & (pcol < side_row), 1.0, 0.0)
        inv_own = 1.0 / (side_row * side_row)

        for q in range(4):
            here = u.at[q, pl.ds(2 * k, 2)]
            pltpu.make_async_copy(here, here, img_r.at[q]).wait()
            pltpu.make_async_remote_copy(
                here,
                here,
                bs.at[10 + q],
                br.at[10 + q],
                device_id=(s, 2 * c + 1 - k),
                device_id_type=MESH,
            ).start()
        for q in range(4):
            here = u.at[q, pl.ds(2 * (1 - k), 2)]
            pltpu.make_async_copy(here, here, br.at[10 + q]).wait()

        def mask_block(b, _):
            r = pl.multiple_of(b * 32, 32)
            rows = pl.ds(r, 32)
            mask = mref[rows, :]
            for q in range(4):
                total = jnp.zeros((32, 128), F32)
                for p in range(4):
                    x = u[q, p, rows, :].astype(F32) * mask
                    um[p, rows, 128 * q : 128 * (q + 1)] = x.astype(BF16)
                    total = total + x
                pool[rows, 128 * q : 128 * (q + 1)] = (total * 0.25).astype(BF16)
            return 0

        lax.fori_loop(0, 8, mask_block, 0)

        def z1_block(p, carry):
            z = dot(um[p], w_in0[k])
            z1[p] = z
            return (carry[0] + fold8(z), carry[1] + fold8(z * z))

        zero8 = jnp.zeros((8, 128), F32)
        t0, t1 = lax.fori_loop(0, 4, z1_block, (zero8, zero8))
        put(0, 0, jnp.sum(t0, axis=0, keepdims=True))
        put(0, 1, jnp.sum(t1, axis=0, keepdims=True))
        put(0, 2, side_row)
        send(0, 8)
        z = dot(pool[...], w_sc[...])
        zs[...] = z
        sum_s = jnp.sum(z, axis=0, keepdims=True)
        sq_s = jnp.sum(z * z, axis=0, keepdims=True)
        receive(0, 8)
        total = totals(0, 8)
        sides = across(0, k, 2, 128)
        inv_area = 1.0 / (sides * sides)
        count1 = jnp.sum(sides * sides, axis=0, keepdims=True)
        counts = {w: lanes(count1, w // 128) for w in (128, 256, 512)}
        mu1, rs1 = mean_rstd(total, 0, 128, 4.0 * count1)
        lin1 = rs1 * vrow((0, "g_in"), 128)
        off1 = vrow((0, "b_in"), 128) - mu1 * lin1

        colpos = lax.broadcasted_iota(jnp.int32, (PX, 128), 0) % SIDE

        def shift_cols(x, by):
            moved = pltpu.roll(x, by % PX, 0)
            edge = 0 if by == 1 else SIDE - 1
            return jnp.where(colpos == edge, 0.0, moved)

        def store_tap(cols, di, dj, x, shift):
            at = 128 * (3 * di + dj)
            span = slice(at, at + 128)
            x = x.astype(BF16)
            if shift == 1:
                cols[0:SIDE, span] = jnp.zeros((SIDE, 128), BF16)
                cols[SIDE:PX, span] = x[0 : PX - SIDE]
            elif shift == -1:
                cols[PX - SIDE : PX, span] = jnp.zeros((SIDE, 128), BF16)
                cols[0 : PX - SIDE, span] = x[SIDE:PX]
            else:
                cols[:, span] = x

        def plane_taps(parity):
            return ((1, 0),) if parity == 0 else ((0, 1), (2, 0))

        for p in range(4):
            v = z1[p] * lin1 + off1
            h = v * sigmoid(v) * mref[...]
            for dj, cshift in plane_taps(p % 2):
                x = shift_cols(h, 1) if cshift else h
                for di, rshift in plane_taps(p // 2):
                    store_tap(cols1, di, dj, x, rshift)

        def conv_forward(ph, cols, w_mid, zref):
            z = dot(cols[...], w_mid[...])
            zref[...] = z
            zm = z * lanes(mref[...], 2)
            put(ph, 0, jnp.sum(zm, axis=0, keepdims=True))
            put(ph, 2, jnp.sum(zm * z, axis=0, keepdims=True))
            send(ph, 8)

        def attention_forward(ph, twin, total, sec, zref, rr, w_sq, w_ex, aref, beside):
            mu, rs = mean_rstd(total, 0, 256, counts[256])
            lin = rs * vrow((sec, "g_mid"), 256)
            off = vrow((sec, "b_mid"), 256) - mu * lin

            def block(b, acc):
                rows = pl.ds(pl.multiple_of(b * 64, 64), 64)
                v = zref[rows, :] * lin + off
                r = v * sigmoid(v) * lanes(mref[rows, :], 2)
                rr[k, rows, :] = r
                return acc + fold8(r)

            acc = lax.fori_loop(0, 4, block, jnp.zeros((8, 256), F32))
            pooled_own = jnp.sum(acc, axis=0, keepdims=True) * lanes(inv_own, 2)
            put(ph, 0, pooled_own)
            send(ph, 16 if beside is not None else 8, both=True)
            swap = to_twin(twin, rr.at[k], rr.at[k])
            swap.start()
            receive(ph, 16 if beside is not None else 8, both=True)
            pooled = across(ph, 0, 0, 256) + across(ph, 1, 0, 256)
            zq = dot_hi(pooled, w_sq[...].astype(F32))
            mq = jnp.mean(zq, axis=0, keepdims=True)
            vq = jnp.mean(zq * zq, axis=0, keepdims=True) - mq * mq
            rq = lax.rsqrt(jnp.maximum(vq, 0.0) + EPS)
            hq = (zq - mq) * rq
            nq = hq * vrow((sec, "g_sq"), 128) + vrow((sec, "b_sq"), 128)
            sgq = sigmoid(nq)
            qq = nq * sgq
            logits = dot_hi(qq, w_ex[...].astype(F32)) + vrow((sec, "b_ex"), 512)
            diff = logits[:, 0:256] - logits[:, 256:512]
            sh0 = sigmoid(diff)
            sh1 = sigmoid(-diff)
            swap.wait()
            s0 = sh0[0:1, :]
            s1 = sh1[0:1, :]

            def mix(b, _):
                rows = pl.ds(pl.multiple_of(b * 64, 64), 64)
                aref[rows, :] = (s0 * rr[0, rows, :] + s1 * rr[1, rows, :]).astype(BF16)
                return 0

            lax.fori_loop(0, 4, mix, 0)
            return (mu, rs, lin, off), (pooled, rq, hq, nq, sgq, qq, sh0, sh1)

        def attention_backward(
            ph, sec, kept_mid, kept_q, zref, rr, w_sq, w_ex, g_sq, g_ex, cols, w_mid, g_mid, da, beside
        ):
            mu, rs, lin, off = kept_mid
            pooled, rq, hq, nq, sgq, qq, sh0, sh1 = kept_q

            def block(b, acc):
                rows = pl.ds(pl.multiple_of(b * 32, 32), 32)
                z = zref[rows, :]
                v = z * lin + off
                hat = (z - mu) * rs
                sg = sigmoid(v)
                sp = sg * (1.0 + v * (1.0 - sg)) * lanes(mref[rows, :], 2)
                grad = da(rows)
                t = grad * sp
                dbuf[rows, :] = grad
                spb[rows, :] = sp
                r = rr[k, rows, :]
                return tuple(
                    x + fold8(y)
                    for x, y in zip(acc, (grad * r, t, sp, t * hat, sp * hat))
                )

            acc = lax.fori_loop(0, 8, block, (jnp.zeros((8, 256), F32),) * 5)
            for j, x in enumerate(acc):
                put(ph, 2 * j, jnp.sum(x, axis=0, keepdims=True))
            send(ph, 16, both=True)
            beside()
            receive(ph, 16, both=True)
            ds0 = across(ph, 0, 0, 256)
            ds1 = across(ph, 1, 0, 256)
            mean = sh0 * ds0 + sh1 * ds1
            dl = jnp.concatenate([sh0 * (ds0 - mean), sh1 * (ds1 - mean)], axis=1)
            set_gvec((sec, "b_ex"), jnp.sum(dl, axis=0, keepdims=True))
            dq = dot_hi(dl, w_ex[...].astype(F32), ((1,), (1,)))
            dn = dq * sgq * (1.0 + nq * (1.0 - sgq))
            set_gvec((sec, "g_sq"), jnp.sum(dn * hq, axis=0, keepdims=True))
            set_gvec((sec, "b_sq"), jnp.sum(dn, axis=0, keepdims=True))
            dn = dn * vrow((sec, "g_sq"), 128)
            dzq = rq * (
                dn
                - jnp.mean(dn, axis=0, keepdims=True)
                - hq * jnp.mean(dn * hq, axis=0, keepdims=True)
            )
            dpool = dot_hi(dzq, w_sq[...].astype(F32), ((1,), (1,))) * lanes(inv_area, 2)
            share = jnp.where(k == 0, sh0, sh1)

            def both_sums(first, second):
                return jnp.sum(
                    share * across(ph, k, first, 256) + dpool * across(ph, k, second, 256),
                    axis=0,
                    keepdims=True,
                )

            sdv = both_sums(2, 4)
            sdh = both_sums(6, 8)
            set_gvec((sec, "b_mid"), sdv)
            set_gvec((sec, "g_mid"), sdh)
            own_share = share[0:1, :]
            own_pool = dpool[0:1, :]
            c1 = sdv / counts[256]
            c2 = sdh / counts[256]

            def block2(b, _):
                rows = pl.ds(pl.multiple_of(b * 32, 32), 32)
                hat = (zref[rows, :] - mu) * rs
                dv = (own_share * dbuf[rows, :] + own_pool) * spb[rows, :]
                dz = lin * (dv - c1 - hat * c2) * lanes(mref[rows, :], 2)
                rows_low[rows, :] = dz.astype(BF16)
                return 0

            rows_low = dz_low
            lax.fori_loop(0, 8, block2, 0)

            def rest():
                g_ex[...] = dot_hi(qq, dl, ((0,), (0,))).astype(g_ex.dtype)
                g_sq[...] = dot_hi(pooled, dzq, ((0,), (0,))).astype(g_sq.dtype)
                g_mid[...] = dot_lt(cols[...], dz_low[...]).astype(g_mid.dtype)

            return rest

        dz_low = dz3.at[:, pl.ds(0, 256)]

        conv_forward(1, cols1, w_mid0, z2)
        receive(1, 8)
        put(2, 8, sum_s)
        put(2, 12, sq_s)
        mid1, q1 = attention_forward(2, 2, totals(1, 8), 0, z2, rr1, w_sq0, w_ex0, a1, True)
        total = totals(2, 16)
        mus, rss = mean_rstd(total, 8, 512, counts[512])
        lins = rss * vrow((0, "g_sc"), 512)
        offs = vrow((0, "b_sc"), 512) - mus * lins

        def wide_forward(ph, aref, w, zref):
            z = dot(aref[...], w[...])
            zref[...] = z
            put(ph, 0, jnp.sum(z, axis=0, keepdims=True))
            put(ph, 4, jnp.sum(z * z, axis=0, keepdims=True))
            send(ph, 8)

        wide_forward(3, a1, w_out1, z3)
        receive(3, 8)
        mu3, rs3 = mean_rstd(totals(3, 8), 0, 512, counts[512])
        lin3 = rs3 * vrow((1, "g_out"), 512)
        off3 = vrow((1, "b_out"), 512) - mu3 * lin3

        def y1_block(b, _):
            rows = pl.ds(pl.multiple_of(b * 32, 32), 32)
            short = (zs[rows, :] * lins + offs).astype(BF16).astype(F32)
            v = z3[rows, :] * lin3 + off3 + short
            v3[rows, :] = v
            y1[rows, :] = (v * sigmoid(v) * lanes(mref[rows, :], 4)).astype(BF16)
            return 0

        lax.fori_loop(0, 8, y1_block, 0)
        pz[0] = dot(y1[...], w_in1[1 - k])
        swap = to_twin(3, pz.at[0], pz.at[1])
        swap.start()
        z = dot(y1[...], w_in1[k])
        swap.wait()
        z = z + pz[1]
        z4[...] = z
        put(4, 0, jnp.sum(z, axis=0, keepdims=True))
        put(4, 1, jnp.sum(z * z, axis=0, keepdims=True))
        send(4, 8)
        receive(4, 8)
        mu4, rs4 = mean_rstd(totals(4, 8), 0, 128, count1)
        lin4 = rs4 * vrow((1, "g_in"), 128)
        off4 = vrow((1, "b_in"), 128) - mu4 * lin4
        v = z4[...] * lin4 + off4
        h = v * sigmoid(v) * mref[...]
        for dj in range(3):
            x = h if dj == 1 else shift_cols(h, 1 - dj)
            for di in range(3):
                store_tap(cols2, di, dj, x, 1 - di)

        conv_forward(5, cols2, w_mid2, z5)
        receive(5, 8)
        mid2, q2 = attention_forward(6, 4, totals(5, 8), 2, z5, rr2, w_sq2, w_ex2, a2, None)
        wide_forward(7, a2, w_out3, z6)
        for i in range(2):
            pltpu.make_async_copy(ctb.at[i], ctb.at[i], ct_r.at[i]).wait()
        receive(7, 8)
        mu6, rs6 = mean_rstd(totals(7, 8), 0, 512, counts[512])
        lin6 = rs6 * vrow((3, "g_out"), 512)
        off6 = vrow((3, "b_out"), 512) - mu6 * lin6

        def out_block(b, acc):
            rows = pl.ds(pl.multiple_of(b * 32, 32), 32)
            z = z6[rows, :]
            mask = lanes(mref[rows, :], 4)
            v = z * lin6 + off6 + y1[rows, :].astype(F32)
            sg = sigmoid(v)
            y = (v * sg * mask).astype(BF16)
            obuf[0, rows, :] = y[:, 0:256]
            obuf[1, rows, :] = y[:, 256:512]
            ct = jnp.concatenate([ctb[0, rows, :], ctb[1, rows, :]], axis=1).astype(F32)
            dv = ct * (sg * (1.0 + v * (1.0 - sg)) * mask)
            dv6[rows, :] = dv
            return (acc[0] + fold8(dv), acc[1] + fold8(dv * ((z - mu6) * rs6)))

        zero512 = jnp.zeros((8, 512), F32)
        t0, t1 = lax.fori_loop(0, 8, out_block, (zero512, zero512))
        put(8, 0, jnp.sum(t0, axis=0, keepdims=True))
        put(8, 4, jnp.sum(t1, axis=0, keepdims=True))
        send(8, 8)
        for j in range(2):
            move(
                obuf.at[j],
                out_o.at[lax.rem(s, 2)],
                oo_s.at[j],
                oo_r.at[lax.rem(s, 2)],
                (2 * k + j, 2 * c + s // 2),
            )
        receive(8, 8)

        def wide_back(total, base, key_g, key_b, lin, mu, rs, zref, dvf, dst):
            sdv = row(total, base, 512)
            sdh = row(total, base + 4, 512)
            set_gvec(key_b, sdv)
            set_gvec(key_g, sdh)
            c1 = sdv / counts[512]
            c2 = sdh / counts[512]

            def block(b, _):
                rows = pl.ds(pl.multiple_of(b * 32, 32), 32)
                hat = (zref[rows, :] - mu) * rs
                dz = lin * (dvf(rows) - c1 - hat * c2) * lanes(mref[rows, :], 4)
                dst[rows, :] = dz.astype(BF16)
                return 0

            lax.fori_loop(0, 8, block, 0)

        wide_back(
            totals(8, 8),
            0,
            (3, "g_out"),
            (3, "b_out"),
            lin6,
            mu6,
            rs6,
            z6,
            lambda rows: dv6[rows, :],
            dz3,
        )

        def attended_grad(twin, w, aref, gw):
            pda[0] = dot_rt(dz3[...], w[...])
            swap = to_twin(twin, pda.at[0], pda.at[1])
            swap.start()
            gw[...] = dot_lt(aref[...], dz3[...]).astype(gw.dtype)
            swap.wait()

        def summed_grad(rows):
            return (pda[0, rows, :] + pda[1, rows, :]).astype(BF16).astype(F32)

        attended_grad(5, w_out3, a2, gw_out3)
        rest2 = attention_backward(
            9,
            2,
            mid2,
            q2,
            z5,
            rr2,
            w_sq2,
            w_ex2,
            gw_sq2,
            gw_ex2,
            cols2,
            w_mid2,
            gw_mid2,
            summed_grad,
            lambda: None,
        )

        ep[...] = jnp.zeros(ep.shape, F32)
        for di in range(3):
            part = dot_rt(dz_low[...], w_mid2[384 * di : 384 * (di + 1), :])
            for dj in range(3):
                lo = SIDE * di
                ep[dj, lo : lo + PX, :] += part[:, 128 * dj : 128 * (dj + 1)]
        grad = ep[1, SIDE : SIDE + PX, :]
        grad = grad + shift_cols(ep[0, SIDE : SIDE + PX, :], -1)
        grad = grad + shift_cols(ep[2, SIDE : SIDE + PX, :], 1)
        grad = grad.astype(BF16).astype(F32)
        v = z4[...] * lin4 + off4
        hat4 = (z4[...] - mu4) * rs4
        sg = sigmoid(v)
        dv4 = grad * (sg * (1.0 + v * (1.0 - sg)) * mref[...])
        dh[0] = dv4
        put(10, 0, jnp.sum(dv4, axis=0, keepdims=True))
        put(10, 1, jnp.sum(dv4 * hat4, axis=0, keepdims=True))
        send(10, 8)
        rest2()
        receive(10, 8)
        total = totals(10, 8)
        set_gvec((1, "b_in"), total[0:1, :])
        set_gvec((1, "g_in"), total[1:2, :])
        hat4 = (z4[...] - mu4) * rs4
        dz = lin4 * (dh[0] - total[0:1, :] / count1 - hat4 * (total[1:2, :] / count1)) * mref[...]
        dz4[k] = dz.astype(BF16)
        swap = to_twin(6, dz4.at[k], dz4.at[k])
        swap.start()
        swap.wait()

        def dy_block(b, acc):
            rows = pl.ds(pl.multiple_of(b * 64, 64), 64)
            dy = dot_rt(dz4[0, rows, :], w_in1[0]) + dot_rt(dz4[1, rows, :], w_in1[1])
            dy = dy + dv6[rows, :].astype(BF16).astype(F32)
            v = v3[rows, :]
            sg = sigmoid(v)
            dv = dy * (sg * (1.0 + v * (1.0 - sg)) * lanes(mref[rows, :], 4))
            v3[rows, :] = dv
            low = dv.astype(BF16).astype(F32)
            hat = (z3[rows, :] - mu3) * rs3
            hats = (zs[rows, :] - mus) * rss
            return tuple(
                x + fold8(y) for x, y in zip(acc, (dv, dv * hat, low, low * hats))
            )

        acc = lax.fori_loop(0, 4, dy_block, (zero512,) * 4)
        for j, x in enumerate(acc):
            put(11, 4 * j, jnp.sum(x, axis=0, keepdims=True))
        send(11, 16)
        both4 = jnp.concatenate([dz4[0], dz4[1]], axis=1)
        gw_in1[...] = dot_lt(y1[...], both4).astype(gw_in1.dtype)
        receive(11, 16)
        total = totals(11, 16)
        wide_back(
            total,
            0,
            (1, "g_out"),
            (1, "b_out"),
            lin3,
            mu3,
            rs3,
            z3,
            lambda rows: v3[rows, :],
            dz3,
        )
        wide_back(
            total,
            8,
            (0, "g_sc"),
            (0, "b_sc"),
            lins,
            mus,
            rss,
            zs,
            lambda rows: v3[rows, :].astype(BF16).astype(F32),
            dzs,
        )
        attended_grad(7, w_out1, a1, gw_out1)

        def short_back():
            part = dot_rt(dzs[...], w_sc[...])
            pdp[0] = jnp.where(k == 0, part[:, 256:512], part[:, 0:256])
            to_twin(8, pdp.at[0], pdp.at[1]).start()
            pdp[2] = jnp.where(k == 0, part[:, 0:256], part[:, 256:512])
            gw_sc[...] = dot_lt(pool[...], dzs[...]).astype(gw_sc.dtype)

        rest1 = attention_backward(
            12,
            0,
            mid1,
            q1,
            z2,
            rr1,
            w_sq0,
            w_ex0,
            gw_sq0,
            gw_ex0,
            cols1,
            w_mid0,
            gw_mid0,
            summed_grad,
            short_back,
        )

        for p in range(4):
            dh[p] = jnp.zeros((PX, 128), F32)
        for di in range(3):
            part = dot_rt(dz_low[...], w_mid0[384 * di : 384 * (di + 1), :])
            pr = 0 if di == 1 else 1
            for dj in range(3):
                x = part[:, 128 * dj : 128 * (dj + 1)]
                if dj == 0:
                    x = shift_cols(x, -1)
                p = 2 * pr + (0 if dj == 1 else 1)
                if di == 0:
                    dh[p, 0 : PX - SIDE, :] += x[SIDE:PX]
                else:
                    dh[p] += x

        def dv1_block(p, acc):
            z = z1[p]
            v = z * lin1 + off1
            sg = sigmoid(v)
            dv = dh[p] * (sg * (1.0 + v * (1.0 - sg)) * mref[...])
            dh[p] = dv
            return (acc[0] + fold8(dv), acc[1] + fold8(dv * ((z - mu1) * rs1)))

        t0, t1 = lax.fori_loop(0, 4, dv1_block, (zero8, zero8))
        put(13, 0, jnp.sum(t0, axis=0, keepdims=True))
        put(13, 1, jnp.sum(t1, axis=0, keepdims=True))
        send(13, 8)
        rest1()
        receive(13, 8)
        total = totals(13, 8)
        set_gvec((0, "b_in"), total[0:1, :])
        set_gvec((0, "g_in"), total[1:2, :])
        k1 = total[0:1, :] / (4.0 * count1)
        k2 = total[1:2, :] / (4.0 * count1)

        def dz1_block(p, _):
            hat = (z1[p] - mu1) * rs1
            dz1[k, p] = (lin1 * (dh[p] - k1 - hat * k2) * mref[...]).astype(BF16)
            return 0

        lax.fori_loop(0, 4, dz1_block, 0)
        swap = to_twin(9, dz1.at[k], dz1.at[k])
        swap.start()
        total = jnp.zeros((CIN, 128), F32)
        for p in range(4):
            total = total + dot_lt(um[p], dz1[k, p])
        gw_in0[...] = total.astype(gw_in0.dtype)
        swap.wait()
        to_twin(8, pdp.at[0], pdp.at[1]).wait()

        def du_block(p, _):
            mine = pl.ds(pl.multiple_of(256 * k, 256), 256)
            grad = dot_rt(dz1[0, p], w_in0[0, mine, :]) + dot_rt(dz1[1, p], w_in0[1, mine, :])
            grad = (grad + 0.25 * (pdp[1] + pdp[2])) * lanes(mref[...], 2)
            low = grad.astype(BF16)
            ibuf[0, p] = low[:, 0:128]
            ibuf[1, p] = low[:, 128:256]
            return 0

        lax.fori_loop(0, 4, du_block, 0)
        for j in range(2):
            move(
                ibuf.at[j],
                out_i.at[lax.rem(s, 2)],
                oi_s.at[j],
                oi_r.at[lax.rem(s, 2)],
                (2 * k + j, 2 * c + s // 2),
            )

        for slot in range(2):
            pltpu.make_async_copy(out_o.at[slot], out_o.at[slot], oo_r.at[slot]).wait()
            pltpu.make_async_copy(out_i.at[slot], out_i.at[slot], oi_r.at[slot]).wait()
        for slot in range(2):
            for kk in range(2):
                end_move(
                    img.at[slot, pl.ds(2 * kk, 2)],
                    img_s.at[slot, kk],
                    (2 * k + slot, 2 * c + kk),
                )
            end_move(cot.at[slot], ct_s.at[slot], (2 * k + slot, 2 * c + s // 2))
        for j in range(2):
            end_move(obuf.at[j], oo_s.at[j], (2 * k + j, 2 * c + s // 2))
            end_move(ibuf.at[j], oi_s.at[j], (2 * k + j, 2 * c + s // 2))
        for q in range(4):
            here = u.at[q, pl.ds(2 * k, 2)]
            pltpu.make_async_copy(here, here, bs.at[10 + q]).wait()
        for ph in range(PHASES):
            end_send(ph, 16 if ph in (2, 9, 11, 12) else 8, ph in (2, 6, 9, 12))

    return kernel


def call_kernel(n, operands):
    def vm(*shape, dtype=F32):
        return pltpu.VMEM(shape, dtype)

    def low(*shape):
        return pltpu.VMEM(shape, BF16)

    dma = pltpu.SemaphoreType.DMA
    scratch = [
        vm(PHASES, 16, 128),
        vm(PHASES, 2, n, 16, 128),
        vm(2, 2, 8, 128),
        low(4, 4, PX, 128),
        low(4, PX, CIN),
        low(PX, CIN),
        low(2, PX, 256),
        vm(PX, 128),
        vm(4, PX, 128),
        vm(PX, 256),
        vm(PX, 512),
        vm(PX, 512),
        vm(PX, 128),
        vm(PX, 256),
        vm(PX, 512),
        vm(PX, 512),
        low(PX, 1152),
        low(PX, 1152),
        vm(2, PX, 256),
        vm(2, PX, 256),
        low(PX, 256),
        low(PX, 256),
        low(PX, 512),
        vm(PX, 512),
        vm(PX, 256),
        vm(PX, 256),
        vm(2, PX, 128),
        vm(2, PX, 256),
        vm(3, PX, 256),
        low(2, PX, 128),
        low(2, 4, PX, 128),
        low(PX, 512),
        low(PX, 512),
        vm(3, PX + 2 * SIDE, 128),
        vm(4, PX, 128),
        low(2, PX, 256),
        low(2, 4, PX, 128),
        dma((PHASES,)),
        dma((PHASES, 2)),
        dma((14,)),
        dma((14,)),
        dma((2, 2)),
        dma((4,)),
        dma((2,)),
        dma((2,)),
        dma((2,)),
        dma((2,)),
        dma((2,)),
        dma((2,)),
    ]
    sds = jax.ShapeDtypeStruct
    outs = (
        sds((2, PX, 256), BF16),
        sds((2, 4, PX, 128), BF16),
        sds((CIN, 128), BF16),
        sds((1152, 256), BF16),
        sds((CMID, CSQ), BF16),
        sds((CSQ, 512), BF16),
        sds((CIN, 512), BF16),
        sds((CMID, 512), BF16),
        sds((512, CMID), BF16),
        sds((1152, 256), BF16),
        sds((CMID, CSQ), BF16),
        sds((CSQ, 512), BF16),
        sds((CMID, 512), BF16),
        sds((VROWS, VCOLS), F32),
    )
    vmem = pl.BlockSpec(memory_space=pltpu.VMEM)
    smem = pl.BlockSpec(memory_space=pltpu.SMEM)
    return pl.pallas_call(
        make_kernel(n),
        out_shape=outs,
        in_specs=[smem if i == 2 else vmem for i in range(len(operands))],
        out_specs=[vmem] * len(outs),
        scratch_shapes=scratch,
        compiler_params=pltpu.CompilerParams(
            collective_id=0, has_side_effects=True, vmem_limit_bytes=56 << 20
        ),
    )(*operands)


def unpack(flat, layout):
    pieces, offset = {}, 0
    for name, shape in layout:
        size = math.prod(shape)
        pieces[name] = flat[offset : offset + size].reshape(shape)
        offset += size
    return pieces


def per_device(images, cotangent, res_codes, section_weights):
    n = lax.axis_size("dp")
    k = lax.axis_index("dp") % 2
    flat = lax.all_gather(section_weights.astype(BF16), "dp", axis=1, tiled=True)
    flat = lax.all_gather(flat, "section", axis=0, tiled=True)
    w = [unpack(flat[i], layout) for i, layout in enumerate(layouts())]

    def half(x):
        size = x.shape[-1] // 2
        return lax.dynamic_slice_in_dim(x, k * size, size, x.ndim - 1)

    def mid(x):
        return half(x).reshape(1152, 256)

    vec = jnp.stack(
        [
            jnp.pad(half(w[i][name]) if cut else w[i][name], (0, VCOLS))[:VCOLS]
            for i, name, cut in VECTORS
        ]
        + [jnp.zeros((VCOLS,), BF16)] * (VROWS - len(VECTORS))
    ).astype(F32)
    planes = images.reshape(2, SIDE, 2, SIDE, 2, 128).transpose(0, 2, 4, 1, 3, 5)
    w_in1 = lax.dynamic_slice_in_dim(w[1]["w_in"], k * 512, 512, 0)
    operands = (
        planes.reshape(2, 4, PX, 128),
        cotangent.reshape(2, PX, 256),
        res_codes,
        w[0]["w_in"].reshape(CIN, 2, 128).transpose(1, 0, 2),
        mid(w[0]["w_mid"]),
        w[0]["w_sq"],
        w[0]["w_ex"],
        half(w[0]["w_sc"]),
        half(w[1]["w_out"]),
        w_in1.reshape(512, 2, 128).transpose(1, 0, 2),
        mid(w[2]["w_mid"]),
        w[2]["w_sq"],
        w[2]["w_ex"],
        half(w[3]["w_out"]),
        vec,
    )
    (
        out_o,
        out_i,
        g_in0,
        g_mid0,
        g_sq0,
        g_ex0,
        g_sc,
        g_out1,
        g_in1,
        g_mid2,
        g_sq2,
        g_ex2,
        g_out3,
        gvec,
    ) = call_kernel(n, operands)
    block_out = out_o.reshape(2, SIDE, SIDE, 256)
    input_grad = (
        out_i.reshape(2, 2, 2, SIDE, SIDE, 128).transpose(0, 3, 1, 4, 2, 5).reshape(images.shape)
    )

    first = (lax.axis_index("section") < 2) & (lax.axis_index("dp") < 2)

    def widen(x):
        zero = jnp.zeros_like(x)
        return jnp.where(
            k == 0, jnp.concatenate([x, zero], -1), jnp.concatenate([zero, x], -1)
        )

    def once(x, cut):
        keep = first if cut else first & (k == 0)
        return jnp.where(keep, x, jnp.zeros_like(x))

    grads = [{}, {}, {}, {}]
    for row, (i, name, cut) in enumerate(VECTORS):
        size = math.prod(dict(layouts()[i])[name])
        value = gvec[row, : size // 2 if cut else size]
        grads[i][name] = once(widen(value) if cut else value, cut).astype(BF16)
    grads[0]["w_in"] = widen(g_in0)
    grads[0]["w_mid"] = widen(g_mid0)
    grads[0]["w_sq"] = once(g_sq0, False)
    grads[0]["w_ex"] = once(g_ex0, False)
    grads[0]["w_sc"] = widen(g_sc)
    grads[1]["w_out"] = widen(g_out1)
    zero = jnp.zeros_like(g_in1)
    grads[1]["w_in"] = jnp.where(
        k == 0, jnp.concatenate([g_in1, zero], 0), jnp.concatenate([zero, g_in1], 0)
    )
    grads[2]["w_mid"] = widen(g_mid2)
    grads[2]["w_sq"] = once(g_sq2, False)
    grads[2]["w_ex"] = once(g_ex2, False)
    grads[3]["w_out"] = widen(g_out3)
    rows = []
    for i, layout in enumerate(layouts()):
        packed = jnp.concatenate([grads[i][name].reshape(-1) for name, _ in layout])
        rows.append(jnp.pad(packed, (0, WSLOTS - packed.shape[0])))
    packed = jnp.stack(rows)
    packed = lax.psum_scatter(packed, "section", scatter_dimension=0, tiled=True)
    packed = lax.psum_scatter(packed, "dp", scatter_dimension=1, tiled=True)
    return block_out, input_grad, packed.astype(F32)


def solution(mesh):
    return jax.shard_map(
        per_device,
        mesh=mesh,
        in_specs=(
            P("dp", None, None, "section"),
            P("dp", None, None, "section"),
            P("dp"),
            P("section", "dp"),
        ),
        out_specs=(
            P("dp", None, None, "section"),
            P("dp", None, None, "section"),
            P("section", "dp"),
        ),
        check_vma=False,
    )
```

```python
import jax
import jax.numpy as jnp
from jax import lax
from jax.experimental import pallas as pl
from jax.experimental.pallas import tpu as pltpu
from jax.sharding import PartitionSpec as P

CIN = 512
COUT = 1024
CMID = 256
CSQ = 128
SIDE = 16
PX = SIDE * SIDE
HALF = 128
WSLOTS = 1351680
EPS = 1e-05
HIGH = lax.Precision.HIGHEST
MESH = pl.DeviceIdType.MESH
F32 = jnp.float32
BF16 = jnp.bfloat16
PHASES = 14


class Matrix:
    def __init__(self, index, row, start, blocks, pieces, rows, first=0, split="columns"):
        self.index = index
        self.row = row
        self.start = start
        self.blocks = blocks
        self.pieces = pieces
        self.rows = rows
        self.first = first
        self.split = split
        self.flat = blocks * rows
        self.width = 128 * (blocks // 2 if split == "columns" else blocks)


IN0 = Matrix(0, 0, 0, 2, 8, 16)
MID0 = Matrix(1, 0, 1028, 4, 6, 48)
REST0 = Matrix(2, 0, 5636, 1, 8, 25, split="none")
SC0 = Matrix(3, 0, 6418, 8, 8, 16)
OUT1 = Matrix(4, 1, 0, 8, 4, 16, first=4)
IN1 = Matrix(5, 1, 2064, 2, 8, 16, split="rows")
MID2 = Matrix(6, 2, 0, 4, 6, 48)
REST2 = Matrix(7, 2, 4608, 1, 8, 25, split="none")
OUT3 = Matrix(8, 3, 0, 8, 4, 16)
MATRICES = (IN0, MID0, REST0, SC0, OUT1, IN1, MID2, REST2, OUT3)
PRODUCTS = (IN0, MID0, SC0, OUT1, IN1, MID2, OUT3)
USED = (10530, 4116, 5390, 2064)
REST_ROWS = 782
HOME_ROWS = 1152
REST_PART = 98
AT_SQ, AT_GSQ, AT_BSQ, AT_EX, AT_BEX = 8, 264, 265, 266, 778
TABLE = {
    (0, "g_in"): (0, 1024, 1),
    (0, "b_in"): (2, 1026, 1),
    (0, "g_sc"): (4, 10514, 4),
    (0, "b_sc"): (12, 10522, 4),
    (1, "g_out"): (20, 2048, 4),
    (1, "b_out"): (28, 2056, 4),
    (1, "g_in"): (36, 4112, 1),
    (1, "b_in"): (38, 4114, 1),
    (3, "g_out"): (40, 2048, 4),
    (3, "b_out"): (48, 2056, 4),
}
TABLE_ROWS = 56
RANGES = ((0, 1024, 4, 0), (0, 10514, 16, 4), (1, 2048, 16, 20), (1, 4112, 4, 36), (3, 2048, 16, 40))


def dot(a, b):
    return lax.dot_general(a, b, (((1,), (0,)), ((), ())), preferred_element_type=F32)


def dot_rt(a, b):
    return lax.dot_general(a, b, (((1,), (1,)), ((), ())), preferred_element_type=F32)


def dot_lt(a, b):
    return lax.dot_general(a, b, (((0,), (0,)), ((), ())), preferred_element_type=F32)


def dot_hi(a, b, dims=((1,), (0,))):
    return lax.dot_general(a, b, (dims, ((), ())), precision=HIGH, preferred_element_type=F32)


def sigmoid(v):
    return 0.5 + 0.5 * jnp.tanh(0.5 * v)


def fold8(x):
    return jnp.sum(x.reshape(x.shape[0] // 8, 8, x.shape[1]), axis=0)


def lanes(x, count):
    return jnp.concatenate([x] * count, axis=1) if count > 1 else x


def make_kernel(n):
    chips = n // 2
    shard_rows = WSLOTS // (128 * n)
    fill_rows = shard_rows + 20 * (4 * n - 1)

    def kernel(
        img,
        cot,
        codes,
        shard,
        out_o,
        out_i,
        out_w,
        snd,
        rcv,
        side_t,
        u,
        um,
        pool,
        ctb,
        mref,
        z1,
        z2,
        zs,
        z3,
        z4,
        z5,
        z6,
        v3,
        cols1,
        cols2,
        rr1,
        rr2,
        a1,
        a2,
        y1,
        dv6,
        dbuf,
        spb,
        pz,
        pda,
        pdp,
        dz4,
        dz1,
        dz3,
        dzs,
        ep,
        dh,
        obuf,
        ibuf,
        sround,
        nought,
        fill,
        fill2,
        table,
        w_in0,
        w_mid0,
        rest0,
        w_sc,
        w_out1,
        w_in1,
        w_mid2,
        rest2,
        w_out3,
        ln_in0,
        ln_mid0,
        ln_rest0,
        ln_sc,
        ln_out1,
        ln_in1,
        ln_mid2,
        ln_rest2,
        ln_out3,
        st_in0,
        st_mid0,
        st_sc,
        st_out1,
        st_in1,
        st_mid2,
        st_out3,
        gw_in0,
        gw_mid0,
        gw_sc,
        gw_out1,
        gw_in1,
        gw_mid2,
        gw_out3,
        ga_mid0,
        ga_sc,
        ga_out1,
        ga_in1,
        ga_mid2,
        ga_out3,
        gp_mid0,
        gp_sc,
        gp_out1,
        gp_in1,
        gp_mid2,
        gp_out3,
        gb_in0,
        gb_mid0,
        gb_sc,
        gb_out1,
        gb_in1,
        gb_mid2,
        gb_out3,
        gf_in0,
        gf_mid0,
        gf_sc,
        gf_out1,
        gf_in1,
        gf_mid2,
        gf_out3,
        rg0,
        rg2,
        rl0,
        rl2,
        rf0,
        rf2,
        gvt,
        gvl,
        gvs,
        ssem,
        rsem,
        bs,
        br,
        img_s,
        img_r,
        ct_s,
        ct_r,
        oo_s,
        oo_r,
        oi_s,
        oi_r,
        h_s,
        t_r,
        h_r,
        a_s,
        c_r,
        f_s,
        q_r,
        ga_s,
        ga_r,
        gb_s,
        gb_r,
        gc_s,
        gc_r,
        v_s,
        v_r,
    ):
        s = lax.axis_index("section")
        d = lax.axis_index("dp")
        c = d // 2
        k = d % 2
        m = s % 2
        g = (s // 2) * chips + c

        def peer(o, kk):
            gg = lax.rem(g + o, n)
            return ((gg // chips) * 2 + m, 2 * (gg % chips) + kk)

        nought[...] = jnp.zeros(nought.shape, F32)
        sround[...] = shard[...].astype(BF16).astype(F32)

        barrier = pltpu.get_barrier_semaphore()
        me = s * n + d

        def greet(i, _):
            e = lax.rem(me + i, 4 * n)
            pl.semaphore_signal(barrier, inc=1, device_id=(e // n, e % n), device_id_type=MESH)
            return 0

        lax.fori_loop(1, 4 * n, greet, 0)
        pl.semaphore_wait(barrier, 4 * n - 1)

        def to_twin(i, src, dst):
            return pltpu.make_async_remote_copy(
                src, dst, bs.at[i], br.at[i], device_id=(s, 2 * c + 1 - k), device_id_type=MESH
            )

        def move(src, dst, s_sem, r_sem, dev):
            own = (dev[0] == s) & (dev[1] == d)

            @pl.when(own)
            def _():
                pltpu.make_async_copy(src, dst, r_sem).start()

            @pl.when(jnp.logical_not(own))
            def _():
                pltpu.make_async_remote_copy(
                    src, dst, s_sem, r_sem, device_id=dev, device_id_type=MESH
                ).start()

        def end_move(src, s_sem, dev):
            own = (dev[0] == s) & (dev[1] == d)

            @pl.when(jnp.logical_not(own))
            def _():
                pltpu.make_async_copy(src, src, s_sem).wait()

        def is_self(dev):
            return (dev[0] == s) & (dev[1] == d)

        def move_rows(src, src_at, dst, dst_at, count, full, s_sem, r_sem, dev):
            def go(size, at):
                move(
                    src.at[pl.ds(src_at + at, size)],
                    dst.at[pl.ds(dst_at + at, size)],
                    s_sem,
                    r_sem,
                    dev,
                )

            def chunks(size, start, many):
                def one(i, _):
                    go(size, start + i * size)
                    return 0

                lax.fori_loop(0, many, one, 0)

            if full > 4:

                @pl.when(count == full)
                def _():
                    go(full, 0)

                @pl.when(count < full)
                def _():
                    if full > 16:
                        chunks(16, 0, count // 16)
                        chunks(1, (count // 16) * 16, count % 16)
                    else:
                        chunks(1, 0, count)

            else:
                chunks(1, 0, count)
            return jnp.where(is_self(dev), 0, count)

        def fill_up(src, dst, first, last, sem):
            def chunks(size, start, many):
                def one(i, _):
                    pltpu.make_async_copy(
                        src.at[pl.ds(0, size)], dst.at[pl.ds(start + i * size, size)], sem
                    ).start()
                    return 0

                lax.fori_loop(0, many, one, 0)

            count = last - first
            chunks(128, first, count // 128)
            chunks(16, first + (count // 128) * 128, count % 128 // 16)
            chunks(1, first + (count // 16) * 16, count % 16)

        used = jnp.where(
            s == 0, USED[0], jnp.where(s == 1, USED[1], jnp.where(s == 2, USED[2], USED[3]))
        )
        fill_up(nought, out_w, jnp.clip(used - d * shard_rows, 0, shard_rows), shard_rows, gc_r)

        mine_from = d * shard_rows
        mine_to = mine_from + shard_rows

        def scatter_pieces(mat, land):
            total = mat.pieces * 4 * (2 if mat.split == "rows" else 1)
            first = jnp.maximum(mine_from - mat.start, 0) // mat.flat
            last = (jnp.maximum(mine_to - mat.start, 0) + mat.flat - 1) // mat.flat

            def one(p, sent):
                start = mat.start + p * mat.flat
                lo = jnp.maximum(start, mine_from)
                count = jnp.minimum(start + mat.flat, mine_to) - lo
                h = p // (4 * mat.pieces)
                q = p % (4 * mat.pieces)
                dev = (q // mat.pieces, mat.first + q % mat.pieces)
                return sent + move_rows(
                    sround,
                    lo - mine_from,
                    land,
                    h * mat.flat + lo - start,
                    count,
                    mat.flat,
                    h_s,
                    h_r.at[mat.index],
                    dev,
                )

            return lax.fori_loop(first, jnp.minimum(last, total), one, jnp.int32(0))

        def scatter_table(start, rows, at):
            lo = jnp.maximum(start, mine_from)
            count = jnp.maximum(jnp.minimum(start + rows, mine_to) - lo, 0)

            def one(i, sent):
                e = lax.rem(me + i, 4 * n)
                return sent + move_rows(
                    sround,
                    lo - mine_from,
                    table,
                    at + lo - start,
                    count,
                    rows,
                    h_s,
                    t_r,
                    (e // n, e % n),
                )

            return lax.fori_loop(0, jnp.where(count > 0, 4 * n, 0), one, jnp.int32(0))

        def when_row(r, body):
            return lax.cond(s == r, body, lambda: jnp.int32(0))

        sent = when_row(0, lambda: scatter_pieces(IN0, ln_in0))

        for slot in range(2):
            for kk in range(2):
                move(
                    img.at[slot, pl.ds(2 * kk, 2)],
                    u.at[s, pl.ds(2 * kk, 2)],
                    img_s.at[slot, kk],
                    img_r.at[s],
                    (2 * k + slot, 2 * c + kk),
                )
        for slot in range(2):
            move(
                cot.at[slot],
                ctb.at[lax.rem(s, 2)],
                ct_s.at[slot],
                ct_r.at[lax.rem(s, 2)],
                (2 * k + slot, 2 * c + s // 2),
            )
        for slot in range(2):
            width = (SIDE - 2 * codes[slot]).astype(F32)
            side_t[k, slot] = jnp.full((8, 128), width, F32)
        side_copy = to_twin(0, side_t.at[k], side_t.at[k])
        side_copy.start()
        snd[...] = jnp.zeros(snd.shape, F32)

        def row0():
            count = scatter_table(*RANGES[0][1:]) + scatter_pieces(MID0, ln_mid0)
            count = count + scatter_pieces(REST0, ln_rest0) + scatter_pieces(SC0, ln_sc)
            return count + scatter_table(*RANGES[1][1:])

        def row1():
            count = scatter_pieces(OUT1, ln_out1) + scatter_table(*RANGES[2][1:])
            return count + scatter_pieces(IN1, ln_in1) + scatter_table(*RANGES[3][1:])

        sent = sent + when_row(0, row0)
        sent = sent + when_row(1, row1)
        sent = sent + when_row(2, lambda: scatter_pieces(MID2, ln_mid2) + scatter_pieces(REST2, ln_rest2))
        sent = sent + when_row(3, lambda: scatter_pieces(OUT3, ln_out3) + scatter_table(*RANGES[4][1:]))

        fill_up(nought, fill, sent, fill_rows, h_s)

        def holds(mat):
            return (d >= mat.first) & (d < mat.first + mat.pieces)

        def full_wait(ref, sem):
            pltpu.make_async_copy(ref, ref, sem).wait()

        def cut(mat, land, stage):
            for j in range(mat.blocks):
                for h in range(2):
                    if mat.split == "rows":
                        x = land[pl.ds(h * mat.flat + j, mat.rows, stride=mat.blocks), :]
                        stage[h, j] = x.astype(BF16)
                    elif j // (mat.blocks // 2) == h:
                        x = land[pl.ds(j, mat.rows, stride=mat.blocks), :]
                        at = 128 * (j % (mat.blocks // 2))
                        stage[h, :, at : at + 128] = x.astype(BF16)

        def spread(mat, land, stage, whole):
            @pl.when(holds(mat))
            def _():
                full_wait(land, h_r.at[mat.index])
                if mat.split != "none":
                    cut(mat, land, stage)
                p = s * mat.pieces + d - mat.first

                def one(i, _):
                    e = lax.rem(d + i, n)
                    h = e % 2
                    if mat.split == "none":
                        src, dst = land, whole.at[pl.ds(p * mat.flat, mat.flat)]
                    elif mat.split == "rows":
                        src, dst = stage.at[h], whole.at[:, p]
                    else:
                        src, dst = stage.at[h], whole.at[p]
                    move(src, dst, a_s.at[mat.index], c_r.at[mat.index], (s, e))
                    return 0

                lax.fori_loop(0, n, one, 0)

        def quarters(mat, whole, first, many):
            if mat.split == "none":
                size = mat.flat * mat.pieces
                return whole.at[pl.ds(first * size, many * size)]
            if mat.split == "rows":
                return whole.at[:, pl.ds(first * mat.pieces, many * mat.pieces)]
            return whole.at[pl.ds(first * mat.pieces, many * mat.pieces)]

        def pass_on(mat, whole):
            here = quarters(mat, whole, s, 1)
            full_wait(here, c_r.at[mat.index])
            for i in range(1, 4):
                pltpu.make_async_remote_copy(
                    here,
                    here,
                    f_s.at[mat.index],
                    q_r.at[mat.index],
                    device_id=(lax.rem(s + i, 4), d),
                    device_id_type=MESH,
                ).start()

        def arrived(mat, whole):
            full_wait(quarters(mat, whole, 0, 3), q_r.at[mat.index])

        def end_spread(mat, land, stage, whole):
            @pl.when(holds(mat))
            def _():
                rows = mat.flat if mat.split == "none" else mat.rows * mat.width // 256
                full_wait(fill.at[pl.ds(0, (n - 1) * rows)], a_s.at[mat.index])

            full_wait(quarters(mat, whole, 0, 3), f_s.at[mat.index])

        @pl.when(holds(IN0))
        def _():
            full_wait(ln_in0, h_r.at[0])
            cut(IN0, ln_in0, st_in0)

            def one(i, _):
                e = lax.rem(me + i, 4 * n)
                h = e % 2
                move(
                    st_in0.at[h],
                    w_in0.at[h, s * 8 + d],
                    a_s.at[0],
                    c_r.at[0],
                    (e // n, e % n),
                )
                return 0

            lax.fori_loop(0, 4 * n, one, 0)

        spread(MID0, ln_mid0, st_mid0, w_mid0)

        def shed(mat, gw, land):
            for i in range(1, 4):
                to = lax.rem(s + i, 4)
                pltpu.make_async_remote_copy(
                    gw.at[pl.ds(to * mat.pieces, mat.pieces)],
                    land.at[i - 1],
                    ga_s.at[mat.index],
                    ga_r.at[mat.index],
                    device_id=(to, d),
                    device_id_type=MESH,
                ).start()

        def shed_more(mat, gw, land, part, land2):
            full_wait(land, ga_r.at[mat.index])

            def one(i, _):
                x = gw[s * mat.pieces + i].astype(F32)
                for j in range(3):
                    x = x + land[j, i].astype(F32)
                part[i] = x.astype(BF16)
                move(
                    part.at[i],
                    land2.at[c, k],
                    gb_s.at[mat.index],
                    gb_r.at[mat.index],
                    (s, mat.first + i),
                )
                return 0

            lax.fori_loop(0, mat.pieces, one, 0)

        def home_rows(src, src_at, start, rows, limit, r, active):
            left = jnp.int32(0)
            for i in range((rows + shard_rows - 2) // shard_rows + 1):
                owner = start // shard_rows + i
                lo = jnp.maximum(start, owner * shard_rows)
                hi = jnp.minimum(jnp.minimum(start + rows, limit), (owner + 1) * shard_rows)
                count = jnp.where(active, jnp.maximum(hi - lo, 0), 0)
                owner = jnp.minimum(owner, n - 1)

                def go():
                    return move_rows(
                        src,
                        src_at + lo - start,
                        out_w,
                        lo - owner * shard_rows,
                        count,
                        rows,
                        gc_s,
                        gc_r,
                        (r, owner),
                    )

                left = left + lax.cond(count > 0, go, lambda: jnp.int32(0))
            return left

        def home(mat, land2, flat):
            @pl.when(holds(mat))
            def _():
                full_wait(land2, gb_r.at[mat.index])
                for h in range(2):
                    x = jnp.sum(land2[:, h].astype(F32), axis=0)
                    for j in range(mat.width // 128):
                        if mat.split == "rows":
                            at = h * mat.flat + j
                        else:
                            at = h * (mat.blocks // 2) + j
                        flat[pl.ds(at, mat.rows, stride=mat.blocks), :] = x[:, 128 * j : 128 * (j + 1)]

            p = s * mat.pieces + d - mat.first
            left = home_rows(
                flat, 0, mat.start + p * mat.flat, mat.flat, USED[mat.row], mat.row, holds(mat)
            )
            if mat.split == "rows":
                p = p + 4 * mat.pieces
                left = left + home_rows(
                    flat,
                    mat.flat,
                    mat.start + p * mat.flat,
                    mat.flat,
                    USED[mat.row],
                    mat.row,
                    holds(mat),
                )
            return left

        def end_shed(mat, gw, land):
            full_wait(land, ga_s.at[mat.index])

            @pl.when(holds(mat))
            def _():
                full_wait(gw.at[pl.ds(0, mat.pieces - 1)], gb_s.at[mat.index])

            @pl.when(jnp.logical_not(holds(mat)))
            def _():
                full_wait(gw.at[pl.ds(0, mat.pieces)], gb_s.at[mat.index])

        def rest_meet(i, mat, rg, land):
            @pl.when((s == mat.row) & (d < 8))
            def _():
                pltpu.make_async_remote_copy(
                    rg.at[pl.ds(REST_PART * d, REST_PART)],
                    land,
                    v_s.at[i],
                    v_r.at[i],
                    device_id=(s + 1, d),
                    device_id_type=MESH,
                ).start()

        def rest_home(i, mat, rg, land, flat):
            active = (s == mat.row + 1) & (d < 8)
            at = REST_PART * jnp.minimum(d, 7)

            @pl.when(active)
            def _():
                full_wait(land, v_r.at[i])
                flat[...] = rg[pl.ds(at, REST_PART), :] + land[...]

            return home_rows(
                flat, 0, mat.start + at, REST_PART, mat.start + REST_ROWS, mat.row, active
            )

        def table_meet(i, first, rows):
            @pl.when((s == 0) & (d < 2))
            def _():
                pltpu.make_async_remote_copy(
                    gvt.at[pl.ds(first, rows)],
                    gvl.at[pl.ds(first, rows)],
                    v_s.at[i],
                    v_r.at[i],
                    device_id=(s + 1, d),
                    device_id_type=MESH,
                ).start()

        def table_home(i, first, rows):
            active = (s == 1) & (d < 2)

            @pl.when(active)
            def _():
                span = pl.ds(first, rows)
                full_wait(gvl.at[span], v_r.at[i])
                gvs[first : first + rows, :] = gvt[first : first + rows, :] + gvl[first : first + rows, :]

            left = jnp.int32(0)
            for (r, _), (at, start, many) in TABLE.items():
                if first <= at < first + rows:
                    left = left + home_rows(
                        gvs,
                        at + many * k,
                        start + many * k,
                        many,
                        start + 2 * many,
                        r,
                        active,
                    )
            return left

        def put(ph, base, value):
            for j in range(value.shape[1] // 128):
                snd[ph, base + j : base + j + 1, :] = value[:, 128 * j : 128 * (j + 1)]

        def send(ph, rows, both=False):
            def one(o, _):
                pltpu.make_async_remote_copy(
                    snd.at[ph, pl.ds(0, rows)],
                    rcv.at[ph, k, o, pl.ds(0, rows)],
                    ssem.at[ph],
                    rsem.at[ph, k],
                    device_id=peer(o, k),
                    device_id_type=MESH,
                ).start()
                return 0

            def other(o, _):
                pltpu.make_async_remote_copy(
                    snd.at[ph, pl.ds(0, rows)],
                    rcv.at[ph, k, o, pl.ds(0, rows)],
                    ssem.at[ph],
                    rsem.at[ph, k],
                    device_id=peer(o, 1 - k),
                    device_id_type=MESH,
                ).start()
                return 0

            lax.fori_loop(1, n, one, 0)
            if both:
                lax.fori_loop(0, n, other, 0)
            rcv[ph, k, 0, 0:rows] = snd[ph, 0:rows]

        def receive(ph, rows, both=False):
            mine = rcv.at[ph, k, pl.ds(1, n - 1), pl.ds(0, rows)]
            pltpu.make_async_copy(mine, mine, rsem.at[ph, k]).wait()
            if both:
                theirs = rcv.at[ph, 1 - k, :, pl.ds(0, rows)]
                pltpu.make_async_copy(theirs, theirs, rsem.at[ph, 1 - k]).wait()

        def end_send(ph, rows, both=False):
            many = 2 * n - 1 if both else n - 1
            full_wait(fill.at[pl.ds(0, many * rows)], ssem.at[ph])

        def totals(ph, rows):
            return jnp.sum(rcv[ph, k, :, 0:rows, :], axis=0)

        def row(total, base, width):
            return jnp.concatenate(
                [total[base + j : base + j + 1, :] for j in range(width // 128)], axis=1
            )

        def across(ph, h, base, width):
            return jnp.concatenate(
                [rcv[ph, h, :, base + j, :] for j in range(width // 128)], axis=1
            )

        def rows_of(ref, at, many):
            return jnp.concatenate([ref[pl.ds(at + j, 1), :] for j in range(many)], axis=1)

        def vrow(key):
            at, _, many = TABLE[key]
            return rows_of(table, at + many * k, many)

        def set_gvec(key, value):
            at, _, many = TABLE[key]
            for j in range(many):
                gvt[pl.ds(at + many * k + j, 1), :] = value[:, 128 * j : 128 * (j + 1)]

        def set_rows(ref, at, value):
            for j in range(value.shape[1] // 128):
                ref[at + j : at + j + 1, :] = value[:, 128 * j : 128 * (j + 1)]

        def mean_rstd(total, base, width, count):
            mu = row(total, base, width) / count
            second = row(total, base + width // 128, width) / count
            return mu, lax.rsqrt(jnp.maximum(second - mu * mu, 0.0) + EPS)

        gvt[...] = jnp.zeros(gvt.shape, F32)

        side_copy.wait()
        side_row = jnp.where(
            m == 0, side_t[s // 2, 0, 0:1, :], side_t[s // 2, 1, 0:1, :]
        )
        pixel = lax.broadcasted_iota(jnp.int32, (PX, 128), 0)
        prow = (pixel // SIDE).astype(F32)
        pcol = (pixel % SIDE).astype(F32)
        mref[...] = jnp.where((prow < side_row) & (pcol < side_row), 1.0, 0.0)
        inv_own = 1.0 / (side_row * side_row)

        for q in range(4):
            here = u.at[q, pl.ds(2 * k, 2)]
            pltpu.make_async_copy(here, here, img_r.at[q]).wait()
            pltpu.make_async_remote_copy(
                here,
                here,
                bs.at[10 + q],
                br.at[10 + q],
                device_id=(s, 2 * c + 1 - k),
                device_id_type=MESH,
            ).start()
        for q in range(4):
            here = u.at[q, pl.ds(2 * (1 - k), 2)]
            pltpu.make_async_copy(here, here, br.at[10 + q]).wait()

        def mask_block(b, _):
            r = pl.multiple_of(b * 32, 32)
            rows = pl.ds(r, 32)
            mask = mref[rows, :]
            for q in range(4):
                total = jnp.zeros((32, 128), F32)
                for p in range(4):
                    x = u[q, p, rows, :].astype(F32) * mask
                    um[p, rows, 128 * q : 128 * (q + 1)] = x.astype(BF16)
                    total = total + x
                pool[rows, 128 * q : 128 * (q + 1)] = (total * 0.25).astype(BF16)
            return 0

        lax.fori_loop(0, 8, mask_block, 0)
        full_wait(w_in0.at[k], c_r.at[0])

        def z1_block(p, carry):
            z = dot(um[p], w_in0[k].reshape(CIN, 128))
            z1[p] = z
            return (carry[0] + fold8(z), carry[1] + fold8(z * z))

        zero8 = jnp.zeros((8, 128), F32)
        t0, t1 = lax.fori_loop(0, 4, z1_block, (zero8, zero8))
        put(0, 0, jnp.sum(t0, axis=0, keepdims=True))
        put(0, 1, jnp.sum(t1, axis=0, keepdims=True))
        put(0, 2, side_row)
        send(0, 8)
        pass_on(MID0, w_mid0)
        spread(REST0, ln_rest0, None, rest0)
        spread(SC0, ln_sc, st_sc, w_sc)
        full_wait(table, t_r)
        receive(0, 8)
        total = totals(0, 8)
        sides = across(0, k, 2, 128)
        inv_area = 1.0 / (sides * sides)
        count1 = jnp.sum(sides * sides, axis=0, keepdims=True)
        counts = {w: lanes(count1, w // 128) for w in (128, 256, 512)}
        mu1, rs1 = mean_rstd(total, 0, 128, 4.0 * count1)
        lin1 = rs1 * vrow((0, "g_in"))
        off1 = vrow((0, "b_in")) - mu1 * lin1

        colpos = lax.broadcasted_iota(jnp.int32, (PX, 128), 0) % SIDE

        def shift_cols(x, by):
            moved = pltpu.roll(x, by % PX, 0)
            edge = 0 if by == 1 else SIDE - 1
            return jnp.where(colpos == edge, 0.0, moved)

        def store_tap(cols, di, dj, x, shift):
            at = 128 * (3 * di + dj)
            span = slice(at, at + 128)
            x = x.astype(BF16)
            if shift == 1:
                cols[0:SIDE, span] = jnp.zeros((SIDE, 128), BF16)
                cols[SIDE:PX, span] = x[0 : PX - SIDE]
            elif shift == -1:
                cols[PX - SIDE : PX, span] = jnp.zeros((SIDE, 128), BF16)
                cols[0 : PX - SIDE, span] = x[SIDE:PX]
            else:
                cols[:, span] = x

        def plane_taps(parity):
            return ((1, 0),) if parity == 0 else ((0, 1), (2, 0))

        for p in range(4):
            v = z1[p] * lin1 + off1
            h = v * sigmoid(v) * mref[...]
            for dj, cshift in plane_taps(p % 2):
                x = shift_cols(h, 1) if cshift else h
                for di, rshift in plane_taps(p // 2):
                    store_tap(cols1, di, dj, x, rshift)

        def conv_forward(ph, cols, w_mid, zref):
            z = dot(cols[...], w_mid[...].reshape(1152, 256))
            zref[...] = z
            zm = z * lanes(mref[...], 2)
            put(ph, 0, jnp.sum(zm, axis=0, keepdims=True))
            put(ph, 2, jnp.sum(zm * z, axis=0, keepdims=True))
            send(ph, 8)

        def small(rest):
            w_sq = rest[AT_SQ : AT_SQ + CMID, :]
            w_ex = jnp.concatenate(
                [rest[pl.ds(AT_EX + j, CSQ, stride=4), :] for j in range(4)], axis=1
            )
            return w_sq, w_ex

        def attention_forward(ph, twin, total, rest, zref, rr, aref, beside):
            mu, rs = mean_rstd(total, 0, 256, counts[256])
            lin = rs * rows_of(rest, 2 * k, 2)
            off = rows_of(rest, 4 + 2 * k, 2) - mu * lin

            def block(b, acc):
                rows = pl.ds(pl.multiple_of(b * 64, 64), 64)
                v = zref[rows, :] * lin + off
                r = v * sigmoid(v) * lanes(mref[rows, :], 2)
                rr[k, rows, :] = r
                return acc + fold8(r)

            acc = lax.fori_loop(0, 4, block, jnp.zeros((8, 256), F32))
            pooled_own = jnp.sum(acc, axis=0, keepdims=True) * lanes(inv_own, 2)
            put(ph, 0, pooled_own)
            send(ph, 8, both=True)
            swap = to_twin(twin, rr.at[k], rr.at[k])
            swap.start()
            beside()
            receive(ph, 8, both=True)
            w_sq, w_ex = small(rest)
            pooled = across(ph, 0, 0, 256) + across(ph, 1, 0, 256)
            zq = dot_hi(pooled, w_sq)
            mq = jnp.mean(zq, axis=0, keepdims=True)
            vq = jnp.mean(zq * zq, axis=0, keepdims=True) - mq * mq
            rq = lax.rsqrt(jnp.maximum(vq, 0.0) + EPS)
            hq = (zq - mq) * rq
            nq = hq * rows_of(rest, AT_GSQ, 1) + rows_of(rest, AT_BSQ, 1)
            sgq = sigmoid(nq)
            qq = nq * sgq
            logits = dot_hi(qq, w_ex) + rows_of(rest, AT_BEX, 4)
            diff = logits[:, 0:256] - logits[:, 256:512]
            sh0 = sigmoid(diff)
            sh1 = sigmoid(-diff)
            swap.wait()
            s0 = sh0[0:1, :]
            s1 = sh1[0:1, :]

            def mix(b, _):
                rows = pl.ds(pl.multiple_of(b * 64, 64), 64)
                aref[rows, :] = (s0 * rr[0, rows, :] + s1 * rr[1, rows, :]).astype(BF16)
                return 0

            lax.fori_loop(0, 4, mix, 0)
            return (mu, rs, lin, off), (pooled, rq, hq, nq, sgq, qq, sh0, sh1)

        def attention_backward(
            ph, kept_mid, kept_q, rest, rg, zref, rr, cols, mat, gw_mid, ga_mid, da, beside
        ):
            mu, rs, lin, off = kept_mid
            pooled, rq, hq, nq, sgq, qq, sh0, sh1 = kept_q

            def block(b, acc):
                rows = pl.ds(pl.multiple_of(b * 32, 32), 32)
                z = zref[rows, :]
                v = z * lin + off
                hat = (z - mu) * rs
                sg = sigmoid(v)
                sp = sg * (1.0 + v * (1.0 - sg)) * lanes(mref[rows, :], 2)
                grad = da(rows)
                t = grad * sp
                dbuf[rows, :] = grad
                spb[rows, :] = sp
                r = rr[k, rows, :]
                return tuple(
                    x + fold8(y)
                    for x, y in zip(acc, (grad * r, t, sp, t * hat, sp * hat))
                )

            acc = lax.fori_loop(0, 8, block, (jnp.zeros((8, 256), F32),) * 5)
            for j, x in enumerate(acc):
                put(ph, 2 * j, jnp.sum(x, axis=0, keepdims=True))
            send(ph, 16, both=True)
            beside()
            receive(ph, 16, both=True)
            ds0 = across(ph, 0, 0, 256)
            ds1 = across(ph, 1, 0, 256)
            mean = sh0 * ds0 + sh1 * ds1
            dl = jnp.concatenate([sh0 * (ds0 - mean), sh1 * (ds1 - mean)], axis=1)
            w_sq, w_ex = small(rest)
            set_rows(rg, AT_BEX, jnp.sum(dl, axis=0, keepdims=True))
            dq = dot_hi(dl, w_ex, ((1,), (1,)))
            dn = dq * sgq * (1.0 + nq * (1.0 - sgq))
            set_rows(rg, AT_GSQ, jnp.sum(dn * hq, axis=0, keepdims=True))
            set_rows(rg, AT_BSQ, jnp.sum(dn, axis=0, keepdims=True))
            dn = dn * rows_of(rest, AT_GSQ, 1)
            dzq = rq * (
                dn
                - jnp.mean(dn, axis=0, keepdims=True)
                - hq * jnp.mean(dn * hq, axis=0, keepdims=True)
            )
            dpool = dot_hi(dzq, w_sq, ((1,), (1,))) * lanes(inv_area, 2)
            share = jnp.where(k == 0, sh0, sh1)

            def both_sums(h, part, first, second):
                return jnp.sum(
                    part * across(ph, h, first, 256) + dpool * across(ph, h, second, 256),
                    axis=0,
                    keepdims=True,
                )

            sums = [(both_sums(h, x, 2, 4), both_sums(h, x, 6, 8)) for h, x in enumerate((sh0, sh1))]
            for h in range(2):
                set_rows(rg, 2 * h, sums[h][1])
                set_rows(rg, 4 + 2 * h, sums[h][0])
            sdv = jnp.where(k == 0, sums[0][0], sums[1][0])
            sdh = jnp.where(k == 0, sums[0][1], sums[1][1])
            own_share = share[0:1, :]
            own_pool = dpool[0:1, :]
            c1 = sdv / counts[256]
            c2 = sdh / counts[256]

            def block2(b, _):
                rows = pl.ds(pl.multiple_of(b * 32, 32), 32)
                hat = (zref[rows, :] - mu) * rs
                dv = (own_share * dbuf[rows, :] + own_pool) * spb[rows, :]
                dz = lin * (dv - c1 - hat * c2) * lanes(mref[rows, :], 2)
                rows_low[rows, :] = dz.astype(BF16)
                return 0

            rows_low = dz_low
            lax.fori_loop(0, 8, block2, 0)

            def rest():
                gw_mid[...] = dot_lt(cols[...], dz_low[...]).astype(BF16).reshape(24, 48, 256)
                shed(mat, gw_mid, ga_mid)
                g_ex = dot_hi(qq, dl, ((0,), (0,)))
                for j in range(4):
                    rg[pl.ds(AT_EX + j, CSQ, stride=4), :] = g_ex[:, 128 * j : 128 * (j + 1)]
                rg[AT_SQ : AT_SQ + CMID, :] = dot_hi(pooled, dzq, ((0,), (0,)))

            return rest

        dz_low = dz3.at[:, pl.ds(0, 256)]

        arrived(MID0, w_mid0)
        conv_forward(1, cols1, w_mid0, z2)
        pass_on(REST0, rest0)
        pass_on(SC0, w_sc)
        spread(OUT1, ln_out1, st_out1, w_out1)
        spread(IN1, ln_in1, st_in1, w_in1)
        arrived(REST0, rest0)
        receive(1, 8)

        def short_forward():
            pass_on(OUT1, w_out1)
            arrived(SC0, w_sc)
            z = dot(pool[...], w_sc[...].reshape(CIN, 512))
            zs[...] = z
            put(3, 8, jnp.sum(z, axis=0, keepdims=True))
            put(3, 12, jnp.sum(z * z, axis=0, keepdims=True))
            pass_on(IN1, w_in1)

        mid1, q1 = attention_forward(2, 2, totals(1, 8), rest0, z2, rr1, a1, short_forward)
        arrived(OUT1, w_out1)

        def wide_forward(ph, rows, aref, w, zref):
            z = dot(aref[...], w[...].reshape(CMID, 512))
            zref[...] = z
            put(ph, 0, jnp.sum(z, axis=0, keepdims=True))
            put(ph, 4, jnp.sum(z * z, axis=0, keepdims=True))
            send(ph, rows)

        wide_forward(3, 16, a1, w_out1, z3)
        spread(MID2, ln_mid2, st_mid2, w_mid2)
        arrived(IN1, w_in1)
        receive(3, 16)
        total = totals(3, 16)
        mus, rss = mean_rstd(total, 8, 512, counts[512])
        lins = rss * vrow((0, "g_sc"))
        offs = vrow((0, "b_sc")) - mus * lins

        mu3, rs3 = mean_rstd(total, 0, 512, counts[512])
        lin3 = rs3 * vrow((1, "g_out"))
        off3 = vrow((1, "b_out")) - mu3 * lin3

        def y1_block(b, _):
            rows = pl.ds(pl.multiple_of(b * 32, 32), 32)
            short = (zs[rows, :] * lins + offs).astype(BF16).astype(F32)
            v = z3[rows, :] * lin3 + off3 + short
            v3[rows, :] = v
            y1[rows, :] = (v * sigmoid(v) * lanes(mref[rows, :], 4)).astype(BF16)
            return 0

        lax.fori_loop(0, 8, y1_block, 0)
        pz[0] = dot(y1[...], w_in1[1 - k].reshape(512, 128))
        swap = to_twin(3, pz.at[0], pz.at[1])
        swap.start()
        z = dot(y1[...], w_in1[k].reshape(512, 128))
        swap.wait()
        z = z + pz[1]
        z4[...] = z
        put(4, 0, jnp.sum(z, axis=0, keepdims=True))
        put(4, 1, jnp.sum(z * z, axis=0, keepdims=True))
        send(4, 8)
        pass_on(MID2, w_mid2)
        spread(REST2, ln_rest2, None, rest2)
        receive(4, 8)
        mu4, rs4 = mean_rstd(totals(4, 8), 0, 128, count1)
        lin4 = rs4 * vrow((1, "g_in"))
        off4 = vrow((1, "b_in")) - mu4 * lin4
        v = z4[...] * lin4 + off4
        h = v * sigmoid(v) * mref[...]
        for dj in range(3):
            x = h if dj == 1 else shift_cols(h, 1 - dj)
            for di in range(3):
                store_tap(cols2, di, dj, x, 1 - di)

        arrived(MID2, w_mid2)
        conv_forward(5, cols2, w_mid2, z5)
        pass_on(REST2, rest2)
        spread(OUT3, ln_out3, st_out3, w_out3)
        arrived(REST2, rest2)
        receive(5, 8)

        def last_weights():
            pass_on(OUT3, w_out3)
            to_twin(14, w_in0.at[k], w_in0.at[k]).start()

        mid2, q2 = attention_forward(6, 4, totals(5, 8), rest2, z5, rr2, a2, last_weights)
        arrived(OUT3, w_out3)
        wide_forward(7, 8, a2, w_out3, z6)
        to_twin(14, w_in0.at[k], w_in0.at[k]).wait()
        for i in range(2):
            pltpu.make_async_copy(ctb.at[i], ctb.at[i], ct_r.at[i]).wait()
        receive(7, 8)
        mu6, rs6 = mean_rstd(totals(7, 8), 0, 512, counts[512])
        lin6 = rs6 * vrow((3, "g_out"))
        off6 = vrow((3, "b_out")) - mu6 * lin6

        def out_block(b, acc):
            rows = pl.ds(pl.multiple_of(b * 32, 32), 32)
            z = z6[rows, :]
            mask = lanes(mref[rows, :], 4)
            v = z * lin6 + off6 + y1[rows, :].astype(F32)
            sg = sigmoid(v)
            y = (v * sg * mask).astype(BF16)
            obuf[0, rows, :] = y[:, 0:256]
            obuf[1, rows, :] = y[:, 256:512]
            ct = jnp.concatenate([ctb[0, rows, :], ctb[1, rows, :]], axis=1).astype(F32)
            dv = ct * (sg * (1.0 + v * (1.0 - sg)) * mask)
            dv6[rows, :] = dv
            return (acc[0] + fold8(dv), acc[1] + fold8(dv * ((z - mu6) * rs6)))

        zero512 = jnp.zeros((8, 512), F32)
        t0, t1 = lax.fori_loop(0, 8, out_block, (zero512, zero512))
        put(8, 0, jnp.sum(t0, axis=0, keepdims=True))
        put(8, 4, jnp.sum(t1, axis=0, keepdims=True))
        send(8, 8)
        for j in range(2):
            move(
                obuf.at[j],
                out_o.at[lax.rem(s, 2)],
                oo_s.at[j],
                oo_r.at[lax.rem(s, 2)],
                (2 * k + j, 2 * c + s // 2),
            )
        for mat, land, stage, whole in (
            (MID0, ln_mid0, st_mid0, w_mid0),
            (REST0, ln_rest0, None, rest0),
            (SC0, ln_sc, st_sc, w_sc),
            (OUT1, ln_out1, st_out1, w_out1),
        ):
            end_spread(mat, land, stage, whole)
        receive(8, 8)

        def wide_back(total, base, key_g, key_b, lin, mu, rs, zref, dvf, dst):
            sdv = row(total, base, 512)
            sdh = row(total, base + 4, 512)
            set_gvec(key_b, sdv)
            set_gvec(key_g, sdh)
            c1 = sdv / counts[512]
            c2 = sdh / counts[512]

            def block(b, _):
                rows = pl.ds(pl.multiple_of(b * 32, 32), 32)
                hat = (zref[rows, :] - mu) * rs
                dz = lin * (dvf(rows) - c1 - hat * c2) * lanes(mref[rows, :], 4)
                dst[rows, :] = dz.astype(BF16)
                return 0

            lax.fori_loop(0, 8, block, 0)

        wide_back(
            totals(8, 8),
            0,
            (3, "g_out"),
            (3, "b_out"),
            lin6,
            mu6,
            rs6,
            z6,
            lambda rows: dv6[rows, :],
            dz3,
        )

        def attended_grad(twin, w, aref, mat, gw, land):
            pda[0] = dot_rt(dz3[...], w[...].reshape(CMID, 512))
            swap = to_twin(twin, pda.at[0], pda.at[1])
            swap.start()
            gw[...] = dot_lt(aref[...], dz3[...]).astype(BF16).reshape(16, 16, 512)
            shed(mat, gw, land)
            swap.wait()

        def summed_grad(rows):
            return (pda[0, rows, :] + pda[1, rows, :]).astype(BF16).astype(F32)

        attended_grad(5, w_out3, a2, OUT3, gw_out3, ga_out3)

        def beside9():
            for mat, land, stage, whole in (
                (IN1, ln_in1, st_in1, w_in1),
                (MID2, ln_mid2, st_mid2, w_mid2),
                (REST2, ln_rest2, None, rest2),
                (OUT3, ln_out3, st_out3, w_out3),
            ):
                end_spread(mat, land, stage, whole)
            shed_more(OUT3, gw_out3, ga_out3, gp_out3, gb_out3)

        grad_rest2 = attention_backward(
            9,
            mid2,
            q2,
            rest2,
            rg2,
            z5,
            rr2,
            cols2,
            MID2,
            gw_mid2,
            ga_mid2,
            summed_grad,
            beside9,
        )

        ep[...] = jnp.zeros(ep.shape, F32)
        for di in range(3):
            part = dot_rt(dz_low[...], w_mid2[8 * di : 8 * (di + 1)].reshape(384, 256))
            for dj in range(3):
                lo = SIDE * di
                ep[dj, lo : lo + PX, :] += part[:, 128 * dj : 128 * (dj + 1)]
        grad = ep[1, SIDE : SIDE + PX, :]
        grad = grad + shift_cols(ep[0, SIDE : SIDE + PX, :], -1)
        grad = grad + shift_cols(ep[2, SIDE : SIDE + PX, :], 1)
        grad = grad.astype(BF16).astype(F32)
        v = z4[...] * lin4 + off4
        hat4 = (z4[...] - mu4) * rs4
        sg = sigmoid(v)
        dv4 = grad * (sg * (1.0 + v * (1.0 - sg)) * mref[...])
        dh[0] = dv4
        put(10, 0, jnp.sum(dv4, axis=0, keepdims=True))
        put(10, 1, jnp.sum(dv4 * hat4, axis=0, keepdims=True))
        send(10, 8)
        grad_rest2()
        rest_meet(2, REST2, rg2, rl2)
        left = home(OUT3, gb_out3, gf_out3)
        receive(10, 8)
        total = totals(10, 8)
        set_gvec((1, "b_in"), total[0:1, :])
        set_gvec((1, "g_in"), total[1:2, :])
        hat4 = (z4[...] - mu4) * rs4
        dz = lin4 * (dh[0] - total[0:1, :] / count1 - hat4 * (total[1:2, :] / count1)) * mref[...]
        dz4[k] = dz.astype(BF16)
        swap = to_twin(6, dz4.at[k], dz4.at[k])
        swap.start()
        swap.wait()

        def dy_block(b, acc):
            rows = pl.ds(pl.multiple_of(b * 64, 64), 64)
            dy = dot_rt(dz4[0, rows, :], w_in1[0].reshape(512, 128))
            dy = dy + dot_rt(dz4[1, rows, :], w_in1[1].reshape(512, 128))
            dy = dy + dv6[rows, :].astype(BF16).astype(F32)
            v = v3[rows, :]
            sg = sigmoid(v)
            dv = dy * (sg * (1.0 + v * (1.0 - sg)) * lanes(mref[rows, :], 4))
            v3[rows, :] = dv
            low = dv.astype(BF16).astype(F32)
            hat = (z3[rows, :] - mu3) * rs3
            hats = (zs[rows, :] - mus) * rss
            return tuple(
                x + fold8(y) for x, y in zip(acc, (dv, dv * hat, low, low * hats))
            )

        acc = lax.fori_loop(0, 4, dy_block, (zero512,) * 4)
        for j, x in enumerate(acc):
            put(11, 4 * j, jnp.sum(x, axis=0, keepdims=True))
        send(11, 16)
        both4 = jnp.concatenate([dz4[0], dz4[1]], axis=1)
        gw_in1[...] = dot_lt(y1[...], both4).astype(BF16).reshape(32, 16, 256)
        shed(IN1, gw_in1, ga_in1)
        shed_more(MID2, gw_mid2, ga_mid2, gp_mid2, gb_mid2)
        left = left + rest_home(2, REST2, rg2, rl2, rf2)
        receive(11, 16)
        total = totals(11, 16)
        wide_back(
            total,
            0,
            (1, "g_out"),
            (1, "b_out"),
            lin3,
            mu3,
            rs3,
            z3,
            lambda rows: v3[rows, :],
            dz3,
        )
        wide_back(
            total,
            8,
            (0, "g_sc"),
            (0, "b_sc"),
            lins,
            mus,
            rss,
            zs,
            lambda rows: v3[rows, :].astype(BF16).astype(F32),
            dzs,
        )
        attended_grad(7, w_out1, a1, OUT1, gw_out1, ga_out1)

        def short_back():
            part = dot_rt(dzs[...], w_sc[...].reshape(CIN, 512))
            pdp[0] = jnp.where(k == 0, part[:, 256:512], part[:, 0:256])
            to_twin(8, pdp.at[0], pdp.at[1]).start()
            pdp[2] = jnp.where(k == 0, part[:, 0:256], part[:, 256:512])
            gw_sc[...] = dot_lt(pool[...], dzs[...]).astype(BF16).reshape(32, 16, 512)
            shed(SC0, gw_sc, ga_sc)
            table_meet(0, 4, TABLE_ROWS - 4)
            shed_more(IN1, gw_in1, ga_in1, gp_in1, gb_in1)
            shed_more(OUT1, gw_out1, ga_out1, gp_out1, gb_out1)

        grad_rest0 = attention_backward(
            12,
            mid1,
            q1,
            rest0,
            rg0,
            z2,
            rr1,
            cols1,
            MID0,
            gw_mid0,
            ga_mid0,
            summed_grad,
            short_back,
        )

        for p in range(4):
            dh[p] = jnp.zeros((PX, 128), F32)
        for di in range(3):
            part = dot_rt(dz_low[...], w_mid0[8 * di : 8 * (di + 1)].reshape(384, 256))
            pr = 0 if di == 1 else 1
            for dj in range(3):
                x = part[:, 128 * dj : 128 * (dj + 1)]
                if dj == 0:
                    x = shift_cols(x, -1)
                p = 2 * pr + (0 if dj == 1 else 1)
                if di == 0:
                    dh[p, 0 : PX - SIDE, :] += x[SIDE:PX]
                else:
                    dh[p] += x

        def dv1_block(p, acc):
            z = z1[p]
            v = z * lin1 + off1
            sg = sigmoid(v)
            dv = dh[p] * (sg * (1.0 + v * (1.0 - sg)) * mref[...])
            dh[p] = dv
            return (acc[0] + fold8(dv), acc[1] + fold8(dv * ((z - mu1) * rs1)))

        t0, t1 = lax.fori_loop(0, 4, dv1_block, (zero8, zero8))
        put(13, 0, jnp.sum(t0, axis=0, keepdims=True))
        put(13, 1, jnp.sum(t1, axis=0, keepdims=True))
        send(13, 8)
        grad_rest0()
        rest_meet(1, REST0, rg0, rl0)
        shed_more(SC0, gw_sc, ga_sc, gp_sc, gb_sc)
        left = left + home(MID2, gb_mid2, gf_mid2)
        left = left + home(IN1, gb_in1, gf_in1)
        left = left + home(OUT1, gb_out1, gf_out1)
        left = left + table_home(0, 4, TABLE_ROWS - 4)
        receive(13, 8)
        total = totals(13, 8)
        set_gvec((0, "b_in"), total[0:1, :])
        set_gvec((0, "g_in"), total[1:2, :])
        table_meet(3, 0, 4)
        k1 = total[0:1, :] / (4.0 * count1)
        k2 = total[1:2, :] / (4.0 * count1)

        def dz1_block(p, _):
            hat = (z1[p] - mu1) * rs1
            dz1[k, p] = (lin1 * (dh[p] - k1 - hat * k2) * mref[...]).astype(BF16)
            return 0

        lax.fori_loop(0, 4, dz1_block, 0)
        swap = to_twin(9, dz1.at[k], dz1.at[k])
        swap.start()
        total = jnp.zeros((CIN, 128), F32)
        for p in range(4):
            total = total + dot_lt(um[p], dz1[k, p])
        gw_in0[...] = total.astype(BF16).reshape(32, 16, 128)

        def shed_in0(i, _):
            p = lax.rem(8 * s + i, 32)
            move(
                gw_in0.at[p],
                gb_in0.at[s * chips + c, k],
                gb_s.at[0],
                gb_r.at[0],
                (p // 8, p % 8),
            )
            return 0

        lax.fori_loop(0, 32, shed_in0, 0)
        shed_more(MID0, gw_mid0, ga_mid0, gp_mid0, gb_mid0)
        swap.wait()
        to_twin(8, pdp.at[0], pdp.at[1]).wait()

        def du_block(p, _):
            mine = pl.ds(16 * k, 16)
            grad = dot_rt(dz1[0, p], w_in0[0, mine].reshape(256, 128))
            grad = grad + dot_rt(dz1[1, p], w_in0[1, mine].reshape(256, 128))
            grad = (grad + 0.25 * (pdp[1] + pdp[2])) * lanes(mref[...], 2)
            low = grad.astype(BF16)
            ibuf[0, p] = low[:, 0:128]
            ibuf[1, p] = low[:, 128:256]
            return 0

        lax.fori_loop(0, 4, du_block, 0)
        for j in range(2):
            move(
                ibuf.at[j],
                out_i.at[lax.rem(s, 2)],
                oi_s.at[j],
                oi_r.at[lax.rem(s, 2)],
                (2 * k + j, 2 * c + s // 2),
            )

        left = left + home(SC0, gb_sc, gf_sc)
        left = left + rest_home(1, REST0, rg0, rl0, rf0)
        left = left + table_home(3, 0, 4)
        left = left + home(IN0, gb_in0, gf_in0)
        left = left + home(MID0, gb_mid0, gf_mid0)

        for mat, gw, land in (
            (MID0, gw_mid0, ga_mid0),
            (SC0, gw_sc, ga_sc),
            (OUT1, gw_out1, ga_out1),
            (IN1, gw_in1, ga_in1),
            (MID2, gw_mid2, ga_mid2),
            (OUT3, gw_out3, ga_out3),
        ):
            end_shed(mat, gw, land)

        @pl.when(holds(IN0))
        def _():
            full_wait(gw_in0.at[pl.ds(0, 31)], gb_s.at[0])
            full_wait(fill.at[pl.ds(0, 8 * (4 * n - 1))], a_s.at[0])

        @pl.when(jnp.logical_not(holds(IN0)))
        def _():
            full_wait(gw_in0, gb_s.at[0])

        for i, mat, land in ((1, REST0, rl0), (2, REST2, rl2)):

            @pl.when((s == mat.row) & (d < 8))
            def _():
                full_wait(land, v_s.at[i])

        @pl.when((s == 0) & (d < 2))
        def _():
            full_wait(gvl.at[pl.ds(4, TABLE_ROWS - 4)], v_s.at[0])
            full_wait(gvl.at[pl.ds(0, 4)], v_s.at[3])

        fill_up(nought, fill2, left, HOME_ROWS, gc_s)
        full_wait(fill2, gc_s)
        full_wait(fill, h_s)
        full_wait(out_w, gc_r)
        for slot in range(2):
            pltpu.make_async_copy(out_o.at[slot], out_o.at[slot], oo_r.at[slot]).wait()
            pltpu.make_async_copy(out_i.at[slot], out_i.at[slot], oi_r.at[slot]).wait()
        for slot in range(2):
            for kk in range(2):
                end_move(
                    img.at[slot, pl.ds(2 * kk, 2)],
                    img_s.at[slot, kk],
                    (2 * k + slot, 2 * c + kk),
                )
            end_move(cot.at[slot], ct_s.at[slot], (2 * k + slot, 2 * c + s // 2))
        for j in range(2):
            end_move(obuf.at[j], oo_s.at[j], (2 * k + j, 2 * c + s // 2))
            end_move(ibuf.at[j], oi_s.at[j], (2 * k + j, 2 * c + s // 2))
        for q in range(4):
            here = u.at[q, pl.ds(2 * k, 2)]
            pltpu.make_async_copy(here, here, bs.at[10 + q]).wait()
        for ph in range(PHASES):
            end_send(ph, 16 if ph in (3, 9, 11, 12) else 8, ph in (2, 6, 9, 12))

    return kernel


def call_kernel(n, operands):
    chips = n // 2
    shard_rows = WSLOTS // (128 * n)
    fill_rows = shard_rows + 20 * (4 * n - 1)

    def vm(*shape, dtype=F32):
        return pltpu.VMEM(shape, dtype)

    def low(*shape):
        return pltpu.VMEM(shape, BF16)

    dma = pltpu.SemaphoreType.DMA
    scratch = [
        vm(PHASES, 16, 128),
        vm(PHASES, 2, n, 16, 128),
        vm(2, 2, 8, 128),
        low(4, 4, PX, 128),
        low(4, PX, CIN),
        low(PX, CIN),
        low(2, PX, 256),
        vm(PX, 128),
        vm(4, PX, 128),
        vm(PX, 256),
        vm(PX, 512),
        vm(PX, 512),
        vm(PX, 128),
        vm(PX, 256),
        vm(PX, 512),
        vm(PX, 512),
        low(PX, 1152),
        low(PX, 1152),
        vm(2, PX, 256),
        vm(2, PX, 256),
        low(PX, 256),
        low(PX, 256),
        low(PX, 512),
        vm(PX, 512),
        vm(PX, 256),
        vm(PX, 256),
        vm(2, PX, 128),
        vm(2, PX, 256),
        vm(3, PX, 256),
        low(2, PX, 128),
        low(2, 4, PX, 128),
        low(PX, 512),
        low(PX, 512),
        vm(3, PX + 2 * SIDE, 128),
        vm(4, PX, 128),
        low(2, PX, 256),
        low(2, 4, PX, 128),
        vm(shard_rows, 128),
        vm(128, 128),
        vm(fill_rows, 128),
        vm(HOME_ROWS, 128),
        vm(TABLE_ROWS, 128),
        low(2, 32, 16, 128),
        low(24, 48, 256),
        vm(800, 128),
        low(32, 16, 512),
        low(16, 16, 512),
        low(2, 32, 16, 128),
        low(24, 48, 256),
        vm(800, 128),
        low(16, 16, 512),
        vm(32, 128),
        vm(192, 128),
        vm(25, 128),
        vm(128, 128),
        vm(128, 128),
        vm(64, 128),
        vm(192, 128),
        vm(25, 128),
        vm(128, 128),
        low(2, 16, 128),
        low(2, 48, 256),
        low(2, 16, 512),
        low(2, 16, 512),
        low(2, 2, 16, 128),
        low(2, 48, 256),
        low(2, 16, 512),
        low(32, 16, 128),
        low(24, 48, 256),
        low(32, 16, 512),
        low(16, 16, 512),
        low(32, 16, 256),
        low(24, 48, 256),
        low(16, 16, 512),
        low(3, 6, 48, 256),
        low(3, 8, 16, 512),
        low(3, 4, 16, 512),
        low(3, 8, 16, 256),
        low(3, 6, 48, 256),
        low(3, 4, 16, 512),
        low(6, 48, 256),
        low(8, 16, 512),
        low(4, 16, 512),
        low(8, 16, 256),
        low(6, 48, 256),
        low(4, 16, 512),
        low(4 * chips, 2, 16, 128),
        low(chips, 2, 48, 256),
        low(chips, 2, 16, 512),
        low(chips, 2, 16, 512),
        low(chips, 2, 16, 256),
        low(chips, 2, 48, 256),
        low(chips, 2, 16, 512),
        vm(32, 128),
        vm(192, 128),
        vm(128, 128),
        vm(128, 128),
        vm(64, 128),
        vm(192, 128),
        vm(128, 128),
        vm(784, 128),
        vm(784, 128),
        vm(REST_PART, 128),
        vm(REST_PART, 128),
        vm(REST_PART, 128),
        vm(REST_PART, 128),
        vm(64, 128),
        vm(64, 128),
        vm(64, 128),
        dma((PHASES,)),
        dma((PHASES, 2)),
        dma((15,)),
        dma((15,)),
        dma((2, 2)),
        dma((4,)),
        dma((2,)),
        dma((2,)),
        dma((2,)),
        dma((2,)),
        dma((2,)),
        dma((2,)),
        dma,
        dma,
        dma((9,)),
        dma((9,)),
        dma((9,)),
        dma((9,)),
        dma((9,)),
        dma((9,)),
        dma((9,)),
        dma((9,)),
        dma((9,)),
        dma,
        dma,
        dma((4,)),
        dma((4,)),
    ]
    sds = jax.ShapeDtypeStruct
    outs = (
        sds((2, PX, 256), BF16),
        sds((2, 4, PX, 128), BF16),
        sds((shard_rows, 128), F32),
    )
    vmem = pl.BlockSpec(memory_space=pltpu.VMEM)
    smem = pl.BlockSpec(memory_space=pltpu.SMEM)
    return pl.pallas_call(
        make_kernel(n),
        out_shape=outs,
        in_specs=[smem if i == 2 else vmem for i in range(len(operands))],
        out_specs=[vmem] * len(outs),
        scratch_shapes=scratch,
        compiler_params=pltpu.CompilerParams(
            collective_id=0, has_side_effects=True, vmem_limit_bytes=60 << 20
        ),
    )(*operands)


def per_device(images, cotangent, res_codes, section_weights):
    n = lax.axis_size("dp")
    planes = images.reshape(2, SIDE, 2, SIDE, 2, 128).transpose(0, 2, 4, 1, 3, 5)
    out_o, out_i, out_w = call_kernel(
        n,
        (
            planes.reshape(2, 4, PX, 128),
            cotangent.reshape(2, PX, 256),
            res_codes,
            section_weights.reshape(-1, 128),
        ),
    )
    block_out = out_o.reshape(2, SIDE, SIDE, 256)
    input_grad = (
        out_i.reshape(2, 2, 2, SIDE, SIDE, 128).transpose(0, 3, 1, 4, 2, 5).reshape(images.shape)
    )
    return block_out, input_grad, out_w.reshape(section_weights.shape)


def solution(mesh):
    return jax.shard_map(
        per_device,
        mesh=mesh,
        in_specs=(
            P("dp", None, None, "section"),
            P("dp", None, None, "section"),
            P("dp"),
            P("section", "dp"),
        ),
        out_specs=(
            P("dp", None, None, "section"),
            P("dp", None, None, "section"),
            P("section", "dp"),
        ),
        check_vma=False,
    )
```

```python
import jax
import jax.numpy as jnp
from jax import lax
from jax.experimental import pallas as pl
from jax.experimental.pallas import tpu as pltpu
from jax.sharding import PartitionSpec as P

CIN = 512
COUT = 1024
CMID = 256
CSQ = 128
SIDE = 16
PX = SIDE * SIDE
HALF = 128
WSLOTS = 1351680
EPS = 1e-05
HIGH = lax.Precision.HIGHEST
MESH = pl.DeviceIdType.MESH
F32 = jnp.float32
BF16 = jnp.bfloat16
PHASES = 14


class Matrix:
    def __init__(self, index, row, start, blocks, pieces, rows, first, step, split="columns"):
        self.index = index
        self.row = row
        self.start = start
        self.blocks = blocks
        self.pieces = pieces
        self.rows = rows
        self.first = first
        self.step = step
        self.split = split
        self.flat = blocks * rows
        self.width = 128 * (blocks // 2 if split == "columns" else blocks)


IN0 = Matrix(0, 0, 0, 2, 8, 16, 0, 1)
MID0 = Matrix(1, 0, 1028, 4, 6, 48, 0, 1)
REST0 = Matrix(2, 0, 5636, 1, 8, 25, 0, 1, split="none")
SC0 = Matrix(3, 0, 6418, 8, 8, 16, 0, 1)
OUT1 = Matrix(4, 1, 0, 8, 4, 16, 1, 2)
IN1 = Matrix(5, 1, 2064, 2, 8, 16, 0, 1, split="rows")
MID2 = Matrix(6, 2, 0, 4, 6, 48, 2, 1)
REST2 = Matrix(7, 2, 4608, 1, 8, 25, 0, 1, split="none")
OUT3 = Matrix(8, 3, 0, 8, 4, 16, 0, 2)
MATRICES = (IN0, MID0, REST0, SC0, OUT1, IN1, MID2, REST2, OUT3)
PRODUCTS = (IN0, MID0, SC0, OUT1, IN1, MID2, OUT3)
USED = (10530, 4116, 5390, 2064)
REST_ROWS = 782
HOME_ROWS = 1152
REST_PART = 98
AT_SQ, AT_GSQ, AT_BSQ, AT_EX, AT_BEX = 8, 264, 265, 266, 778
TABLE = {
    (0, "g_in"): (0, 1024, 1),
    (0, "b_in"): (2, 1026, 1),
    (0, "g_sc"): (4, 10514, 4),
    (0, "b_sc"): (12, 10522, 4),
    (1, "g_out"): (28, 2048, 4),
    (1, "b_out"): (36, 2056, 4),
    (1, "g_in"): (44, 4112, 1),
    (1, "b_in"): (46, 4114, 1),
    (3, "g_out"): (48, 2048, 4),
    (3, "b_out"): (56, 2056, 4),
}
TABLE_ROWS = 72
SECTION_ROWS = {0: (0, 28), 1: (28, 20), 2: (64, 8), 3: (48, 16)}
AT_MID = {0: 20, 2: 64}
RANGES = (
    (0, 1024, 4, 0),
    (0, 5636, 8, 20),
    (0, 10514, 16, 4),
    (1, 2048, 16, 28),
    (1, 4112, 4, 44),
    (2, 4608, 8, 64),
    (3, 2048, 16, 48),
)


def dot(a, b):
    return lax.dot_general(a, b, (((1,), (0,)), ((), ())), preferred_element_type=F32)


def dot_rt(a, b):
    return lax.dot_general(a, b, (((1,), (1,)), ((), ())), preferred_element_type=F32)


def dot_lt(a, b):
    return lax.dot_general(a, b, (((0,), (0,)), ((), ())), preferred_element_type=F32)


def dot_hi(a, b, dims=((1,), (0,))):
    return lax.dot_general(a, b, (dims, ((), ())), precision=HIGH, preferred_element_type=F32)


def sigmoid(v):
    return 0.5 + 0.5 * jnp.tanh(0.5 * v)


def fold8(x):
    return jnp.sum(x.reshape(x.shape[0] // 8, 8, x.shape[1]), axis=0)


def lanes(x, count):
    return jnp.concatenate([x] * count, axis=1) if count > 1 else x


def make_kernel(n):
    chips = n // 2
    shard_rows = WSLOTS // (128 * n)
    fill_rows = max(shard_rows + 28 * n, 96 * (n - 1), 100 * n, 8 * (4 * n - 1), 16 * (2 * n - 1))

    def kernel(
        img,
        cot,
        codes,
        shard,
        out_o,
        out_i,
        out_w,
        snd,
        rcv,
        side_t,
        u,
        um,
        pool,
        ctb,
        mref,
        z1,
        z2,
        zs,
        z3,
        z4,
        z5,
        z6,
        v3,
        cols1,
        cols2,
        rr1,
        rr2,
        a1,
        a2,
        y1,
        dv6,
        dbuf,
        spb,
        pz,
        pda,
        pdp,
        dz4,
        dz1,
        dz3,
        dzs,
        ep,
        dh,
        obuf,
        ibuf,
        sround,
        nought,
        fill,
        fill2,
        table,
        w_in0,
        w_mid0,
        rest0,
        w_sc,
        w_out1,
        w_in1,
        w_mid2,
        rest2,
        w_out3,
        ln_in0,
        ln_mid0,
        ln_rest0,
        ln_sc,
        ln_out1,
        ln_in1,
        ln_mid2,
        ln_rest2,
        ln_out3,
        st_in0,
        st_mid0,
        st_sc,
        st_out1,
        st_in1,
        st_mid2,
        st_out3,
        cu_in0,
        cu_mid0,
        cu_sc,
        cu_out1,
        cu_mid2,
        cu_out3,
        gw_in0,
        gw_mid0,
        gw_sc,
        gw_out1,
        gw_in1,
        gw_mid2,
        gw_out3,
        ga_mid0,
        ga_sc,
        ga_out1,
        ga_in1,
        ga_mid2,
        ga_out3,
        gp_mid0,
        gp_sc,
        gp_out1,
        gp_in1,
        gp_mid2,
        gp_out3,
        gb_in0,
        gb_mid0,
        gb_sc,
        gb_out1,
        gb_in1,
        gb_mid2,
        gb_out3,
        gf_in0,
        gf_mid0,
        gf_sc,
        gf_out1,
        gf_in1,
        gf_mid2,
        gf_out3,
        rg0,
        rg2,
        rl0,
        rl2,
        rf0,
        rf2,
        gvt,
        gvl,
        gvs,
        ssem,
        rsem,
        bs,
        br,
        img_s,
        img_r,
        ct_s,
        ct_r,
        oo_s,
        oo_r,
        oi_s,
        oi_r,
        h_s,
        t_s,
        t_r,
        h_r,
        a_s,
        c_r,
        f_s,
        q_r,
        ga_s,
        ga_r,
        gb_s,
        gb_r,
        gc_s,
        gc_r,
        v_s,
        v_r,
    ):
        s = lax.axis_index("section")
        d = lax.axis_index("dp")
        c = d // 2
        k = d % 2
        m = s % 2
        g = (s // 2) * chips + c

        def peer(o, kk):
            gg = lax.rem(g + o, n)
            return ((gg // chips) * 2 + m, 2 * (gg % chips) + kk)

        nought[...] = jnp.zeros(nought.shape, F32)
        sround[...] = shard[...].astype(BF16).astype(F32)

        barrier = pltpu.get_barrier_semaphore()
        me = s * n + d
        beside_x = s + 1 - 2 * (s % 2)
        beside_y = lax.rem(s + 2, 4)

        def greet(i, _):
            e = lax.rem(me + i, 4 * n)
            pl.semaphore_signal(barrier, inc=1, device_id=(e // n, e % n), device_id_type=MESH)
            return 0

        lax.fori_loop(1, 4 * n, greet, 0)
        pl.semaphore_wait(barrier, 4 * n - 1)

        def to_twin(i, src, dst):
            return pltpu.make_async_remote_copy(
                src, dst, bs.at[i], br.at[i], device_id=(s, 2 * c + 1 - k), device_id_type=MESH
            )

        def move(src, dst, s_sem, r_sem, dev):
            own = (dev[0] == s) & (dev[1] == d)

            @pl.when(own)
            def _():
                pltpu.make_async_copy(src, dst, r_sem).start()

            @pl.when(jnp.logical_not(own))
            def _():
                pltpu.make_async_remote_copy(
                    src, dst, s_sem, r_sem, device_id=dev, device_id_type=MESH
                ).start()

        def end_move(src, s_sem, dev):
            own = (dev[0] == s) & (dev[1] == d)

            @pl.when(jnp.logical_not(own))
            def _():
                pltpu.make_async_copy(src, src, s_sem).wait()

        def is_self(dev):
            return (dev[0] == s) & (dev[1] == d)

        def move_rows(src, src_at, dst, dst_at, count, full, s_sem, r_sem, dev):
            def go(size, at):
                move(
                    src.at[pl.ds(src_at + at, size)],
                    dst.at[pl.ds(dst_at + at, size)],
                    s_sem,
                    r_sem,
                    dev,
                )

            def chunks(size, start, many):
                def one(i, _):
                    go(size, start + i * size)
                    return 0

                lax.fori_loop(0, many, one, 0)

            if full > 1:

                @pl.when(count == full)
                def _():
                    go(full, 0)

                @pl.when(count < full)
                def _():
                    if full > 16:
                        chunks(16, 0, count // 16)
                        chunks(1, (count // 16) * 16, count % 16)
                    else:
                        chunks(1, 0, count)

            else:
                chunks(1, 0, count)
            return jnp.where(is_self(dev), 0, count)

        def fill_up(src, dst, first, last, sem):
            def chunks(size, start, many):
                def one(i, _):
                    pltpu.make_async_copy(
                        src.at[pl.ds(0, size)], dst.at[pl.ds(start + i * size, size)], sem
                    ).start()
                    return 0

                lax.fori_loop(0, many, one, 0)

            count = last - first
            chunks(128, first, count // 128)
            chunks(16, first + (count // 128) * 128, count % 128 // 16)
            chunks(1, first + (count // 16) * 16, count % 16)

        used = jnp.where(
            s == 0, USED[0], jnp.where(s == 1, USED[1], jnp.where(s == 2, USED[2], USED[3]))
        )
        fill_up(nought, out_w, jnp.clip(used - d * shard_rows, 0, shard_rows), shard_rows, gc_r)

        mine_from = d * shard_rows
        mine_to = mine_from + shard_rows

        def cut(mat, land, stage, base):
            for j in range(mat.blocks):
                for h in range(2):
                    if mat.split == "rows":
                        x = land[pl.ds(base + h * mat.flat + j, mat.rows, stride=mat.blocks), :]
                        stage[h, j] = x.astype(BF16)
                    elif j // (mat.blocks // 2) == h:
                        x = land[pl.ds(base + j, mat.rows, stride=mat.blocks), :]
                        at = 128 * (j % (mat.blocks // 2))
                        stage[h, :, at : at + 128] = x.astype(BF16)

        def holds(mat):
            i = d - mat.first
            inside = (i >= 0) & (i < mat.step * mat.pieces)
            return inside & (i % mat.step == 0) if mat.step > 1 else inside

        def piece(mat):
            return s * mat.pieces + jnp.maximum(d - mat.first, 0) // mat.step

        def scatter_cut(mat, land, stage, ready, part=0, parts=1):
            first = jnp.maximum(mine_from - mat.start, 0) // mat.flat
            last = (jnp.maximum(mine_to - mat.start, 0) + mat.flat - 1) // mat.flat
            last = jnp.minimum(last, 4 * mat.pieces)

            def one(p, sent):
                start = mat.start + p * mat.flat
                lo = jnp.maximum(start, mine_from)
                count = jnp.minimum(start + mat.flat, mine_to) - lo
                dev = (p // mat.pieces, mat.first + mat.step * (p % mat.pieces))

                def in_one():
                    to = ready.at[p - first]
                    cut(mat, sround, to, lo - mine_from)
                    move(to, stage, h_s, h_r.at[mat.index], dev)
                    return jnp.where(is_self(dev), 0, mat.flat // 2)

                def in_rows():
                    return move_rows(
                        sround,
                        lo - mine_from,
                        land,
                        lo - start,
                        count,
                        mat.flat,
                        h_s,
                        h_r.at[mat.index],
                        dev,
                    )

                return sent + lax.cond(count == mat.flat, in_one, in_rows)

            step = (jnp.maximum(last - first, 0) + parts - 1) // parts
            begin = first + part * step
            end = jnp.minimum(last, begin + step)
            return lax.fori_loop(begin, end, one, jnp.int32(0))

        def stage_ready(mat, land, stage):
            start = mat.start + piece(mat) * mat.flat
            whole = start // shard_rows == (start + mat.flat - 1) // shard_rows

            @pl.when(whole)
            def _():
                full_wait(stage, h_r.at[mat.index])

            @pl.when(jnp.logical_not(whole))
            def _():
                full_wait(land, h_r.at[mat.index])
                cut(mat, land, stage, 0)

        def scatter_pieces(mat, land, part=0, parts=1):
            total = mat.pieces * 4 * (2 if mat.split == "rows" else 1)
            first = jnp.maximum(mine_from - mat.start, 0) // mat.flat
            last = (jnp.maximum(mine_to - mat.start, 0) + mat.flat - 1) // mat.flat

            def one(p, sent):
                start = mat.start + p * mat.flat
                lo = jnp.maximum(start, mine_from)
                count = jnp.minimum(start + mat.flat, mine_to) - lo
                h = p // (4 * mat.pieces)
                q = p % (4 * mat.pieces)
                dev = (q // mat.pieces, mat.first + mat.step * (q % mat.pieces))
                return sent + move_rows(
                    sround,
                    lo - mine_from,
                    land,
                    h * mat.flat + lo - start,
                    count,
                    mat.flat,
                    h_s,
                    h_r.at[mat.index],
                    dev,
                )

            last = jnp.minimum(last, total)
            step = (jnp.maximum(last - first, 0) + parts - 1) // parts
            begin = first + part * step
            end = jnp.minimum(last, begin + step)
            return lax.fori_loop(begin, end, one, jnp.int32(0))

        def scatter_table(start, rows, at):
            lo = jnp.maximum(start, mine_from)
            count = jnp.maximum(jnp.minimum(start + rows, mine_to) - lo, 0)

            def one(i, sent):
                e = lax.rem(d + i, n)
                return sent + move_rows(
                    sround,
                    lo - mine_from,
                    table,
                    at + lo - start,
                    count,
                    rows,
                    h_s,
                    t_r.at[0],
                    (s, e),
                )

            return lax.fori_loop(0, jnp.where(count > 0, n, 0), one, jnp.int32(0))

        def pass_table():
            for r, (at, many) in SECTION_ROWS.items():

                @pl.when(s == r)
                def _():
                    here = table.at[pl.ds(at, many)]
                    full_wait(here, t_r.at[0])
                    for i in range(1, 4):
                        pltpu.make_async_remote_copy(
                            here,
                            here,
                            t_s,
                            t_r.at[1],
                            device_id=(lax.rem(s + i, 4), d),
                            device_id_type=MESH,
                        ).start()

        def table_arrived():
            for r in range(4):
                rest = TABLE_ROWS - SECTION_ROWS.get(r, (0, 0))[1]

                @pl.when(s == r)
                def _():
                    full_wait(table.at[pl.ds(0, rest)], t_r.at[1])

        def end_table():
            for r, (_, many) in SECTION_ROWS.items():

                @pl.when(s == r)
                def _():
                    full_wait(fill.at[pl.ds(0, 3 * many)], t_s)

        def full_wait(ref, sem):
            pltpu.make_async_copy(ref, ref, sem).wait()

        def when_row(r, body):
            return lax.cond(s == r, body, lambda: jnp.int32(0))

        sent = when_row(0, lambda: scatter_cut(IN0, ln_in0, st_in0, cu_in0))

        for slot in range(2):
            for kk in range(2):
                move(
                    img.at[slot, pl.ds(2 * kk, 2)],
                    u.at[s, pl.ds(2 * kk, 2)],
                    img_s.at[slot, kk],
                    img_r.at[s],
                    (2 * k + slot, 2 * c + kk),
                )
        for slot in range(2):
            width = (SIDE - 2 * codes[slot]).astype(F32)
            side_t[k, slot] = jnp.full((8, 128), width, F32)
        side_copy = to_twin(0, side_t.at[k], side_t.at[k])
        side_copy.start()
        snd[...] = jnp.zeros(snd.shape, F32)

        def row0():
            count = scatter_cut(MID0, ln_mid0, st_mid0, cu_mid0) + scatter_table(*RANGES[0][1:])
            count = count + scatter_table(*RANGES[1][1:]) + scatter_table(*RANGES[2][1:])
            return count + scatter_cut(SC0, ln_sc, st_sc, cu_sc)

        def row1():
            count = scatter_cut(OUT1, ln_out1, st_out1, cu_out1) + scatter_table(*RANGES[3][1:])
            return count + scatter_table(*RANGES[4][1:])

        sent = sent + when_row(0, row0)
        sent = sent + when_row(1, row1)
        sent = sent + when_row(2, lambda: scatter_table(*RANGES[5][1:]))
        sent = sent + when_row(3, lambda: scatter_table(*RANGES[6][1:]))

        def scatter_some(sent, part, parts):
            sent = sent + when_row(2, lambda: scatter_cut(MID2, ln_mid2, st_mid2, cu_mid2, part, parts))
            return sent + when_row(3, lambda: scatter_cut(OUT3, ln_out3, st_out3, cu_out3, part, parts))

        def scatter_early(sent):
            sent = sent + when_row(0, lambda: scatter_pieces(REST0, ln_rest0))
            sent = sent + when_row(1, lambda: scatter_pieces(IN1, ln_in1))
            return scatter_some(sent, 1, 3)

        def scatter_late(sent):
            sent = scatter_some(sent, 2, 3)
            sent = sent + when_row(2, lambda: scatter_pieces(REST2, ln_rest2))
            fill_up(nought, fill, sent, fill_rows, h_s)

        sent = scatter_some(sent, 0, 3)

        def spread(mat, land, stage, whole):
            @pl.when(holds(mat))
            def _():
                if mat.split == "rows":
                    full_wait(land, h_r.at[mat.index])
                    cut(mat, land, stage, 0)
                else:
                    stage_ready(mat, land, stage)
                p = piece(mat)

                def one(i, _):
                    e = lax.rem(d + i, n)
                    h = e % 2
                    dst = whole.at[:, p] if mat.split == "rows" else whole.at[p]
                    move(stage.at[h], dst, a_s.at[mat.index], c_r.at[mat.index], (s, e))
                    return 0

                lax.fori_loop(0, n, one, 0)

        def quarters(mat, whole, first, many, part=None):
            if part is None:
                span = pl.ds(first * mat.pieces, many * mat.pieces)
            else:
                half = mat.pieces // 2
                span = pl.ds(first * mat.pieces + part * half, half)
            return whole.at[:, span] if mat.split == "rows" else whole.at[span]

        def hand(mat, here, i, to):
            pltpu.make_async_remote_copy(
                here,
                here,
                f_s.at[mat.index],
                q_r.at[mat.index, i],
                device_id=(to, d),
                device_id_type=MESH,
            ).start()

        def pass_on(mat, whole):
            here = quarters(mat, whole, s, 1)
            full_wait(here, c_r.at[mat.index])
            hand(mat, here, 0, beside_x)
            hand(mat, here, 1, beside_y)

        def pass_far(mat, whole):
            full_wait(quarters(mat, whole, beside_x, 1), q_r.at[mat.index, 0])
            hand(mat, quarters(mat, whole, beside_x, 1, 0), 2, beside_y)
            full_wait(quarters(mat, whole, beside_y, 1), q_r.at[mat.index, 1])
            hand(mat, quarters(mat, whole, beside_y, 1, 1), 3, beside_x)

        def arrived(mat, whole):
            far = 3 - s
            for i in range(2):
                full_wait(quarters(mat, whole, far, 1, i), q_r.at[mat.index, 2 + i])

        def end_spread(mat, whole):
            @pl.when(holds(mat))
            def _():
                rows = mat.rows * mat.width // 256
                full_wait(fill.at[pl.ds(0, (n - 1) * rows)], a_s.at[mat.index])

            full_wait(quarters(mat, whole, 0, 3), f_s.at[mat.index])

        def spread_rest(mat, land, whole):
            @pl.when(holds(mat))
            def _():
                full_wait(land, h_r.at[mat.index])
                at = piece(mat) * mat.flat

                def one(i, _):
                    e = lax.rem(s * chips + c + i, 4 * chips)
                    move(
                        land,
                        whole.at[pl.ds(at, mat.flat)],
                        a_s.at[mat.index],
                        c_r.at[mat.index],
                        (e // chips, 2 * (e % chips)),
                    )
                    return 0

                lax.fori_loop(0, 4 * chips, one, 0)

        def share_rest(mat, whole, i):
            @pl.when(k == 0)
            def _():
                full_wait(whole, c_r.at[mat.index])
                to_twin(i, whole, whole).start()

        def rest_arrived(whole, i):
            @pl.when(k == 1)
            def _():
                to_twin(i, whole, whole).wait_recv()

        def end_rest(mat, whole, i):
            @pl.when(k == 0)
            def _():
                to_twin(i, whole, whole).wait_send()

            for kk in range(2):

                @pl.when(holds(mat) & (k == kk))
                def _():
                    rows = (4 * chips - 1 + kk) * mat.flat
                    full_wait(fill.at[pl.ds(0, rows)], a_s.at[mat.index])

        @pl.when(holds(IN0))
        def _():
            stage_ready(IN0, ln_in0, st_in0)

            def one(i, _):
                e = lax.rem(me + i, 4 * n)
                h = e % 2
                move(
                    st_in0.at[h],
                    w_in0.at[h, s * 8 + d],
                    a_s.at[0],
                    c_r.at[0],
                    (e // n, e % n),
                )
                return 0

            lax.fori_loop(0, 4 * n, one, 0)

        def shed(mat, gw, land):
            for i in range(1, 4):
                to = lax.rem(s + i, 4)
                pltpu.make_async_remote_copy(
                    gw.at[pl.ds(to * mat.pieces, mat.pieces)],
                    land.at[i - 1],
                    ga_s.at[mat.index],
                    ga_r.at[mat.index],
                    device_id=(to, d),
                    device_id_type=MESH,
                ).start()

        def shed_more(mat, gw, land, part, land2):
            full_wait(land, ga_r.at[mat.index])

            def one(i, _):
                x = gw[s * mat.pieces + i].astype(F32)
                for j in range(3):
                    x = x + land[j, i].astype(F32)
                part[i] = x.astype(BF16)
                move(
                    part.at[i],
                    land2.at[c, k],
                    gb_s.at[mat.index],
                    gb_r.at[mat.index],
                    (s, mat.first + mat.step * i),
                )
                return 0

            lax.fori_loop(0, mat.pieces, one, 0)

        def home_rows(src, src_at, start, rows, limit, r, active):
            left = jnp.int32(0)
            for i in range((rows + shard_rows - 2) // shard_rows + 1):
                owner = start // shard_rows + i
                lo = jnp.maximum(start, owner * shard_rows)
                hi = jnp.minimum(jnp.minimum(start + rows, limit), (owner + 1) * shard_rows)
                count = jnp.where(active, jnp.maximum(hi - lo, 0), 0)
                owner = jnp.minimum(owner, n - 1)

                def go():
                    return move_rows(
                        src,
                        src_at + lo - start,
                        out_w,
                        lo - owner * shard_rows,
                        count,
                        rows,
                        gc_s,
                        gc_r,
                        (r, owner),
                    )

                left = left + lax.cond(count > 0, go, lambda: jnp.int32(0))
            return left

        def home(mat, land2, flat):
            @pl.when(holds(mat))
            def _():
                full_wait(land2, gb_r.at[mat.index])
                for h in range(2):
                    x = jnp.sum(land2[:, h].astype(F32), axis=0)
                    for j in range(mat.width // 128):
                        if mat.split == "rows":
                            at = h * mat.flat + j
                        else:
                            at = h * (mat.blocks // 2) + j
                        flat[pl.ds(at, mat.rows, stride=mat.blocks), :] = x[:, 128 * j : 128 * (j + 1)]

            p = piece(mat)
            left = home_rows(
                flat, 0, mat.start + p * mat.flat, mat.flat, USED[mat.row], mat.row, holds(mat)
            )
            if mat.split == "rows":
                p = p + 4 * mat.pieces
                left = left + home_rows(
                    flat,
                    mat.flat,
                    mat.start + p * mat.flat,
                    mat.flat,
                    USED[mat.row],
                    mat.row,
                    holds(mat),
                )
            return left

        def end_shed(mat, gw, land):
            full_wait(land, ga_s.at[mat.index])

            @pl.when(holds(mat))
            def _():
                full_wait(gw.at[pl.ds(0, mat.pieces - 1)], gb_s.at[mat.index])

            @pl.when(jnp.logical_not(holds(mat)))
            def _():
                full_wait(gw.at[pl.ds(0, mat.pieces)], gb_s.at[mat.index])

        def rest_meet(i, mat, rg, land):
            @pl.when((s == mat.row) & (d < 8))
            def _():
                pltpu.make_async_remote_copy(
                    rg.at[pl.ds(REST_PART * d, REST_PART)],
                    land,
                    v_s.at[i],
                    v_r.at[i],
                    device_id=(s + 1, d),
                    device_id_type=MESH,
                ).start()

        def rest_home(i, mat, rg, land, flat):
            active = (s == mat.row + 1) & (d < 8)
            at = REST_PART * jnp.minimum(d, 7)

            @pl.when(active)
            def _():
                full_wait(land, v_r.at[i])
                flat[...] = rg[pl.ds(at, REST_PART), :] + land[...]

            return home_rows(
                flat, 0, mat.start + at, REST_PART, mat.start + REST_ROWS, mat.row, active
            )

        def table_meet(i, first, rows):
            @pl.when((s == 0) & (d < 2))
            def _():
                pltpu.make_async_remote_copy(
                    gvt.at[pl.ds(first, rows)],
                    gvl.at[pl.ds(first, rows)],
                    v_s.at[i],
                    v_r.at[i],
                    device_id=(s + 1, d),
                    device_id_type=MESH,
                ).start()

        def table_home(i, first, rows):
            active = (s == 1) & (d < 2)

            @pl.when(active)
            def _():
                span = pl.ds(first, rows)
                full_wait(gvl.at[span], v_r.at[i])
                gvs[first : first + rows, :] = gvt[first : first + rows, :] + gvl[first : first + rows, :]

            left = jnp.int32(0)
            for (r, _), (at, start, many) in TABLE.items():
                if first <= at < first + rows:
                    left = left + home_rows(
                        gvs,
                        at + many * k,
                        start + many * k,
                        many,
                        start + 2 * many,
                        r,
                        active,
                    )
            return left

        def put(ph, base, value):
            for j in range(value.shape[1] // 128):
                snd[ph, base + j : base + j + 1, :] = value[:, 128 * j : 128 * (j + 1)]

        def send(ph, rows, both=False):
            def one(o, _):
                pltpu.make_async_remote_copy(
                    snd.at[ph, pl.ds(0, rows)],
                    rcv.at[ph, k, o, pl.ds(0, rows)],
                    ssem.at[ph],
                    rsem.at[ph, k],
                    device_id=peer(o, k),
                    device_id_type=MESH,
                ).start()
                return 0

            def other(o, _):
                pltpu.make_async_remote_copy(
                    snd.at[ph, pl.ds(0, rows)],
                    rcv.at[ph, k, o, pl.ds(0, rows)],
                    ssem.at[ph],
                    rsem.at[ph, k],
                    device_id=peer(o, 1 - k),
                    device_id_type=MESH,
                ).start()
                return 0

            lax.fori_loop(1, n, one, 0)
            if both:
                lax.fori_loop(0, n, other, 0)
            rcv[ph, k, 0, 0:rows] = snd[ph, 0:rows]

        def receive(ph, rows, both=False):
            mine = rcv.at[ph, k, pl.ds(1, n - 1), pl.ds(0, rows)]
            pltpu.make_async_copy(mine, mine, rsem.at[ph, k]).wait()
            if both:
                theirs = rcv.at[ph, 1 - k, :, pl.ds(0, rows)]
                pltpu.make_async_copy(theirs, theirs, rsem.at[ph, 1 - k]).wait()

        def end_send(ph, rows, both=False):
            many = 2 * n - 1 if both else n - 1
            full_wait(fill.at[pl.ds(0, many * rows)], ssem.at[ph])

        def totals(ph, rows):
            return jnp.sum(rcv[ph, k, :, 0:rows, :], axis=0)

        def row(total, base, width):
            return jnp.concatenate(
                [total[base + j : base + j + 1, :] for j in range(width // 128)], axis=1
            )

        def across(ph, h, base, width):
            return jnp.concatenate(
                [rcv[ph, h, :, base + j, :] for j in range(width // 128)], axis=1
            )

        def rows_of(ref, at, many):
            return jnp.concatenate([ref[pl.ds(at + j, 1), :] for j in range(many)], axis=1)

        def vrow(key):
            at, _, many = TABLE[key]
            return rows_of(table, at + many * k, many)

        def set_gvec(key, value):
            at, _, many = TABLE[key]
            for j in range(many):
                gvt[pl.ds(at + many * k + j, 1), :] = value[:, 128 * j : 128 * (j + 1)]

        def set_rows(ref, at, value):
            for j in range(value.shape[1] // 128):
                ref[at + j : at + j + 1, :] = value[:, 128 * j : 128 * (j + 1)]

        def mean_rstd(total, base, width, count):
            mu = row(total, base, width) / count
            second = row(total, base + width // 128, width) / count
            return mu, lax.rsqrt(jnp.maximum(second - mu * mu, 0.0) + EPS)

        gvt[...] = jnp.zeros(gvt.shape, F32)

        side_copy.wait()
        side_row = jnp.where(
            m == 0, side_t[s // 2, 0, 0:1, :], side_t[s // 2, 1, 0:1, :]
        )
        pixel = lax.broadcasted_iota(jnp.int32, (PX, 128), 0)
        prow = (pixel // SIDE).astype(F32)
        pcol = (pixel % SIDE).astype(F32)
        mref[...] = jnp.where((prow < side_row) & (pcol < side_row), 1.0, 0.0)
        inv_own = 1.0 / (side_row * side_row)

        for q in range(4):
            here = u.at[q, pl.ds(2 * k, 2)]
            pltpu.make_async_copy(here, here, img_r.at[q]).wait()
            pltpu.make_async_remote_copy(
                here,
                here,
                bs.at[10 + q],
                br.at[10 + q],
                device_id=(s, 2 * c + 1 - k),
                device_id_type=MESH,
            ).start()
        spread(MID0, ln_mid0, st_mid0, w_mid0)
        for q in range(4):
            here = u.at[q, pl.ds(2 * (1 - k), 2)]
            pltpu.make_async_copy(here, here, br.at[10 + q]).wait()

        def mask_block(b, _):
            r = pl.multiple_of(b * 32, 32)
            rows = pl.ds(r, 32)
            mask = mref[rows, :]
            for q in range(4):
                total = jnp.zeros((32, 128), F32)
                for p in range(4):
                    x = u[q, p, rows, :].astype(F32) * mask
                    um[p, rows, 128 * q : 128 * (q + 1)] = x.astype(BF16)
                    total = total + x
                pool[rows, 128 * q : 128 * (q + 1)] = (total * 0.25).astype(BF16)
            return 0

        lax.fori_loop(0, 8, mask_block, 0)
        pass_table()
        pass_on(MID0, w_mid0)
        full_wait(w_in0.at[k], c_r.at[0])

        def z1_block(p, carry):
            z = dot(um[p], w_in0[k].reshape(CIN, 128))
            z1[p] = z
            return (carry[0] + fold8(z), carry[1] + fold8(z * z))

        zero8 = jnp.zeros((8, 128), F32)
        t0, t1 = lax.fori_loop(0, 4, z1_block, (zero8, zero8))
        put(0, 0, jnp.sum(t0, axis=0, keepdims=True))
        put(0, 1, jnp.sum(t1, axis=0, keepdims=True))
        put(0, 2, side_row)
        send(0, 8)
        sent = scatter_early(sent)
        pass_far(MID0, w_mid0)
        spread(SC0, ln_sc, st_sc, w_sc)
        spread(OUT1, ln_out1, st_out1, w_out1)
        table_arrived()
        receive(0, 8)
        total = totals(0, 8)
        sides = across(0, k, 2, 128)
        inv_area = 1.0 / (sides * sides)
        count1 = jnp.sum(sides * sides, axis=0, keepdims=True)
        counts = {w: lanes(count1, w // 128) for w in (128, 256, 512)}
        mu1, rs1 = mean_rstd(total, 0, 128, 4.0 * count1)
        lin1 = rs1 * vrow((0, "g_in"))
        off1 = vrow((0, "b_in")) - mu1 * lin1

        colpos = lax.broadcasted_iota(jnp.int32, (PX, 128), 0) % SIDE

        def shift_cols(x, by):
            moved = pltpu.roll(x, by % PX, 0)
            edge = 0 if by == 1 else SIDE - 1
            return jnp.where(colpos == edge, 0.0, moved)

        def store_tap(cols, di, dj, x, shift):
            at = 128 * (3 * di + dj)
            span = slice(at, at + 128)
            x = x.astype(BF16)
            if shift == 1:
                cols[0:SIDE, span] = jnp.zeros((SIDE, 128), BF16)
                cols[SIDE:PX, span] = x[0 : PX - SIDE]
            elif shift == -1:
                cols[PX - SIDE : PX, span] = jnp.zeros((SIDE, 128), BF16)
                cols[0 : PX - SIDE, span] = x[SIDE:PX]
            else:
                cols[:, span] = x

        def plane_taps(parity):
            return ((1, 0),) if parity == 0 else ((0, 1), (2, 0))

        for p in range(4):
            v = z1[p] * lin1 + off1
            h = v * sigmoid(v) * mref[...]
            for dj, cshift in plane_taps(p % 2):
                x = shift_cols(h, 1) if cshift else h
                for di, rshift in plane_taps(p // 2):
                    store_tap(cols1, di, dj, x, rshift)

        def conv_forward(ph, cols, w_mid, zref):
            z = dot(cols[...], w_mid[...].reshape(1152, 256))
            zref[...] = z
            zm = z * lanes(mref[...], 2)
            put(ph, 0, jnp.sum(zm, axis=0, keepdims=True))
            put(ph, 2, jnp.sum(zm * z, axis=0, keepdims=True))
            send(ph, 8)

        def small(rest):
            w_sq = rest[AT_SQ : AT_SQ + CMID, :]
            w_ex = jnp.concatenate(
                [rest[pl.ds(AT_EX + j, CSQ, stride=4), :] for j in range(4)], axis=1
            )
            return w_sq, w_ex

        def attention_forward(ph, twin, total, at, rest, zref, rr, aref, beside):
            mu, rs = mean_rstd(total, 0, 256, counts[256])
            lin = rs * rows_of(table, at + 2 * k, 2)
            off = rows_of(table, at + 4 + 2 * k, 2) - mu * lin

            def block(b, acc):
                rows = pl.ds(pl.multiple_of(b * 64, 64), 64)
                v = zref[rows, :] * lin + off
                r = v * sigmoid(v) * lanes(mref[rows, :], 2)
                rr[k, rows, :] = r
                return acc + fold8(r)

            acc = lax.fori_loop(0, 4, block, jnp.zeros((8, 256), F32))
            pooled_own = jnp.sum(acc, axis=0, keepdims=True) * lanes(inv_own, 2)
            put(ph, 0, pooled_own)
            send(ph, 8, both=True)
            swap = to_twin(twin, rr.at[k], rr.at[k])
            swap.start()
            beside()
            receive(ph, 8, both=True)
            w_sq, w_ex = small(rest)
            pooled = across(ph, 0, 0, 256) + across(ph, 1, 0, 256)
            zq = dot_hi(pooled, w_sq)
            mq = jnp.mean(zq, axis=0, keepdims=True)
            vq = jnp.mean(zq * zq, axis=0, keepdims=True) - mq * mq
            rq = lax.rsqrt(jnp.maximum(vq, 0.0) + EPS)
            hq = (zq - mq) * rq
            nq = hq * rows_of(rest, AT_GSQ, 1) + rows_of(rest, AT_BSQ, 1)
            sgq = sigmoid(nq)
            qq = nq * sgq
            logits = dot_hi(qq, w_ex) + rows_of(rest, AT_BEX, 4)
            diff = logits[:, 0:256] - logits[:, 256:512]
            sh0 = sigmoid(diff)
            sh1 = sigmoid(-diff)
            swap.wait()
            s0 = sh0[0:1, :]
            s1 = sh1[0:1, :]

            def mix(b, _):
                rows = pl.ds(pl.multiple_of(b * 64, 64), 64)
                aref[rows, :] = (s0 * rr[0, rows, :] + s1 * rr[1, rows, :]).astype(BF16)
                return 0

            lax.fori_loop(0, 4, mix, 0)
            return (mu, rs, lin, off), (pooled, rq, hq, nq, sgq, qq, sh0, sh1)

        def attention_backward(
            ph, kept_mid, kept_q, rest, rg, zref, rr, cols, mat, gw_mid, ga_mid, da, beside
        ):
            mu, rs, lin, off = kept_mid
            pooled, rq, hq, nq, sgq, qq, sh0, sh1 = kept_q

            def block(b, acc):
                rows = pl.ds(pl.multiple_of(b * 32, 32), 32)
                z = zref[rows, :]
                v = z * lin + off
                hat = (z - mu) * rs
                sg = sigmoid(v)
                sp = sg * (1.0 + v * (1.0 - sg)) * lanes(mref[rows, :], 2)
                grad = da(rows)
                t = grad * sp
                dbuf[rows, :] = grad
                spb[rows, :] = sp
                r = rr[k, rows, :]
                return tuple(
                    x + fold8(y)
                    for x, y in zip(acc, (grad * r, t, sp, t * hat, sp * hat))
                )

            acc = lax.fori_loop(0, 8, block, (jnp.zeros((8, 256), F32),) * 5)
            for j, x in enumerate(acc):
                put(ph, 2 * j, jnp.sum(x, axis=0, keepdims=True))
            send(ph, 16, both=True)
            beside()
            receive(ph, 16, both=True)
            ds0 = across(ph, 0, 0, 256)
            ds1 = across(ph, 1, 0, 256)
            mean = sh0 * ds0 + sh1 * ds1
            dl = jnp.concatenate([sh0 * (ds0 - mean), sh1 * (ds1 - mean)], axis=1)
            w_sq, w_ex = small(rest)
            set_rows(rg, AT_BEX, jnp.sum(dl, axis=0, keepdims=True))
            dq = dot_hi(dl, w_ex, ((1,), (1,)))
            dn = dq * sgq * (1.0 + nq * (1.0 - sgq))
            set_rows(rg, AT_GSQ, jnp.sum(dn * hq, axis=0, keepdims=True))
            set_rows(rg, AT_BSQ, jnp.sum(dn, axis=0, keepdims=True))
            dn = dn * rows_of(rest, AT_GSQ, 1)
            dzq = rq * (
                dn
                - jnp.mean(dn, axis=0, keepdims=True)
                - hq * jnp.mean(dn * hq, axis=0, keepdims=True)
            )
            dpool = dot_hi(dzq, w_sq, ((1,), (1,))) * lanes(inv_area, 2)
            share = jnp.where(k == 0, sh0, sh1)

            def both_sums(h, part, first, second):
                return jnp.sum(
                    part * across(ph, h, first, 256) + dpool * across(ph, h, second, 256),
                    axis=0,
                    keepdims=True,
                )

            sums = [(both_sums(h, x, 2, 4), both_sums(h, x, 6, 8)) for h, x in enumerate((sh0, sh1))]
            for h in range(2):
                set_rows(rg, 2 * h, sums[h][1])
                set_rows(rg, 4 + 2 * h, sums[h][0])
            sdv = jnp.where(k == 0, sums[0][0], sums[1][0])
            sdh = jnp.where(k == 0, sums[0][1], sums[1][1])
            own_share = share[0:1, :]
            own_pool = dpool[0:1, :]
            c1 = sdv / counts[256]
            c2 = sdh / counts[256]

            def block2(b, _):
                rows = pl.ds(pl.multiple_of(b * 32, 32), 32)
                hat = (zref[rows, :] - mu) * rs
                dv = (own_share * dbuf[rows, :] + own_pool) * spb[rows, :]
                dz = lin * (dv - c1 - hat * c2) * lanes(mref[rows, :], 2)
                rows_low[rows, :] = dz.astype(BF16)
                return 0

            rows_low = dz_low
            lax.fori_loop(0, 8, block2, 0)

            def rest():
                gw_mid[...] = dot_lt(cols[...], dz_low[...]).astype(BF16).reshape(24, 48, 256)
                shed(mat, gw_mid, ga_mid)
                g_ex = dot_hi(qq, dl, ((0,), (0,)))
                for j in range(4):
                    rg[pl.ds(AT_EX + j, CSQ, stride=4), :] = g_ex[:, 128 * j : 128 * (j + 1)]
                rg[AT_SQ : AT_SQ + CMID, :] = dot_hi(pooled, dzq, ((0,), (0,)))

            return rest

        dz_low = dz3.at[:, pl.ds(0, 256)]

        arrived(MID0, w_mid0)
        conv_forward(1, cols1, w_mid0, z2)
        spread_rest(REST0, ln_rest0, rest0)
        scatter_late(sent)
        pass_on(SC0, w_sc)
        pass_on(OUT1, w_out1)
        spread(IN1, ln_in1, st_in1, w_in1)
        receive(1, 8)

        def short_forward():
            share_rest(REST0, rest0, 15)
            pass_far(SC0, w_sc)
            pass_far(OUT1, w_out1)
            pass_on(IN1, w_in1)
            spread(MID2, ln_mid2, st_mid2, w_mid2)
            arrived(SC0, w_sc)
            z = dot(pool[...], w_sc[...].reshape(CIN, 512))
            zs[...] = z
            put(3, 8, jnp.sum(z, axis=0, keepdims=True))
            put(3, 12, jnp.sum(z * z, axis=0, keepdims=True))
            rest_arrived(rest0, 15)

        mid1, q1 = attention_forward(2, 2, totals(1, 8), AT_MID[0], rest0, z2, rr1, a1, short_forward)
        arrived(OUT1, w_out1)

        def wide_forward(ph, rows, aref, w, zref):
            z = dot(aref[...], w[...].reshape(CMID, 512))
            zref[...] = z
            put(ph, 0, jnp.sum(z, axis=0, keepdims=True))
            put(ph, 4, jnp.sum(z * z, axis=0, keepdims=True))
            send(ph, rows)

        wide_forward(3, 16, a1, w_out1, z3)
        pass_far(IN1, w_in1)
        pass_on(MID2, w_mid2)
        receive(3, 16)
        total = totals(3, 16)
        mus, rss = mean_rstd(total, 8, 512, counts[512])
        lins = rss * vrow((0, "g_sc"))
        offs = vrow((0, "b_sc")) - mus * lins

        mu3, rs3 = mean_rstd(total, 0, 512, counts[512])
        lin3 = rs3 * vrow((1, "g_out"))
        off3 = vrow((1, "b_out")) - mu3 * lin3

        def y1_block(b, _):
            rows = pl.ds(pl.multiple_of(b * 32, 32), 32)
            short = (zs[rows, :] * lins + offs).astype(BF16).astype(F32)
            v = z3[rows, :] * lin3 + off3 + short
            v3[rows, :] = v
            y1[rows, :] = (v * sigmoid(v) * lanes(mref[rows, :], 4)).astype(BF16)
            return 0

        lax.fori_loop(0, 8, y1_block, 0)
        arrived(IN1, w_in1)
        pz[0] = dot(y1[...], w_in1[1 - k].reshape(512, 128))
        swap = to_twin(3, pz.at[0], pz.at[1])
        swap.start()
        z = dot(y1[...], w_in1[k].reshape(512, 128))
        swap.wait()
        z = z + pz[1]
        z4[...] = z
        put(4, 0, jnp.sum(z, axis=0, keepdims=True))
        put(4, 1, jnp.sum(z * z, axis=0, keepdims=True))
        send(4, 8)
        pass_far(MID2, w_mid2)
        spread_rest(REST2, ln_rest2, rest2)
        spread(OUT3, ln_out3, st_out3, w_out3)
        receive(4, 8)
        mu4, rs4 = mean_rstd(totals(4, 8), 0, 128, count1)
        lin4 = rs4 * vrow((1, "g_in"))
        off4 = vrow((1, "b_in")) - mu4 * lin4
        v = z4[...] * lin4 + off4
        h = v * sigmoid(v) * mref[...]
        for dj in range(3):
            x = h if dj == 1 else shift_cols(h, 1 - dj)
            for di in range(3):
                store_tap(cols2, di, dj, x, 1 - di)

        arrived(MID2, w_mid2)
        conv_forward(5, cols2, w_mid2, z5)
        share_rest(REST2, rest2, 16)
        pass_on(OUT3, w_out3)
        receive(5, 8)

        def last_weights():
            pass_far(OUT3, w_out3)
            rest_arrived(rest2, 16)
            for slot in range(2):
                move(
                    cot.at[slot],
                    ctb.at[lax.rem(s, 2)],
                    ct_s.at[slot],
                    ct_r.at[lax.rem(s, 2)],
                    (2 * k + slot, 2 * c + s // 2),
                )
            to_twin(14, w_in0.at[k], w_in0.at[k]).start()

        mid2, q2 = attention_forward(6, 4, totals(5, 8), AT_MID[2], rest2, z5, rr2, a2, last_weights)
        arrived(OUT3, w_out3)
        wide_forward(7, 8, a2, w_out3, z6)
        to_twin(14, w_in0.at[k], w_in0.at[k]).wait()
        for i in range(2):
            pltpu.make_async_copy(ctb.at[i], ctb.at[i], ct_r.at[i]).wait()
        receive(7, 8)
        mu6, rs6 = mean_rstd(totals(7, 8), 0, 512, counts[512])
        lin6 = rs6 * vrow((3, "g_out"))
        off6 = vrow((3, "b_out")) - mu6 * lin6

        def out_block(b, acc):
            rows = pl.ds(pl.multiple_of(b * 32, 32), 32)
            z = z6[rows, :]
            mask = lanes(mref[rows, :], 4)
            v = z * lin6 + off6 + y1[rows, :].astype(F32)
            sg = sigmoid(v)
            y = (v * sg * mask).astype(BF16)
            obuf[0, rows, :] = y[:, 0:256]
            obuf[1, rows, :] = y[:, 256:512]
            ct = jnp.concatenate([ctb[0, rows, :], ctb[1, rows, :]], axis=1).astype(F32)
            dv = ct * (sg * (1.0 + v * (1.0 - sg)) * mask)
            dv6[rows, :] = dv
            return (acc[0] + fold8(dv), acc[1] + fold8(dv * ((z - mu6) * rs6)))

        zero512 = jnp.zeros((8, 512), F32)
        t0, t1 = lax.fori_loop(0, 8, out_block, (zero512, zero512))
        put(8, 0, jnp.sum(t0, axis=0, keepdims=True))
        put(8, 4, jnp.sum(t1, axis=0, keepdims=True))
        send(8, 8)
        for j in range(2):
            move(
                obuf.at[j],
                out_o.at[lax.rem(s, 2)],
                oo_s.at[j],
                oo_r.at[lax.rem(s, 2)],
                (2 * k + j, 2 * c + s // 2),
            )
        for mat, whole in ((MID0, w_mid0), (SC0, w_sc), (OUT1, w_out1)):
            end_spread(mat, whole)
        end_rest(REST0, rest0, 15)
        end_table()
        receive(8, 8)

        def wide_back(total, base, key_g, key_b, lin, mu, rs, zref, dvf, dst):
            sdv = row(total, base, 512)
            sdh = row(total, base + 4, 512)
            set_gvec(key_b, sdv)
            set_gvec(key_g, sdh)
            c1 = sdv / counts[512]
            c2 = sdh / counts[512]

            def block(b, _):
                rows = pl.ds(pl.multiple_of(b * 32, 32), 32)
                hat = (zref[rows, :] - mu) * rs
                dz = lin * (dvf(rows) - c1 - hat * c2) * lanes(mref[rows, :], 4)
                dst[rows, :] = dz.astype(BF16)
                return 0

            lax.fori_loop(0, 8, block, 0)

        wide_back(
            totals(8, 8),
            0,
            (3, "g_out"),
            (3, "b_out"),
            lin6,
            mu6,
            rs6,
            z6,
            lambda rows: dv6[rows, :],
            dz3,
        )

        def attended_grad(twin, w, aref, mat, gw, land):
            pda[0] = dot_rt(dz3[...], w[...].reshape(CMID, 512))
            swap = to_twin(twin, pda.at[0], pda.at[1])
            swap.start()
            gw[...] = dot_lt(aref[...], dz3[...]).astype(BF16).reshape(16, 16, 512)
            shed(mat, gw, land)
            swap.wait()

        def summed_grad(rows):
            return (pda[0, rows, :] + pda[1, rows, :]).astype(BF16).astype(F32)

        attended_grad(5, w_out3, a2, OUT3, gw_out3, ga_out3)

        def beside9():
            for mat, whole in ((IN1, w_in1), (MID2, w_mid2), (OUT3, w_out3)):
                end_spread(mat, whole)
            end_rest(REST2, rest2, 16)
            shed_more(OUT3, gw_out3, ga_out3, gp_out3, gb_out3)

        grad_rest2 = attention_backward(
            9,
            mid2,
            q2,
            rest2,
            rg2,
            z5,
            rr2,
            cols2,
            MID2,
            gw_mid2,
            ga_mid2,
            summed_grad,
            beside9,
        )

        ep[...] = jnp.zeros(ep.shape, F32)
        for di in range(3):
            part = dot_rt(dz_low[...], w_mid2[8 * di : 8 * (di + 1)].reshape(384, 256))
            for dj in range(3):
                lo = SIDE * di
                ep[dj, lo : lo + PX, :] += part[:, 128 * dj : 128 * (dj + 1)]
        grad = ep[1, SIDE : SIDE + PX, :]
        grad = grad + shift_cols(ep[0, SIDE : SIDE + PX, :], -1)
        grad = grad + shift_cols(ep[2, SIDE : SIDE + PX, :], 1)
        grad = grad.astype(BF16).astype(F32)
        v = z4[...] * lin4 + off4
        hat4 = (z4[...] - mu4) * rs4
        sg = sigmoid(v)
        dv4 = grad * (sg * (1.0 + v * (1.0 - sg)) * mref[...])
        dh[0] = dv4
        put(10, 0, jnp.sum(dv4, axis=0, keepdims=True))
        put(10, 1, jnp.sum(dv4 * hat4, axis=0, keepdims=True))
        send(10, 8)
        grad_rest2()
        rest_meet(2, REST2, rg2, rl2)
        left = home(OUT3, gb_out3, gf_out3)
        receive(10, 8)
        total = totals(10, 8)
        set_gvec((1, "b_in"), total[0:1, :])
        set_gvec((1, "g_in"), total[1:2, :])
        hat4 = (z4[...] - mu4) * rs4
        dz = lin4 * (dh[0] - total[0:1, :] / count1 - hat4 * (total[1:2, :] / count1)) * mref[...]
        dz4[k] = dz.astype(BF16)
        swap = to_twin(6, dz4.at[k], dz4.at[k])
        swap.start()
        swap.wait()

        def dy_block(b, acc):
            rows = pl.ds(pl.multiple_of(b * 64, 64), 64)
            dy = dot_rt(dz4[0, rows, :], w_in1[0].reshape(512, 128))
            dy = dy + dot_rt(dz4[1, rows, :], w_in1[1].reshape(512, 128))
            dy = dy + dv6[rows, :].astype(BF16).astype(F32)
            v = v3[rows, :]
            sg = sigmoid(v)
            dv = dy * (sg * (1.0 + v * (1.0 - sg)) * lanes(mref[rows, :], 4))
            v3[rows, :] = dv
            low = dv.astype(BF16).astype(F32)
            hat = (z3[rows, :] - mu3) * rs3
            hats = (zs[rows, :] - mus) * rss
            return tuple(
                x + fold8(y) for x, y in zip(acc, (dv, dv * hat, low, low * hats))
            )

        acc = lax.fori_loop(0, 4, dy_block, (zero512,) * 4)
        for j, x in enumerate(acc):
            put(11, 4 * j, jnp.sum(x, axis=0, keepdims=True))
        send(11, 16)
        both4 = jnp.concatenate([dz4[0], dz4[1]], axis=1)
        gw_in1[...] = dot_lt(y1[...], both4).astype(BF16).reshape(32, 16, 256)
        shed(IN1, gw_in1, ga_in1)
        shed_more(MID2, gw_mid2, ga_mid2, gp_mid2, gb_mid2)
        left = left + rest_home(2, REST2, rg2, rl2, rf2)
        receive(11, 16)
        total = totals(11, 16)
        wide_back(
            total,
            0,
            (1, "g_out"),
            (1, "b_out"),
            lin3,
            mu3,
            rs3,
            z3,
            lambda rows: v3[rows, :],
            dz3,
        )
        wide_back(
            total,
            8,
            (0, "g_sc"),
            (0, "b_sc"),
            lins,
            mus,
            rss,
            zs,
            lambda rows: v3[rows, :].astype(BF16).astype(F32),
            dzs,
        )
        attended_grad(7, w_out1, a1, OUT1, gw_out1, ga_out1)

        def short_back():
            part = dot_rt(dzs[...], w_sc[...].reshape(CIN, 512))
            pdp[0] = jnp.where(k == 0, part[:, 256:512], part[:, 0:256])
            to_twin(8, pdp.at[0], pdp.at[1]).start()
            pdp[2] = jnp.where(k == 0, part[:, 0:256], part[:, 256:512])
            gw_sc[...] = dot_lt(pool[...], dzs[...]).astype(BF16).reshape(32, 16, 512)
            shed(SC0, gw_sc, ga_sc)
            table_meet(0, 4, TABLE_ROWS - 4)
            shed_more(IN1, gw_in1, ga_in1, gp_in1, gb_in1)
            shed_more(OUT1, gw_out1, ga_out1, gp_out1, gb_out1)

        grad_rest0 = attention_backward(
            12,
            mid1,
            q1,
            rest0,
            rg0,
            z2,
            rr1,
            cols1,
            MID0,
            gw_mid0,
            ga_mid0,
            summed_grad,
            short_back,
        )

        for p in range(4):
            dh[p] = jnp.zeros((PX, 128), F32)
        for di in range(3):
            part = dot_rt(dz_low[...], w_mid0[8 * di : 8 * (di + 1)].reshape(384, 256))
            pr = 0 if di == 1 else 1
            for dj in range(3):
                x = part[:, 128 * dj : 128 * (dj + 1)]
                if dj == 0:
                    x = shift_cols(x, -1)
                p = 2 * pr + (0 if dj == 1 else 1)
                if di == 0:
                    dh[p, 0 : PX - SIDE, :] += x[SIDE:PX]
                else:
                    dh[p] += x

        def dv1_block(p, acc):
            z = z1[p]
            v = z * lin1 + off1
            sg = sigmoid(v)
            dv = dh[p] * (sg * (1.0 + v * (1.0 - sg)) * mref[...])
            dh[p] = dv
            return (acc[0] + fold8(dv), acc[1] + fold8(dv * ((z - mu1) * rs1)))

        t0, t1 = lax.fori_loop(0, 4, dv1_block, (zero8, zero8))
        put(13, 0, jnp.sum(t0, axis=0, keepdims=True))
        put(13, 1, jnp.sum(t1, axis=0, keepdims=True))
        send(13, 8)
        grad_rest0()
        rest_meet(1, REST0, rg0, rl0)
        shed_more(SC0, gw_sc, ga_sc, gp_sc, gb_sc)
        left = left + home(MID2, gb_mid2, gf_mid2)
        left = left + home(IN1, gb_in1, gf_in1)
        left = left + home(OUT1, gb_out1, gf_out1)
        left = left + table_home(0, 4, TABLE_ROWS - 4)
        receive(13, 8)
        total = totals(13, 8)
        set_gvec((0, "b_in"), total[0:1, :])
        set_gvec((0, "g_in"), total[1:2, :])
        table_meet(3, 0, 4)
        k1 = total[0:1, :] / (4.0 * count1)
        k2 = total[1:2, :] / (4.0 * count1)

        def dz1_block(p, _):
            hat = (z1[p] - mu1) * rs1
            dz1[k, p] = (lin1 * (dh[p] - k1 - hat * k2) * mref[...]).astype(BF16)
            return 0

        lax.fori_loop(0, 4, dz1_block, 0)
        swap = to_twin(9, dz1.at[k], dz1.at[k])
        swap.start()
        total = jnp.zeros((CIN, 128), F32)
        for p in range(4):
            total = total + dot_lt(um[p], dz1[k, p])
        gw_in0[...] = total.astype(BF16).reshape(32, 16, 128)

        def shed_in0(i, _):
            p = lax.rem(8 * s + i, 32)
            move(
                gw_in0.at[p],
                gb_in0.at[s * chips + c, k],
                gb_s.at[0],
                gb_r.at[0],
                (p // 8, p % 8),
            )
            return 0

        lax.fori_loop(0, 32, shed_in0, 0)
        shed_more(MID0, gw_mid0, ga_mid0, gp_mid0, gb_mid0)
        swap.wait()
        to_twin(8, pdp.at[0], pdp.at[1]).wait()

        def du_block(p, _):
            mine = pl.ds(16 * k, 16)
            grad = dot_rt(dz1[0, p], w_in0[0, mine].reshape(256, 128))
            grad = grad + dot_rt(dz1[1, p], w_in0[1, mine].reshape(256, 128))
            grad = (grad + 0.25 * (pdp[1] + pdp[2])) * lanes(mref[...], 2)
            low = grad.astype(BF16)
            ibuf[0, p] = low[:, 0:128]
            ibuf[1, p] = low[:, 128:256]
            return 0

        lax.fori_loop(0, 4, du_block, 0)
        for j in range(2):
            move(
                ibuf.at[j],
                out_i.at[lax.rem(s, 2)],
                oi_s.at[j],
                oi_r.at[lax.rem(s, 2)],
                (2 * k + j, 2 * c + s // 2),
            )

        left = left + home(SC0, gb_sc, gf_sc)
        left = left + rest_home(1, REST0, rg0, rl0, rf0)
        left = left + table_home(3, 0, 4)
        left = left + home(IN0, gb_in0, gf_in0)
        left = left + home(MID0, gb_mid0, gf_mid0)

        for mat, gw, land in (
            (MID0, gw_mid0, ga_mid0),
            (SC0, gw_sc, ga_sc),
            (OUT1, gw_out1, ga_out1),
            (IN1, gw_in1, ga_in1),
            (MID2, gw_mid2, ga_mid2),
            (OUT3, gw_out3, ga_out3),
        ):
            end_shed(mat, gw, land)

        @pl.when(holds(IN0))
        def _():
            full_wait(gw_in0.at[pl.ds(0, 31)], gb_s.at[0])
            full_wait(fill.at[pl.ds(0, 8 * (4 * n - 1))], a_s.at[0])

        @pl.when(jnp.logical_not(holds(IN0)))
        def _():
            full_wait(gw_in0, gb_s.at[0])

        for i, mat, land in ((1, REST0, rl0), (2, REST2, rl2)):

            @pl.when((s == mat.row) & (d < 8))
            def _():
                full_wait(land, v_s.at[i])

        @pl.when((s == 0) & (d < 2))
        def _():
            full_wait(gvl.at[pl.ds(4, TABLE_ROWS - 4)], v_s.at[0])
            full_wait(gvl.at[pl.ds(0, 4)], v_s.at[3])

        fill_up(nought, fill2, left, HOME_ROWS, gc_s)
        full_wait(fill2, gc_s)
        full_wait(fill, h_s)
        full_wait(out_w, gc_r)
        for slot in range(2):
            pltpu.make_async_copy(out_o.at[slot], out_o.at[slot], oo_r.at[slot]).wait()
            pltpu.make_async_copy(out_i.at[slot], out_i.at[slot], oi_r.at[slot]).wait()
        for slot in range(2):
            for kk in range(2):
                end_move(
                    img.at[slot, pl.ds(2 * kk, 2)],
                    img_s.at[slot, kk],
                    (2 * k + slot, 2 * c + kk),
                )
            end_move(cot.at[slot], ct_s.at[slot], (2 * k + slot, 2 * c + s // 2))
        for j in range(2):
            end_move(obuf.at[j], oo_s.at[j], (2 * k + j, 2 * c + s // 2))
            end_move(ibuf.at[j], oi_s.at[j], (2 * k + j, 2 * c + s // 2))
        for q in range(4):
            here = u.at[q, pl.ds(2 * k, 2)]
            pltpu.make_async_copy(here, here, bs.at[10 + q]).wait()
        for ph in range(PHASES):
            end_send(ph, 16 if ph in (3, 9, 11, 12) else 8, ph in (2, 6, 9, 12))

    return kernel


def call_kernel(n, operands):
    chips = n // 2
    shard_rows = WSLOTS // (128 * n)
    fill_rows = max(shard_rows + 28 * n, 96 * (n - 1), 100 * n, 8 * (4 * n - 1), 16 * (2 * n - 1))

    def vm(*shape, dtype=F32):
        return pltpu.VMEM(shape, dtype)

    def low(*shape):
        return pltpu.VMEM(shape, BF16)

    dma = pltpu.SemaphoreType.DMA
    scratch = [
        vm(PHASES, 16, 128),
        vm(PHASES, 2, n, 16, 128),
        vm(2, 2, 8, 128),
        low(4, 4, PX, 128),
        low(4, PX, CIN),
        low(PX, CIN),
        low(2, PX, 256),
        vm(PX, 128),
        vm(4, PX, 128),
        vm(PX, 256),
        vm(PX, 512),
        vm(PX, 512),
        vm(PX, 128),
        vm(PX, 256),
        vm(PX, 512),
        vm(PX, 512),
        low(PX, 1152),
        low(PX, 1152),
        vm(2, PX, 256),
        vm(2, PX, 256),
        low(PX, 256),
        low(PX, 256),
        low(PX, 512),
        vm(PX, 512),
        vm(PX, 256),
        vm(PX, 256),
        vm(2, PX, 128),
        vm(2, PX, 256),
        vm(3, PX, 256),
        low(2, PX, 128),
        low(2, 4, PX, 128),
        low(PX, 512),
        low(PX, 512),
        vm(3, PX + 2 * SIDE, 128),
        vm(4, PX, 128),
        low(2, PX, 256),
        low(2, 4, PX, 128),
        vm(shard_rows, 128),
        vm(128, 128),
        vm(fill_rows, 128),
        vm(HOME_ROWS, 128),
        vm(TABLE_ROWS, 128),
        low(2, 32, 16, 128),
        low(24, 48, 256),
        vm(800, 128),
        low(32, 16, 512),
        low(16, 16, 512),
        low(2, 32, 16, 128),
        low(24, 48, 256),
        vm(800, 128),
        low(16, 16, 512),
        vm(32, 128),
        vm(192, 128),
        vm(25, 128),
        vm(128, 128),
        vm(128, 128),
        vm(64, 128),
        vm(192, 128),
        vm(25, 128),
        vm(128, 128),
        low(2, 16, 128),
        low(2, 48, 256),
        low(2, 16, 512),
        low(2, 16, 512),
        low(2, 2, 16, 128),
        low(2, 48, 256),
        low(2, 16, 512),
        low(shard_rows // 32 + 2, 2, 16, 128),
        low(shard_rows // 192 + 2, 2, 48, 256),
        low(shard_rows // 128 + 2, 2, 16, 512),
        low(shard_rows // 128 + 2, 2, 16, 512),
        low(shard_rows // 192 + 2, 2, 48, 256),
        low(shard_rows // 128 + 2, 2, 16, 512),
        low(32, 16, 128),
        low(24, 48, 256),
        low(32, 16, 512),
        low(16, 16, 512),
        low(32, 16, 256),
        low(24, 48, 256),
        low(16, 16, 512),
        low(3, 6, 48, 256),
        low(3, 8, 16, 512),
        low(3, 4, 16, 512),
        low(3, 8, 16, 256),
        low(3, 6, 48, 256),
        low(3, 4, 16, 512),
        low(6, 48, 256),
        low(8, 16, 512),
        low(4, 16, 512),
        low(8, 16, 256),
        low(6, 48, 256),
        low(4, 16, 512),
        low(4 * chips, 2, 16, 128),
        low(chips, 2, 48, 256),
        low(chips, 2, 16, 512),
        low(chips, 2, 16, 512),
        low(chips, 2, 16, 256),
        low(chips, 2, 48, 256),
        low(chips, 2, 16, 512),
        vm(32, 128),
        vm(192, 128),
        vm(128, 128),
        vm(128, 128),
        vm(64, 128),
        vm(192, 128),
        vm(128, 128),
        vm(784, 128),
        vm(784, 128),
        vm(REST_PART, 128),
        vm(REST_PART, 128),
        vm(REST_PART, 128),
        vm(REST_PART, 128),
        vm(TABLE_ROWS, 128),
        vm(TABLE_ROWS, 128),
        vm(TABLE_ROWS, 128),
        dma((PHASES,)),
        dma((PHASES, 2)),
        dma((17,)),
        dma((17,)),
        dma((2, 2)),
        dma((4,)),
        dma((2,)),
        dma((2,)),
        dma((2,)),
        dma((2,)),
        dma((2,)),
        dma((2,)),
        dma,
        dma,
        dma((2,)),
        dma((9,)),
        dma((9,)),
        dma((9,)),
        dma((9,)),
        dma((9, 4)),
        dma((9,)),
        dma((9,)),
        dma((9,)),
        dma((9,)),
        dma,
        dma,
        dma((4,)),
        dma((4,)),
    ]
    sds = jax.ShapeDtypeStruct
    outs = (
        sds((2, PX, 256), BF16),
        sds((2, 4, PX, 128), BF16),
        sds((shard_rows, 128), F32),
    )
    vmem = pl.BlockSpec(memory_space=pltpu.VMEM)
    smem = pl.BlockSpec(memory_space=pltpu.SMEM)
    return pl.pallas_call(
        make_kernel(n),
        out_shape=outs,
        in_specs=[smem if i == 2 else vmem for i in range(len(operands))],
        out_specs=[vmem] * len(outs),
        scratch_shapes=scratch,
        compiler_params=pltpu.CompilerParams(
            collective_id=0, has_side_effects=True, vmem_limit_bytes=60 << 20
        ),
    )(*operands)


def per_device(images, cotangent, res_codes, section_weights):
    n = lax.axis_size("dp")
    planes = images.reshape(2, SIDE, 2, SIDE, 2, 128).transpose(0, 2, 4, 1, 3, 5)
    out_o, out_i, out_w = call_kernel(
        n,
        (
            planes.reshape(2, 4, PX, 128),
            cotangent.reshape(2, PX, 256),
            res_codes,
            section_weights.reshape(-1, 128),
        ),
    )
    block_out = out_o.reshape(2, SIDE, SIDE, 256)
    input_grad = (
        out_i.reshape(2, 2, 2, SIDE, SIDE, 128).transpose(0, 3, 1, 4, 2, 5).reshape(images.shape)
    )
    return block_out, input_grad, out_w.reshape(section_weights.shape)


def solution(mesh):
    return jax.shard_map(
        per_device,
        mesh=mesh,
        in_specs=(
            P("dp", None, None, "section"),
            P("dp", None, None, "section"),
            P("dp"),
            P("section", "dp"),
        ),
        out_specs=(
            P("dp", None, None, "section"),
            P("dp", None, None, "section"),
            P("section", "dp"),
        ),
        check_vma=False,
    )
```

```python
import jax
import jax.numpy as jnp
from jax import lax
from jax.experimental import pallas as pl
from jax.experimental.pallas import tpu as pltpu
from jax.sharding import PartitionSpec as P

CIN = 512
COUT = 1024
CMID = 256
CSQ = 128
SIDE = 16
PX = SIDE * SIDE
HALF = 128
WSLOTS = 1351680
EPS = 1e-05
HIGH = lax.Precision.HIGHEST
MESH = pl.DeviceIdType.MESH
F32 = jnp.float32
BF16 = jnp.bfloat16
PHASES = 14
ROWS = (
    (3, 0),
    (4, 0),
    (2, 2),
    (16, 0),
    (2, 0),
    (4, 0),
    (2, 2),
    (8, 0),
    (8, 0),
    (10, 2),
    (2, 0),
    (16, 0),
    (10, 2),
    (2, 0),
)


class Matrix:
    def __init__(self, index, row, start, blocks, pieces, rows, first, step, split="columns"):
        self.index = index
        self.row = row
        self.start = start
        self.blocks = blocks
        self.pieces = pieces
        self.rows = rows
        self.first = first
        self.step = step
        self.split = split
        self.flat = blocks * rows
        self.width = 128 * (blocks // 2 if split == "columns" else blocks)


IN0 = Matrix(0, 0, 0, 2, 8, 16, 0, 1)
MID0 = Matrix(1, 0, 1028, 4, 6, 48, 0, 1)
REST0 = Matrix(2, 0, 5636, 1, 8, 25, 0, 1, split="none")
SC0 = Matrix(3, 0, 6418, 8, 8, 16, 0, 1)
OUT1 = Matrix(4, 1, 0, 8, 4, 16, 1, 2)
IN1 = Matrix(5, 1, 2064, 2, 8, 16, 0, 1, split="rows")
MID2 = Matrix(6, 2, 0, 4, 6, 48, 2, 1)
REST2 = Matrix(7, 2, 4608, 1, 8, 25, 0, 1, split="none")
OUT3 = Matrix(8, 3, 0, 8, 4, 16, 0, 2)
MATRICES = (IN0, MID0, REST0, SC0, OUT1, IN1, MID2, REST2, OUT3)
PRODUCTS = (IN0, MID0, SC0, OUT1, IN1, MID2, OUT3)
USED = (10530, 4116, 5390, 2064)
REST_ROWS = 782
HOME_ROWS = 1152
REST_PART = 97
AT_SQ, AT_GSQ, AT_BSQ, AT_EX, AT_BEX = 8, 264, 265, 266, 778
TABLE = {
    (0, "g_in"): (0, 1024, 1),
    (0, "b_in"): (2, 1026, 1),
    (0, "g_mid"): (4, 5636, 2),
    (0, "b_mid"): (8, 5640, 2),
    (0, "g_sc"): (12, 10514, 4),
    (0, "b_sc"): (20, 10522, 4),
    (1, "g_out"): (28, 2048, 4),
    (1, "b_out"): (36, 2056, 4),
    (1, "g_in"): (44, 4112, 1),
    (1, "b_in"): (46, 4114, 1),
    (3, "g_out"): (48, 2048, 4),
    (3, "b_out"): (56, 2056, 4),
    (2, "g_mid"): (64, 4608, 2),
    (2, "b_mid"): (68, 4612, 2),
}
TABLE_ROWS = 72
LATE_ROWS = 12
SECTION_ROWS = {0: (0, 28), 1: (28, 20), 2: (64, 8), 3: (48, 16)}
AT_MID = {0: 4, 2: 64}
RANGES = (
    (0, 1024, 4, 0),
    (0, 5636, 8, 4),
    (0, 10514, 16, 12),
    (1, 2048, 16, 28),
    (1, 4112, 4, 44),
    (2, 4608, 8, 64),
    (3, 2048, 16, 48),
)


def dot(a, b):
    return lax.dot_general(a, b, (((1,), (0,)), ((), ())), preferred_element_type=F32)


def dot_rt(a, b):
    return lax.dot_general(a, b, (((1,), (1,)), ((), ())), preferred_element_type=F32)


def dot_lt(a, b):
    return lax.dot_general(a, b, (((0,), (0,)), ((), ())), preferred_element_type=F32)


def dot_hi(a, b, dims=((1,), (0,))):
    return lax.dot_general(a, b, (dims, ((), ())), precision=HIGH, preferred_element_type=F32)


def sigmoid(v):
    return 0.5 + 0.5 * jnp.tanh(0.5 * v)


def fold8(x):
    return jnp.sum(x.reshape(x.shape[0] // 8, 8, x.shape[1]), axis=0)


def lanes(x, count):
    return jnp.concatenate([x] * count, axis=1) if count > 1 else x


def make_kernel(n):
    chips = n // 2
    shard_rows = WSLOTS // (128 * n)
    fill_rows = max(shard_rows + 28 * n, 96 * (n - 1), 100 * n, 8 * (4 * n - 1), 16 * (2 * n - 1))

    def kernel(
        img,
        cot,
        codes,
        shard,
        out_o,
        out_i,
        out_w,
        snd,
        rcv,
        side_t,
        u,
        um,
        pool,
        ctb,
        mref,
        z1,
        z2,
        zs,
        z3,
        z4,
        z5,
        z6,
        v3,
        cols1,
        cols2,
        rr1,
        rr2,
        a1,
        a2,
        y1,
        dv6,
        dbuf,
        spb,
        pz,
        pda,
        pdp,
        dz4,
        dz1,
        dz3,
        dzs,
        ep,
        dh,
        obuf,
        ibuf,
        sround,
        nought,
        fill,
        fill2,
        table,
        w_in0,
        w_mid0,
        rest0,
        w_sc,
        w_out1,
        w_in1,
        w_mid2,
        rest2,
        w_out3,
        ln_in0,
        ln_mid0,
        ln_rest0,
        ln_sc,
        ln_out1,
        ln_in1,
        ln_mid2,
        ln_rest2,
        ln_out3,
        st_in0,
        st_mid0,
        st_sc,
        st_out1,
        st_in1,
        st_mid2,
        st_out3,
        cu_in0,
        cu_mid0,
        cu_sc,
        cu_out1,
        cu_mid2,
        cu_out3,
        gw_in0,
        gw_mid0,
        gw_sc,
        gw_out1,
        gw_in1,
        gw_mid2,
        gw_out3,
        ga_mid0,
        ga_sc,
        ga_out1,
        ga_in1,
        ga_mid2,
        ga_out3,
        gp_mid0,
        gp_sc,
        gp_out1,
        gp_in1,
        gp_mid2,
        gp_out3,
        gb_in0,
        gb_mid0,
        gb_sc,
        gb_out1,
        gb_in1,
        gb_mid2,
        gb_out3,
        gf_in0,
        gf_mid0,
        gf_sc,
        gf_out1,
        gf_in1,
        gf_mid2,
        gf_out3,
        rg0,
        rg2,
        rl0,
        rl2,
        rf0,
        rf2,
        gvt,
        gvl,
        gvs,
        gd_mid0,
        gt_mid0,
        gd_mid2,
        gt_mid2,
        gd_sc,
        gt_sc,
        gd_out1,
        gt_out1,
        gd_out3,
        gt_out3,
        gd_in1,
        gt_in1,
        ssem,
        rsem,
        bs,
        br,
        img_s,
        img_r,
        ct_s,
        ct_r,
        oo_s,
        oo_r,
        oi_s,
        oi_r,
        h_s,
        t_s,
        t_r,
        h_r,
        a_s,
        c_r,
        f_s,
        q_r,
        ga_s,
        ga_r,
        gb_s,
        gb_r,
        gc_s,
        gc_r,
        v_s,
        v_r,
        gd_s,
        gd_r,
    ):
        s = lax.axis_index("section")
        d = lax.axis_index("dp")
        c = d // 2
        k = d % 2
        m = s % 2
        g = (s // 2) * chips + c

        def peer(o, kk):
            gg = lax.rem(g + o, n)
            return ((gg // chips) * 2 + m, 2 * (gg % chips) + kk)

        nought[...] = jnp.zeros(nought.shape, F32)
        sround[...] = shard[...].astype(BF16).astype(F32)

        barrier = pltpu.get_barrier_semaphore()
        me = s * n + d
        beside_x = s + 1 - 2 * (s % 2)
        beside_y = lax.rem(s + 2, 4)

        def greet(i, _):
            e = lax.rem(me + i, 4 * n)
            pl.semaphore_signal(barrier, inc=1, device_id=(e // n, e % n), device_id_type=MESH)
            return 0

        lax.fori_loop(1, 4 * n, greet, 0)
        pl.semaphore_wait(barrier, 4 * n - 1)

        def to_twin(i, src, dst):
            return pltpu.make_async_remote_copy(
                src, dst, bs.at[i], br.at[i], device_id=(s, 2 * c + 1 - k), device_id_type=MESH
            )

        def move(src, dst, s_sem, r_sem, dev):
            own = (dev[0] == s) & (dev[1] == d)

            @pl.when(own)
            def _():
                pltpu.make_async_copy(src, dst, r_sem).start()

            @pl.when(jnp.logical_not(own))
            def _():
                pltpu.make_async_remote_copy(
                    src, dst, s_sem, r_sem, device_id=dev, device_id_type=MESH
                ).start()

        def end_move(src, s_sem, dev):
            own = (dev[0] == s) & (dev[1] == d)

            @pl.when(jnp.logical_not(own))
            def _():
                pltpu.make_async_copy(src, src, s_sem).wait()

        def is_self(dev):
            return (dev[0] == s) & (dev[1] == d)

        def move_rows(src, src_at, dst, dst_at, count, full, s_sem, r_sem, dev):
            def go(size, at):
                move(
                    src.at[pl.ds(src_at + at, size)],
                    dst.at[pl.ds(dst_at + at, size)],
                    s_sem,
                    r_sem,
                    dev,
                )

            def chunks(size, start, many):
                def one(i, _):
                    go(size, start + i * size)
                    return 0

                lax.fori_loop(0, many, one, 0)

            if full > 1:

                @pl.when(count == full)
                def _():
                    go(full, 0)

                @pl.when(count < full)
                def _():
                    if full > 16:
                        chunks(16, 0, count // 16)
                        chunks(1, (count // 16) * 16, count % 16)
                    else:
                        chunks(1, 0, count)

            else:
                chunks(1, 0, count)
            return jnp.where(is_self(dev), 0, count)

        def fill_up(src, dst, first, last, sem):
            def chunks(size, start, many):
                def one(i, _):
                    pltpu.make_async_copy(
                        src.at[pl.ds(0, size)], dst.at[pl.ds(start + i * size, size)], sem
                    ).start()
                    return 0

                lax.fori_loop(0, many, one, 0)

            count = last - first
            chunks(128, first, count // 128)
            chunks(16, first + (count // 128) * 128, count % 128 // 16)
            chunks(1, first + (count // 16) * 16, count % 16)

        used = jnp.where(
            s == 0, USED[0], jnp.where(s == 1, USED[1], jnp.where(s == 2, USED[2], USED[3]))
        )
        fill_up(nought, out_w, jnp.clip(used - d * shard_rows, 0, shard_rows), shard_rows, gc_r)

        mine_from = d * shard_rows
        mine_to = mine_from + shard_rows

        def cut(mat, land, stage, base):
            for j in range(mat.blocks):
                for h in range(2):
                    if mat.split == "rows":
                        x = land[pl.ds(base + h * mat.flat + j, mat.rows, stride=mat.blocks), :]
                        stage[h, j] = x.astype(BF16)
                    elif j // (mat.blocks // 2) == h:
                        x = land[pl.ds(base + j, mat.rows, stride=mat.blocks), :]
                        at = 128 * (j % (mat.blocks // 2))
                        stage[h, :, at : at + 128] = x.astype(BF16)

        def holds(mat):
            i = d - mat.first
            inside = (i >= 0) & (i < mat.step * mat.pieces)
            return inside & (i % mat.step == 0) if mat.step > 1 else inside

        def piece(mat):
            return s * mat.pieces + jnp.maximum(d - mat.first, 0) // mat.step

        def scatter_cut(mat, land, stage, ready, part=0, parts=1):
            first = jnp.maximum(mine_from - mat.start, 0) // mat.flat
            last = (jnp.maximum(mine_to - mat.start, 0) + mat.flat - 1) // mat.flat
            last = jnp.minimum(last, 4 * mat.pieces)

            def one(p, sent):
                start = mat.start + p * mat.flat
                lo = jnp.maximum(start, mine_from)
                count = jnp.minimum(start + mat.flat, mine_to) - lo
                dev = (p // mat.pieces, mat.first + mat.step * (p % mat.pieces))

                def in_one():
                    to = ready.at[p - first]
                    cut(mat, sround, to, lo - mine_from)
                    move(to, stage, h_s, h_r.at[mat.index], dev)
                    return jnp.where(is_self(dev), 0, mat.flat // 2)

                def in_rows():
                    return move_rows(
                        sround,
                        lo - mine_from,
                        land,
                        lo - start,
                        count,
                        mat.flat,
                        h_s,
                        h_r.at[mat.index],
                        dev,
                    )

                return sent + lax.cond(count == mat.flat, in_one, in_rows)

            step = (jnp.maximum(last - first, 0) + parts - 1) // parts
            begin = first + part * step
            end = jnp.minimum(last, begin + step)
            return lax.fori_loop(begin, end, one, jnp.int32(0))

        def stage_ready(mat, land, stage):
            start = mat.start + piece(mat) * mat.flat
            whole = start // shard_rows == (start + mat.flat - 1) // shard_rows

            @pl.when(whole)
            def _():
                full_wait(stage, h_r.at[mat.index])

            @pl.when(jnp.logical_not(whole))
            def _():
                full_wait(land, h_r.at[mat.index])
                cut(mat, land, stage, 0)

        def scatter_pieces(mat, land, part=0, parts=1):
            total = mat.pieces * 4 * (2 if mat.split == "rows" else 1)
            first = jnp.maximum(mine_from - mat.start, 0) // mat.flat
            last = (jnp.maximum(mine_to - mat.start, 0) + mat.flat - 1) // mat.flat

            def one(p, sent):
                start = mat.start + p * mat.flat
                lo = jnp.maximum(start, mine_from)
                count = jnp.minimum(start + mat.flat, mine_to) - lo
                h = p // (4 * mat.pieces)
                q = p % (4 * mat.pieces)
                dev = (q // mat.pieces, mat.first + mat.step * (q % mat.pieces))
                return sent + move_rows(
                    sround,
                    lo - mine_from,
                    land,
                    h * mat.flat + lo - start,
                    count,
                    mat.flat,
                    h_s,
                    h_r.at[mat.index],
                    dev,
                )

            last = jnp.minimum(last, total)
            step = (jnp.maximum(last - first, 0) + parts - 1) // parts
            begin = first + part * step
            end = jnp.minimum(last, begin + step)
            return lax.fori_loop(begin, end, one, jnp.int32(0))

        def scatter_table(start, rows, at):
            lo = jnp.maximum(start, mine_from)
            count = jnp.maximum(jnp.minimum(start + rows, mine_to) - lo, 0)

            def one(i, sent):
                e = lax.rem(d + i, n)
                return sent + move_rows(
                    sround,
                    lo - mine_from,
                    table,
                    at + lo - start,
                    count,
                    rows,
                    h_s,
                    t_r.at[0],
                    (s, e),
                )

            return lax.fori_loop(0, jnp.where(count > 0, n, 0), one, jnp.int32(0))

        def pass_table():
            for r, (at, many) in SECTION_ROWS.items():

                @pl.when(s == r)
                def _():
                    here = table.at[pl.ds(at, many)]
                    full_wait(here, t_r.at[0])
                    for i in range(1, 4):
                        pltpu.make_async_remote_copy(
                            here,
                            here,
                            t_s,
                            t_r.at[1],
                            device_id=(lax.rem(s + i, 4), d),
                            device_id_type=MESH,
                        ).start()

        def table_arrived():
            for r in range(4):
                rest = TABLE_ROWS - SECTION_ROWS.get(r, (0, 0))[1]

                @pl.when(s == r)
                def _():
                    full_wait(table.at[pl.ds(0, rest)], t_r.at[1])

        def end_table():
            for r, (_, many) in SECTION_ROWS.items():

                @pl.when(s == r)
                def _():
                    full_wait(fill.at[pl.ds(0, 3 * many)], t_s)

        def full_wait(ref, sem):
            pltpu.make_async_copy(ref, ref, sem).wait()

        def when_row(r, body):
            return lax.cond(s == r, body, lambda: jnp.int32(0))

        sent = when_row(0, lambda: scatter_cut(IN0, ln_in0, st_in0, cu_in0))

        for slot in range(2):
            for kk in range(2):
                move(
                    img.at[slot, pl.ds(2 * kk, 2)],
                    u.at[s, pl.ds(2 * kk, 2)],
                    img_s.at[slot, kk],
                    img_r.at[s],
                    (2 * k + slot, 2 * c + kk),
                )
        for slot in range(2):
            width = (SIDE - 2 * codes[slot]).astype(F32)
            side_t[k, slot] = jnp.full((8, 128), width, F32)
        side_copy = to_twin(0, side_t.at[k], side_t.at[k])
        side_copy.start()
        snd[...] = jnp.zeros(snd.shape, F32)

        def row0():
            count = scatter_cut(MID0, ln_mid0, st_mid0, cu_mid0) + scatter_table(*RANGES[0][1:])
            count = count + scatter_table(*RANGES[1][1:]) + scatter_table(*RANGES[2][1:])
            return count + scatter_cut(SC0, ln_sc, st_sc, cu_sc)

        def row1():
            count = scatter_cut(OUT1, ln_out1, st_out1, cu_out1) + scatter_table(*RANGES[3][1:])
            return count + scatter_table(*RANGES[4][1:])

        sent = sent + when_row(0, row0)
        sent = sent + when_row(1, row1)
        sent = sent + when_row(2, lambda: scatter_table(*RANGES[5][1:]))
        sent = sent + when_row(3, lambda: scatter_table(*RANGES[6][1:]))

        def scatter_some(sent, part, parts):
            sent = sent + when_row(2, lambda: scatter_cut(MID2, ln_mid2, st_mid2, cu_mid2, part, parts))
            return sent + when_row(3, lambda: scatter_cut(OUT3, ln_out3, st_out3, cu_out3, part, parts))

        def scatter_early(sent):
            sent = sent + when_row(0, lambda: scatter_pieces(REST0, ln_rest0))
            sent = sent + when_row(1, lambda: scatter_pieces(IN1, ln_in1))
            return scatter_some(sent, 1, 3)

        def scatter_late(sent):
            sent = scatter_some(sent, 2, 3)
            sent = sent + when_row(2, lambda: scatter_pieces(REST2, ln_rest2))
            fill_up(nought, fill, sent, fill_rows, h_s)

        sent = scatter_some(sent, 0, 3)

        def spread(mat, land, stage, whole):
            @pl.when(holds(mat))
            def _():
                if mat.split == "rows":
                    full_wait(land, h_r.at[mat.index])
                    cut(mat, land, stage, 0)
                else:
                    stage_ready(mat, land, stage)
                p = piece(mat)

                def one(i, _):
                    e = lax.rem(d + i, n)
                    h = e % 2
                    dst = whole.at[:, p] if mat.split == "rows" else whole.at[p]
                    move(stage.at[h], dst, a_s.at[mat.index], c_r.at[mat.index], (s, e))
                    return 0

                lax.fori_loop(0, n, one, 0)

        def quarters(mat, whole, first, many, part=None):
            if part is None:
                span = pl.ds(first * mat.pieces, many * mat.pieces)
            else:
                half = mat.pieces // 2
                span = pl.ds(first * mat.pieces + part * half, half)
            return whole.at[:, span] if mat.split == "rows" else whole.at[span]

        def hand(mat, here, i, to):
            pltpu.make_async_remote_copy(
                here,
                here,
                f_s.at[mat.index],
                q_r.at[mat.index, i],
                device_id=(to, d),
                device_id_type=MESH,
            ).start()

        def pass_on(mat, whole):
            here = quarters(mat, whole, s, 1)
            full_wait(here, c_r.at[mat.index])
            hand(mat, here, 0, beside_x)
            hand(mat, here, 1, beside_y)

        def pass_far(mat, whole):
            full_wait(quarters(mat, whole, beside_x, 1), q_r.at[mat.index, 0])
            hand(mat, quarters(mat, whole, beside_x, 1, 0), 2, beside_y)
            full_wait(quarters(mat, whole, beside_y, 1), q_r.at[mat.index, 1])
            hand(mat, quarters(mat, whole, beside_y, 1, 1), 3, beside_x)

        def arrived(mat, whole):
            far = 3 - s
            for i in range(2):
                full_wait(quarters(mat, whole, far, 1, i), q_r.at[mat.index, 2 + i])

        def end_spread(mat, whole):
            @pl.when(holds(mat))
            def _():
                rows = mat.rows * mat.width // 256
                full_wait(fill.at[pl.ds(0, (n - 1) * rows)], a_s.at[mat.index])

            full_wait(quarters(mat, whole, 0, 3), f_s.at[mat.index])

        def spread_rest(mat, land, whole):
            @pl.when(holds(mat))
            def _():
                full_wait(land, h_r.at[mat.index])
                at = piece(mat) * mat.flat

                def one(i, _):
                    e = lax.rem(s * chips + c + i, 4 * chips)
                    move(
                        land,
                        whole.at[pl.ds(at, mat.flat)],
                        a_s.at[mat.index],
                        c_r.at[mat.index],
                        (e // chips, 2 * (e % chips)),
                    )
                    return 0

                lax.fori_loop(0, 4 * chips, one, 0)

        def share_rest(mat, whole, i):
            @pl.when(k == 0)
            def _():
                full_wait(whole, c_r.at[mat.index])
                to_twin(i, whole, whole).start()

        def rest_arrived(whole, i):
            @pl.when(k == 1)
            def _():
                to_twin(i, whole, whole).wait_recv()

        def end_rest(mat, whole, i):
            @pl.when(k == 0)
            def _():
                to_twin(i, whole, whole).wait_send()

            for kk in range(2):

                @pl.when(holds(mat) & (k == kk))
                def _():
                    rows = (4 * chips - 1 + kk) * mat.flat
                    full_wait(fill.at[pl.ds(0, rows)], a_s.at[mat.index])

        @pl.when(holds(IN0))
        def _():
            stage_ready(IN0, ln_in0, st_in0)

            def one(i, _):
                e = lax.rem(me + i, 4 * n)
                h = e % 2
                move(
                    st_in0.at[h],
                    w_in0.at[h, s * 8 + d],
                    a_s.at[0],
                    c_r.at[0],
                    (e // n, e % n),
                )
                return 0

            lax.fori_loop(0, 4 * n, one, 0)

        def part_of(mat, ref, quarter, part):
            half = mat.pieces // 2
            return ref.at[pl.ds(quarter * mat.pieces + part * half, half)]

        def shed(mat, gw, land):
            for part, to in enumerate((beside_x, beside_y)):
                for i, quarter in enumerate((to, 3 - s)):
                    pltpu.make_async_remote_copy(
                        part_of(mat, gw, quarter, part),
                        land.at[part, i],
                        ga_s.at[mat.index],
                        ga_r.at[mat.index, part],
                        device_id=(to, d),
                        device_id_type=MESH,
                    ).start()

        def shed_mid(mat, gw, land, add, land3):
            half = mat.pieces // 2
            for part, to in enumerate((beside_y, beside_x)):
                full_wait(land.at[part], ga_r.at[mat.index, part])
                base = to * mat.pieces + part * half

                def one(i, _):
                    x = gw[base + i].astype(F32) + land[part, 1, i].astype(F32)
                    add[part, i] = x.astype(BF16)
                    return 0

                lax.fori_loop(0, half, one, 0)
                pltpu.make_async_remote_copy(
                    add.at[part],
                    land3.at[part],
                    gd_s.at[mat.index],
                    gd_r.at[mat.index, part],
                    device_id=(to, d),
                    device_id_type=MESH,
                ).start()

        def shed_more(mat, gw, land, land3, part_sum, land2):
            half = mat.pieces // 2
            for part in range(2):
                full_wait(land3.at[part], gd_r.at[mat.index, part])

                def one(j, _):
                    i = part * half + j
                    x = gw[s * mat.pieces + i].astype(F32) + land[part, 0, j].astype(F32)
                    part_sum[i] = (x + land3[part, j].astype(F32)).astype(BF16)
                    move(
                        part_sum.at[i],
                        land2.at[c, k],
                        gb_s.at[mat.index],
                        gb_r.at[mat.index],
                        (s, mat.first + mat.step * i),
                    )
                    return 0

                lax.fori_loop(0, half, one, 0)

        def home_rows(src, src_at, start, rows, limit, r, active):
            left = jnp.int32(0)
            for i in range((rows + shard_rows - 2) // shard_rows + 1):
                owner = start // shard_rows + i
                lo = jnp.maximum(start, owner * shard_rows)
                hi = jnp.minimum(jnp.minimum(start + rows, limit), (owner + 1) * shard_rows)
                count = jnp.where(active, jnp.maximum(hi - lo, 0), 0)
                owner = jnp.minimum(owner, n - 1)

                def go():
                    return move_rows(
                        src,
                        src_at + lo - start,
                        out_w,
                        lo - owner * shard_rows,
                        count,
                        rows,
                        gc_s,
                        gc_r,
                        (r, owner),
                    )

                left = left + lax.cond(count > 0, go, lambda: jnp.int32(0))
            return left

        def home(mat, land2, flat):
            @pl.when(holds(mat))
            def _():
                full_wait(land2, gb_r.at[mat.index])
                for h in range(2):
                    x = jnp.sum(land2[:, h].astype(F32), axis=0)
                    for j in range(mat.width // 128):
                        if mat.split == "rows":
                            at = h * mat.flat + j
                        else:
                            at = h * (mat.blocks // 2) + j
                        flat[pl.ds(at, mat.rows, stride=mat.blocks), :] = x[:, 128 * j : 128 * (j + 1)]

            p = piece(mat)
            left = home_rows(
                flat, 0, mat.start + p * mat.flat, mat.flat, USED[mat.row], mat.row, holds(mat)
            )
            if mat.split == "rows":
                p = p + 4 * mat.pieces
                left = left + home_rows(
                    flat,
                    mat.flat,
                    mat.start + p * mat.flat,
                    mat.flat,
                    USED[mat.row],
                    mat.row,
                    holds(mat),
                )
            return left

        def end_shed(mat, gw):
            full_wait(gw.at[pl.ds(0, 2 * mat.pieces)], ga_s.at[mat.index])
            full_wait(gw.at[pl.ds(0, mat.pieces)], gd_s.at[mat.index])

            @pl.when(holds(mat))
            def _():
                full_wait(gw.at[pl.ds(0, mat.pieces - 1)], gb_s.at[mat.index])

            @pl.when(jnp.logical_not(holds(mat)))
            def _():
                full_wait(gw.at[pl.ds(0, mat.pieces)], gb_s.at[mat.index])

        def rest_meet(i, mat, rg, land):
            @pl.when((s == mat.row) & (d < 8))
            def _():
                pltpu.make_async_remote_copy(
                    rg.at[pl.ds(AT_SQ + REST_PART * d, REST_PART)],
                    land,
                    v_s.at[i],
                    v_r.at[i],
                    device_id=(s + 1, d),
                    device_id_type=MESH,
                ).start()

        def rest_home(i, mat, rg, land, flat):
            active = (s == mat.row + 1) & (d < 8)
            at = AT_SQ + REST_PART * jnp.minimum(d, 7)

            @pl.when(active)
            def _():
                full_wait(land, v_r.at[i])
                flat[...] = rg[pl.ds(at, REST_PART), :] + land[...]

            return home_rows(
                flat, 0, mat.start + at, REST_PART, mat.start + REST_ROWS, mat.row, active
            )

        def table_meet(i, first, rows):
            @pl.when((s == 0) & (d < 2))
            def _():
                pltpu.make_async_remote_copy(
                    gvt.at[pl.ds(first, rows)],
                    gvl.at[pl.ds(first, rows)],
                    v_s.at[i],
                    v_r.at[i],
                    device_id=(s + 1, d),
                    device_id_type=MESH,
                ).start()

        def table_home(i, first, rows):
            active = (s == 1) & (d < 2)

            @pl.when(active)
            def _():
                span = pl.ds(first, rows)
                full_wait(gvl.at[span], v_r.at[i])
                gvs[first : first + rows, :] = gvt[first : first + rows, :] + gvl[first : first + rows, :]

            left = jnp.int32(0)
            for (r, _), (at, start, many) in TABLE.items():
                if first <= at < first + rows:
                    left = left + home_rows(
                        gvs,
                        at + many * k,
                        start + many * k,
                        many,
                        start + 2 * many,
                        r,
                        active,
                    )
            return left

        def put(ph, base, value):
            for j in range(value.shape[1] // 128):
                snd[ph, base + j : base + j + 1, :] = value[:, 128 * j : 128 * (j + 1)]

        def send(ph):
            mine, theirs = ROWS[ph]

            def to(o, kk, rows):
                pltpu.make_async_remote_copy(
                    snd.at[ph, pl.ds(0, rows)],
                    rcv.at[ph, k, o, pl.ds(0, rows)],
                    ssem.at[ph],
                    rsem.at[ph, k],
                    device_id=peer(o, kk),
                    device_id_type=MESH,
                ).start()
                return 0

            lax.fori_loop(1, n, lambda o, _: to(o, k, mine), 0)
            if theirs:
                lax.fori_loop(0, n, lambda o, _: to(o, 1 - k, theirs), 0)
            rcv[ph, k, 0] = snd[ph]

        def receive(ph):
            mine, theirs = ROWS[ph]
            full_wait(rcv.at[ph, k, pl.ds(1, n - 1), pl.ds(0, mine)], rsem.at[ph, k])
            if theirs:
                full_wait(rcv.at[ph, 1 - k, :, pl.ds(0, theirs)], rsem.at[ph, 1 - k])

        def end_send(ph):
            mine, theirs = ROWS[ph]
            full_wait(fill.at[pl.ds(0, (n - 1) * mine + n * theirs)], ssem.at[ph])

        def totals(ph):
            return jnp.sum(rcv[ph, k, :, 0 : -(-ROWS[ph][0] // 8) * 8, :], axis=0)

        def row(total, base, width):
            return jnp.concatenate(
                [total[base + j : base + j + 1, :] for j in range(width // 128)], axis=1
            )

        def across(ph, h, base, width):
            return jnp.concatenate(
                [rcv[ph, h, :, base + j, :] for j in range(width // 128)], axis=1
            )

        def rows_of(ref, at, many):
            return jnp.concatenate([ref[pl.ds(at + j, 1), :] for j in range(many)], axis=1)

        def vrow(key):
            at, _, many = TABLE[key]
            return rows_of(table, at + many * k, many)

        def set_gvec(key, value):
            at, _, many = TABLE[key]
            for j in range(many):
                gvt[pl.ds(at + many * k + j, 1), :] = value[:, 128 * j : 128 * (j + 1)]

        def set_rows(ref, at, value):
            for j in range(value.shape[1] // 128):
                ref[at + j : at + j + 1, :] = value[:, 128 * j : 128 * (j + 1)]

        def mean_rstd(total, base, width, count):
            mu = row(total, base, width) / count
            second = row(total, base + width // 128, width) / count
            return mu, lax.rsqrt(jnp.maximum(second - mu * mu, 0.0) + EPS)

        gvt[...] = jnp.zeros(gvt.shape, F32)

        side_copy.wait()
        side_row = jnp.where(
            m == 0, side_t[s // 2, 0, 0:1, :], side_t[s // 2, 1, 0:1, :]
        )
        pixel = lax.broadcasted_iota(jnp.int32, (PX, 128), 0)
        prow = (pixel // SIDE).astype(F32)
        pcol = (pixel % SIDE).astype(F32)
        mref[...] = jnp.where((prow < side_row) & (pcol < side_row), 1.0, 0.0)
        inv_own = 1.0 / (side_row * side_row)

        for q in range(4):
            here = u.at[q, pl.ds(2 * k, 2)]
            pltpu.make_async_copy(here, here, img_r.at[q]).wait()
            pltpu.make_async_remote_copy(
                here,
                here,
                bs.at[10 + q],
                br.at[10 + q],
                device_id=(s, 2 * c + 1 - k),
                device_id_type=MESH,
            ).start()
        spread(MID0, ln_mid0, st_mid0, w_mid0)
        for q in range(4):
            here = u.at[q, pl.ds(2 * (1 - k), 2)]
            pltpu.make_async_copy(here, here, br.at[10 + q]).wait()

        def mask_block(b, _):
            r = pl.multiple_of(b * 32, 32)
            rows = pl.ds(r, 32)
            mask = mref[rows, :]
            for q in range(4):
                total = jnp.zeros((32, 128), F32)
                for p in range(4):
                    x = u[q, p, rows, :].astype(F32) * mask
                    um[p, rows, 128 * q : 128 * (q + 1)] = x.astype(BF16)
                    total = total + x
                pool[rows, 128 * q : 128 * (q + 1)] = (total * 0.25).astype(BF16)
            return 0

        lax.fori_loop(0, 8, mask_block, 0)
        pass_table()
        pass_on(MID0, w_mid0)
        full_wait(w_in0.at[k], c_r.at[0])

        def z1_block(p, carry):
            z = dot(um[p], w_in0[k].reshape(CIN, 128))
            z1[p] = z
            return (carry[0] + fold8(z), carry[1] + fold8(z * z))

        zero8 = jnp.zeros((8, 128), F32)
        t0, t1 = lax.fori_loop(0, 4, z1_block, (zero8, zero8))
        put(0, 0, jnp.sum(t0, axis=0, keepdims=True))
        put(0, 1, jnp.sum(t1, axis=0, keepdims=True))
        put(0, 2, side_row)
        send(0)
        sent = scatter_early(sent)
        pass_far(MID0, w_mid0)
        spread(SC0, ln_sc, st_sc, w_sc)
        spread(OUT1, ln_out1, st_out1, w_out1)
        table_arrived()
        receive(0)
        total = totals(0)
        sides = across(0, k, 2, 128)
        inv_area = 1.0 / (sides * sides)
        count1 = jnp.sum(sides * sides, axis=0, keepdims=True)
        counts = {w: lanes(count1, w // 128) for w in (128, 256, 512)}
        mu1, rs1 = mean_rstd(total, 0, 128, 4.0 * count1)
        lin1 = rs1 * vrow((0, "g_in"))
        off1 = vrow((0, "b_in")) - mu1 * lin1

        colpos = lax.broadcasted_iota(jnp.int32, (PX, 128), 0) % SIDE

        def shift_cols(x, by):
            moved = pltpu.roll(x, by % PX, 0)
            edge = 0 if by == 1 else SIDE - 1
            return jnp.where(colpos == edge, 0.0, moved)

        def store_tap(cols, di, dj, x, shift):
            at = 128 * (3 * di + dj)
            span = slice(at, at + 128)
            x = x.astype(BF16)
            if shift == 1:
                cols[0:SIDE, span] = jnp.zeros((SIDE, 128), BF16)
                cols[SIDE:PX, span] = x[0 : PX - SIDE]
            elif shift == -1:
                cols[PX - SIDE : PX, span] = jnp.zeros((SIDE, 128), BF16)
                cols[0 : PX - SIDE, span] = x[SIDE:PX]
            else:
                cols[:, span] = x

        def plane_taps(parity):
            return ((1, 0),) if parity == 0 else ((0, 1), (2, 0))

        for p in range(4):
            v = z1[p] * lin1 + off1
            h = v * sigmoid(v) * mref[...]
            for dj, cshift in plane_taps(p % 2):
                x = shift_cols(h, 1) if cshift else h
                for di, rshift in plane_taps(p // 2):
                    store_tap(cols1, di, dj, x, rshift)

        def conv_forward(ph, cols, w_mid, zref):
            z = dot(cols[...], w_mid[...].reshape(1152, 256))
            zref[...] = z
            zm = z * lanes(mref[...], 2)
            put(ph, 0, jnp.sum(zm, axis=0, keepdims=True))
            put(ph, 2, jnp.sum(zm * z, axis=0, keepdims=True))
            send(ph)

        def small(rest):
            w_sq = rest[AT_SQ : AT_SQ + CMID, :]
            w_ex = jnp.concatenate(
                [rest[pl.ds(AT_EX + j, CSQ, stride=4), :] for j in range(4)], axis=1
            )
            return w_sq, w_ex

        def attention_forward(ph, twin, total, at, rest, zref, rr, aref, beside):
            mu, rs = mean_rstd(total, 0, 256, counts[256])
            lin = rs * rows_of(table, at + 2 * k, 2)
            off = rows_of(table, at + 4 + 2 * k, 2) - mu * lin

            def block(b, acc):
                rows = pl.ds(pl.multiple_of(b * 64, 64), 64)
                v = zref[rows, :] * lin + off
                r = v * sigmoid(v) * lanes(mref[rows, :], 2)
                rr[k, rows, :] = r
                return acc + fold8(r)

            acc = lax.fori_loop(0, 4, block, jnp.zeros((8, 256), F32))
            pooled_own = jnp.sum(acc, axis=0, keepdims=True) * lanes(inv_own, 2)
            put(ph, 0, pooled_own)
            send(ph)
            swap = to_twin(twin, rr.at[k], rr.at[k])
            swap.start()
            beside()
            receive(ph)
            w_sq, w_ex = small(rest)
            pooled = across(ph, 0, 0, 256) + across(ph, 1, 0, 256)
            zq = dot_hi(pooled, w_sq)
            mq = jnp.mean(zq, axis=0, keepdims=True)
            vq = jnp.mean(zq * zq, axis=0, keepdims=True) - mq * mq
            rq = lax.rsqrt(jnp.maximum(vq, 0.0) + EPS)
            hq = (zq - mq) * rq
            nq = hq * rows_of(rest, AT_GSQ, 1) + rows_of(rest, AT_BSQ, 1)
            sgq = sigmoid(nq)
            qq = nq * sgq
            logits = dot_hi(qq, w_ex) + rows_of(rest, AT_BEX, 4)
            diff = logits[:, 0:256] - logits[:, 256:512]
            sh0 = sigmoid(diff)
            sh1 = sigmoid(-diff)
            swap.wait()
            s0 = sh0[0:1, :]
            s1 = sh1[0:1, :]

            def mix(b, _):
                rows = pl.ds(pl.multiple_of(b * 64, 64), 64)
                aref[rows, :] = (s0 * rr[0, rows, :] + s1 * rr[1, rows, :]).astype(BF16)
                return 0

            lax.fori_loop(0, 4, mix, 0)
            return (mu, rs, lin, off), (pooled, rq, hq, nq, sgq, qq, sh0, sh1)

        def attention_backward(
            ph, kept_mid, kept_q, rest, rg, zref, rr, cols, mat, gw_mid, ga_mid, da, beside
        ):
            mu, rs, lin, off = kept_mid
            pooled, rq, hq, nq, sgq, qq, sh0, sh1 = kept_q

            def block(b, acc):
                rows = pl.ds(pl.multiple_of(b * 32, 32), 32)
                z = zref[rows, :]
                v = z * lin + off
                hat = (z - mu) * rs
                sg = sigmoid(v)
                sp = sg * (1.0 + v * (1.0 - sg)) * lanes(mref[rows, :], 2)
                grad = da(rows)
                t = grad * sp
                dbuf[rows, :] = grad
                spb[rows, :] = sp
                r = rr[k, rows, :]
                return tuple(
                    x + fold8(y)
                    for x, y in zip(acc, (grad * r, t, sp, t * hat, sp * hat))
                )

            acc = lax.fori_loop(0, 8, block, (jnp.zeros((8, 256), F32),) * 5)
            for j, x in enumerate(acc):
                put(ph, 2 * j, jnp.sum(x, axis=0, keepdims=True))
            send(ph)
            beside()
            receive(ph)
            ds0 = across(ph, 0, 0, 256)
            ds1 = across(ph, 1, 0, 256)
            mean = sh0 * ds0 + sh1 * ds1
            dl = jnp.concatenate([sh0 * (ds0 - mean), sh1 * (ds1 - mean)], axis=1)
            w_sq, w_ex = small(rest)
            set_rows(rg, AT_BEX, jnp.sum(dl, axis=0, keepdims=True))
            dq = dot_hi(dl, w_ex, ((1,), (1,)))
            dn = dq * sgq * (1.0 + nq * (1.0 - sgq))
            set_rows(rg, AT_GSQ, jnp.sum(dn * hq, axis=0, keepdims=True))
            set_rows(rg, AT_BSQ, jnp.sum(dn, axis=0, keepdims=True))
            dn = dn * rows_of(rest, AT_GSQ, 1)
            dzq = rq * (
                dn
                - jnp.mean(dn, axis=0, keepdims=True)
                - hq * jnp.mean(dn * hq, axis=0, keepdims=True)
            )
            dpool = dot_hi(dzq, w_sq, ((1,), (1,))) * lanes(inv_area, 2)
            share = jnp.where(k == 0, sh0, sh1)

            def both_sums(first, second):
                return jnp.sum(
                    share * across(ph, k, first, 256) + dpool * across(ph, k, second, 256),
                    axis=0,
                    keepdims=True,
                )

            sdv = both_sums(2, 4)
            sdh = both_sums(6, 8)
            set_gvec((mat.row, "b_mid"), sdv)
            set_gvec((mat.row, "g_mid"), sdh)
            own_share = share[0:1, :]
            own_pool = dpool[0:1, :]
            c1 = sdv / counts[256]
            c2 = sdh / counts[256]

            def block2(b, _):
                rows = pl.ds(pl.multiple_of(b * 32, 32), 32)
                hat = (zref[rows, :] - mu) * rs
                dv = (own_share * dbuf[rows, :] + own_pool) * spb[rows, :]
                dz = lin * (dv - c1 - hat * c2) * lanes(mref[rows, :], 2)
                rows_low[rows, :] = dz.astype(BF16)
                return 0

            rows_low = dz_low
            lax.fori_loop(0, 8, block2, 0)

            def rest():
                gw_mid[...] = dot_lt(cols[...], dz_low[...]).astype(BF16).reshape(24, 48, 256)
                shed(mat, gw_mid, ga_mid)
                g_ex = dot_hi(qq, dl, ((0,), (0,)))
                for j in range(4):
                    rg[pl.ds(AT_EX + j, CSQ, stride=4), :] = g_ex[:, 128 * j : 128 * (j + 1)]
                rg[AT_SQ : AT_SQ + CMID, :] = dot_hi(pooled, dzq, ((0,), (0,)))

            return rest

        dz_low = dz3.at[:, pl.ds(0, 256)]

        arrived(MID0, w_mid0)
        conv_forward(1, cols1, w_mid0, z2)
        spread_rest(REST0, ln_rest0, rest0)
        scatter_late(sent)
        pass_on(SC0, w_sc)
        pass_on(OUT1, w_out1)
        spread(IN1, ln_in1, st_in1, w_in1)
        receive(1)

        def short_forward():
            share_rest(REST0, rest0, 15)
            pass_far(SC0, w_sc)
            pass_far(OUT1, w_out1)
            pass_on(IN1, w_in1)
            spread(MID2, ln_mid2, st_mid2, w_mid2)
            arrived(SC0, w_sc)
            z = dot(pool[...], w_sc[...].reshape(CIN, 512))
            zs[...] = z
            put(3, 8, jnp.sum(z, axis=0, keepdims=True))
            put(3, 12, jnp.sum(z * z, axis=0, keepdims=True))
            rest_arrived(rest0, 15)

        mid1, q1 = attention_forward(2, 2, totals(1), AT_MID[0], rest0, z2, rr1, a1, short_forward)
        arrived(OUT1, w_out1)

        def wide_forward(ph, aref, w, zref):
            z = dot(aref[...], w[...].reshape(CMID, 512))
            zref[...] = z
            put(ph, 0, jnp.sum(z, axis=0, keepdims=True))
            put(ph, 4, jnp.sum(z * z, axis=0, keepdims=True))
            send(ph)

        wide_forward(3, a1, w_out1, z3)
        pass_far(IN1, w_in1)
        pass_on(MID2, w_mid2)
        receive(3)
        total = totals(3)
        mus, rss = mean_rstd(total, 8, 512, counts[512])
        lins = rss * vrow((0, "g_sc"))
        offs = vrow((0, "b_sc")) - mus * lins

        mu3, rs3 = mean_rstd(total, 0, 512, counts[512])
        lin3 = rs3 * vrow((1, "g_out"))
        off3 = vrow((1, "b_out")) - mu3 * lin3

        def y1_block(b, _):
            rows = pl.ds(pl.multiple_of(b * 32, 32), 32)
            short = (zs[rows, :] * lins + offs).astype(BF16).astype(F32)
            v = z3[rows, :] * lin3 + off3 + short
            v3[rows, :] = v
            y1[rows, :] = (v * sigmoid(v) * lanes(mref[rows, :], 4)).astype(BF16)
            return 0

        lax.fori_loop(0, 8, y1_block, 0)
        arrived(IN1, w_in1)
        pz[0] = dot(y1[...], w_in1[1 - k].reshape(512, 128))
        swap = to_twin(3, pz.at[0], pz.at[1])
        swap.start()
        z = dot(y1[...], w_in1[k].reshape(512, 128))
        swap.wait()
        z = z + pz[1]
        z4[...] = z
        put(4, 0, jnp.sum(z, axis=0, keepdims=True))
        put(4, 1, jnp.sum(z * z, axis=0, keepdims=True))
        send(4)
        pass_far(MID2, w_mid2)
        spread_rest(REST2, ln_rest2, rest2)
        spread(OUT3, ln_out3, st_out3, w_out3)
        receive(4)
        mu4, rs4 = mean_rstd(totals(4), 0, 128, count1)
        lin4 = rs4 * vrow((1, "g_in"))
        off4 = vrow((1, "b_in")) - mu4 * lin4
        v = z4[...] * lin4 + off4
        h = v * sigmoid(v) * mref[...]
        for dj in range(3):
            x = h if dj == 1 else shift_cols(h, 1 - dj)
            for di in range(3):
                store_tap(cols2, di, dj, x, 1 - di)

        arrived(MID2, w_mid2)
        conv_forward(5, cols2, w_mid2, z5)
        share_rest(REST2, rest2, 16)
        pass_on(OUT3, w_out3)
        receive(5)

        def last_weights():
            pass_far(OUT3, w_out3)
            rest_arrived(rest2, 16)
            for slot in range(2):
                move(
                    cot.at[slot],
                    ctb.at[lax.rem(s, 2)],
                    ct_s.at[slot],
                    ct_r.at[lax.rem(s, 2)],
                    (2 * k + slot, 2 * c + s // 2),
                )
            to_twin(14, w_in0.at[k], w_in0.at[k]).start()

        mid2, q2 = attention_forward(6, 4, totals(5), AT_MID[2], rest2, z5, rr2, a2, last_weights)
        arrived(OUT3, w_out3)
        wide_forward(7, a2, w_out3, z6)
        to_twin(14, w_in0.at[k], w_in0.at[k]).wait()
        for i in range(2):
            pltpu.make_async_copy(ctb.at[i], ctb.at[i], ct_r.at[i]).wait()
        receive(7)
        mu6, rs6 = mean_rstd(totals(7), 0, 512, counts[512])
        lin6 = rs6 * vrow((3, "g_out"))
        off6 = vrow((3, "b_out")) - mu6 * lin6

        def out_block(b, acc):
            rows = pl.ds(pl.multiple_of(b * 32, 32), 32)
            z = z6[rows, :]
            mask = lanes(mref[rows, :], 4)
            v = z * lin6 + off6 + y1[rows, :].astype(F32)
            sg = sigmoid(v)
            y = (v * sg * mask).astype(BF16)
            obuf[0, rows, :] = y[:, 0:256]
            obuf[1, rows, :] = y[:, 256:512]
            ct = jnp.concatenate([ctb[0, rows, :], ctb[1, rows, :]], axis=1).astype(F32)
            dv = ct * (sg * (1.0 + v * (1.0 - sg)) * mask)
            dv6[rows, :] = dv
            return (acc[0] + fold8(dv), acc[1] + fold8(dv * ((z - mu6) * rs6)))

        zero512 = jnp.zeros((8, 512), F32)
        t0, t1 = lax.fori_loop(0, 8, out_block, (zero512, zero512))
        put(8, 0, jnp.sum(t0, axis=0, keepdims=True))
        put(8, 4, jnp.sum(t1, axis=0, keepdims=True))
        send(8)
        for j in range(2):
            move(
                obuf.at[j],
                out_o.at[lax.rem(s, 2)],
                oo_s.at[j],
                oo_r.at[lax.rem(s, 2)],
                (2 * k + j, 2 * c + s // 2),
            )
        for mat, whole in ((MID0, w_mid0), (SC0, w_sc), (OUT1, w_out1)):
            end_spread(mat, whole)
        end_rest(REST0, rest0, 15)
        end_table()
        receive(8)

        def wide_back(total, base, key_g, key_b, lin, mu, rs, zref, dvf, dst):
            sdv = row(total, base, 512)
            sdh = row(total, base + 4, 512)
            set_gvec(key_b, sdv)
            set_gvec(key_g, sdh)
            c1 = sdv / counts[512]
            c2 = sdh / counts[512]

            def block(b, _):
                rows = pl.ds(pl.multiple_of(b * 32, 32), 32)
                hat = (zref[rows, :] - mu) * rs
                dz = lin * (dvf(rows) - c1 - hat * c2) * lanes(mref[rows, :], 4)
                dst[rows, :] = dz.astype(BF16)
                return 0

            lax.fori_loop(0, 8, block, 0)

        wide_back(
            totals(8),
            0,
            (3, "g_out"),
            (3, "b_out"),
            lin6,
            mu6,
            rs6,
            z6,
            lambda rows: dv6[rows, :],
            dz3,
        )

        def attended_grad(twin, w, aref, mat, gw, land):
            pda[0] = dot_rt(dz3[...], w[...].reshape(CMID, 512))
            swap = to_twin(twin, pda.at[0], pda.at[1])
            swap.start()
            gw[...] = dot_lt(aref[...], dz3[...]).astype(BF16).reshape(16, 16, 512)
            shed(mat, gw, land)
            swap.wait()

        def summed_grad(rows):
            return (pda[0, rows, :] + pda[1, rows, :]).astype(BF16).astype(F32)

        attended_grad(5, w_out3, a2, OUT3, gw_out3, ga_out3)

        def beside9():
            for mat, whole in ((IN1, w_in1), (MID2, w_mid2), (OUT3, w_out3)):
                end_spread(mat, whole)
            end_rest(REST2, rest2, 16)
            shed_mid(OUT3, gw_out3, ga_out3, gt_out3, gd_out3)

        grad_rest2 = attention_backward(
            9,
            mid2,
            q2,
            rest2,
            rg2,
            z5,
            rr2,
            cols2,
            MID2,
            gw_mid2,
            ga_mid2,
            summed_grad,
            beside9,
        )

        ep[...] = jnp.zeros(ep.shape, F32)
        for di in range(3):
            part = dot_rt(dz_low[...], w_mid2[8 * di : 8 * (di + 1)].reshape(384, 256))
            for dj in range(3):
                lo = SIDE * di
                ep[dj, lo : lo + PX, :] += part[:, 128 * dj : 128 * (dj + 1)]
        grad = ep[1, SIDE : SIDE + PX, :]
        grad = grad + shift_cols(ep[0, SIDE : SIDE + PX, :], -1)
        grad = grad + shift_cols(ep[2, SIDE : SIDE + PX, :], 1)
        grad = grad.astype(BF16).astype(F32)
        v = z4[...] * lin4 + off4
        hat4 = (z4[...] - mu4) * rs4
        sg = sigmoid(v)
        dv4 = grad * (sg * (1.0 + v * (1.0 - sg)) * mref[...])
        dh[0] = dv4
        put(10, 0, jnp.sum(dv4, axis=0, keepdims=True))
        put(10, 1, jnp.sum(dv4 * hat4, axis=0, keepdims=True))
        send(10)
        grad_rest2()
        rest_meet(2, REST2, rg2, rl2)
        shed_more(OUT3, gw_out3, ga_out3, gd_out3, gp_out3, gb_out3)
        receive(10)
        total = totals(10)
        set_gvec((1, "b_in"), total[0:1, :])
        set_gvec((1, "g_in"), total[1:2, :])
        hat4 = (z4[...] - mu4) * rs4
        dz = lin4 * (dh[0] - total[0:1, :] / count1 - hat4 * (total[1:2, :] / count1)) * mref[...]
        dz4[k] = dz.astype(BF16)
        swap = to_twin(6, dz4.at[k], dz4.at[k])
        swap.start()
        swap.wait()

        def dy_block(b, acc):
            rows = pl.ds(pl.multiple_of(b * 64, 64), 64)
            dy = dot_rt(dz4[0, rows, :], w_in1[0].reshape(512, 128))
            dy = dy + dot_rt(dz4[1, rows, :], w_in1[1].reshape(512, 128))
            dy = dy + dv6[rows, :].astype(BF16).astype(F32)
            v = v3[rows, :]
            sg = sigmoid(v)
            dv = dy * (sg * (1.0 + v * (1.0 - sg)) * lanes(mref[rows, :], 4))
            v3[rows, :] = dv
            low = dv.astype(BF16).astype(F32)
            hat = (z3[rows, :] - mu3) * rs3
            hats = (zs[rows, :] - mus) * rss
            return tuple(
                x + fold8(y) for x, y in zip(acc, (dv, dv * hat, low, low * hats))
            )

        acc = lax.fori_loop(0, 4, dy_block, (zero512,) * 4)
        for j, x in enumerate(acc):
            put(11, 4 * j, jnp.sum(x, axis=0, keepdims=True))
        send(11)
        both4 = jnp.concatenate([dz4[0], dz4[1]], axis=1)
        gw_in1[...] = dot_lt(y1[...], both4).astype(BF16).reshape(32, 16, 256)
        shed(IN1, gw_in1, ga_in1)
        shed_mid(MID2, gw_mid2, ga_mid2, gt_mid2, gd_mid2)
        left = home(OUT3, gb_out3, gf_out3) + rest_home(2, REST2, rg2, rl2, rf2)
        receive(11)
        total = totals(11)
        wide_back(
            total,
            0,
            (1, "g_out"),
            (1, "b_out"),
            lin3,
            mu3,
            rs3,
            z3,
            lambda rows: v3[rows, :],
            dz3,
        )
        wide_back(
            total,
            8,
            (0, "g_sc"),
            (0, "b_sc"),
            lins,
            mus,
            rss,
            zs,
            lambda rows: v3[rows, :].astype(BF16).astype(F32),
            dzs,
        )
        attended_grad(7, w_out1, a1, OUT1, gw_out1, ga_out1)

        def short_back():
            part = dot_rt(dzs[...], w_sc[...].reshape(CIN, 512))
            pdp[0] = jnp.where(k == 0, part[:, 256:512], part[:, 0:256])
            to_twin(8, pdp.at[0], pdp.at[1]).start()
            pdp[2] = jnp.where(k == 0, part[:, 0:256], part[:, 256:512])
            gw_sc[...] = dot_lt(pool[...], dzs[...]).astype(BF16).reshape(32, 16, 512)
            shed(SC0, gw_sc, ga_sc)
            table_meet(0, LATE_ROWS, TABLE_ROWS - LATE_ROWS)
            shed_mid(IN1, gw_in1, ga_in1, gt_in1, gd_in1)
            shed_mid(OUT1, gw_out1, ga_out1, gt_out1, gd_out1)
            shed_more(MID2, gw_mid2, ga_mid2, gd_mid2, gp_mid2, gb_mid2)

        grad_rest0 = attention_backward(
            12,
            mid1,
            q1,
            rest0,
            rg0,
            z2,
            rr1,
            cols1,
            MID0,
            gw_mid0,
            ga_mid0,
            summed_grad,
            short_back,
        )

        for p in range(4):
            dh[p] = jnp.zeros((PX, 128), F32)
        for di in range(3):
            part = dot_rt(dz_low[...], w_mid0[8 * di : 8 * (di + 1)].reshape(384, 256))
            pr = 0 if di == 1 else 1
            for dj in range(3):
                x = part[:, 128 * dj : 128 * (dj + 1)]
                if dj == 0:
                    x = shift_cols(x, -1)
                p = 2 * pr + (0 if dj == 1 else 1)
                if di == 0:
                    dh[p, 0 : PX - SIDE, :] += x[SIDE:PX]
                else:
                    dh[p] += x

        def dv1_block(p, acc):
            z = z1[p]
            v = z * lin1 + off1
            sg = sigmoid(v)
            dv = dh[p] * (sg * (1.0 + v * (1.0 - sg)) * mref[...])
            dh[p] = dv
            return (acc[0] + fold8(dv), acc[1] + fold8(dv * ((z - mu1) * rs1)))

        t0, t1 = lax.fori_loop(0, 4, dv1_block, (zero8, zero8))
        put(13, 0, jnp.sum(t0, axis=0, keepdims=True))
        put(13, 1, jnp.sum(t1, axis=0, keepdims=True))
        send(13)
        grad_rest0()
        rest_meet(1, REST0, rg0, rl0)
        shed_more(IN1, gw_in1, ga_in1, gd_in1, gp_in1, gb_in1)
        shed_more(OUT1, gw_out1, ga_out1, gd_out1, gp_out1, gb_out1)
        shed_mid(SC0, gw_sc, ga_sc, gt_sc, gd_sc)
        left = left + home(MID2, gb_mid2, gf_mid2)
        left = left + table_home(0, LATE_ROWS, TABLE_ROWS - LATE_ROWS)
        receive(13)
        total = totals(13)
        set_gvec((0, "b_in"), total[0:1, :])
        set_gvec((0, "g_in"), total[1:2, :])
        table_meet(3, 0, LATE_ROWS)
        k1 = total[0:1, :] / (4.0 * count1)
        k2 = total[1:2, :] / (4.0 * count1)

        def dz1_block(p, _):
            hat = (z1[p] - mu1) * rs1
            dz1[k, p] = (lin1 * (dh[p] - k1 - hat * k2) * mref[...]).astype(BF16)
            return 0

        lax.fori_loop(0, 4, dz1_block, 0)
        swap = to_twin(9, dz1.at[k], dz1.at[k])
        swap.start()
        total = jnp.zeros((CIN, 128), F32)
        for p in range(4):
            total = total + dot_lt(um[p], dz1[k, p])
        gw_in0[...] = total.astype(BF16).reshape(32, 16, 128)

        def shed_in0(i, _):
            p = lax.rem(8 * s + i, 32)
            move(
                gw_in0.at[p],
                gb_in0.at[s * chips + c, k],
                gb_s.at[0],
                gb_r.at[0],
                (p // 8, p % 8),
            )
            return 0

        lax.fori_loop(0, 32, shed_in0, 0)
        shed_more(SC0, gw_sc, ga_sc, gd_sc, gp_sc, gb_sc)
        shed_mid(MID0, gw_mid0, ga_mid0, gt_mid0, gd_mid0)
        swap.wait()
        to_twin(8, pdp.at[0], pdp.at[1]).wait()

        def du_block(p, _):
            mine = pl.ds(16 * k, 16)
            grad = dot_rt(dz1[0, p], w_in0[0, mine].reshape(256, 128))
            grad = grad + dot_rt(dz1[1, p], w_in0[1, mine].reshape(256, 128))
            grad = (grad + 0.25 * (pdp[1] + pdp[2])) * lanes(mref[...], 2)
            low = grad.astype(BF16)
            ibuf[0, p] = low[:, 0:128]
            ibuf[1, p] = low[:, 128:256]
            return 0

        lax.fori_loop(0, 4, du_block, 0)
        for j in range(2):
            move(
                ibuf.at[j],
                out_i.at[lax.rem(s, 2)],
                oi_s.at[j],
                oi_r.at[lax.rem(s, 2)],
                (2 * k + j, 2 * c + s // 2),
            )

        left = left + home(IN1, gb_in1, gf_in1)
        left = left + home(OUT1, gb_out1, gf_out1)
        shed_more(MID0, gw_mid0, ga_mid0, gd_mid0, gp_mid0, gb_mid0)
        left = left + home(SC0, gb_sc, gf_sc)
        left = left + rest_home(1, REST0, rg0, rl0, rf0)
        left = left + table_home(3, 0, LATE_ROWS)
        left = left + home(IN0, gb_in0, gf_in0)
        left = left + home(MID0, gb_mid0, gf_mid0)

        for mat, gw in (
            (MID0, gw_mid0),
            (SC0, gw_sc),
            (OUT1, gw_out1),
            (IN1, gw_in1),
            (MID2, gw_mid2),
            (OUT3, gw_out3),
        ):
            end_shed(mat, gw)

        @pl.when(holds(IN0))
        def _():
            full_wait(gw_in0.at[pl.ds(0, 31)], gb_s.at[0])
            full_wait(fill.at[pl.ds(0, 8 * (4 * n - 1))], a_s.at[0])

        @pl.when(jnp.logical_not(holds(IN0)))
        def _():
            full_wait(gw_in0, gb_s.at[0])

        for i, mat, land in ((1, REST0, rl0), (2, REST2, rl2)):

            @pl.when((s == mat.row) & (d < 8))
            def _():
                full_wait(land, v_s.at[i])

        @pl.when((s == 0) & (d < 2))
        def _():
            full_wait(gvl.at[pl.ds(LATE_ROWS, TABLE_ROWS - LATE_ROWS)], v_s.at[0])
            full_wait(gvl.at[pl.ds(0, LATE_ROWS)], v_s.at[3])

        fill_up(nought, fill2, left, HOME_ROWS, gc_s)
        full_wait(fill2, gc_s)
        full_wait(fill, h_s)
        full_wait(out_w, gc_r)
        for slot in range(2):
            pltpu.make_async_copy(out_o.at[slot], out_o.at[slot], oo_r.at[slot]).wait()
            pltpu.make_async_copy(out_i.at[slot], out_i.at[slot], oi_r.at[slot]).wait()
        for slot in range(2):
            for kk in range(2):
                end_move(
                    img.at[slot, pl.ds(2 * kk, 2)],
                    img_s.at[slot, kk],
                    (2 * k + slot, 2 * c + kk),
                )
            end_move(cot.at[slot], ct_s.at[slot], (2 * k + slot, 2 * c + s // 2))
        for j in range(2):
            end_move(obuf.at[j], oo_s.at[j], (2 * k + j, 2 * c + s // 2))
            end_move(ibuf.at[j], oi_s.at[j], (2 * k + j, 2 * c + s // 2))
        for q in range(4):
            here = u.at[q, pl.ds(2 * k, 2)]
            pltpu.make_async_copy(here, here, bs.at[10 + q]).wait()
        for ph in range(PHASES):
            end_send(ph)

    return kernel


def call_kernel(n, operands):
    chips = n // 2
    shard_rows = WSLOTS // (128 * n)
    fill_rows = max(shard_rows + 28 * n, 96 * (n - 1), 100 * n, 8 * (4 * n - 1), 16 * (2 * n - 1))

    def vm(*shape, dtype=F32):
        return pltpu.VMEM(shape, dtype)

    def low(*shape):
        return pltpu.VMEM(shape, BF16)

    dma = pltpu.SemaphoreType.DMA
    scratch = [
        vm(PHASES, 16, 128),
        vm(PHASES, 2, n, 16, 128),
        vm(2, 2, 8, 128),
        low(4, 4, PX, 128),
        low(4, PX, CIN),
        low(PX, CIN),
        low(2, PX, 256),
        vm(PX, 128),
        vm(4, PX, 128),
        vm(PX, 256),
        vm(PX, 512),
        vm(PX, 512),
        vm(PX, 128),
        vm(PX, 256),
        vm(PX, 512),
        vm(PX, 512),
        low(PX, 1152),
        low(PX, 1152),
        vm(2, PX, 256),
        vm(2, PX, 256),
        low(PX, 256),
        low(PX, 256),
        low(PX, 512),
        vm(PX, 512),
        vm(PX, 256),
        vm(PX, 256),
        vm(2, PX, 128),
        vm(2, PX, 256),
        vm(3, PX, 256),
        low(2, PX, 128),
        low(2, 4, PX, 128),
        low(PX, 512),
        low(PX, 512),
        vm(3, PX + 2 * SIDE, 128),
        vm(4, PX, 128),
        low(2, PX, 256),
        low(2, 4, PX, 128),
        vm(shard_rows, 128),
        vm(128, 128),
        vm(fill_rows, 128),
        vm(HOME_ROWS, 128),
        vm(TABLE_ROWS, 128),
        low(2, 32, 16, 128),
        low(24, 48, 256),
        vm(800, 128),
        low(32, 16, 512),
        low(16, 16, 512),
        low(2, 32, 16, 128),
        low(24, 48, 256),
        vm(800, 128),
        low(16, 16, 512),
        vm(32, 128),
        vm(192, 128),
        vm(25, 128),
        vm(128, 128),
        vm(128, 128),
        vm(64, 128),
        vm(192, 128),
        vm(25, 128),
        vm(128, 128),
        low(2, 16, 128),
        low(2, 48, 256),
        low(2, 16, 512),
        low(2, 16, 512),
        low(2, 2, 16, 128),
        low(2, 48, 256),
        low(2, 16, 512),
        low(shard_rows // 32 + 2, 2, 16, 128),
        low(shard_rows // 192 + 2, 2, 48, 256),
        low(shard_rows // 128 + 2, 2, 16, 512),
        low(shard_rows // 128 + 2, 2, 16, 512),
        low(shard_rows // 192 + 2, 2, 48, 256),
        low(shard_rows // 128 + 2, 2, 16, 512),
        low(32, 16, 128),
        low(24, 48, 256),
        low(32, 16, 512),
        low(16, 16, 512),
        low(32, 16, 256),
        low(24, 48, 256),
        low(16, 16, 512),
        low(2, 2, 3, 48, 256),
        low(2, 2, 4, 16, 512),
        low(2, 2, 2, 16, 512),
        low(2, 2, 4, 16, 256),
        low(2, 2, 3, 48, 256),
        low(2, 2, 2, 16, 512),
        low(6, 48, 256),
        low(8, 16, 512),
        low(4, 16, 512),
        low(8, 16, 256),
        low(6, 48, 256),
        low(4, 16, 512),
        low(4 * chips, 2, 16, 128),
        low(chips, 2, 48, 256),
        low(chips, 2, 16, 512),
        low(chips, 2, 16, 512),
        low(chips, 2, 16, 256),
        low(chips, 2, 48, 256),
        low(chips, 2, 16, 512),
        vm(32, 128),
        vm(192, 128),
        vm(128, 128),
        vm(128, 128),
        vm(64, 128),
        vm(192, 128),
        vm(128, 128),
        vm(784, 128),
        vm(784, 128),
        vm(REST_PART, 128),
        vm(REST_PART, 128),
        vm(REST_PART, 128),
        vm(REST_PART, 128),
        vm(TABLE_ROWS, 128),
        vm(TABLE_ROWS, 128),
        vm(TABLE_ROWS, 128),
        low(2, 3, 48, 256),
        low(2, 3, 48, 256),
        low(2, 3, 48, 256),
        low(2, 3, 48, 256),
        low(2, 4, 16, 512),
        low(2, 4, 16, 512),
        low(2, 2, 16, 512),
        low(2, 2, 16, 512),
        low(2, 2, 16, 512),
        low(2, 2, 16, 512),
        low(2, 4, 16, 256),
        low(2, 4, 16, 256),
        dma((PHASES,)),
        dma((PHASES, 2)),
        dma((17,)),
        dma((17,)),
        dma((2, 2)),
        dma((4,)),
        dma((2,)),
        dma((2,)),
        dma((2,)),
        dma((2,)),
        dma((2,)),
        dma((2,)),
        dma,
        dma,
        dma((2,)),
        dma((9,)),
        dma((9,)),
        dma((9,)),
        dma((9,)),
        dma((9, 4)),
        dma((9,)),
        dma((9, 2)),
        dma((9,)),
        dma((9,)),
        dma,
        dma,
        dma((4,)),
        dma((4,)),
        dma((9,)),
        dma((9, 2)),
    ]
    sds = jax.ShapeDtypeStruct
    outs = (
        sds((2, PX, 256), BF16),
        sds((2, 4, PX, 128), BF16),
        sds((shard_rows, 128), F32),
    )
    vmem = pl.BlockSpec(memory_space=pltpu.VMEM)
    smem = pl.BlockSpec(memory_space=pltpu.SMEM)
    return pl.pallas_call(
        make_kernel(n),
        out_shape=outs,
        in_specs=[smem if i == 2 else vmem for i in range(len(operands))],
        out_specs=[vmem] * len(outs),
        scratch_shapes=scratch,
        compiler_params=pltpu.CompilerParams(
            collective_id=0, has_side_effects=True, vmem_limit_bytes=60 << 20
        ),
    )(*operands)


def per_device(images, cotangent, res_codes, section_weights):
    n = lax.axis_size("dp")
    planes = images.reshape(2, SIDE, 2, SIDE, 2, 128).transpose(0, 2, 4, 1, 3, 5)
    out_o, out_i, out_w = call_kernel(
        n,
        (
            planes.reshape(2, 4, PX, 128),
            cotangent.reshape(2, PX, 256),
            res_codes,
            section_weights.reshape(-1, 128),
        ),
    )
    block_out = out_o.reshape(2, SIDE, SIDE, 256)
    input_grad = (
        out_i.reshape(2, 2, 2, SIDE, SIDE, 128).transpose(0, 3, 1, 4, 2, 5).reshape(images.shape)
    )
    return block_out, input_grad, out_w.reshape(section_weights.shape)


def solution(mesh):
    return jax.shard_map(
        per_device,
        mesh=mesh,
        in_specs=(
            P("dp", None, None, "section"),
            P("dp", None, None, "section"),
            P("dp"),
            P("section", "dp"),
        ),
        out_specs=(
            P("dp", None, None, "section"),
            P("dp", None, None, "section"),
            P("section", "dp"),
        ),
        check_vma=False,
    )
```

```python
import jax
import jax.numpy as jnp
from jax import lax
from jax.experimental import pallas as pl
from jax.experimental.pallas import tpu as pltpu
from jax.sharding import PartitionSpec as P

CIN = 512
COUT = 1024
CMID = 256
CSQ = 128
SIDE = 16
PX = SIDE * SIDE
HALF = 128
WSLOTS = 1351680
EPS = 1e-05
HIGH = lax.Precision.HIGHEST
MESH = pl.DeviceIdType.MESH
F32 = jnp.float32
BF16 = jnp.bfloat16
PHASES = 14
ROWS = (
    (3, 0),
    (4, 0),
    (2, 2),
    (16, 0),
    (2, 0),
    (4, 0),
    (2, 2),
    (8, 0),
    (8, 0),
    (10, 2),
    (2, 0),
    (16, 0),
    (10, 2),
    (2, 0),
)


class Matrix:
    def __init__(self, index, row, start, blocks, pieces, rows, first, step, split="columns"):
        self.index = index
        self.row = row
        self.start = start
        self.blocks = blocks
        self.pieces = pieces
        self.rows = rows
        self.first = first
        self.step = step
        self.split = split
        self.flat = blocks * rows
        self.width = 128 * (blocks // 2 if split == "columns" else blocks)


IN0 = Matrix(0, 0, 0, 2, 8, 16, 0, 1)
MID0 = Matrix(1, 0, 1028, 4, 6, 48, 0, 1)
REST0 = Matrix(2, 0, 5636, 1, 8, 25, 0, 1, split="none")
SC0 = Matrix(3, 0, 6418, 8, 8, 16, 0, 1)
OUT1 = Matrix(4, 1, 0, 8, 4, 16, 1, 2)
IN1 = Matrix(5, 1, 2064, 2, 8, 16, 0, 1, split="rows")
MID2 = Matrix(6, 2, 0, 4, 6, 48, 2, 1)
REST2 = Matrix(7, 2, 4608, 1, 8, 25, 0, 1, split="none")
OUT3 = Matrix(8, 3, 0, 8, 4, 16, 0, 2)
MATRICES = (IN0, MID0, REST0, SC0, OUT1, IN1, MID2, REST2, OUT3)
CUT = (IN0, MID0, SC0, OUT1, MID2, OUT3)
USED = (10530, 4116, 5390, 2064)
REST_ROWS = 782
HOME_ROWS = 1152
REST_PART = 97
AT_SQ, AT_GSQ, AT_BSQ, AT_EX, AT_BEX = 8, 264, 265, 266, 778
TABLE = {
    (0, "g_in"): (0, 1024, 1),
    (0, "b_in"): (2, 1026, 1),
    (0, "g_mid"): (4, 5636, 2),
    (0, "b_mid"): (8, 5640, 2),
    (0, "g_sc"): (12, 10514, 4),
    (0, "b_sc"): (20, 10522, 4),
    (1, "g_out"): (28, 2048, 4),
    (1, "b_out"): (36, 2056, 4),
    (1, "g_in"): (44, 4112, 1),
    (1, "b_in"): (46, 4114, 1),
    (3, "g_out"): (48, 2048, 4),
    (3, "b_out"): (56, 2056, 4),
    (2, "g_mid"): (64, 4608, 2),
    (2, "b_mid"): (68, 4612, 2),
}
TABLE_ROWS = 72
LATE_ROWS = 12
SECTION_ROWS = {0: (0, 28), 1: (28, 20), 2: (64, 8), 3: (48, 16)}
AT_MID = {0: 4, 2: 64}
RANGES = (
    (0, 1024, 4, 0),
    (0, 5636, 8, 4),
    (0, 10514, 16, 12),
    (1, 2048, 16, 28),
    (1, 4112, 4, 44),
    (2, 4608, 8, 64),
    (3, 2048, 16, 48),
)


def dot(a, b):
    return lax.dot_general(a, b, (((1,), (0,)), ((), ())), preferred_element_type=F32)


def dot_rt(a, b):
    return lax.dot_general(a, b, (((1,), (1,)), ((), ())), preferred_element_type=F32)


def dot_lt(a, b):
    return lax.dot_general(a, b, (((0,), (0,)), ((), ())), preferred_element_type=F32)


def dot_hi(a, b, dims=((1,), (0,))):
    return lax.dot_general(a, b, (dims, ((), ())), precision=HIGH, preferred_element_type=F32)


def sigmoid(v):
    return 0.5 + 0.5 * jnp.tanh(0.5 * v)


def fold8(x):
    return jnp.sum(x.reshape(x.shape[0] // 8, 8, x.shape[1]), axis=0)


def lanes(x, count):
    return jnp.concatenate([x] * count, axis=1) if count > 1 else x


def make_kernel(n):
    chips = n // 2
    shard_rows = WSLOTS // (128 * n)
    fill_rows = max(shard_rows + 28 * n, 96 * (n - 1), 100 * n, 8 * (4 * n - 1), 16 * (2 * n - 1))

    def kernel(
        img,
        cot,
        codes,
        shard,
        out_o,
        out_i,
        out_w,
        snd,
        rcv,
        side_t,
        u,
        um,
        pool,
        ctb,
        mref,
        z1,
        z2,
        zs,
        z3,
        z4,
        z5,
        z6,
        v3,
        cols1,
        cols2,
        rr1,
        rr2,
        a1,
        a2,
        y1,
        dv6,
        dbuf,
        spb,
        pz,
        pda,
        pdp,
        dz4,
        dz1,
        dz3,
        dzs,
        ep,
        dh,
        obuf,
        ibuf,
        sround,
        nought,
        fill,
        fill2,
        table,
        w_in0,
        w_mid0,
        rest0,
        w_sc,
        w_out1,
        w_in1,
        w_mid2,
        rest2,
        w_out3,
        ln_in0,
        ln_mid0,
        ln_rest0,
        ln_sc,
        ln_out1,
        ln_in1,
        ln_mid2,
        ln_rest2,
        ln_out3,
        st_in0,
        st_mid0,
        st_sc,
        st_out1,
        st_in1,
        st_mid2,
        st_out3,
        cu_in0,
        cu_mid0,
        cu_sc,
        cu_out1,
        cu_mid2,
        cu_out3,
        gw_in0,
        gw_mid0,
        gw_sc,
        gw_out1,
        gw_in1,
        gw_mid2,
        gw_out3,
        ga_mid0,
        ga_sc,
        ga_out1,
        ga_in1,
        ga_mid2,
        ga_out3,
        gp_mid0,
        gp_sc,
        gp_out1,
        gp_in1,
        gp_mid2,
        gp_out3,
        gb_in0,
        gb_mid0,
        gb_sc,
        gb_out1,
        gb_in1,
        gb_mid2,
        gb_out3,
        gf_in0,
        gf_mid0,
        gf_sc,
        gf_out1,
        gf_in1,
        gf_mid2,
        gf_out3,
        rg0,
        rg2,
        rl0,
        rl2,
        rf0,
        rf2,
        gvt,
        gvl,
        gvs,
        gd_mid0,
        gt_mid0,
        gd_mid2,
        gt_mid2,
        gd_sc,
        gt_sc,
        gd_out1,
        gt_out1,
        gd_out3,
        gt_out3,
        gd_in1,
        gt_in1,
        hb_in0,
        hi_in0,
        hb_mid0,
        hi_mid0,
        hb_sc,
        hi_sc,
        hb_out1,
        hi_out1,
        hb_mid2,
        hi_mid2,
        hb_out3,
        hi_out3,
        fill3,
        pixels,
        planes,
        merged,
        ssem,
        rsem,
        bs,
        br,
        img_s,
        img_r,
        ct_s,
        ct_r,
        oo_s,
        oo_r,
        oi_s,
        oi_r,
        h_s,
        t_s,
        t_r,
        h_r,
        a_s,
        c_r,
        f_s,
        q_r,
        ga_s,
        ga_r,
        gb_s,
        gb_r,
        gc_s,
        gc_r,
        v_s,
        v_r,
        gd_s,
        gd_r,
        hr_in0,
        hr_mid0,
        hr_sc,
        hr_out1,
        hr_mid2,
        hr_out3,
        hs_s,
    ):
        s = lax.axis_index("section")
        d = lax.axis_index("dp")
        c = d // 2
        k = d % 2
        m = s % 2
        g = (s // 2) * chips + c

        def peer(o, kk):
            gg = g ^ o
            return ((gg // chips) * 2 + m, 2 * (gg % chips) + kk)

        order = sorted(range(1, n), key=lambda o: (o % chips) + o // chips, reverse=True)

        nought[...] = jnp.zeros(nought.shape, F32)
        barrier = pltpu.get_barrier_semaphore()
        me = s * n + d
        beside_x = s + 1 - 2 * (s % 2)
        beside_y = lax.rem(s + 2, 4)

        def greet(i, _):
            e = lax.rem(me + i, 4 * n)
            pl.semaphore_signal(barrier, inc=1, device_id=(e // n, e % n), device_id_type=MESH)
            return 0

        lax.fori_loop(1, 4 * n, greet, 0)
        sround[...] = shard[...].astype(BF16).astype(F32)

        for slot in range(2):

            def widen(i, _):
                rows = pl.ds(pl.multiple_of(i * 128, 128), 128)
                pixels[rows, :] = img[slot, rows, :].astype(F32)
                return 0

            lax.fori_loop(0, 8, widen, 0)

            def split(r, _):
                for p in range(4):
                    at = (2 * r + p // 2) * 2 * SIDE + p % 2
                    x = pixels[pl.ds(at, SIDE, stride=2), :]
                    planes[slot, p, pl.ds(pl.multiple_of(r * SIDE, SIDE), SIDE), :] = x.astype(BF16)
                return 0

            lax.fori_loop(0, SIDE, split, 0)
        pl.semaphore_wait(barrier, 4 * n - 1)

        def to_twin(i, src, dst):
            return pltpu.make_async_remote_copy(
                src, dst, bs.at[i], br.at[i], device_id=(s, 2 * c + 1 - k), device_id_type=MESH
            )

        def move(src, dst, s_sem, r_sem, dev):
            own = (dev[0] == s) & (dev[1] == d)

            @pl.when(own)
            def _():
                pltpu.make_async_copy(src, dst, r_sem).start()

            @pl.when(jnp.logical_not(own))
            def _():
                pltpu.make_async_remote_copy(
                    src, dst, s_sem, r_sem, device_id=dev, device_id_type=MESH
                ).start()

        def end_move(src, s_sem, dev):
            own = (dev[0] == s) & (dev[1] == d)

            @pl.when(jnp.logical_not(own))
            def _():
                pltpu.make_async_copy(src, src, s_sem).wait()

        def is_self(dev):
            return (dev[0] == s) & (dev[1] == d)

        def move_rows(src, src_at, dst, dst_at, count, full, s_sem, r_sem, dev):
            def go(size, at):
                move(
                    src.at[pl.ds(src_at + at, size)],
                    dst.at[pl.ds(dst_at + at, size)],
                    s_sem,
                    r_sem,
                    dev,
                )

            def chunks(size, start, many):
                def one(i, _):
                    go(size, start + i * size)
                    return 0

                lax.fori_loop(0, many, one, 0)

            if full > 1:

                @pl.when(count == full)
                def _():
                    go(full, 0)

                @pl.when(count < full)
                def _():
                    if full > 16:
                        chunks(16, 0, count // 16)
                        chunks(1, (count // 16) * 16, count % 16)
                    else:
                        chunks(1, 0, count)

            else:
                chunks(1, 0, count)
            return jnp.where(is_self(dev), 0, count)

        def fill_up(src, dst, first, last, sem):
            def chunks(size, start, many):
                def one(i, _):
                    pltpu.make_async_copy(
                        src.at[pl.ds(0, size)], dst.at[pl.ds(start + i * size, size)], sem
                    ).start()
                    return 0

                lax.fori_loop(0, many, one, 0)

            count = last - first
            chunks(128, first, count // 128)
            chunks(16, first + (count // 128) * 128, count % 128 // 16)
            chunks(1, first + (count // 16) * 16, count % 16)

        used = jnp.where(
            s == 0, USED[0], jnp.where(s == 1, USED[1], jnp.where(s == 2, USED[2], USED[3]))
        )

        mine_from = d * shard_rows
        mine_to = mine_from + shard_rows

        def cut(mat, land, stage, base):
            for j in range(mat.blocks):
                for h in range(2):
                    if mat.split == "rows":
                        x = land[pl.ds(base + h * mat.flat + j, mat.rows, stride=mat.blocks), :]
                        stage[h, j] = x.astype(BF16)
                    elif j // (mat.blocks // 2) == h:
                        x = land[pl.ds(base + j, mat.rows, stride=mat.blocks), :]
                        at = 128 * (j % (mat.blocks // 2))
                        stage[h, :, at : at + 128] = x.astype(BF16)

        def holds(mat):
            i = d - mat.first
            inside = (i >= 0) & (i < mat.step * mat.pieces)
            return inside & (i % mat.step == 0) if mat.step > 1 else inside

        def piece(mat):
            return s * mat.pieces + jnp.maximum(d - mat.first, 0) // mat.step

        def scatter_cut(mat, land, stage, ready, part=0, parts=1):
            first = jnp.maximum(mine_from - mat.start, 0) // mat.flat
            last = (jnp.maximum(mine_to - mat.start, 0) + mat.flat - 1) // mat.flat
            last = jnp.minimum(last, 4 * mat.pieces)

            def one(p, sent):
                start = mat.start + p * mat.flat
                lo = jnp.maximum(start, mine_from)
                count = jnp.minimum(start + mat.flat, mine_to) - lo
                dev = (p // mat.pieces, mat.first + mat.step * (p % mat.pieces))

                def in_one():
                    to = ready.at[p - first]
                    cut(mat, sround, to, lo - mine_from)
                    move(to, stage, h_s, h_r.at[mat.index], dev)
                    return jnp.where(is_self(dev), 0, mat.flat // 2)

                def in_rows():
                    return move_rows(
                        sround,
                        lo - mine_from,
                        land,
                        lo - start,
                        count,
                        mat.flat,
                        h_s,
                        h_r.at[mat.index],
                        dev,
                    )

                return sent + lax.cond(count == mat.flat, in_one, in_rows)

            step = (jnp.maximum(last - first, 0) + parts - 1) // parts
            begin = first + part * step
            end = jnp.minimum(last, begin + step)
            return lax.fori_loop(begin, end, one, jnp.int32(0))

        def stage_ready(mat, land, stage):
            start = mat.start + piece(mat) * mat.flat
            whole = start // shard_rows == (start + mat.flat - 1) // shard_rows

            @pl.when(whole)
            def _():
                full_wait(stage, h_r.at[mat.index])

            @pl.when(jnp.logical_not(whole))
            def _():
                full_wait(land, h_r.at[mat.index])
                cut(mat, land, stage, 0)

        def scatter_pieces(mat, land, part=0, parts=1):
            total = mat.pieces * 4 * (2 if mat.split == "rows" else 1)
            first = jnp.maximum(mine_from - mat.start, 0) // mat.flat
            last = (jnp.maximum(mine_to - mat.start, 0) + mat.flat - 1) // mat.flat

            def one(p, sent):
                start = mat.start + p * mat.flat
                lo = jnp.maximum(start, mine_from)
                count = jnp.minimum(start + mat.flat, mine_to) - lo
                h = p // (4 * mat.pieces)
                q = p % (4 * mat.pieces)
                dev = (q // mat.pieces, mat.first + mat.step * (q % mat.pieces))
                return sent + move_rows(
                    sround,
                    lo - mine_from,
                    land,
                    h * mat.flat + lo - start,
                    count,
                    mat.flat,
                    h_s,
                    h_r.at[mat.index],
                    dev,
                )

            last = jnp.minimum(last, total)
            step = (jnp.maximum(last - first, 0) + parts - 1) // parts
            begin = first + part * step
            end = jnp.minimum(last, begin + step)
            return lax.fori_loop(begin, end, one, jnp.int32(0))

        def scatter_table(start, rows, at):
            lo = jnp.maximum(start, mine_from)
            count = jnp.maximum(jnp.minimum(start + rows, mine_to) - lo, 0)

            def one(i, sent):
                e = lax.rem(d + i, n)
                return sent + move_rows(
                    sround,
                    lo - mine_from,
                    table,
                    at + lo - start,
                    count,
                    rows,
                    h_s,
                    t_r.at[0],
                    (s, e),
                )

            return lax.fori_loop(0, jnp.where(count > 0, n, 0), one, jnp.int32(0))

        def pass_table():
            for r, (at, many) in SECTION_ROWS.items():

                @pl.when(s == r)
                def _():
                    here = table.at[pl.ds(at, many)]
                    full_wait(here, t_r.at[0])
                    for i in range(1, 4):
                        pltpu.make_async_remote_copy(
                            here,
                            here,
                            t_s,
                            t_r.at[1],
                            device_id=(lax.rem(s + i, 4), d),
                            device_id_type=MESH,
                        ).start()

        def table_arrived():
            for r in range(4):
                rest = TABLE_ROWS - SECTION_ROWS.get(r, (0, 0))[1]

                @pl.when(s == r)
                def _():
                    full_wait(table.at[pl.ds(0, rest)], t_r.at[1])

        def end_table():
            for r, (_, many) in SECTION_ROWS.items():

                @pl.when(s == r)
                def _():
                    full_wait(fill.at[pl.ds(0, 3 * many)], t_s)

        def full_wait(ref, sem):
            pltpu.make_async_copy(ref, ref, sem).wait()

        def when_row(r, body):
            return lax.cond(s == r, body, lambda: jnp.int32(0))

        sent = when_row(
            0,
            lambda: scatter_cut(MID0, ln_mid0, st_mid0, cu_mid0) + scatter_cut(IN0, ln_in0, st_in0, cu_in0),
        )

        for slot in range(2):
            for kk in range(2):
                move(
                    planes.at[slot, pl.ds(2 * kk, 2)],
                    u.at[s, pl.ds(2 * kk, 2)],
                    img_s.at[slot, kk],
                    img_r.at[s],
                    (2 * k + slot, 2 * c + kk),
                )
        for slot in range(2):
            width = (SIDE - 2 * codes[slot]).astype(F32)
            side_t[k, slot] = jnp.full((8, 128), width, F32)
        side_copy = to_twin(0, side_t.at[k], side_t.at[k])
        side_copy.start()
        snd[...] = jnp.zeros(snd.shape, F32)

        def row0():
            count = scatter_table(*RANGES[0][1:])
            count = count + scatter_table(*RANGES[1][1:]) + scatter_table(*RANGES[2][1:])
            return count + scatter_cut(SC0, ln_sc, st_sc, cu_sc)

        def row1():
            count = scatter_cut(OUT1, ln_out1, st_out1, cu_out1) + scatter_table(*RANGES[3][1:])
            return count + scatter_table(*RANGES[4][1:])

        sent = sent + when_row(0, row0)
        sent = sent + when_row(1, row1)
        sent = sent + when_row(2, lambda: scatter_table(*RANGES[5][1:]))
        sent = sent + when_row(3, lambda: scatter_table(*RANGES[6][1:]))

        def scatter_some(sent, part, parts):
            sent = sent + when_row(2, lambda: scatter_cut(MID2, ln_mid2, st_mid2, cu_mid2, part, parts))
            return sent + when_row(3, lambda: scatter_cut(OUT3, ln_out3, st_out3, cu_out3, part, parts))

        def scatter_early(sent):
            sent = sent + when_row(1, lambda: scatter_pieces(IN1, ln_in1))
            return scatter_some(sent, 1, 3)

        def scatter_late(sent):
            sent = scatter_some(sent, 2, 3)
            sent = sent + when_row(2, lambda: scatter_pieces(REST2, ln_rest2))
            fill_up(nought, fill, sent, fill_rows, h_s)

        sent = scatter_some(sent, 0, 3)
        sent = sent + when_row(0, lambda: scatter_pieces(REST0, ln_rest0))

        def spread(mat, land, stage, whole):
            @pl.when(holds(mat))
            def _():
                if mat.split == "rows":
                    full_wait(land, h_r.at[mat.index])
                    cut(mat, land, stage, 0)
                else:
                    stage_ready(mat, land, stage)
                p = piece(mat)

                def one(i, _):
                    e = lax.rem(d + i, n)
                    h = e % 2
                    dst = whole.at[:, p] if mat.split == "rows" else whole.at[p]
                    move(stage.at[h], dst, a_s.at[mat.index], c_r.at[mat.index], (s, e))
                    return 0

                lax.fori_loop(0, n, one, 0)

        def quarters(mat, whole, first, many, part=None):
            if part is None:
                span = pl.ds(first * mat.pieces, many * mat.pieces)
            else:
                half = mat.pieces // 2
                span = pl.ds(first * mat.pieces + part * half, half)
            return whole.at[:, span] if mat.split == "rows" else whole.at[span]

        def hand(mat, here, i, to):
            pltpu.make_async_remote_copy(
                here,
                here,
                f_s.at[mat.index],
                q_r.at[mat.index, i],
                device_id=(to, d),
                device_id_type=MESH,
            ).start()

        def pass_on(mat, whole):
            here = quarters(mat, whole, s, 1)
            full_wait(here, c_r.at[mat.index])
            hand(mat, here, 0, beside_x)
            hand(mat, here, 1, beside_y)

        def pass_far(mat, whole):
            full_wait(quarters(mat, whole, beside_x, 1), q_r.at[mat.index, 0])
            hand(mat, quarters(mat, whole, beside_x, 1, 0), 2, beside_y)
            full_wait(quarters(mat, whole, beside_y, 1), q_r.at[mat.index, 1])
            hand(mat, quarters(mat, whole, beside_y, 1, 1), 3, beside_x)

        def arrived(mat, whole):
            far = 3 - s
            for i in range(2):
                full_wait(quarters(mat, whole, far, 1, i), q_r.at[mat.index, 2 + i])

        def end_spread(mat, whole):
            @pl.when(holds(mat))
            def _():
                rows = mat.rows * mat.width // 256
                full_wait(fill.at[pl.ds(0, (n - 1) * rows)], a_s.at[mat.index])

            full_wait(quarters(mat, whole, 0, 3), f_s.at[mat.index])

        def spread_rest(mat, land, whole):
            @pl.when(holds(mat))
            def _():
                full_wait(land, h_r.at[mat.index])
                at = piece(mat) * mat.flat

                def one(i, _):
                    e = lax.rem(s * chips + c + i, 4 * chips)
                    move(
                        land,
                        whole.at[pl.ds(at, mat.flat)],
                        a_s.at[mat.index],
                        c_r.at[mat.index],
                        (e // chips, 2 * (e % chips)),
                    )
                    return 0

                lax.fori_loop(0, 4 * chips, one, 0)

        def share_rest(mat, whole, i):
            @pl.when(k == 0)
            def _():
                full_wait(whole, c_r.at[mat.index])
                to_twin(i, whole, whole).start()

        def rest_arrived(whole, i):
            @pl.when(k == 1)
            def _():
                to_twin(i, whole, whole).wait_recv()

        def end_rest(mat, whole, i):
            @pl.when(k == 0)
            def _():
                to_twin(i, whole, whole).wait_send()

            for kk in range(2):

                @pl.when(holds(mat) & (k == kk))
                def _():
                    rows = (4 * chips - 1 + kk) * mat.flat
                    full_wait(fill.at[pl.ds(0, rows)], a_s.at[mat.index])

        @pl.when(holds(IN0))
        def _():
            stage_ready(IN0, ln_in0, st_in0)

            def one(i, _):
                e = lax.rem(me + i, 4 * n)
                h = e % 2
                move(
                    st_in0.at[h],
                    w_in0.at[h, s * 8 + d],
                    a_s.at[0],
                    c_r.at[0],
                    (e // n, e % n),
                )
                return 0

            lax.fori_loop(0, 4 * n, one, 0)

        def whole_rows():
            count = jnp.int32(0)
            for mat in CUT:
                low, high = whole_range(mat)
                count = count + jnp.where(s == mat.row, (high - low) * mat.flat, 0)
            return count

        def part_of(mat, ref, quarter, part):
            half = mat.pieces // 2
            return ref.at[pl.ds(quarter * mat.pieces + part * half, half)]

        def shed(mat, gw, land):
            for part, to in enumerate((beside_x, beside_y)):
                for i, quarter in enumerate((to, 3 - s)):
                    pltpu.make_async_remote_copy(
                        part_of(mat, gw, quarter, part),
                        land.at[part, i],
                        ga_s.at[mat.index],
                        ga_r.at[mat.index, part],
                        device_id=(to, d),
                        device_id_type=MESH,
                    ).start()

        def shed_mid(mat, gw, land, add, land3):
            half = mat.pieces // 2
            for part, to in enumerate((beside_y, beside_x)):
                full_wait(land.at[part], ga_r.at[mat.index, part])
                base = to * mat.pieces + part * half

                def one(i, _):
                    x = gw[base + i].astype(F32) + land[part, 1, i].astype(F32)
                    add[part, i] = x.astype(BF16)
                    return 0

                lax.fori_loop(0, half, one, 0)
                pltpu.make_async_remote_copy(
                    add.at[part],
                    land3.at[part],
                    gd_s.at[mat.index],
                    gd_r.at[mat.index, part],
                    device_id=(to, d),
                    device_id_type=MESH,
                ).start()

        def shed_more(mat, gw, land, land3, part_sum, land2):
            half = mat.pieces // 2
            for part in range(2):
                full_wait(land3.at[part], gd_r.at[mat.index, part])

                def one(j, _):
                    i = part * half + j
                    x = gw[s * mat.pieces + i].astype(F32) + land[part, 0, j].astype(F32)
                    part_sum[i] = (x + land3[part, j].astype(F32)).astype(BF16)
                    move(
                        part_sum.at[i],
                        land2.at[c, k],
                        gb_s.at[mat.index],
                        gb_r.at[mat.index],
                        (s, mat.first + mat.step * i),
                    )
                    return 0

                lax.fori_loop(0, half, one, 0)

        def home_rows(src, src_at, start, rows, limit, r, active):
            left = jnp.int32(0)
            for i in range((rows + shard_rows - 2) // shard_rows + 1):
                owner = start // shard_rows + i
                lo = jnp.maximum(start, owner * shard_rows)
                hi = jnp.minimum(jnp.minimum(start + rows, limit), (owner + 1) * shard_rows)
                count = jnp.where(active, jnp.maximum(hi - lo, 0), 0)
                owner = jnp.minimum(owner, n - 1)

                def go():
                    return move_rows(
                        src,
                        src_at + lo - start,
                        out_w,
                        lo - owner * shard_rows,
                        count,
                        rows,
                        gc_s,
                        gc_r,
                        (r, owner),
                    )

                left = left + lax.cond(count > 0, go, lambda: jnp.int32(0))
            return left

        def home(mat, land2, flat):
            @pl.when(holds(mat))
            def _():
                full_wait(land2, gb_r.at[mat.index])
                for h in range(2):
                    x = jnp.sum(land2[:, h].astype(F32), axis=0)
                    for j in range(mat.width // 128):
                        if mat.split == "rows":
                            at = h * mat.flat + j
                        else:
                            at = h * (mat.blocks // 2) + j
                        flat[pl.ds(at, mat.rows, stride=mat.blocks), :] = x[:, 128 * j : 128 * (j + 1)]

            p = piece(mat)
            left = home_rows(
                flat, 0, mat.start + p * mat.flat, mat.flat, USED[mat.row], mat.row, holds(mat)
            )
            if mat.split == "rows":
                p = p + 4 * mat.pieces
                left = left + home_rows(
                    flat,
                    mat.flat,
                    mat.start + p * mat.flat,
                    mat.flat,
                    USED[mat.row],
                    mat.row,
                    holds(mat),
                )
            return left

        def first_piece(mat, owner):
            return jnp.maximum(owner * shard_rows - mat.start, 0) // mat.flat

        def home_whole(mat):
            start = mat.start + piece(mat) * mat.flat
            return start, start // shard_rows == (start + mat.flat - 1) // shard_rows

        def home_cut(mat, land2, flat, ready, inbox, in_sem, turn=None):
            start, whole = home_whole(mat)
            owner = jnp.minimum(start // shard_rows, n - 1)
            held = holds(mat)
            if turn is not None:
                held = held & ((c < chips // 2) if turn == 0 else (c >= chips // 2))

            @pl.when(held)
            def _():
                full_wait(land2, gb_r.at[mat.index])

            @pl.when(held & whole)
            def _():
                for h in range(2):
                    ready[h] = jnp.sum(land2[:, h].astype(F32), axis=0).astype(BF16)
                slot = piece(mat) - first_piece(mat, owner)
                move(ready, inbox.at[slot], hs_s.at[mat.index], in_sem.at[slot], (mat.row, owner))

            @pl.when(held & jnp.logical_not(whole))
            def _():
                for h in range(2):
                    x = jnp.sum(land2[:, h].astype(F32), axis=0)
                    for j in range(mat.width // 128):
                        at = h * (mat.blocks // 2) + j
                        flat[pl.ds(at, mat.rows, stride=mat.blocks), :] = x[:, 128 * j : 128 * (j + 1)]

            return home_rows(
                flat,
                0,
                start,
                mat.flat,
                USED[mat.row],
                mat.row,
                held & jnp.logical_not(whole),
            )

        def end_home_cut(mat, ready):
            start, whole = home_whole(mat)
            away = (s != mat.row) | (d != start // shard_rows)

            @pl.when(holds(mat) & whole & away)
            def _():
                full_wait(ready, hs_s.at[mat.index])

        def whole_range(mat):
            low = (jnp.maximum(mine_from - mat.start, 0) + mat.flat - 1) // mat.flat
            high = jnp.minimum(jnp.maximum(mine_to - mat.start, 0) // mat.flat, 4 * mat.pieces)
            return low, jnp.maximum(high, low)

        def take(mat, inbox, in_sem):
            @pl.when(s == mat.row)
            def _():
                low, high = whole_range(mat)
                first = first_piece(mat, d)

                def one(p, _):
                    slot = p - first
                    full_wait(inbox.at[slot], in_sem.at[slot])
                    at = mat.start + p * mat.flat - mine_from
                    for h in range(2):
                        for j in range(mat.width // 128):
                            x = inbox[slot, h, :, 128 * j : 128 * (j + 1)].astype(F32)
                            row_at = at + h * (mat.blocks // 2) + j
                            out_w[pl.ds(row_at, mat.rows, stride=mat.blocks), :] = x
                    return 0

                lax.fori_loop(low, high, one, 0)

        def end_shed(mat, gw):
            full_wait(gw.at[pl.ds(0, 2 * mat.pieces)], ga_s.at[mat.index])
            full_wait(gw.at[pl.ds(0, mat.pieces)], gd_s.at[mat.index])

            @pl.when(holds(mat))
            def _():
                full_wait(gw.at[pl.ds(0, mat.pieces - 1)], gb_s.at[mat.index])

            @pl.when(jnp.logical_not(holds(mat)))
            def _():
                full_wait(gw.at[pl.ds(0, mat.pieces)], gb_s.at[mat.index])

        def rest_meet(i, mat, rg, land):
            @pl.when((s == mat.row) & (d < 8))
            def _():
                pltpu.make_async_remote_copy(
                    rg.at[pl.ds(AT_SQ + REST_PART * d, REST_PART)],
                    land,
                    v_s.at[i],
                    v_r.at[i],
                    device_id=(s + 1, d),
                    device_id_type=MESH,
                ).start()

        def rest_home(i, mat, rg, land, flat):
            active = (s == mat.row + 1) & (d < 8)
            at = AT_SQ + REST_PART * jnp.minimum(d, 7)

            @pl.when(active)
            def _():
                full_wait(land, v_r.at[i])
                flat[...] = rg[pl.ds(at, REST_PART), :] + land[...]

            return home_rows(
                flat, 0, mat.start + at, REST_PART, mat.start + REST_ROWS, mat.row, active
            )

        def table_meet(i, first, rows):
            @pl.when((s == 0) & (d < 2))
            def _():
                pltpu.make_async_remote_copy(
                    gvt.at[pl.ds(first, rows)],
                    gvl.at[pl.ds(first, rows)],
                    v_s.at[i],
                    v_r.at[i],
                    device_id=(s + 1, d),
                    device_id_type=MESH,
                ).start()

        def table_home(i, first, rows):
            active = (s == 1) & (d < 2)

            @pl.when(active)
            def _():
                span = pl.ds(first, rows)
                full_wait(gvl.at[span], v_r.at[i])
                gvs[first : first + rows, :] = gvt[first : first + rows, :] + gvl[first : first + rows, :]

            left = jnp.int32(0)
            for (r, _), (at, start, many) in TABLE.items():
                if first <= at < first + rows:
                    left = left + home_rows(
                        gvs,
                        at + many * k,
                        start + many * k,
                        many,
                        start + 2 * many,
                        r,
                        active,
                    )
            return left

        def put(ph, base, value):
            for j in range(value.shape[1] // 128):
                snd[ph, base + j : base + j + 1, :] = value[:, 128 * j : 128 * (j + 1)]

        def send(ph):
            mine, theirs = ROWS[ph]

            def to(o, kk, rows):
                pltpu.make_async_remote_copy(
                    snd.at[ph, pl.ds(0, rows)],
                    rcv.at[ph, k, o, pl.ds(0, rows)],
                    ssem.at[ph],
                    rsem.at[ph, k],
                    device_id=peer(o, kk),
                    device_id_type=MESH,
                ).start()
                return 0

            if n > 8:
                lax.fori_loop(1, n, lambda o, _: to(o, k, mine), 0)
                if theirs:
                    lax.fori_loop(0, n, lambda o, _: to(o, 1 - k, theirs), 0)
            else:
                for o in order:
                    to(o, k, mine)
                    if theirs:
                        to(o, 1 - k, theirs)
                if theirs:
                    to(0, 1 - k, theirs)
            rcv[ph, k, 0] = snd[ph]

        def receive(ph):
            mine, theirs = ROWS[ph]
            full_wait(rcv.at[ph, k, pl.ds(1, n - 1), pl.ds(0, mine)], rsem.at[ph, k])
            if theirs:
                full_wait(rcv.at[ph, 1 - k, :, pl.ds(0, theirs)], rsem.at[ph, 1 - k])

        def end_send(ph):
            mine, theirs = ROWS[ph]
            full_wait(fill.at[pl.ds(0, (n - 1) * mine + n * theirs)], ssem.at[ph])

        def totals(ph):
            return jnp.sum(rcv[ph, k, :, 0 : -(-ROWS[ph][0] // 8) * 8, :], axis=0)

        def row(total, base, width):
            return jnp.concatenate(
                [total[base + j : base + j + 1, :] for j in range(width // 128)], axis=1
            )

        def across(ph, h, base, width):
            return jnp.concatenate(
                [rcv[ph, h, :, base + j, :] for j in range(width // 128)], axis=1
            )

        def rows_of(ref, at, many):
            return jnp.concatenate([ref[pl.ds(at + j, 1), :] for j in range(many)], axis=1)

        def vrow(key):
            at, _, many = TABLE[key]
            return rows_of(table, at + many * k, many)

        def set_gvec(key, value):
            at, _, many = TABLE[key]
            for j in range(many):
                gvt[pl.ds(at + many * k + j, 1), :] = value[:, 128 * j : 128 * (j + 1)]

        def set_rows(ref, at, value):
            for j in range(value.shape[1] // 128):
                ref[at + j : at + j + 1, :] = value[:, 128 * j : 128 * (j + 1)]

        def mean_rstd(total, base, width, count):
            mu = row(total, base, width) / count
            second = row(total, base + width // 128, width) / count
            return mu, lax.rsqrt(jnp.maximum(second - mu * mu, 0.0) + EPS)

        gvt[...] = jnp.zeros(gvt.shape, F32)

        side_copy.wait()
        side_row = jnp.where(
            m == 0, side_t[s // 2, 0, 0:1, :], side_t[s // 2, 1, 0:1, :]
        )
        pixel = lax.broadcasted_iota(jnp.int32, (PX, 128), 0)
        prow = (pixel // SIDE).astype(F32)
        pcol = (pixel % SIDE).astype(F32)
        mref[...] = jnp.where((prow < side_row) & (pcol < side_row), 1.0, 0.0)
        inv_own = 1.0 / (side_row * side_row)

        spread(MID0, ln_mid0, st_mid0, w_mid0)
        for q in range(4):
            here = u.at[q, pl.ds(2 * k, 2)]
            pltpu.make_async_copy(here, here, img_r.at[q]).wait()
            pltpu.make_async_remote_copy(
                here,
                here,
                bs.at[10 + q],
                br.at[10 + q],
                device_id=(s, 2 * c + 1 - k),
                device_id_type=MESH,
            ).start()
        for q in range(4):
            here = u.at[q, pl.ds(2 * (1 - k), 2)]
            pltpu.make_async_copy(here, here, br.at[10 + q]).wait()

        def mask_block(b, _):
            r = pl.multiple_of(b * 32, 32)
            rows = pl.ds(r, 32)
            mask = mref[rows, :]
            for q in range(4):
                total = jnp.zeros((32, 128), F32)
                for p in range(4):
                    x = u[q, p, rows, :].astype(F32) * mask
                    um[p, rows, 128 * q : 128 * (q + 1)] = x.astype(BF16)
                    total = total + x
                pool[rows, 128 * q : 128 * (q + 1)] = (total * 0.25).astype(BF16)
            return 0

        lax.fori_loop(0, 8, mask_block, 0)
        pass_table()
        full_wait(w_in0.at[k], c_r.at[0])

        def z1_block(p, carry):
            z = dot(um[p], w_in0[k].reshape(CIN, 128))
            z1[p] = z
            return (carry[0] + fold8(z), carry[1] + fold8(z * z))

        zero8 = jnp.zeros((8, 128), F32)
        t0, t1 = lax.fori_loop(0, 4, z1_block, (zero8, zero8))
        put(0, 0, jnp.sum(t0, axis=0, keepdims=True))
        put(0, 1, jnp.sum(t1, axis=0, keepdims=True))
        put(0, 2, side_row)
        send(0)
        pass_on(MID0, w_mid0)
        sent = scatter_early(sent)
        pass_far(MID0, w_mid0)
        spread(SC0, ln_sc, st_sc, w_sc)
        spread(OUT1, ln_out1, st_out1, w_out1)
        table_arrived()
        receive(0)
        total = totals(0)
        sides = across(0, k, 2, 128)
        inv_area = 1.0 / (sides * sides)
        count1 = jnp.sum(sides * sides, axis=0, keepdims=True)
        counts = {w: lanes(count1, w // 128) for w in (128, 256, 512)}
        mu1, rs1 = mean_rstd(total, 0, 128, 4.0 * count1)
        lin1 = rs1 * vrow((0, "g_in"))
        off1 = vrow((0, "b_in")) - mu1 * lin1

        colpos = lax.broadcasted_iota(jnp.int32, (PX, 128), 0) % SIDE

        def shift_cols(x, by):
            moved = pltpu.roll(x, by % PX, 0)
            edge = 0 if by == 1 else SIDE - 1
            return jnp.where(colpos == edge, 0.0, moved)

        def store_tap(cols, di, dj, x, shift):
            at = 128 * (3 * di + dj)
            span = slice(at, at + 128)
            x = x.astype(BF16)
            if shift == 1:
                cols[0:SIDE, span] = jnp.zeros((SIDE, 128), BF16)
                cols[SIDE:PX, span] = x[0 : PX - SIDE]
            elif shift == -1:
                cols[PX - SIDE : PX, span] = jnp.zeros((SIDE, 128), BF16)
                cols[0 : PX - SIDE, span] = x[SIDE:PX]
            else:
                cols[:, span] = x

        def plane_taps(parity):
            return ((1, 0),) if parity == 0 else ((0, 1), (2, 0))

        for p in range(4):
            v = z1[p] * lin1 + off1
            h = v * sigmoid(v) * mref[...]
            for dj, cshift in plane_taps(p % 2):
                x = shift_cols(h, 1) if cshift else h
                for di, rshift in plane_taps(p // 2):
                    store_tap(cols1, di, dj, x, rshift)

        def conv_forward(ph, cols, w_mid, zref):
            z = dot(cols[...], w_mid[...].reshape(1152, 256))
            zref[...] = z
            zm = z * lanes(mref[...], 2)
            put(ph, 0, jnp.sum(zm, axis=0, keepdims=True))
            put(ph, 2, jnp.sum(zm * z, axis=0, keepdims=True))
            send(ph)

        def small(rest):
            w_sq = rest[AT_SQ : AT_SQ + CMID, :]
            w_ex = jnp.concatenate(
                [rest[pl.ds(AT_EX + j, CSQ, stride=4), :] for j in range(4)], axis=1
            )
            return w_sq, w_ex

        def attention_forward(ph, twin, total, at, rest, zref, rr, aref, beside):
            mu, rs = mean_rstd(total, 0, 256, counts[256])
            lin = rs * rows_of(table, at + 2 * k, 2)
            off = rows_of(table, at + 4 + 2 * k, 2) - mu * lin

            def block(b, acc):
                rows = pl.ds(pl.multiple_of(b * 64, 64), 64)
                v = zref[rows, :] * lin + off
                r = v * sigmoid(v) * lanes(mref[rows, :], 2)
                rr[k, rows, :] = r
                return acc + fold8(r)

            acc = lax.fori_loop(0, 4, block, jnp.zeros((8, 256), F32))
            pooled_own = jnp.sum(acc, axis=0, keepdims=True) * lanes(inv_own, 2)
            put(ph, 0, pooled_own)
            send(ph)
            swap = to_twin(twin, rr.at[k], rr.at[k])
            swap.start()
            beside()
            receive(ph)
            w_sq, w_ex = small(rest)
            pooled = across(ph, 0, 0, 256) + across(ph, 1, 0, 256)
            zq = dot_hi(pooled, w_sq)
            mq = jnp.mean(zq, axis=0, keepdims=True)
            vq = jnp.mean(zq * zq, axis=0, keepdims=True) - mq * mq
            rq = lax.rsqrt(jnp.maximum(vq, 0.0) + EPS)
            hq = (zq - mq) * rq
            nq = hq * rows_of(rest, AT_GSQ, 1) + rows_of(rest, AT_BSQ, 1)
            sgq = sigmoid(nq)
            qq = nq * sgq
            logits = dot_hi(qq, w_ex) + rows_of(rest, AT_BEX, 4)
            diff = logits[:, 0:256] - logits[:, 256:512]
            sh0 = sigmoid(diff)
            sh1 = sigmoid(-diff)
            swap.wait()
            s0 = sh0[0:1, :]
            s1 = sh1[0:1, :]

            def mix(b, _):
                rows = pl.ds(pl.multiple_of(b * 64, 64), 64)
                aref[rows, :] = (s0 * rr[0, rows, :] + s1 * rr[1, rows, :]).astype(BF16)
                return 0

            lax.fori_loop(0, 4, mix, 0)
            return (mu, rs, lin, off), (pooled, rq, hq, nq, sgq, qq, sh0, sh1)

        def attention_backward(
            ph, kept_mid, kept_q, rest, rg, zref, rr, cols, mat, gw_mid, ga_mid, da, beside
        ):
            mu, rs, lin, off = kept_mid
            pooled, rq, hq, nq, sgq, qq, sh0, sh1 = kept_q

            def block(b, acc):
                rows = pl.ds(pl.multiple_of(b * 32, 32), 32)
                z = zref[rows, :]
                v = z * lin + off
                hat = (z - mu) * rs
                sg = sigmoid(v)
                sp = sg * (1.0 + v * (1.0 - sg)) * lanes(mref[rows, :], 2)
                grad = da(rows)
                t = grad * sp
                dbuf[rows, :] = grad
                spb[rows, :] = sp
                r = rr[k, rows, :]
                return tuple(
                    x + fold8(y)
                    for x, y in zip(acc, (grad * r, t, sp, t * hat, sp * hat))
                )

            acc = lax.fori_loop(0, 8, block, (jnp.zeros((8, 256), F32),) * 5)
            for j, x in enumerate(acc):
                put(ph, 2 * j, jnp.sum(x, axis=0, keepdims=True))
            send(ph)
            beside()
            receive(ph)
            ds0 = across(ph, 0, 0, 256)
            ds1 = across(ph, 1, 0, 256)
            mean = sh0 * ds0 + sh1 * ds1
            dl = jnp.concatenate([sh0 * (ds0 - mean), sh1 * (ds1 - mean)], axis=1)
            w_sq, w_ex = small(rest)
            set_rows(rg, AT_BEX, jnp.sum(dl, axis=0, keepdims=True))
            dq = dot_hi(dl, w_ex, ((1,), (1,)))
            dn = dq * sgq * (1.0 + nq * (1.0 - sgq))
            set_rows(rg, AT_GSQ, jnp.sum(dn * hq, axis=0, keepdims=True))
            set_rows(rg, AT_BSQ, jnp.sum(dn, axis=0, keepdims=True))
            dn = dn * rows_of(rest, AT_GSQ, 1)
            dzq = rq * (
                dn
                - jnp.mean(dn, axis=0, keepdims=True)
                - hq * jnp.mean(dn * hq, axis=0, keepdims=True)
            )
            dpool = dot_hi(dzq, w_sq, ((1,), (1,))) * lanes(inv_area, 2)
            share = jnp.where(k == 0, sh0, sh1)

            def both_sums(first, second):
                return jnp.sum(
                    share * across(ph, k, first, 256) + dpool * across(ph, k, second, 256),
                    axis=0,
                    keepdims=True,
                )

            sdv = both_sums(2, 4)
            sdh = both_sums(6, 8)
            set_gvec((mat.row, "b_mid"), sdv)
            set_gvec((mat.row, "g_mid"), sdh)
            own_share = share[0:1, :]
            own_pool = dpool[0:1, :]
            c1 = sdv / counts[256]
            c2 = sdh / counts[256]

            def block2(b, _):
                rows = pl.ds(pl.multiple_of(b * 32, 32), 32)
                hat = (zref[rows, :] - mu) * rs
                dv = (own_share * dbuf[rows, :] + own_pool) * spb[rows, :]
                dz = lin * (dv - c1 - hat * c2) * lanes(mref[rows, :], 2)
                rows_low[rows, :] = dz.astype(BF16)
                return 0

            rows_low = dz_low
            lax.fori_loop(0, 8, block2, 0)

            def rest():
                gw_mid[...] = dot_lt(cols[...], dz_low[...]).astype(BF16).reshape(24, 48, 256)
                shed(mat, gw_mid, ga_mid)
                g_ex = dot_hi(qq, dl, ((0,), (0,)))
                for j in range(4):
                    rg[pl.ds(AT_EX + j, CSQ, stride=4), :] = g_ex[:, 128 * j : 128 * (j + 1)]
                rg[AT_SQ : AT_SQ + CMID, :] = dot_hi(pooled, dzq, ((0,), (0,)))

            return rest

        dz_low = dz3.at[:, pl.ds(0, 256)]

        arrived(MID0, w_mid0)
        conv_forward(1, cols1, w_mid0, z2)
        spread_rest(REST0, ln_rest0, rest0)
        scatter_late(sent)
        pass_on(SC0, w_sc)
        pass_on(OUT1, w_out1)
        spread(IN1, ln_in1, st_in1, w_in1)
        receive(1)

        def short_forward():
            share_rest(REST0, rest0, 15)
            pass_far(SC0, w_sc)
            pass_far(OUT1, w_out1)
            pass_on(IN1, w_in1)
            spread(MID2, ln_mid2, st_mid2, w_mid2)
            arrived(SC0, w_sc)
            z = dot(pool[...], w_sc[...].reshape(CIN, 512))
            zs[...] = z
            put(3, 8, jnp.sum(z, axis=0, keepdims=True))
            put(3, 12, jnp.sum(z * z, axis=0, keepdims=True))
            rest_arrived(rest0, 15)

        mid1, q1 = attention_forward(2, 2, totals(1), AT_MID[0], rest0, z2, rr1, a1, short_forward)
        arrived(OUT1, w_out1)

        def wide_forward(ph, aref, w, zref):
            z = dot(aref[...], w[...].reshape(CMID, 512))
            zref[...] = z
            put(ph, 0, jnp.sum(z, axis=0, keepdims=True))
            put(ph, 4, jnp.sum(z * z, axis=0, keepdims=True))
            send(ph)

        wide_forward(3, a1, w_out1, z3)
        pass_far(IN1, w_in1)
        pass_on(MID2, w_mid2)
        spread_rest(REST2, ln_rest2, rest2)
        receive(3)
        total = totals(3)
        mus, rss = mean_rstd(total, 8, 512, counts[512])
        lins = rss * vrow((0, "g_sc"))
        offs = vrow((0, "b_sc")) - mus * lins

        mu3, rs3 = mean_rstd(total, 0, 512, counts[512])
        lin3 = rs3 * vrow((1, "g_out"))
        off3 = vrow((1, "b_out")) - mu3 * lin3

        def y1_block(b, _):
            rows = pl.ds(pl.multiple_of(b * 32, 32), 32)
            short = (zs[rows, :] * lins + offs).astype(BF16).astype(F32)
            v = z3[rows, :] * lin3 + off3 + short
            v3[rows, :] = v
            y1[rows, :] = (v * sigmoid(v) * lanes(mref[rows, :], 4)).astype(BF16)
            return 0

        lax.fori_loop(0, 8, y1_block, 0)
        arrived(IN1, w_in1)
        pz[0] = dot(y1[...], w_in1[1 - k].reshape(512, 128))
        swap = to_twin(3, pz.at[0], pz.at[1])
        swap.start()
        z = dot(y1[...], w_in1[k].reshape(512, 128))
        swap.wait()
        z = z + pz[1]
        z4[...] = z
        put(4, 0, jnp.sum(z, axis=0, keepdims=True))
        put(4, 1, jnp.sum(z * z, axis=0, keepdims=True))
        send(4)
        pass_far(MID2, w_mid2)
        spread(OUT3, ln_out3, st_out3, w_out3)
        receive(4)
        mu4, rs4 = mean_rstd(totals(4), 0, 128, count1)
        lin4 = rs4 * vrow((1, "g_in"))
        off4 = vrow((1, "b_in")) - mu4 * lin4
        v = z4[...] * lin4 + off4
        h = v * sigmoid(v) * mref[...]
        for dj in range(3):
            x = h if dj == 1 else shift_cols(h, 1 - dj)
            for di in range(3):
                store_tap(cols2, di, dj, x, 1 - di)

        arrived(MID2, w_mid2)
        conv_forward(5, cols2, w_mid2, z5)
        share_rest(REST2, rest2, 16)
        pass_on(OUT3, w_out3)
        receive(5)

        def last_weights():
            pass_far(OUT3, w_out3)
            rest_arrived(rest2, 16)
            for slot in range(2):
                move(
                    cot.at[slot],
                    ctb.at[lax.rem(s, 2)],
                    ct_s.at[slot],
                    ct_r.at[lax.rem(s, 2)],
                    (2 * k + slot, 2 * c + s // 2),
                )
            to_twin(14, w_in0.at[k], w_in0.at[k]).start()

        mid2, q2 = attention_forward(6, 4, totals(5), AT_MID[2], rest2, z5, rr2, a2, last_weights)
        arrived(OUT3, w_out3)
        wide_forward(7, a2, w_out3, z6)
        to_twin(14, w_in0.at[k], w_in0.at[k]).wait()
        for i in range(2):
            pltpu.make_async_copy(ctb.at[i], ctb.at[i], ct_r.at[i]).wait()
        receive(7)
        mu6, rs6 = mean_rstd(totals(7), 0, 512, counts[512])
        lin6 = rs6 * vrow((3, "g_out"))
        off6 = vrow((3, "b_out")) - mu6 * lin6

        def out_block(b, acc):
            rows = pl.ds(pl.multiple_of(b * 32, 32), 32)
            z = z6[rows, :]
            mask = lanes(mref[rows, :], 4)
            v = z * lin6 + off6 + y1[rows, :].astype(F32)
            sg = sigmoid(v)
            y = (v * sg * mask).astype(BF16)
            obuf[0, rows, :] = y[:, 0:256]
            obuf[1, rows, :] = y[:, 256:512]
            ct = jnp.concatenate([ctb[0, rows, :], ctb[1, rows, :]], axis=1).astype(F32)
            dv = ct * (sg * (1.0 + v * (1.0 - sg)) * mask)
            dv6[rows, :] = dv
            return (acc[0] + fold8(dv), acc[1] + fold8(dv * ((z - mu6) * rs6)))

        zero512 = jnp.zeros((8, 512), F32)
        t0, t1 = lax.fori_loop(0, 8, out_block, (zero512, zero512))
        put(8, 0, jnp.sum(t0, axis=0, keepdims=True))
        put(8, 4, jnp.sum(t1, axis=0, keepdims=True))
        send(8)
        fill_up(nought, out_w, jnp.clip(used - d * shard_rows, 0, shard_rows), shard_rows, gc_r)
        fill_up(nought, fill3, 0, whole_rows(), gc_r)
        for j in range(2):
            move(
                obuf.at[j],
                out_o.at[lax.rem(s, 2)],
                oo_s.at[j],
                oo_r.at[lax.rem(s, 2)],
                (2 * k + j, 2 * c + s // 2),
            )
        for mat, whole in ((MID0, w_mid0), (SC0, w_sc), (OUT1, w_out1)):
            end_spread(mat, whole)
        end_rest(REST0, rest0, 15)
        end_table()
        receive(8)

        def wide_back(total, base, key_g, key_b, lin, mu, rs, zref, dvf, dst):
            sdv = row(total, base, 512)
            sdh = row(total, base + 4, 512)
            set_gvec(key_b, sdv)
            set_gvec(key_g, sdh)
            c1 = sdv / counts[512]
            c2 = sdh / counts[512]

            def block(b, _):
                rows = pl.ds(pl.multiple_of(b * 32, 32), 32)
                hat = (zref[rows, :] - mu) * rs
                dz = lin * (dvf(rows) - c1 - hat * c2) * lanes(mref[rows, :], 4)
                dst[rows, :] = dz.astype(BF16)
                return 0

            lax.fori_loop(0, 8, block, 0)

        wide_back(
            totals(8),
            0,
            (3, "g_out"),
            (3, "b_out"),
            lin6,
            mu6,
            rs6,
            z6,
            lambda rows: dv6[rows, :],
            dz3,
        )

        def attended_grad(twin, w, aref, mat, gw, land):
            pda[0] = dot_rt(dz3[...], w[...].reshape(CMID, 512))
            swap = to_twin(twin, pda.at[0], pda.at[1])
            swap.start()
            gw[...] = dot_lt(aref[...], dz3[...]).astype(BF16).reshape(16, 16, 512)
            shed(mat, gw, land)
            swap.wait()

        def summed_grad(rows):
            return (pda[0, rows, :] + pda[1, rows, :]).astype(BF16).astype(F32)

        attended_grad(5, w_out3, a2, OUT3, gw_out3, ga_out3)

        def beside9():
            for mat, whole in ((IN1, w_in1), (MID2, w_mid2), (OUT3, w_out3)):
                end_spread(mat, whole)
            end_rest(REST2, rest2, 16)
            shed_mid(OUT3, gw_out3, ga_out3, gt_out3, gd_out3)

        grad_rest2 = attention_backward(
            9,
            mid2,
            q2,
            rest2,
            rg2,
            z5,
            rr2,
            cols2,
            MID2,
            gw_mid2,
            ga_mid2,
            summed_grad,
            beside9,
        )

        ep[...] = jnp.zeros(ep.shape, F32)
        for di in range(3):
            part = dot_rt(dz_low[...], w_mid2[8 * di : 8 * (di + 1)].reshape(384, 256))
            for dj in range(3):
                lo = SIDE * di
                ep[dj, lo : lo + PX, :] += part[:, 128 * dj : 128 * (dj + 1)]
        grad = ep[1, SIDE : SIDE + PX, :]
        grad = grad + shift_cols(ep[0, SIDE : SIDE + PX, :], -1)
        grad = grad + shift_cols(ep[2, SIDE : SIDE + PX, :], 1)
        grad = grad.astype(BF16).astype(F32)
        v = z4[...] * lin4 + off4
        hat4 = (z4[...] - mu4) * rs4
        sg = sigmoid(v)
        dv4 = grad * (sg * (1.0 + v * (1.0 - sg)) * mref[...])
        dh[0] = dv4
        put(10, 0, jnp.sum(dv4, axis=0, keepdims=True))
        put(10, 1, jnp.sum(dv4 * hat4, axis=0, keepdims=True))
        send(10)
        grad_rest2()
        rest_meet(2, REST2, rg2, rl2)
        shed_more(OUT3, gw_out3, ga_out3, gd_out3, gp_out3, gb_out3)
        receive(10)
        total = totals(10)
        set_gvec((1, "b_in"), total[0:1, :])
        set_gvec((1, "g_in"), total[1:2, :])
        hat4 = (z4[...] - mu4) * rs4
        dz = lin4 * (dh[0] - total[0:1, :] / count1 - hat4 * (total[1:2, :] / count1)) * mref[...]
        dz4[k] = dz.astype(BF16)
        swap = to_twin(6, dz4.at[k], dz4.at[k])
        swap.start()
        swap.wait()

        def dy_block(b, acc):
            rows = pl.ds(pl.multiple_of(b * 64, 64), 64)
            dy = dot_rt(dz4[0, rows, :], w_in1[0].reshape(512, 128))
            dy = dy + dot_rt(dz4[1, rows, :], w_in1[1].reshape(512, 128))
            dy = dy + dv6[rows, :].astype(BF16).astype(F32)
            v = v3[rows, :]
            sg = sigmoid(v)
            dv = dy * (sg * (1.0 + v * (1.0 - sg)) * lanes(mref[rows, :], 4))
            v3[rows, :] = dv
            low = dv.astype(BF16).astype(F32)
            hat = (z3[rows, :] - mu3) * rs3
            hats = (zs[rows, :] - mus) * rss
            return tuple(
                x + fold8(y) for x, y in zip(acc, (dv, dv * hat, low, low * hats))
            )

        acc = lax.fori_loop(0, 4, dy_block, (zero512,) * 4)
        for j, x in enumerate(acc):
            put(11, 4 * j, jnp.sum(x, axis=0, keepdims=True))
        send(11)
        both4 = jnp.concatenate([dz4[0], dz4[1]], axis=1)
        gw_in1[...] = dot_lt(y1[...], both4).astype(BF16).reshape(32, 16, 256)
        shed(IN1, gw_in1, ga_in1)
        shed_mid(MID2, gw_mid2, ga_mid2, gt_mid2, gd_mid2)
        left = rest_home(2, REST2, rg2, rl2, rf2)
        receive(11)
        total = totals(11)
        wide_back(
            total,
            0,
            (1, "g_out"),
            (1, "b_out"),
            lin3,
            mu3,
            rs3,
            z3,
            lambda rows: v3[rows, :],
            dz3,
        )
        wide_back(
            total,
            8,
            (0, "g_sc"),
            (0, "b_sc"),
            lins,
            mus,
            rss,
            zs,
            lambda rows: v3[rows, :].astype(BF16).astype(F32),
            dzs,
        )
        attended_grad(7, w_out1, a1, OUT1, gw_out1, ga_out1)

        def short_back():
            part = dot_rt(dzs[...], w_sc[...].reshape(CIN, 512))
            pdp[0] = jnp.where(k == 0, part[:, 256:512], part[:, 0:256])
            to_twin(8, pdp.at[0], pdp.at[1]).start()
            pdp[2] = jnp.where(k == 0, part[:, 0:256], part[:, 256:512])
            gw_sc[...] = dot_lt(pool[...], dzs[...]).astype(BF16).reshape(32, 16, 512)
            shed(SC0, gw_sc, ga_sc)
            table_meet(0, LATE_ROWS, TABLE_ROWS - LATE_ROWS)
            shed_mid(IN1, gw_in1, ga_in1, gt_in1, gd_in1)
            shed_mid(OUT1, gw_out1, ga_out1, gt_out1, gd_out1)
            shed_more(MID2, gw_mid2, ga_mid2, gd_mid2, gp_mid2, gb_mid2)

        grad_rest0 = attention_backward(
            12,
            mid1,
            q1,
            rest0,
            rg0,
            z2,
            rr1,
            cols1,
            MID0,
            gw_mid0,
            ga_mid0,
            summed_grad,
            short_back,
        )

        for p in range(4):
            dh[p] = jnp.zeros((PX, 128), F32)
        for di in range(3):
            part = dot_rt(dz_low[...], w_mid0[8 * di : 8 * (di + 1)].reshape(384, 256))
            pr = 0 if di == 1 else 1
            for dj in range(3):
                x = part[:, 128 * dj : 128 * (dj + 1)]
                if dj == 0:
                    x = shift_cols(x, -1)
                p = 2 * pr + (0 if dj == 1 else 1)
                if di == 0:
                    dh[p, 0 : PX - SIDE, :] += x[SIDE:PX]
                else:
                    dh[p] += x

        def dv1_block(p, acc):
            z = z1[p]
            v = z * lin1 + off1
            sg = sigmoid(v)
            dv = dh[p] * (sg * (1.0 + v * (1.0 - sg)) * mref[...])
            dh[p] = dv
            return (acc[0] + fold8(dv), acc[1] + fold8(dv * ((z - mu1) * rs1)))

        t0, t1 = lax.fori_loop(0, 4, dv1_block, (zero8, zero8))
        put(13, 0, jnp.sum(t0, axis=0, keepdims=True))
        put(13, 1, jnp.sum(t1, axis=0, keepdims=True))
        send(13)
        grad_rest0()
        rest_meet(1, REST0, rg0, rl0)
        shed_more(IN1, gw_in1, ga_in1, gd_in1, gp_in1, gb_in1)
        shed_more(OUT1, gw_out1, ga_out1, gd_out1, gp_out1, gb_out1)
        shed_mid(SC0, gw_sc, ga_sc, gt_sc, gd_sc)
        left = left + home_cut(OUT3, gb_out3, gf_out3, hb_out3, hi_out3, hr_out3)
        left = left + table_home(0, LATE_ROWS, TABLE_ROWS - LATE_ROWS)
        receive(13)
        total = totals(13)
        set_gvec((0, "b_in"), total[0:1, :])
        set_gvec((0, "g_in"), total[1:2, :])
        table_meet(3, 0, LATE_ROWS)
        k1 = total[0:1, :] / (4.0 * count1)
        k2 = total[1:2, :] / (4.0 * count1)

        def dz1_block(p, _):
            hat = (z1[p] - mu1) * rs1
            dz1[k, p] = (lin1 * (dh[p] - k1 - hat * k2) * mref[...]).astype(BF16)
            return 0

        lax.fori_loop(0, 4, dz1_block, 0)
        swap = to_twin(9, dz1.at[k], dz1.at[k])
        swap.start()
        total = jnp.zeros((CIN, 128), F32)
        for p in range(4):
            total = total + dot_lt(um[p], dz1[k, p])
        gw_in0[...] = total.astype(BF16).reshape(32, 16, 128)

        def shed_in0(i, _):
            p = lax.rem(8 * s + i, 32)
            move(
                gw_in0.at[p],
                gb_in0.at[s * chips + c, k],
                gb_s.at[0],
                gb_r.at[0],
                (p // 8, p % 8),
            )
            return 0

        lax.fori_loop(0, 32, shed_in0, 0)
        shed_mid(MID0, gw_mid0, ga_mid0, gt_mid0, gd_mid0)
        shed_more(SC0, gw_sc, ga_sc, gd_sc, gp_sc, gb_sc)
        left = left + home_cut(MID2, gb_mid2, gf_mid2, hb_mid2, hi_mid2, hr_mid2)
        left = left + home(IN1, gb_in1, gf_in1)
        left = left + home_cut(OUT1, gb_out1, gf_out1, hb_out1, hi_out1, hr_out1)
        swap.wait()
        to_twin(8, pdp.at[0], pdp.at[1]).wait()

        def du_block(p, _):
            mine = pl.ds(16 * k, 16)
            grad = dot_rt(dz1[0, p], w_in0[0, mine].reshape(256, 128))
            grad = grad + dot_rt(dz1[1, p], w_in0[1, mine].reshape(256, 128))
            grad = (grad + 0.25 * (pdp[1] + pdp[2])) * lanes(mref[...], 2)
            for r in range(SIDE):
                at = (2 * r + p // 2) * 2 * SIDE + p % 2
                for j in range(2):
                    x = grad[SIDE * r : SIDE * (r + 1), 128 * j : 128 * (j + 1)]
                    merged[j, pl.ds(at, SIDE, stride=2), :] = x
            return 0

        lax.fori_loop(0, 4, du_block, 0)

        def narrow(i, _):
            rows = pl.ds(pl.multiple_of(i * 128, 128), 128)
            for j in range(2):
                ibuf[j, rows, :] = merged[j, rows, :].astype(BF16)
            return 0

        lax.fori_loop(0, 8, narrow, 0)
        for j in range(2):
            move(
                ibuf.at[j],
                out_i.at[lax.rem(s, 2)],
                oi_s.at[j],
                oi_r.at[lax.rem(s, 2)],
                (2 * k + j, 2 * c + s // 2),
            )

        shed_more(MID0, gw_mid0, ga_mid0, gd_mid0, gp_mid0, gb_mid0)
        left = left + home_cut(SC0, gb_sc, gf_sc, hb_sc, hi_sc, hr_sc)
        left = left + rest_home(1, REST0, rg0, rl0, rf0)
        left = left + table_home(3, 0, LATE_ROWS)
        left = left + home_cut(IN0, gb_in0, gf_in0, hb_in0, hi_in0, hr_in0)
        left = left + home_cut(MID0, gb_mid0, gf_mid0, hb_mid0, hi_mid0, hr_mid0)

        take(OUT3, hi_out3, hr_out3)
        take(MID2, hi_mid2, hr_mid2)
        take(OUT1, hi_out1, hr_out1)
        take(SC0, hi_sc, hr_sc)
        take(IN0, hi_in0, hr_in0)
        take(MID0, hi_mid0, hr_mid0)

        for mat, ready in (
            (IN0, hb_in0),
            (MID0, hb_mid0),
            (SC0, hb_sc),
            (OUT1, hb_out1),
            (MID2, hb_mid2),
            (OUT3, hb_out3),
        ):
            end_home_cut(mat, ready)
        for mat, gw in (
            (MID0, gw_mid0),
            (SC0, gw_sc),
            (OUT1, gw_out1),
            (IN1, gw_in1),
            (MID2, gw_mid2),
            (OUT3, gw_out3),
        ):
            end_shed(mat, gw)

        @pl.when(holds(IN0))
        def _():
            full_wait(gw_in0.at[pl.ds(0, 31)], gb_s.at[0])
            full_wait(fill.at[pl.ds(0, 8 * (4 * n - 1))], a_s.at[0])

        @pl.when(jnp.logical_not(holds(IN0)))
        def _():
            full_wait(gw_in0, gb_s.at[0])

        for i, mat, land in ((1, REST0, rl0), (2, REST2, rl2)):

            @pl.when((s == mat.row) & (d < 8))
            def _():
                full_wait(land, v_s.at[i])

        @pl.when((s == 0) & (d < 2))
        def _():
            full_wait(gvl.at[pl.ds(LATE_ROWS, TABLE_ROWS - LATE_ROWS)], v_s.at[0])
            full_wait(gvl.at[pl.ds(0, LATE_ROWS)], v_s.at[3])

        fill_up(nought, fill2, left, HOME_ROWS, gc_s)
        full_wait(fill2, gc_s)
        full_wait(fill, h_s)
        full_wait(out_w, gc_r)
        for slot in range(2):
            pltpu.make_async_copy(out_o.at[slot], out_o.at[slot], oo_r.at[slot]).wait()
            pltpu.make_async_copy(out_i.at[slot], out_i.at[slot], oi_r.at[slot]).wait()
        for slot in range(2):
            for kk in range(2):
                end_move(
                    planes.at[slot, pl.ds(2 * kk, 2)],
                    img_s.at[slot, kk],
                    (2 * k + slot, 2 * c + kk),
                )
            end_move(cot.at[slot], ct_s.at[slot], (2 * k + slot, 2 * c + s // 2))
        for j in range(2):
            end_move(obuf.at[j], oo_s.at[j], (2 * k + j, 2 * c + s // 2))
            end_move(ibuf.at[j], oi_s.at[j], (2 * k + j, 2 * c + s // 2))
        for q in range(4):
            here = u.at[q, pl.ds(2 * k, 2)]
            pltpu.make_async_copy(here, here, bs.at[10 + q]).wait()
        for ph in range(PHASES):
            end_send(ph)

    return kernel


def call_kernel(n, operands):
    chips = n // 2
    shard_rows = WSLOTS // (128 * n)
    fill_rows = max(shard_rows + 28 * n, 96 * (n - 1), 100 * n, 8 * (4 * n - 1), 16 * (2 * n - 1))

    def vm(*shape, dtype=F32):
        return pltpu.VMEM(shape, dtype)

    def low(*shape):
        return pltpu.VMEM(shape, BF16)

    dma = pltpu.SemaphoreType.DMA
    scratch = [
        vm(PHASES, 16, 128),
        vm(PHASES, 2, n, 16, 128),
        vm(2, 2, 8, 128),
        low(4, 4, PX, 128),
        low(4, PX, CIN),
        low(PX, CIN),
        low(2, PX, 256),
        vm(PX, 128),
        vm(4, PX, 128),
        vm(PX, 256),
        vm(PX, 512),
        vm(PX, 512),
        vm(PX, 128),
        vm(PX, 256),
        vm(PX, 512),
        vm(PX, 512),
        low(PX, 1152),
        low(PX, 1152),
        vm(2, PX, 256),
        vm(2, PX, 256),
        low(PX, 256),
        low(PX, 256),
        low(PX, 512),
        vm(PX, 512),
        vm(PX, 256),
        vm(PX, 256),
        vm(2, PX, 128),
        vm(2, PX, 256),
        vm(3, PX, 256),
        low(2, PX, 128),
        low(2, 4, PX, 128),
        low(PX, 512),
        low(PX, 512),
        vm(3, PX + 2 * SIDE, 128),
        vm(4, PX, 128),
        low(2, PX, 256),
        low(2, 4 * PX, 128),
        vm(shard_rows, 128),
        vm(128, 128),
        vm(fill_rows, 128),
        vm(HOME_ROWS, 128),
        vm(TABLE_ROWS, 128),
        low(2, 32, 16, 128),
        low(24, 48, 256),
        vm(800, 128),
        low(32, 16, 512),
        low(16, 16, 512),
        low(2, 32, 16, 128),
        low(24, 48, 256),
        vm(800, 128),
        low(16, 16, 512),
        vm(32, 128),
        vm(192, 128),
        vm(25, 128),
        vm(128, 128),
        vm(128, 128),
        vm(64, 128),
        vm(192, 128),
        vm(25, 128),
        vm(128, 128),
        low(2, 16, 128),
        low(2, 48, 256),
        low(2, 16, 512),
        low(2, 16, 512),
        low(2, 2, 16, 128),
        low(2, 48, 256),
        low(2, 16, 512),
        low(shard_rows // 32 + 2, 2, 16, 128),
        low(shard_rows // 192 + 2, 2, 48, 256),
        low(shard_rows // 128 + 2, 2, 16, 512),
        low(shard_rows // 128 + 2, 2, 16, 512),
        low(shard_rows // 192 + 2, 2, 48, 256),
        low(shard_rows // 128 + 2, 2, 16, 512),
        low(32, 16, 128),
        low(24, 48, 256),
        low(32, 16, 512),
        low(16, 16, 512),
        low(32, 16, 256),
        low(24, 48, 256),
        low(16, 16, 512),
        low(2, 2, 3, 48, 256),
        low(2, 2, 4, 16, 512),
        low(2, 2, 2, 16, 512),
        low(2, 2, 4, 16, 256),
        low(2, 2, 3, 48, 256),
        low(2, 2, 2, 16, 512),
        low(6, 48, 256),
        low(8, 16, 512),
        low(4, 16, 512),
        low(8, 16, 256),
        low(6, 48, 256),
        low(4, 16, 512),
        low(4 * chips, 2, 16, 128),
        low(chips, 2, 48, 256),
        low(chips, 2, 16, 512),
        low(chips, 2, 16, 512),
        low(chips, 2, 16, 256),
        low(chips, 2, 48, 256),
        low(chips, 2, 16, 512),
        vm(32, 128),
        vm(192, 128),
        vm(128, 128),
        vm(128, 128),
        vm(64, 128),
        vm(192, 128),
        vm(128, 128),
        vm(784, 128),
        vm(784, 128),
        vm(REST_PART, 128),
        vm(REST_PART, 128),
        vm(REST_PART, 128),
        vm(REST_PART, 128),
        vm(TABLE_ROWS, 128),
        vm(TABLE_ROWS, 128),
        vm(TABLE_ROWS, 128),
        low(2, 3, 48, 256),
        low(2, 3, 48, 256),
        low(2, 3, 48, 256),
        low(2, 3, 48, 256),
        low(2, 4, 16, 512),
        low(2, 4, 16, 512),
        low(2, 2, 16, 512),
        low(2, 2, 16, 512),
        low(2, 2, 16, 512),
        low(2, 2, 16, 512),
        low(2, 4, 16, 256),
        low(2, 4, 16, 256),
        low(2, 16, 128),
        low(shard_rows // 32 + 2, 2, 16, 128),
        low(2, 48, 256),
        low(shard_rows // 192 + 2, 2, 48, 256),
        low(2, 16, 512),
        low(shard_rows // 128 + 2, 2, 16, 512),
        low(2, 16, 512),
        low(shard_rows // 128 + 2, 2, 16, 512),
        low(2, 48, 256),
        low(shard_rows // 192 + 2, 2, 48, 256),
        low(2, 16, 512),
        low(shard_rows // 128 + 2, 2, 16, 512),
        vm(shard_rows, 128),
        vm(4 * PX, 128),
        low(2, 4, PX, 128),
        vm(2, 4 * PX, 128),
        dma((PHASES,)),
        dma((PHASES, 2)),
        dma((17,)),
        dma((17,)),
        dma((2, 2)),
        dma((4,)),
        dma((2,)),
        dma((2,)),
        dma((2,)),
        dma((2,)),
        dma((2,)),
        dma((2,)),
        dma,
        dma,
        dma((2,)),
        dma((9,)),
        dma((9,)),
        dma((9,)),
        dma((9,)),
        dma((9, 4)),
        dma((9,)),
        dma((9, 2)),
        dma((9,)),
        dma((9,)),
        dma,
        dma,
        dma((4,)),
        dma((4,)),
        dma((9,)),
        dma((9, 2)),
        dma((shard_rows // 32 + 2,)),
        dma((shard_rows // 192 + 2,)),
        dma((shard_rows // 128 + 2,)),
        dma((shard_rows // 128 + 2,)),
        dma((shard_rows // 192 + 2,)),
        dma((shard_rows // 128 + 2,)),
        dma((9,)),
    ]
    sds = jax.ShapeDtypeStruct
    outs = (
        sds((2, PX, 256), BF16),
        sds((2, 4 * PX, 128), BF16),
        sds((shard_rows, 128), F32),
    )
    vmem = pl.BlockSpec(memory_space=pltpu.VMEM)
    smem = pl.BlockSpec(memory_space=pltpu.SMEM)
    return pl.pallas_call(
        make_kernel(n),
        out_shape=outs,
        in_specs=[smem if i == 2 else vmem for i in range(len(operands))],
        out_specs=[vmem] * len(outs),
        scratch_shapes=scratch,
        compiler_params=pltpu.CompilerParams(
            collective_id=0, has_side_effects=True, vmem_limit_bytes=60 << 20
        ),
    )(*operands)


def per_device(images, cotangent, res_codes, section_weights):
    n = lax.axis_size("dp")
    out_o, out_i, out_w = call_kernel(
        n,
        (
            images.reshape(2, 4 * PX, 128),
            cotangent.reshape(2, PX, 256),
            res_codes,
            section_weights.reshape(-1, 128),
        ),
    )
    block_out = out_o.reshape(2, SIDE, SIDE, 256)
    input_grad = out_i.reshape(images.shape)
    return block_out, input_grad, out_w.reshape(section_weights.shape)


def solution(mesh):
    return jax.shard_map(
        per_device,
        mesh=mesh,
        in_specs=(
            P("dp", None, None, "section"),
            P("dp", None, None, "section"),
            P("dp"),
            P("section", "dp"),
        ),
        out_specs=(
            P("dp", None, None, "section"),
            P("dp", None, None, "section"),
            P("section", "dp"),
        ),
        check_vma=False,
    )
```

```python
import jax
import jax.numpy as jnp
from jax import lax
from jax.experimental import pallas as pl
from jax.experimental.pallas import tpu as pltpu
from jax.sharding import PartitionSpec as P

CIN = 512
COUT = 1024
CMID = 256
CSQ = 128
SIDE = 16
PX = SIDE * SIDE
HALF = 128
WSLOTS = 1351680
EPS = 1e-05
HIGH = lax.Precision.HIGHEST
MESH = pl.DeviceIdType.MESH
F32 = jnp.float32
BF16 = jnp.bfloat16
PHASES = 14
ROWS = (
    (3, 0),
    (4, 0),
    (2, 2),
    (16, 0),
    (2, 0),
    (4, 0),
    (2, 2),
    (8, 0),
    (8, 0),
    (10, 2),
    (2, 0),
    (16, 0),
    (10, 2),
    (2, 0),
)


class Matrix:
    def __init__(self, index, row, start, blocks, pieces, rows, first, step, split="columns"):
        self.index = index
        self.row = row
        self.start = start
        self.blocks = blocks
        self.pieces = pieces
        self.rows = rows
        self.first = first
        self.step = step
        self.split = split
        self.flat = blocks * rows
        self.width = 128 * (blocks // 2 if split == "columns" else blocks)


IN0 = Matrix(0, 0, 0, 2, 8, 16, 0, 1)
MID0 = Matrix(1, 0, 1028, 4, 6, 48, 0, 1)
REST0 = Matrix(2, 0, 5636, 1, 8, 25, 0, 1, split="none")
SC0 = Matrix(3, 0, 6418, 8, 8, 16, 0, 1)
OUT1 = Matrix(4, 1, 0, 8, 4, 16, 1, 2)
IN1 = Matrix(5, 1, 2064, 2, 8, 16, 0, 1, split="rows")
MID2 = Matrix(6, 2, 0, 4, 6, 48, 2, 1)
REST2 = Matrix(7, 2, 4608, 1, 8, 25, 0, 1, split="none")
OUT3 = Matrix(8, 3, 0, 8, 4, 16, 0, 2)
SQ0 = Matrix(2, 0, 5644, 1, 4, 16, 0, 2, split="none")
EX0 = Matrix(9, 0, 5902, 1, 8, 16, 0, 1, split="none")
SQ2 = Matrix(7, 2, 4616, 1, 4, 16, 1, 2, split="none")
EX2 = Matrix(10, 2, 4874, 1, 8, 16, 0, 1, split="none")
CUT = (IN0, MID0, SC0, OUT1, MID2, OUT3)
USED = (10530, 4116, 5390, 2064)
REST_ROWS = 782
HOME_ROWS = 1152
REST_PART = 97
AT_SQ, AT_GSQ, AT_BSQ, AT_EX, AT_BEX = 8, 264, 265, 266, 778
TABLE = {
    (0, "g_in"): (0, 1024, 1),
    (0, "b_in"): (2, 1026, 1),
    (0, "g_mid"): (4, 5636, 2),
    (0, "b_mid"): (8, 5640, 2),
    (0, "g_sc"): (12, 10514, 4),
    (0, "b_sc"): (20, 10522, 4),
    (1, "g_out"): (34, 2048, 4),
    (1, "b_out"): (42, 2056, 4),
    (1, "g_in"): (50, 4112, 1),
    (1, "b_in"): (52, 4114, 1),
    (3, "g_out"): (54, 2048, 4),
    (3, "b_out"): (62, 2056, 4),
    (2, "g_mid"): (70, 4608, 2),
    (2, "b_mid"): (74, 4612, 2),
}
TABLE_ROWS = 84
LATE_ROWS = 12
SECTION_ROWS = {0: (0, 34), 1: (34, 20), 2: (70, 14), 3: (54, 16)}
AT_MID = {0: 4, 2: 70}
AT_SMALL = {0: 28, 2: 78}
RANGES = (
    (0, 1024, 4, 0),
    (0, 5636, 8, 4),
    (0, 10514, 16, 12),
    (0, 5900, 2, 28),
    (0, 6414, 4, 30),
    (1, 2048, 16, 34),
    (1, 4112, 4, 50),
    (2, 4608, 8, 70),
    (2, 4872, 2, 78),
    (2, 5386, 4, 80),
    (3, 2048, 16, 54),
)


def dot(a, b):
    return lax.dot_general(a, b, (((1,), (0,)), ((), ())), preferred_element_type=F32)


def dot_rt(a, b):
    return lax.dot_general(a, b, (((1,), (1,)), ((), ())), preferred_element_type=F32)


def dot_lt(a, b):
    return lax.dot_general(a, b, (((0,), (0,)), ((), ())), preferred_element_type=F32)


def dot_hi(a, b, dims=((1,), (0,))):
    return lax.dot_general(a, b, (dims, ((), ())), precision=HIGH, preferred_element_type=F32)


def sigmoid(v):
    return 0.5 + 0.5 * jnp.tanh(0.5 * v)


def fold8(x):
    return jnp.sum(x.reshape(x.shape[0] // 8, 8, x.shape[1]), axis=0)


def lanes(x, count):
    return jnp.concatenate([x] * count, axis=1) if count > 1 else x


def make_kernel(n):
    chips = n // 2
    shard_rows = WSLOTS // (128 * n)
    fill_rows = max(shard_rows + 34 * n, 96 * (n - 1), 100 * n, 8 * (4 * n - 1), 16 * (2 * n - 1))

    def kernel(
        img,
        cot,
        codes,
        shard,
        out_o,
        out_i,
        out_w,
        snd,
        rcv,
        side_t,
        u,
        um,
        pool,
        ctb,
        mref,
        z1,
        z2,
        zs,
        z3,
        z4,
        z5,
        z6,
        v3,
        cols1,
        cols2,
        rr1,
        rr2,
        a1,
        a2,
        y1,
        dv6,
        dbuf,
        spb,
        pz,
        pda,
        pdp,
        dz4,
        dz1,
        dz3,
        dzs,
        ep,
        dh,
        obuf,
        ibuf,
        sround,
        nought,
        fill,
        fill2,
        table,
        w_in0,
        w_mid0,
        w_sc,
        w_out1,
        w_in1,
        w_mid2,
        w_out3,
        ln_in0,
        ln_mid0,
        ln_sc,
        ln_out1,
        ln_in1,
        ln_mid2,
        ln_out3,
        st_in0,
        st_mid0,
        st_sc,
        st_out1,
        st_in1,
        st_mid2,
        st_out3,
        cu_in0,
        cu_mid0,
        cu_sc,
        cu_out1,
        cu_mid2,
        cu_out3,
        gw_in0,
        gw_mid0,
        gw_sc,
        gw_out1,
        gw_in1,
        gw_mid2,
        gw_out3,
        ga_mid0,
        ga_sc,
        ga_out1,
        ga_in1,
        ga_mid2,
        ga_out3,
        gp_mid0,
        gp_sc,
        gp_out1,
        gp_in1,
        gp_mid2,
        gp_out3,
        gb_in0,
        gb_mid0,
        gb_sc,
        gb_out1,
        gb_in1,
        gb_mid2,
        gb_out3,
        gf_in0,
        gf_mid0,
        gf_sc,
        gf_out1,
        gf_in1,
        gf_mid2,
        gf_out3,
        rg0,
        rg2,
        rl0,
        rl2,
        rf0,
        rf2,
        gvt,
        gvl,
        gvs,
        gd_mid0,
        gt_mid0,
        gd_mid2,
        gt_mid2,
        gd_sc,
        gt_sc,
        gd_out1,
        gt_out1,
        gd_out3,
        gt_out3,
        gd_in1,
        gt_in1,
        hb_in0,
        hi_in0,
        hb_mid0,
        hi_mid0,
        hb_sc,
        hi_sc,
        hb_out1,
        hi_out1,
        hb_mid2,
        hi_mid2,
        hb_out3,
        hi_out3,
        fill3,
        pixels,
        planes,
        merged,
        w_sq0,
        ln_sq0,
        st_sq0,
        cu_sq0,
        w_ex0,
        ln_ex0,
        st_ex0,
        cu_ex0,
        ex0,
        w_sq2,
        ln_sq2,
        st_sq2,
        cu_sq2,
        w_ex2,
        ln_ex2,
        st_ex2,
        cu_ex2,
        ex2,
        ssem,
        rsem,
        bs,
        br,
        img_s,
        img_r,
        ct_s,
        ct_r,
        oo_s,
        oo_r,
        oi_s,
        oi_r,
        h_s,
        t_s,
        t_r,
        h_r,
        a_s,
        c_r,
        f_s,
        q_r,
        ga_s,
        ga_r,
        gb_s,
        gb_r,
        gc_s,
        gc_r,
        v_s,
        v_r,
        gd_s,
        gd_r,
        hr_in0,
        hr_mid0,
        hr_sc,
        hr_out1,
        hr_mid2,
        hr_out3,
        hs_s,
    ):
        s = lax.axis_index("section")
        d = lax.axis_index("dp")
        c = d // 2
        k = d % 2
        m = s % 2
        g = (s // 2) * chips + c

        def peer(o, kk):
            gg = g ^ o
            return ((gg // chips) * 2 + m, 2 * (gg % chips) + kk)

        order = sorted(range(1, n), key=lambda o: (o % chips) + o // chips, reverse=True)

        nought[...] = jnp.zeros(nought.shape, F32)
        barrier = pltpu.get_barrier_semaphore()
        me = s * n + d
        beside_x = s + 1 - 2 * (s % 2)
        beside_y = lax.rem(s + 2, 4)

        def greet(i, _):
            e = lax.rem(me + i, 4 * n)
            pl.semaphore_signal(barrier, inc=1, device_id=(e // n, e % n), device_id_type=MESH)
            return 0

        lax.fori_loop(1, 4 * n, greet, 0)
        sround[...] = shard[...].astype(BF16).astype(F32)

        for slot in range(2):

            def widen(i, _):
                rows = pl.ds(pl.multiple_of(i * 128, 128), 128)
                pixels[rows, :] = img[slot, rows, :].astype(F32)
                return 0

            lax.fori_loop(0, 8, widen, 0)

            def split(r, _):
                for p in range(4):
                    at = (2 * r + p // 2) * 2 * SIDE + p % 2
                    x = pixels[pl.ds(at, SIDE, stride=2), :]
                    planes[slot, p, pl.ds(pl.multiple_of(r * SIDE, SIDE), SIDE), :] = x.astype(BF16)
                return 0

            lax.fori_loop(0, SIDE, split, 0)
        pl.semaphore_wait(barrier, 4 * n - 1)

        def to_twin(i, src, dst):
            return pltpu.make_async_remote_copy(
                src, dst, bs.at[i], br.at[i], device_id=(s, 2 * c + 1 - k), device_id_type=MESH
            )

        def move(src, dst, s_sem, r_sem, dev):
            own = (dev[0] == s) & (dev[1] == d)

            @pl.when(own)
            def _():
                pltpu.make_async_copy(src, dst, r_sem).start()

            @pl.when(jnp.logical_not(own))
            def _():
                pltpu.make_async_remote_copy(
                    src, dst, s_sem, r_sem, device_id=dev, device_id_type=MESH
                ).start()

        def end_move(src, s_sem, dev):
            own = (dev[0] == s) & (dev[1] == d)

            @pl.when(jnp.logical_not(own))
            def _():
                pltpu.make_async_copy(src, src, s_sem).wait()

        def is_self(dev):
            return (dev[0] == s) & (dev[1] == d)

        def move_rows(src, src_at, dst, dst_at, count, full, s_sem, r_sem, dev):
            def go(size, at):
                move(
                    src.at[pl.ds(src_at + at, size)],
                    dst.at[pl.ds(dst_at + at, size)],
                    s_sem,
                    r_sem,
                    dev,
                )

            def chunks(size, start, many):
                def one(i, _):
                    go(size, start + i * size)
                    return 0

                lax.fori_loop(0, many, one, 0)

            if full > 1:

                @pl.when(count == full)
                def _():
                    go(full, 0)

                @pl.when(count < full)
                def _():
                    if full > 16:
                        chunks(16, 0, count // 16)
                        chunks(1, (count // 16) * 16, count % 16)
                    else:
                        chunks(1, 0, count)

            else:
                chunks(1, 0, count)
            return jnp.where(is_self(dev), 0, count)

        def fill_up(src, dst, first, last, sem):
            def chunks(size, start, many):
                def one(i, _):
                    pltpu.make_async_copy(
                        src.at[pl.ds(0, size)], dst.at[pl.ds(start + i * size, size)], sem
                    ).start()
                    return 0

                lax.fori_loop(0, many, one, 0)

            count = last - first
            chunks(128, first, count // 128)
            chunks(16, first + (count // 128) * 128, count % 128 // 16)
            chunks(1, first + (count // 16) * 16, count % 16)

        used = jnp.where(
            s == 0, USED[0], jnp.where(s == 1, USED[1], jnp.where(s == 2, USED[2], USED[3]))
        )

        mine_from = d * shard_rows
        mine_to = mine_from + shard_rows

        def cut(mat, land, stage, base):
            if mat.split == "none":
                stage[...] = land[pl.ds(base, mat.flat), :].astype(BF16)
                return
            for j in range(mat.blocks):
                for h in range(2):
                    if mat.split == "rows":
                        x = land[pl.ds(base + h * mat.flat + j, mat.rows, stride=mat.blocks), :]
                        stage[h, j] = x.astype(BF16)
                    elif j // (mat.blocks // 2) == h:
                        x = land[pl.ds(base + j, mat.rows, stride=mat.blocks), :]
                        at = 128 * (j % (mat.blocks // 2))
                        stage[h, :, at : at + 128] = x.astype(BF16)

        def holds(mat):
            i = d - mat.first
            inside = (i >= 0) & (i < mat.step * mat.pieces)
            return inside & (i % mat.step == 0) if mat.step > 1 else inside

        def piece(mat):
            return s * mat.pieces + jnp.maximum(d - mat.first, 0) // mat.step

        def scatter_cut(mat, land, stage, ready, part=0, parts=1):
            first = jnp.maximum(mine_from - mat.start, 0) // mat.flat
            last = (jnp.maximum(mine_to - mat.start, 0) + mat.flat - 1) // mat.flat
            last = jnp.minimum(last, 4 * mat.pieces)

            def one(p, sent):
                start = mat.start + p * mat.flat
                lo = jnp.maximum(start, mine_from)
                count = jnp.minimum(start + mat.flat, mine_to) - lo
                dev = (p // mat.pieces, mat.first + mat.step * (p % mat.pieces))

                def in_one():
                    to = ready.at[p - first]
                    cut(mat, sround, to, lo - mine_from)
                    move(to, stage, h_s, h_r.at[mat.index], dev)
                    return jnp.where(is_self(dev), 0, mat.flat // 2)

                def in_rows():
                    return move_rows(
                        sround,
                        lo - mine_from,
                        land,
                        lo - start,
                        count,
                        mat.flat,
                        h_s,
                        h_r.at[mat.index],
                        dev,
                    )

                return sent + lax.cond(count == mat.flat, in_one, in_rows)

            step = (jnp.maximum(last - first, 0) + parts - 1) // parts
            begin = first + part * step
            end = jnp.minimum(last, begin + step)
            return lax.fori_loop(begin, end, one, jnp.int32(0))

        def stage_ready(mat, land, stage):
            start = mat.start + piece(mat) * mat.flat
            whole = start // shard_rows == (start + mat.flat - 1) // shard_rows

            @pl.when(whole)
            def _():
                full_wait(stage, h_r.at[mat.index])

            @pl.when(jnp.logical_not(whole))
            def _():
                full_wait(land, h_r.at[mat.index])
                cut(mat, land, stage, 0)

        def scatter_pieces(mat, land, part=0, parts=1):
            total = mat.pieces * 4 * (2 if mat.split == "rows" else 1)
            first = jnp.maximum(mine_from - mat.start, 0) // mat.flat
            last = (jnp.maximum(mine_to - mat.start, 0) + mat.flat - 1) // mat.flat

            def one(p, sent):
                start = mat.start + p * mat.flat
                lo = jnp.maximum(start, mine_from)
                count = jnp.minimum(start + mat.flat, mine_to) - lo
                h = p // (4 * mat.pieces)
                q = p % (4 * mat.pieces)
                dev = (q // mat.pieces, mat.first + mat.step * (q % mat.pieces))
                return sent + move_rows(
                    sround,
                    lo - mine_from,
                    land,
                    h * mat.flat + lo - start,
                    count,
                    mat.flat,
                    h_s,
                    h_r.at[mat.index],
                    dev,
                )

            last = jnp.minimum(last, total)
            step = (jnp.maximum(last - first, 0) + parts - 1) // parts
            begin = first + part * step
            end = jnp.minimum(last, begin + step)
            return lax.fori_loop(begin, end, one, jnp.int32(0))

        def scatter_table(start, rows, at):
            lo = jnp.maximum(start, mine_from)
            count = jnp.maximum(jnp.minimum(start + rows, mine_to) - lo, 0)

            def one(i, sent):
                e = lax.rem(d + i, n)
                return sent + move_rows(
                    sround,
                    lo - mine_from,
                    table,
                    at + lo - start,
                    count,
                    rows,
                    h_s,
                    t_r.at[0],
                    (s, e),
                )

            return lax.fori_loop(0, jnp.where(count > 0, n, 0), one, jnp.int32(0))

        def pass_table():
            for r, (at, many) in SECTION_ROWS.items():

                @pl.when(s == r)
                def _():
                    here = table.at[pl.ds(at, many)]
                    full_wait(here, t_r.at[0])
                    for i in range(1, 4):
                        pltpu.make_async_remote_copy(
                            here,
                            here,
                            t_s,
                            t_r.at[1],
                            device_id=(lax.rem(s + i, 4), d),
                            device_id_type=MESH,
                        ).start()

        def table_arrived():
            for r in range(4):
                rest = TABLE_ROWS - SECTION_ROWS.get(r, (0, 0))[1]

                @pl.when(s == r)
                def _():
                    full_wait(table.at[pl.ds(0, rest)], t_r.at[1])

        def end_table():
            for r, (_, many) in SECTION_ROWS.items():

                @pl.when(s == r)
                def _():
                    full_wait(fill.at[pl.ds(0, 3 * many)], t_s)

        def full_wait(ref, sem):
            pltpu.make_async_copy(ref, ref, sem).wait()

        def when_row(r, body):
            return lax.cond(s == r, body, lambda: jnp.int32(0))

        sent = when_row(
            0,
            lambda: scatter_cut(MID0, ln_mid0, st_mid0, cu_mid0) + scatter_cut(IN0, ln_in0, st_in0, cu_in0),
        )

        for slot in range(2):
            for kk in range(2):
                move(
                    planes.at[slot, pl.ds(2 * kk, 2)],
                    u.at[s, pl.ds(2 * kk, 2)],
                    img_s.at[slot, kk],
                    img_r.at[s],
                    (2 * k + slot, 2 * c + kk),
                )
        for slot in range(2):
            width = (SIDE - 2 * codes[slot]).astype(F32)
            side_t[k, slot] = jnp.full((8, 128), width, F32)
        side_copy = to_twin(0, side_t.at[k], side_t.at[k])
        side_copy.start()
        snd[...] = jnp.zeros(snd.shape, F32)

        def tables(r):
            count = jnp.int32(0)
            for row_of, start, rows, at in RANGES:
                if row_of == r:
                    count = count + scatter_table(start, rows, at)
            return count

        sent = sent + when_row(0, lambda: tables(0) + scatter_cut(SC0, ln_sc, st_sc, cu_sc))
        sent = sent + when_row(1, lambda: scatter_cut(OUT1, ln_out1, st_out1, cu_out1) + tables(1))
        sent = sent + when_row(2, lambda: tables(2))
        sent = sent + when_row(3, lambda: tables(3))

        def scatter_some(sent, part, parts):
            sent = sent + when_row(2, lambda: scatter_cut(MID2, ln_mid2, st_mid2, cu_mid2, part, parts))
            return sent + when_row(3, lambda: scatter_cut(OUT3, ln_out3, st_out3, cu_out3, part, parts))

        def scatter_early(sent):
            sent = sent + when_row(1, lambda: scatter_pieces(IN1, ln_in1))
            return scatter_some(sent, 1, 3)

        def scatter_late(sent):
            sent = scatter_some(sent, 2, 3)
            sent = sent + when_row(
                2,
                lambda: scatter_cut(SQ2, ln_sq2, st_sq2, cu_sq2)
                + scatter_cut(EX2, ln_ex2, st_ex2, cu_ex2),
            )
            fill_up(nought, fill, sent, fill_rows, h_s)

        sent = scatter_some(sent, 0, 3)
        sent = sent + when_row(
            0,
            lambda: scatter_cut(SQ0, ln_sq0, st_sq0, cu_sq0) + scatter_cut(EX0, ln_ex0, st_ex0, cu_ex0),
        )

        def spread(mat, land, stage, whole):
            @pl.when(holds(mat))
            def _():
                if mat.split == "rows":
                    full_wait(land, h_r.at[mat.index])
                    cut(mat, land, stage, 0)
                else:
                    stage_ready(mat, land, stage)
                p = piece(mat)

                def one(i, _):
                    e = lax.rem(d + i, n)
                    h = e % 2
                    dst = whole.at[:, p] if mat.split == "rows" else whole.at[p]
                    move(stage.at[h], dst, a_s.at[mat.index], c_r.at[mat.index], (s, e))
                    return 0

                lax.fori_loop(0, n, one, 0)

        def quarters(mat, whole, first, many, part=None):
            if part is None:
                span = pl.ds(first * mat.pieces, many * mat.pieces)
            else:
                half = mat.pieces // 2
                span = pl.ds(first * mat.pieces + part * half, half)
            return whole.at[:, span] if mat.split == "rows" else whole.at[span]

        def hand(mat, here, i, to):
            pltpu.make_async_remote_copy(
                here,
                here,
                f_s.at[mat.index],
                q_r.at[mat.index, i],
                device_id=(to, d),
                device_id_type=MESH,
            ).start()

        def pass_on(mat, whole):
            here = quarters(mat, whole, s, 1)
            full_wait(here, c_r.at[mat.index])
            hand(mat, here, 0, beside_x)
            hand(mat, here, 1, beside_y)

        def pass_all(mat, whole):
            here = quarters(mat, whole, s, 1)
            full_wait(here, c_r.at[mat.index])
            for i, to in enumerate((beside_x, beside_y, 3 - s)):
                hand(mat, here, i, to)

        def all_arrived(mat, whole):
            for i, q in enumerate((beside_x, beside_y, 3 - s)):
                full_wait(quarters(mat, whole, q, 1), q_r.at[mat.index, i])

        def pass_far(mat, whole):
            full_wait(quarters(mat, whole, beside_x, 1), q_r.at[mat.index, 0])
            hand(mat, quarters(mat, whole, beside_x, 1, 0), 2, beside_y)
            full_wait(quarters(mat, whole, beside_y, 1), q_r.at[mat.index, 1])
            hand(mat, quarters(mat, whole, beside_y, 1, 1), 3, beside_x)

        def arrived(mat, whole):
            far = 3 - s
            for i in range(2):
                full_wait(quarters(mat, whole, far, 1, i), q_r.at[mat.index, 2 + i])

        def end_spread(mat, whole):
            @pl.when(holds(mat))
            def _():
                rows = mat.rows * mat.width // 256
                full_wait(fill.at[pl.ds(0, (n - 1) * rows)], a_s.at[mat.index])

            full_wait(quarters(mat, whole, 0, 3), f_s.at[mat.index])

        def spread_small(mat, land, stage, whole):
            @pl.when(holds(mat))
            def _():
                stage_ready(mat, land, stage)
                p = piece(mat)

                def one(i, _):
                    e = lax.rem(s * chips + c + i, 4 * chips)
                    move(
                        stage,
                        whole.at[p],
                        a_s.at[mat.index],
                        c_r.at[mat.index],
                        (e // chips, 2 * (e % chips)),
                    )
                    return 0

                lax.fori_loop(0, 4 * chips, one, 0)

        def share_small(mat, whole, i):
            @pl.when(k == 0)
            def _():
                full_wait(whole, c_r.at[mat.index])
                to_twin(i, whole, whole).start()

        def small_arrived(whole, i):
            @pl.when(k == 1)
            def _():
                to_twin(i, whole, whole).wait_recv()

        def end_small(mat, whole, i):
            @pl.when(k == 0)
            def _():
                to_twin(i, whole, whole).wait_send()

            for kk in range(2):

                @pl.when(holds(mat) & (k == kk))
                def _():
                    rows = (4 * chips - 1 + kk) * mat.flat // 2
                    full_wait(fill.at[pl.ds(0, rows)], a_s.at[mat.index])

        @pl.when(holds(IN0))
        def _():
            stage_ready(IN0, ln_in0, st_in0)

            def one(i, _):
                e = lax.rem(me + i, 4 * n)
                h = e % 2
                move(
                    st_in0.at[h],
                    w_in0.at[h, s * 8 + d],
                    a_s.at[0],
                    c_r.at[0],
                    (e // n, e % n),
                )
                return 0

            lax.fori_loop(0, 4 * n, one, 0)

        def whole_rows():
            count = jnp.int32(0)
            for mat in CUT:
                low, high = whole_range(mat)
                count = count + jnp.where(s == mat.row, (high - low) * mat.flat, 0)
            return count

        def part_of(mat, ref, quarter, part):
            half = mat.pieces // 2
            return ref.at[pl.ds(quarter * mat.pieces + part * half, half)]

        def shed(mat, gw, land):
            for part, to in enumerate((beside_x, beside_y)):
                for i, quarter in enumerate((to, 3 - s)):
                    pltpu.make_async_remote_copy(
                        part_of(mat, gw, quarter, part),
                        land.at[part, i],
                        ga_s.at[mat.index],
                        ga_r.at[mat.index, part],
                        device_id=(to, d),
                        device_id_type=MESH,
                    ).start()

        def shed_mid(mat, gw, land, add, land3):
            half = mat.pieces // 2
            for part, to in enumerate((beside_y, beside_x)):
                full_wait(land.at[part], ga_r.at[mat.index, part])
                base = to * mat.pieces + part * half

                def one(i, _):
                    x = gw[base + i].astype(F32) + land[part, 1, i].astype(F32)
                    add[part, i] = x.astype(BF16)
                    return 0

                lax.fori_loop(0, half, one, 0)
                pltpu.make_async_remote_copy(
                    add.at[part],
                    land3.at[part],
                    gd_s.at[mat.index],
                    gd_r.at[mat.index, part],
                    device_id=(to, d),
                    device_id_type=MESH,
                ).start()

        def shed_more(mat, gw, land, land3, part_sum, land2):
            half = mat.pieces // 2
            for part in range(2):
                full_wait(land3.at[part], gd_r.at[mat.index, part])

                def one(j, _):
                    i = part * half + j
                    x = gw[s * mat.pieces + i].astype(F32) + land[part, 0, j].astype(F32)
                    part_sum[i] = (x + land3[part, j].astype(F32)).astype(BF16)
                    move(
                        part_sum.at[i],
                        land2.at[c, k],
                        gb_s.at[mat.index],
                        gb_r.at[mat.index],
                        (s, mat.first + mat.step * i),
                    )
                    return 0

                lax.fori_loop(0, half, one, 0)

        def home_rows(src, src_at, start, rows, limit, r, active):
            left = jnp.int32(0)
            for i in range((rows + shard_rows - 2) // shard_rows + 1):
                owner = start // shard_rows + i
                lo = jnp.maximum(start, owner * shard_rows)
                hi = jnp.minimum(jnp.minimum(start + rows, limit), (owner + 1) * shard_rows)
                count = jnp.where(active, jnp.maximum(hi - lo, 0), 0)
                owner = jnp.minimum(owner, n - 1)

                def go():
                    return move_rows(
                        src,
                        src_at + lo - start,
                        out_w,
                        lo - owner * shard_rows,
                        count,
                        rows,
                        gc_s,
                        gc_r,
                        (r, owner),
                    )

                left = left + lax.cond(count > 0, go, lambda: jnp.int32(0))
            return left

        def home(mat, land2, flat):
            @pl.when(holds(mat))
            def _():
                full_wait(land2, gb_r.at[mat.index])
                for h in range(2):
                    x = jnp.sum(land2[:, h].astype(F32), axis=0)
                    for j in range(mat.width // 128):
                        if mat.split == "rows":
                            at = h * mat.flat + j
                        else:
                            at = h * (mat.blocks // 2) + j
                        flat[pl.ds(at, mat.rows, stride=mat.blocks), :] = x[:, 128 * j : 128 * (j + 1)]

            p = piece(mat)
            left = home_rows(
                flat, 0, mat.start + p * mat.flat, mat.flat, USED[mat.row], mat.row, holds(mat)
            )
            if mat.split == "rows":
                p = p + 4 * mat.pieces
                left = left + home_rows(
                    flat,
                    mat.flat,
                    mat.start + p * mat.flat,
                    mat.flat,
                    USED[mat.row],
                    mat.row,
                    holds(mat),
                )
            return left

        def first_piece(mat, owner):
            return jnp.maximum(owner * shard_rows - mat.start, 0) // mat.flat

        def home_whole(mat):
            start = mat.start + piece(mat) * mat.flat
            return start, start // shard_rows == (start + mat.flat - 1) // shard_rows

        def home_cut(mat, land2, flat, ready, inbox, in_sem, turn=None):
            start, whole = home_whole(mat)
            owner = jnp.minimum(start // shard_rows, n - 1)
            held = holds(mat)
            if turn is not None:
                held = held & ((c < chips // 2) if turn == 0 else (c >= chips // 2))

            @pl.when(held)
            def _():
                full_wait(land2, gb_r.at[mat.index])

            @pl.when(held & whole)
            def _():
                for h in range(2):
                    ready[h] = jnp.sum(land2[:, h].astype(F32), axis=0).astype(BF16)
                slot = piece(mat) - first_piece(mat, owner)
                move(ready, inbox.at[slot], hs_s.at[mat.index], in_sem.at[slot], (mat.row, owner))

            @pl.when(held & jnp.logical_not(whole))
            def _():
                for h in range(2):
                    x = jnp.sum(land2[:, h].astype(F32), axis=0)
                    for j in range(mat.width // 128):
                        at = h * (mat.blocks // 2) + j
                        flat[pl.ds(at, mat.rows, stride=mat.blocks), :] = x[:, 128 * j : 128 * (j + 1)]

            return home_rows(
                flat,
                0,
                start,
                mat.flat,
                USED[mat.row],
                mat.row,
                held & jnp.logical_not(whole),
            )

        def end_home_cut(mat, ready):
            start, whole = home_whole(mat)
            away = (s != mat.row) | (d != start // shard_rows)

            @pl.when(holds(mat) & whole & away)
            def _():
                full_wait(ready, hs_s.at[mat.index])

        def whole_range(mat):
            low = (jnp.maximum(mine_from - mat.start, 0) + mat.flat - 1) // mat.flat
            high = jnp.minimum(jnp.maximum(mine_to - mat.start, 0) // mat.flat, 4 * mat.pieces)
            return low, jnp.maximum(high, low)

        def take(mat, inbox, in_sem):
            @pl.when(s == mat.row)
            def _():
                low, high = whole_range(mat)
                first = first_piece(mat, d)

                def one(p, _):
                    slot = p - first
                    full_wait(inbox.at[slot], in_sem.at[slot])
                    at = mat.start + p * mat.flat - mine_from
                    for h in range(2):
                        for j in range(mat.width // 128):
                            x = inbox[slot, h, :, 128 * j : 128 * (j + 1)].astype(F32)
                            row_at = at + h * (mat.blocks // 2) + j
                            out_w[pl.ds(row_at, mat.rows, stride=mat.blocks), :] = x
                    return 0

                lax.fori_loop(low, high, one, 0)

        def end_shed(mat, gw):
            full_wait(gw.at[pl.ds(0, 2 * mat.pieces)], ga_s.at[mat.index])
            full_wait(gw.at[pl.ds(0, mat.pieces)], gd_s.at[mat.index])

            @pl.when(holds(mat))
            def _():
                full_wait(gw.at[pl.ds(0, mat.pieces - 1)], gb_s.at[mat.index])

            @pl.when(jnp.logical_not(holds(mat)))
            def _():
                full_wait(gw.at[pl.ds(0, mat.pieces)], gb_s.at[mat.index])

        def rest_meet(i, mat, rg, land):
            @pl.when((s == mat.row) & (d < 8))
            def _():
                pltpu.make_async_remote_copy(
                    rg.at[pl.ds(AT_SQ + REST_PART * d, REST_PART)],
                    land,
                    v_s.at[i],
                    v_r.at[i],
                    device_id=(s + 1, d),
                    device_id_type=MESH,
                ).start()

        def rest_home(i, mat, rg, land, flat):
            active = (s == mat.row + 1) & (d < 8)
            at = AT_SQ + REST_PART * jnp.minimum(d, 7)

            @pl.when(active)
            def _():
                full_wait(land, v_r.at[i])
                flat[...] = rg[pl.ds(at, REST_PART), :] + land[...]

            return home_rows(
                flat, 0, mat.start + at, REST_PART, mat.start + REST_ROWS, mat.row, active
            )

        def table_meet(i, first, rows):
            @pl.when((s == 0) & (d < 2))
            def _():
                pltpu.make_async_remote_copy(
                    gvt.at[pl.ds(first, rows)],
                    gvl.at[pl.ds(first, rows)],
                    v_s.at[i],
                    v_r.at[i],
                    device_id=(s + 1, d),
                    device_id_type=MESH,
                ).start()

        def table_home(i, first, rows):
            active = (s == 1) & (d < 2)

            @pl.when(active)
            def _():
                span = pl.ds(first, rows)
                full_wait(gvl.at[span], v_r.at[i])
                gvs[first : first + rows, :] = gvt[first : first + rows, :] + gvl[first : first + rows, :]

            left = jnp.int32(0)
            for (r, _), (at, start, many) in TABLE.items():
                if first <= at < first + rows:
                    left = left + home_rows(
                        gvs,
                        at + many * k,
                        start + many * k,
                        many,
                        start + 2 * many,
                        r,
                        active,
                    )
            return left

        def put(ph, base, value):
            for j in range(value.shape[1] // 128):
                snd[ph, base + j : base + j + 1, :] = value[:, 128 * j : 128 * (j + 1)]

        def send(ph):
            mine, theirs = ROWS[ph]

            def to(o, kk, rows):
                pltpu.make_async_remote_copy(
                    snd.at[ph, pl.ds(0, rows)],
                    rcv.at[ph, k, o, pl.ds(0, rows)],
                    ssem.at[ph],
                    rsem.at[ph, k],
                    device_id=peer(o, kk),
                    device_id_type=MESH,
                ).start()
                return 0

            if n > 8:
                lax.fori_loop(1, n, lambda o, _: to(o, k, mine), 0)
                if theirs:
                    lax.fori_loop(0, n, lambda o, _: to(o, 1 - k, theirs), 0)
            else:
                for o in order:
                    to(o, k, mine)
                    if theirs:
                        to(o, 1 - k, theirs)
                if theirs:
                    to(0, 1 - k, theirs)
            rcv[ph, k, 0] = snd[ph]

        def receive(ph):
            mine, theirs = ROWS[ph]
            full_wait(rcv.at[ph, k, pl.ds(1, n - 1), pl.ds(0, mine)], rsem.at[ph, k])
            if theirs:
                full_wait(rcv.at[ph, 1 - k, :, pl.ds(0, theirs)], rsem.at[ph, 1 - k])

        def end_send(ph):
            mine, theirs = ROWS[ph]
            full_wait(fill.at[pl.ds(0, (n - 1) * mine + n * theirs)], ssem.at[ph])

        def totals(ph):
            return jnp.sum(rcv[ph, k, :, 0 : -(-ROWS[ph][0] // 8) * 8, :], axis=0)

        def row(total, base, width):
            return jnp.concatenate(
                [total[base + j : base + j + 1, :] for j in range(width // 128)], axis=1
            )

        def across(ph, h, base, width):
            return jnp.concatenate(
                [rcv[ph, h, :, base + j, :] for j in range(width // 128)], axis=1
            )

        def rows_of(ref, at, many):
            return jnp.concatenate([ref[pl.ds(at + j, 1), :] for j in range(many)], axis=1)

        def vrow(key):
            at, _, many = TABLE[key]
            return rows_of(table, at + many * k, many)

        def set_gvec(key, value):
            at, _, many = TABLE[key]
            for j in range(many):
                gvt[pl.ds(at + many * k + j, 1), :] = value[:, 128 * j : 128 * (j + 1)]

        def set_rows(ref, at, value):
            for j in range(value.shape[1] // 128):
                ref[at + j : at + j + 1, :] = value[:, 128 * j : 128 * (j + 1)]

        def mean_rstd(total, base, width, count):
            mu = row(total, base, width) / count
            second = row(total, base + width // 128, width) / count
            return mu, lax.rsqrt(jnp.maximum(second - mu * mu, 0.0) + EPS)

        gvt[...] = jnp.zeros(gvt.shape, F32)

        side_copy.wait()
        side_row = jnp.where(
            m == 0, side_t[s // 2, 0, 0:1, :], side_t[s // 2, 1, 0:1, :]
        )
        pixel = lax.broadcasted_iota(jnp.int32, (PX, 128), 0)
        prow = (pixel // SIDE).astype(F32)
        pcol = (pixel % SIDE).astype(F32)
        mref[...] = jnp.where((prow < side_row) & (pcol < side_row), 1.0, 0.0)
        inv_own = 1.0 / (side_row * side_row)

        spread(MID0, ln_mid0, st_mid0, w_mid0)
        for q in range(4):
            here = u.at[q, pl.ds(2 * k, 2)]
            pltpu.make_async_copy(here, here, img_r.at[q]).wait()
            pltpu.make_async_remote_copy(
                here,
                here,
                bs.at[10 + q],
                br.at[10 + q],
                device_id=(s, 2 * c + 1 - k),
                device_id_type=MESH,
            ).start()
        for q in range(4):
            here = u.at[q, pl.ds(2 * (1 - k), 2)]
            pltpu.make_async_copy(here, here, br.at[10 + q]).wait()

        def mask_block(b, _):
            r = pl.multiple_of(b * 32, 32)
            rows = pl.ds(r, 32)
            mask = mref[rows, :]
            for q in range(4):
                total = jnp.zeros((32, 128), F32)
                for p in range(4):
                    x = u[q, p, rows, :].astype(F32) * mask
                    um[p, rows, 128 * q : 128 * (q + 1)] = x.astype(BF16)
                    total = total + x
                pool[rows, 128 * q : 128 * (q + 1)] = (total * 0.25).astype(BF16)
            return 0

        lax.fori_loop(0, 8, mask_block, 0)
        pass_table()
        full_wait(w_in0.at[k], c_r.at[0])

        def z1_block(p, carry):
            z = dot(um[p], w_in0[k].reshape(CIN, 128))
            z1[p] = z
            return (carry[0] + fold8(z), carry[1] + fold8(z * z))

        zero8 = jnp.zeros((8, 128), F32)
        t0, t1 = lax.fori_loop(0, 4, z1_block, (zero8, zero8))
        put(0, 0, jnp.sum(t0, axis=0, keepdims=True))
        put(0, 1, jnp.sum(t1, axis=0, keepdims=True))
        put(0, 2, side_row)
        send(0)
        pass_on(MID0, w_mid0)
        sent = scatter_early(sent)
        pass_far(MID0, w_mid0)
        spread(SC0, ln_sc, st_sc, w_sc)
        spread(OUT1, ln_out1, st_out1, w_out1)
        table_arrived()
        receive(0)
        total = totals(0)
        sides = across(0, k, 2, 128)
        inv_area = 1.0 / (sides * sides)
        count1 = jnp.sum(sides * sides, axis=0, keepdims=True)
        counts = {w: lanes(count1, w // 128) for w in (128, 256, 512)}
        mu1, rs1 = mean_rstd(total, 0, 128, 4.0 * count1)
        lin1 = rs1 * vrow((0, "g_in"))
        off1 = vrow((0, "b_in")) - mu1 * lin1

        colpos = lax.broadcasted_iota(jnp.int32, (PX, 128), 0) % SIDE

        def shift_cols(x, by):
            moved = pltpu.roll(x, by % PX, 0)
            edge = 0 if by == 1 else SIDE - 1
            return jnp.where(colpos == edge, 0.0, moved)

        def store_tap(cols, di, dj, x, shift):
            at = 128 * (3 * di + dj)
            span = slice(at, at + 128)
            x = x.astype(BF16)
            if shift == 1:
                cols[0:SIDE, span] = jnp.zeros((SIDE, 128), BF16)
                cols[SIDE:PX, span] = x[0 : PX - SIDE]
            elif shift == -1:
                cols[PX - SIDE : PX, span] = jnp.zeros((SIDE, 128), BF16)
                cols[0 : PX - SIDE, span] = x[SIDE:PX]
            else:
                cols[:, span] = x

        def plane_taps(parity):
            return ((1, 0),) if parity == 0 else ((0, 1), (2, 0))

        for p in range(4):
            v = z1[p] * lin1 + off1
            h = v * sigmoid(v) * mref[...]
            for dj, cshift in plane_taps(p % 2):
                x = shift_cols(h, 1) if cshift else h
                for di, rshift in plane_taps(p // 2):
                    store_tap(cols1, di, dj, x, rshift)

        def conv_forward(ph, cols, w_mid, zref):
            z = dot(cols[...], w_mid[...].reshape(1152, 256))
            zref[...] = z
            zm = z * lanes(mref[...], 2)
            put(ph, 0, jnp.sum(zm, axis=0, keepdims=True))
            put(ph, 2, jnp.sum(zm * z, axis=0, keepdims=True))
            send(ph)

        def small(rest):
            _, w_sq, ex = rest
            w_ex = jnp.concatenate([ex[pl.ds(j, CSQ, stride=4), :] for j in range(4)], axis=1)
            return w_sq[...].reshape(CMID, CSQ).astype(F32), w_ex

        def attention_forward(ph, twin, total, at, rest, zref, rr, aref, beside):
            mu, rs = mean_rstd(total, 0, 256, counts[256])
            lin = rs * rows_of(table, at + 2 * k, 2)
            off = rows_of(table, at + 4 + 2 * k, 2) - mu * lin

            def block(b, acc):
                rows = pl.ds(pl.multiple_of(b * 64, 64), 64)
                v = zref[rows, :] * lin + off
                r = v * sigmoid(v) * lanes(mref[rows, :], 2)
                rr[k, rows, :] = r
                return acc + fold8(r)

            acc = lax.fori_loop(0, 4, block, jnp.zeros((8, 256), F32))
            pooled_own = jnp.sum(acc, axis=0, keepdims=True) * lanes(inv_own, 2)
            put(ph, 0, pooled_own)
            send(ph)
            swap = to_twin(twin, rr.at[k], rr.at[k])
            swap.start()
            beside()
            receive(ph)
            w_sq, w_ex = small(rest)
            pooled = across(ph, 0, 0, 256) + across(ph, 1, 0, 256)
            zq = dot_hi(pooled, w_sq)
            mq = jnp.mean(zq, axis=0, keepdims=True)
            vq = jnp.mean(zq * zq, axis=0, keepdims=True) - mq * mq
            rq = lax.rsqrt(jnp.maximum(vq, 0.0) + EPS)
            hq = (zq - mq) * rq
            nq = hq * rows_of(table, rest[0], 1) + rows_of(table, rest[0] + 1, 1)
            sgq = sigmoid(nq)
            qq = nq * sgq
            logits = dot_hi(qq, w_ex) + rows_of(table, rest[0] + 2, 4)
            diff = logits[:, 0:256] - logits[:, 256:512]
            sh0 = sigmoid(diff)
            sh1 = sigmoid(-diff)
            swap.wait()
            s0 = sh0[0:1, :]
            s1 = sh1[0:1, :]

            def mix(b, _):
                rows = pl.ds(pl.multiple_of(b * 64, 64), 64)
                aref[rows, :] = (s0 * rr[0, rows, :] + s1 * rr[1, rows, :]).astype(BF16)
                return 0

            lax.fori_loop(0, 4, mix, 0)
            return (mu, rs, lin, off), (pooled, rq, hq, nq, sgq, qq, sh0, sh1)

        def attention_backward(
            ph, kept_mid, kept_q, rest, rg, zref, rr, cols, mat, gw_mid, ga_mid, da, beside
        ):
            mu, rs, lin, off = kept_mid
            pooled, rq, hq, nq, sgq, qq, sh0, sh1 = kept_q

            def block(b, acc):
                rows = pl.ds(pl.multiple_of(b * 32, 32), 32)
                z = zref[rows, :]
                v = z * lin + off
                hat = (z - mu) * rs
                sg = sigmoid(v)
                sp = sg * (1.0 + v * (1.0 - sg)) * lanes(mref[rows, :], 2)
                grad = da(rows)
                t = grad * sp
                dbuf[rows, :] = grad
                spb[rows, :] = sp
                r = rr[k, rows, :]
                return tuple(
                    x + fold8(y)
                    for x, y in zip(acc, (grad * r, t, sp, t * hat, sp * hat))
                )

            acc = lax.fori_loop(0, 8, block, (jnp.zeros((8, 256), F32),) * 5)
            for j, x in enumerate(acc):
                put(ph, 2 * j, jnp.sum(x, axis=0, keepdims=True))
            send(ph)
            beside()
            receive(ph)
            ds0 = across(ph, 0, 0, 256)
            ds1 = across(ph, 1, 0, 256)
            mean = sh0 * ds0 + sh1 * ds1
            dl = jnp.concatenate([sh0 * (ds0 - mean), sh1 * (ds1 - mean)], axis=1)
            w_sq, w_ex = small(rest)
            set_rows(rg, AT_BEX, jnp.sum(dl, axis=0, keepdims=True))
            dq = dot_hi(dl, w_ex, ((1,), (1,)))
            dn = dq * sgq * (1.0 + nq * (1.0 - sgq))
            set_rows(rg, AT_GSQ, jnp.sum(dn * hq, axis=0, keepdims=True))
            set_rows(rg, AT_BSQ, jnp.sum(dn, axis=0, keepdims=True))
            dn = dn * rows_of(table, rest[0], 1)
            dzq = rq * (
                dn
                - jnp.mean(dn, axis=0, keepdims=True)
                - hq * jnp.mean(dn * hq, axis=0, keepdims=True)
            )
            dpool = dot_hi(dzq, w_sq, ((1,), (1,))) * lanes(inv_area, 2)
            share = jnp.where(k == 0, sh0, sh1)

            def both_sums(first, second):
                return jnp.sum(
                    share * across(ph, k, first, 256) + dpool * across(ph, k, second, 256),
                    axis=0,
                    keepdims=True,
                )

            sdv = both_sums(2, 4)
            sdh = both_sums(6, 8)
            set_gvec((mat.row, "b_mid"), sdv)
            set_gvec((mat.row, "g_mid"), sdh)
            own_share = share[0:1, :]
            own_pool = dpool[0:1, :]
            c1 = sdv / counts[256]
            c2 = sdh / counts[256]

            def block2(b, _):
                rows = pl.ds(pl.multiple_of(b * 32, 32), 32)
                hat = (zref[rows, :] - mu) * rs
                dv = (own_share * dbuf[rows, :] + own_pool) * spb[rows, :]
                dz = lin * (dv - c1 - hat * c2) * lanes(mref[rows, :], 2)
                rows_low[rows, :] = dz.astype(BF16)
                return 0

            rows_low = dz_low
            lax.fori_loop(0, 8, block2, 0)

            def rest():
                gw_mid[...] = dot_lt(cols[...], dz_low[...]).astype(BF16).reshape(24, 48, 256)
                shed(mat, gw_mid, ga_mid)
                g_ex = dot_hi(qq, dl, ((0,), (0,)))
                for j in range(4):
                    rg[pl.ds(AT_EX + j, CSQ, stride=4), :] = g_ex[:, 128 * j : 128 * (j + 1)]
                rg[AT_SQ : AT_SQ + CMID, :] = dot_hi(pooled, dzq, ((0,), (0,)))

            return rest

        dz_low = dz3.at[:, pl.ds(0, 256)]

        rest0 = (AT_SMALL[0], w_sq0, ex0)
        rest2 = (AT_SMALL[2], w_sq2, ex2)
        arrived(MID0, w_mid0)
        conv_forward(1, cols1, w_mid0, z2)
        spread_small(SQ0, ln_sq0, st_sq0, w_sq0)
        spread_small(EX0, ln_ex0, st_ex0, w_ex0)
        scatter_late(sent)
        pass_on(SC0, w_sc)
        pass_on(OUT1, w_out1)
        spread(IN1, ln_in1, st_in1, w_in1)
        receive(1)

        def short_forward():
            spread(MID2, ln_mid2, st_mid2, w_mid2)
            share_small(SQ0, w_sq0, 15)
            share_small(EX0, w_ex0, 17)
            pass_far(SC0, w_sc)
            pass_far(OUT1, w_out1)
            pass_all(IN1, w_in1)
            arrived(SC0, w_sc)
            z = dot(pool[...], w_sc[...].reshape(CIN, 512))
            zs[...] = z
            put(3, 8, jnp.sum(z, axis=0, keepdims=True))
            put(3, 12, jnp.sum(z * z, axis=0, keepdims=True))
            small_arrived(w_sq0, 15)
            small_arrived(w_ex0, 17)
            ex0[...] = w_ex0[...].reshape(512, 128).astype(F32)

        mid1, q1 = attention_forward(2, 2, totals(1), AT_MID[0], rest0, z2, rr1, a1, short_forward)
        arrived(OUT1, w_out1)

        def wide_forward(ph, aref, w, zref):
            z = dot(aref[...], w[...].reshape(CMID, 512))
            zref[...] = z
            put(ph, 0, jnp.sum(z, axis=0, keepdims=True))
            put(ph, 4, jnp.sum(z * z, axis=0, keepdims=True))
            send(ph)

        wide_forward(3, a1, w_out1, z3)
        pass_all(MID2, w_mid2)
        spread_small(SQ2, ln_sq2, st_sq2, w_sq2)
        spread_small(EX2, ln_ex2, st_ex2, w_ex2)
        receive(3)
        total = totals(3)
        mus, rss = mean_rstd(total, 8, 512, counts[512])
        lins = rss * vrow((0, "g_sc"))
        offs = vrow((0, "b_sc")) - mus * lins

        mu3, rs3 = mean_rstd(total, 0, 512, counts[512])
        lin3 = rs3 * vrow((1, "g_out"))
        off3 = vrow((1, "b_out")) - mu3 * lin3

        def y1_block(b, _):
            rows = pl.ds(pl.multiple_of(b * 32, 32), 32)
            short = (zs[rows, :] * lins + offs).astype(BF16).astype(F32)
            v = z3[rows, :] * lin3 + off3 + short
            v3[rows, :] = v
            y1[rows, :] = (v * sigmoid(v) * lanes(mref[rows, :], 4)).astype(BF16)
            return 0

        lax.fori_loop(0, 8, y1_block, 0)
        all_arrived(IN1, w_in1)
        pz[0] = dot(y1[...], w_in1[1 - k].reshape(512, 128))
        swap = to_twin(3, pz.at[0], pz.at[1])
        swap.start()
        z = dot(y1[...], w_in1[k].reshape(512, 128))
        swap.wait()
        z = z + pz[1]
        z4[...] = z
        put(4, 0, jnp.sum(z, axis=0, keepdims=True))
        put(4, 1, jnp.sum(z * z, axis=0, keepdims=True))
        send(4)
        spread(OUT3, ln_out3, st_out3, w_out3)
        receive(4)
        mu4, rs4 = mean_rstd(totals(4), 0, 128, count1)
        lin4 = rs4 * vrow((1, "g_in"))
        off4 = vrow((1, "b_in")) - mu4 * lin4
        v = z4[...] * lin4 + off4
        h = v * sigmoid(v) * mref[...]
        for dj in range(3):
            x = h if dj == 1 else shift_cols(h, 1 - dj)
            for di in range(3):
                store_tap(cols2, di, dj, x, 1 - di)

        all_arrived(MID2, w_mid2)
        conv_forward(5, cols2, w_mid2, z5)
        share_small(SQ2, w_sq2, 16)
        share_small(EX2, w_ex2, 18)
        pass_on(OUT3, w_out3)
        receive(5)

        def last_weights():
            pass_far(OUT3, w_out3)
            small_arrived(w_sq2, 16)
            small_arrived(w_ex2, 18)
            ex2[...] = w_ex2[...].reshape(512, 128).astype(F32)
            for slot in range(2):
                move(
                    cot.at[slot],
                    ctb.at[lax.rem(s, 2)],
                    ct_s.at[slot],
                    ct_r.at[lax.rem(s, 2)],
                    (2 * k + slot, 2 * c + s // 2),
                )
            to_twin(14, w_in0.at[k], w_in0.at[k]).start()

        mid2, q2 = attention_forward(6, 4, totals(5), AT_MID[2], rest2, z5, rr2, a2, last_weights)
        arrived(OUT3, w_out3)
        wide_forward(7, a2, w_out3, z6)
        to_twin(14, w_in0.at[k], w_in0.at[k]).wait()
        for i in range(2):
            pltpu.make_async_copy(ctb.at[i], ctb.at[i], ct_r.at[i]).wait()
        receive(7)
        mu6, rs6 = mean_rstd(totals(7), 0, 512, counts[512])
        lin6 = rs6 * vrow((3, "g_out"))
        off6 = vrow((3, "b_out")) - mu6 * lin6

        def out_block(b, acc):
            rows = pl.ds(pl.multiple_of(b * 32, 32), 32)
            z = z6[rows, :]
            mask = lanes(mref[rows, :], 4)
            v = z * lin6 + off6 + y1[rows, :].astype(F32)
            sg = sigmoid(v)
            y = (v * sg * mask).astype(BF16)
            obuf[0, rows, :] = y[:, 0:256]
            obuf[1, rows, :] = y[:, 256:512]
            ct = jnp.concatenate([ctb[0, rows, :], ctb[1, rows, :]], axis=1).astype(F32)
            dv = ct * (sg * (1.0 + v * (1.0 - sg)) * mask)
            dv6[rows, :] = dv
            return (acc[0] + fold8(dv), acc[1] + fold8(dv * ((z - mu6) * rs6)))

        zero512 = jnp.zeros((8, 512), F32)
        t0, t1 = lax.fori_loop(0, 8, out_block, (zero512, zero512))
        put(8, 0, jnp.sum(t0, axis=0, keepdims=True))
        put(8, 4, jnp.sum(t1, axis=0, keepdims=True))
        send(8)
        fill_up(nought, out_w, jnp.clip(used - d * shard_rows, 0, shard_rows), shard_rows, gc_r)
        fill_up(nought, fill3, 0, whole_rows(), gc_r)
        for j in range(2):
            move(
                obuf.at[j],
                out_o.at[lax.rem(s, 2)],
                oo_s.at[j],
                oo_r.at[lax.rem(s, 2)],
                (2 * k + j, 2 * c + s // 2),
            )
        for mat, whole in ((MID0, w_mid0), (SC0, w_sc), (OUT1, w_out1)):
            end_spread(mat, whole)
        end_small(SQ0, w_sq0, 15)
        end_small(EX0, w_ex0, 17)
        end_table()
        receive(8)

        def wide_back(total, base, key_g, key_b, lin, mu, rs, zref, dvf, dst):
            sdv = row(total, base, 512)
            sdh = row(total, base + 4, 512)
            set_gvec(key_b, sdv)
            set_gvec(key_g, sdh)
            c1 = sdv / counts[512]
            c2 = sdh / counts[512]

            def block(b, _):
                rows = pl.ds(pl.multiple_of(b * 32, 32), 32)
                hat = (zref[rows, :] - mu) * rs
                dz = lin * (dvf(rows) - c1 - hat * c2) * lanes(mref[rows, :], 4)
                dst[rows, :] = dz.astype(BF16)
                return 0

            lax.fori_loop(0, 8, block, 0)

        wide_back(
            totals(8),
            0,
            (3, "g_out"),
            (3, "b_out"),
            lin6,
            mu6,
            rs6,
            z6,
            lambda rows: dv6[rows, :],
            dz3,
        )

        def attended_grad(twin, w, aref, mat, gw, land):
            pda[0] = dot_rt(dz3[...], w[...].reshape(CMID, 512))
            swap = to_twin(twin, pda.at[0], pda.at[1])
            swap.start()
            gw[...] = dot_lt(aref[...], dz3[...]).astype(BF16).reshape(16, 16, 512)
            shed(mat, gw, land)
            swap.wait()

        def summed_grad(rows):
            return (pda[0, rows, :] + pda[1, rows, :]).astype(BF16).astype(F32)

        attended_grad(5, w_out3, a2, OUT3, gw_out3, ga_out3)

        def beside9():
            for mat, whole in ((IN1, w_in1), (MID2, w_mid2), (OUT3, w_out3)):
                end_spread(mat, whole)
            end_small(SQ2, w_sq2, 16)
            end_small(EX2, w_ex2, 18)
            shed_mid(OUT3, gw_out3, ga_out3, gt_out3, gd_out3)

        grad_rest2 = attention_backward(
            9,
            mid2,
            q2,
            rest2,
            rg2,
            z5,
            rr2,
            cols2,
            MID2,
            gw_mid2,
            ga_mid2,
            summed_grad,
            beside9,
        )

        ep[...] = jnp.zeros(ep.shape, F32)
        for di in range(3):
            part = dot_rt(dz_low[...], w_mid2[8 * di : 8 * (di + 1)].reshape(384, 256))
            for dj in range(3):
                lo = SIDE * di
                ep[dj, lo : lo + PX, :] += part[:, 128 * dj : 128 * (dj + 1)]
        grad = ep[1, SIDE : SIDE + PX, :]
        grad = grad + shift_cols(ep[0, SIDE : SIDE + PX, :], -1)
        grad = grad + shift_cols(ep[2, SIDE : SIDE + PX, :], 1)
        grad = grad.astype(BF16).astype(F32)
        v = z4[...] * lin4 + off4
        hat4 = (z4[...] - mu4) * rs4
        sg = sigmoid(v)
        dv4 = grad * (sg * (1.0 + v * (1.0 - sg)) * mref[...])
        dh[0] = dv4
        put(10, 0, jnp.sum(dv4, axis=0, keepdims=True))
        put(10, 1, jnp.sum(dv4 * hat4, axis=0, keepdims=True))
        send(10)
        grad_rest2()
        rest_meet(2, REST2, rg2, rl2)
        shed_more(OUT3, gw_out3, ga_out3, gd_out3, gp_out3, gb_out3)
        receive(10)
        total = totals(10)
        set_gvec((1, "b_in"), total[0:1, :])
        set_gvec((1, "g_in"), total[1:2, :])
        hat4 = (z4[...] - mu4) * rs4
        dz = lin4 * (dh[0] - total[0:1, :] / count1 - hat4 * (total[1:2, :] / count1)) * mref[...]
        dz4[k] = dz.astype(BF16)
        swap = to_twin(6, dz4.at[k], dz4.at[k])
        swap.start()
        swap.wait()

        def dy_block(b, acc):
            rows = pl.ds(pl.multiple_of(b * 64, 64), 64)
            dy = dot_rt(dz4[0, rows, :], w_in1[0].reshape(512, 128))
            dy = dy + dot_rt(dz4[1, rows, :], w_in1[1].reshape(512, 128))
            dy = dy + dv6[rows, :].astype(BF16).astype(F32)
            v = v3[rows, :]
            sg = sigmoid(v)
            dv = dy * (sg * (1.0 + v * (1.0 - sg)) * lanes(mref[rows, :], 4))
            v3[rows, :] = dv
            low = dv.astype(BF16).astype(F32)
            hat = (z3[rows, :] - mu3) * rs3
            hats = (zs[rows, :] - mus) * rss
            return tuple(
                x + fold8(y) for x, y in zip(acc, (dv, dv * hat, low, low * hats))
            )

        acc = lax.fori_loop(0, 4, dy_block, (zero512,) * 4)
        for j, x in enumerate(acc):
            put(11, 4 * j, jnp.sum(x, axis=0, keepdims=True))
        send(11)
        both4 = jnp.concatenate([dz4[0], dz4[1]], axis=1)
        gw_in1[...] = dot_lt(y1[...], both4).astype(BF16).reshape(32, 16, 256)
        shed(IN1, gw_in1, ga_in1)
        shed_mid(MID2, gw_mid2, ga_mid2, gt_mid2, gd_mid2)
        left = rest_home(2, REST2, rg2, rl2, rf2)
        receive(11)
        total = totals(11)
        wide_back(
            total,
            0,
            (1, "g_out"),
            (1, "b_out"),
            lin3,
            mu3,
            rs3,
            z3,
            lambda rows: v3[rows, :],
            dz3,
        )
        wide_back(
            total,
            8,
            (0, "g_sc"),
            (0, "b_sc"),
            lins,
            mus,
            rss,
            zs,
            lambda rows: v3[rows, :].astype(BF16).astype(F32),
            dzs,
        )
        attended_grad(7, w_out1, a1, OUT1, gw_out1, ga_out1)

        def short_back():
            part = dot_rt(dzs[...], w_sc[...].reshape(CIN, 512))
            pdp[0] = jnp.where(k == 0, part[:, 256:512], part[:, 0:256])
            to_twin(8, pdp.at[0], pdp.at[1]).start()
            pdp[2] = jnp.where(k == 0, part[:, 0:256], part[:, 256:512])
            gw_sc[...] = dot_lt(pool[...], dzs[...]).astype(BF16).reshape(32, 16, 512)
            shed(SC0, gw_sc, ga_sc)
            table_meet(0, LATE_ROWS, TABLE_ROWS - LATE_ROWS)
            shed_mid(IN1, gw_in1, ga_in1, gt_in1, gd_in1)
            shed_mid(OUT1, gw_out1, ga_out1, gt_out1, gd_out1)
            shed_more(MID2, gw_mid2, ga_mid2, gd_mid2, gp_mid2, gb_mid2)

        grad_rest0 = attention_backward(
            12,
            mid1,
            q1,
            rest0,
            rg0,
            z2,
            rr1,
            cols1,
            MID0,
            gw_mid0,
            ga_mid0,
            summed_grad,
            short_back,
        )

        for p in range(4):
            dh[p] = jnp.zeros((PX, 128), F32)
        for di in range(3):
            part = dot_rt(dz_low[...], w_mid0[8 * di : 8 * (di + 1)].reshape(384, 256))
            pr = 0 if di == 1 else 1
            for dj in range(3):
                x = part[:, 128 * dj : 128 * (dj + 1)]
                if dj == 0:
                    x = shift_cols(x, -1)
                p = 2 * pr + (0 if dj == 1 else 1)
                if di == 0:
                    dh[p, 0 : PX - SIDE, :] += x[SIDE:PX]
                else:
                    dh[p] += x

        def dv1_block(p, acc):
            z = z1[p]
            v = z * lin1 + off1
            sg = sigmoid(v)
            dv = dh[p] * (sg * (1.0 + v * (1.0 - sg)) * mref[...])
            dh[p] = dv
            return (acc[0] + fold8(dv), acc[1] + fold8(dv * ((z - mu1) * rs1)))

        t0, t1 = lax.fori_loop(0, 4, dv1_block, (zero8, zero8))
        put(13, 0, jnp.sum(t0, axis=0, keepdims=True))
        put(13, 1, jnp.sum(t1, axis=0, keepdims=True))
        send(13)
        grad_rest0()
        rest_meet(1, REST0, rg0, rl0)
        shed_more(IN1, gw_in1, ga_in1, gd_in1, gp_in1, gb_in1)
        shed_more(OUT1, gw_out1, ga_out1, gd_out1, gp_out1, gb_out1)
        shed_mid(SC0, gw_sc, ga_sc, gt_sc, gd_sc)
        left = left + home_cut(OUT3, gb_out3, gf_out3, hb_out3, hi_out3, hr_out3)
        left = left + table_home(0, LATE_ROWS, TABLE_ROWS - LATE_ROWS)
        receive(13)
        total = totals(13)
        set_gvec((0, "b_in"), total[0:1, :])
        set_gvec((0, "g_in"), total[1:2, :])
        table_meet(3, 0, LATE_ROWS)
        k1 = total[0:1, :] / (4.0 * count1)
        k2 = total[1:2, :] / (4.0 * count1)

        def dz1_block(p, _):
            hat = (z1[p] - mu1) * rs1
            dz1[k, p] = (lin1 * (dh[p] - k1 - hat * k2) * mref[...]).astype(BF16)
            return 0

        lax.fori_loop(0, 4, dz1_block, 0)
        swap = to_twin(9, dz1.at[k], dz1.at[k])
        swap.start()
        total = jnp.zeros((CIN, 128), F32)
        for p in range(4):
            total = total + dot_lt(um[p], dz1[k, p])
        gw_in0[...] = total.astype(BF16).reshape(32, 16, 128)

        def shed_in0(i, _):
            p = lax.rem(8 * s + i, 32)
            move(
                gw_in0.at[p],
                gb_in0.at[s * chips + c, k],
                gb_s.at[0],
                gb_r.at[0],
                (p // 8, p % 8),
            )
            return 0

        lax.fori_loop(0, 32, shed_in0, 0)
        shed_mid(MID0, gw_mid0, ga_mid0, gt_mid0, gd_mid0)
        shed_more(SC0, gw_sc, ga_sc, gd_sc, gp_sc, gb_sc)
        swap.wait()
        to_twin(8, pdp.at[0], pdp.at[1]).wait()

        def du_block(p, _):
            mine = pl.ds(16 * k, 16)
            grad = dot_rt(dz1[0, p], w_in0[0, mine].reshape(256, 128))
            grad = grad + dot_rt(dz1[1, p], w_in0[1, mine].reshape(256, 128))
            grad = (grad + 0.25 * (pdp[1] + pdp[2])) * lanes(mref[...], 2)
            for r in range(SIDE):
                at = (2 * r + p // 2) * 2 * SIDE + p % 2
                for j in range(2):
                    x = grad[SIDE * r : SIDE * (r + 1), 128 * j : 128 * (j + 1)]
                    merged[j, pl.ds(at, SIDE, stride=2), :] = x
            return 0

        lax.fori_loop(0, 4, du_block, 0)

        def narrow(i, _):
            rows = pl.ds(pl.multiple_of(i * 128, 128), 128)
            for j in range(2):
                ibuf[j, rows, :] = merged[j, rows, :].astype(BF16)
            return 0

        lax.fori_loop(0, 8, narrow, 0)
        for j in range(2):
            move(
                ibuf.at[j],
                out_i.at[lax.rem(s, 2)],
                oi_s.at[j],
                oi_r.at[lax.rem(s, 2)],
                (2 * k + j, 2 * c + s // 2),
            )

        shed_more(MID0, gw_mid0, ga_mid0, gd_mid0, gp_mid0, gb_mid0)
        left = left + home_cut(MID2, gb_mid2, gf_mid2, hb_mid2, hi_mid2, hr_mid2)
        left = left + home(IN1, gb_in1, gf_in1)
        left = left + home_cut(OUT1, gb_out1, gf_out1, hb_out1, hi_out1, hr_out1)
        left = left + home_cut(SC0, gb_sc, gf_sc, hb_sc, hi_sc, hr_sc)
        left = left + rest_home(1, REST0, rg0, rl0, rf0)
        left = left + table_home(3, 0, LATE_ROWS)
        left = left + home_cut(IN0, gb_in0, gf_in0, hb_in0, hi_in0, hr_in0)
        left = left + home_cut(MID0, gb_mid0, gf_mid0, hb_mid0, hi_mid0, hr_mid0)

        take(OUT3, hi_out3, hr_out3)
        take(MID2, hi_mid2, hr_mid2)
        take(OUT1, hi_out1, hr_out1)
        take(SC0, hi_sc, hr_sc)
        take(IN0, hi_in0, hr_in0)
        take(MID0, hi_mid0, hr_mid0)

        for mat, ready in (
            (IN0, hb_in0),
            (MID0, hb_mid0),
            (SC0, hb_sc),
            (OUT1, hb_out1),
            (MID2, hb_mid2),
            (OUT3, hb_out3),
        ):
            end_home_cut(mat, ready)
        for mat, gw in (
            (MID0, gw_mid0),
            (SC0, gw_sc),
            (OUT1, gw_out1),
            (IN1, gw_in1),
            (MID2, gw_mid2),
            (OUT3, gw_out3),
        ):
            end_shed(mat, gw)

        @pl.when(holds(IN0))
        def _():
            full_wait(gw_in0.at[pl.ds(0, 31)], gb_s.at[0])
            full_wait(fill.at[pl.ds(0, 8 * (4 * n - 1))], a_s.at[0])

        @pl.when(jnp.logical_not(holds(IN0)))
        def _():
            full_wait(gw_in0, gb_s.at[0])

        for i, mat, land in ((1, REST0, rl0), (2, REST2, rl2)):

            @pl.when((s == mat.row) & (d < 8))
            def _():
                full_wait(land, v_s.at[i])

        @pl.when((s == 0) & (d < 2))
        def _():
            full_wait(gvl.at[pl.ds(LATE_ROWS, TABLE_ROWS - LATE_ROWS)], v_s.at[0])
            full_wait(gvl.at[pl.ds(0, LATE_ROWS)], v_s.at[3])

        fill_up(nought, fill2, left, HOME_ROWS, gc_s)
        full_wait(fill2, gc_s)
        full_wait(fill, h_s)
        full_wait(out_w, gc_r)
        for slot in range(2):
            pltpu.make_async_copy(out_o.at[slot], out_o.at[slot], oo_r.at[slot]).wait()
            pltpu.make_async_copy(out_i.at[slot], out_i.at[slot], oi_r.at[slot]).wait()
        for slot in range(2):
            for kk in range(2):
                end_move(
                    planes.at[slot, pl.ds(2 * kk, 2)],
                    img_s.at[slot, kk],
                    (2 * k + slot, 2 * c + kk),
                )
            end_move(cot.at[slot], ct_s.at[slot], (2 * k + slot, 2 * c + s // 2))
        for j in range(2):
            end_move(obuf.at[j], oo_s.at[j], (2 * k + j, 2 * c + s // 2))
            end_move(ibuf.at[j], oi_s.at[j], (2 * k + j, 2 * c + s // 2))
        for q in range(4):
            here = u.at[q, pl.ds(2 * k, 2)]
            pltpu.make_async_copy(here, here, bs.at[10 + q]).wait()
        for ph in range(PHASES):
            end_send(ph)

    return kernel


def call_kernel(n, operands):
    chips = n // 2
    shard_rows = WSLOTS // (128 * n)
    fill_rows = max(shard_rows + 34 * n, 96 * (n - 1), 100 * n, 8 * (4 * n - 1), 16 * (2 * n - 1))

    def vm(*shape, dtype=F32):
        return pltpu.VMEM(shape, dtype)

    def low(*shape):
        return pltpu.VMEM(shape, BF16)

    dma = pltpu.SemaphoreType.DMA
    scratch = [
        vm(PHASES, 16, 128),
        vm(PHASES, 2, n, 16, 128),
        vm(2, 2, 8, 128),
        low(4, 4, PX, 128),
        low(4, PX, CIN),
        low(PX, CIN),
        low(2, PX, 256),
        vm(PX, 128),
        vm(4, PX, 128),
        vm(PX, 256),
        vm(PX, 512),
        vm(PX, 512),
        vm(PX, 128),
        vm(PX, 256),
        vm(PX, 512),
        vm(PX, 512),
        low(PX, 1152),
        low(PX, 1152),
        vm(2, PX, 256),
        vm(2, PX, 256),
        low(PX, 256),
        low(PX, 256),
        low(PX, 512),
        vm(PX, 512),
        vm(PX, 256),
        vm(PX, 256),
        vm(2, PX, 128),
        vm(2, PX, 256),
        vm(3, PX, 256),
        low(2, PX, 128),
        low(2, 4, PX, 128),
        low(PX, 512),
        low(PX, 512),
        vm(3, PX + 2 * SIDE, 128),
        vm(4, PX, 128),
        low(2, PX, 256),
        low(2, 4 * PX, 128),
        vm(shard_rows, 128),
        vm(128, 128),
        vm(fill_rows, 128),
        vm(HOME_ROWS, 128),
        vm(TABLE_ROWS, 128),
        low(2, 32, 16, 128),
        low(24, 48, 256),
        low(32, 16, 512),
        low(16, 16, 512),
        low(2, 32, 16, 128),
        low(24, 48, 256),
        low(16, 16, 512),
        vm(32, 128),
        vm(192, 128),
        vm(128, 128),
        vm(128, 128),
        vm(64, 128),
        vm(192, 128),
        vm(128, 128),
        low(2, 16, 128),
        low(2, 48, 256),
        low(2, 16, 512),
        low(2, 16, 512),
        low(2, 2, 16, 128),
        low(2, 48, 256),
        low(2, 16, 512),
        low(shard_rows // 32 + 2, 2, 16, 128),
        low(shard_rows // 192 + 2, 2, 48, 256),
        low(shard_rows // 128 + 2, 2, 16, 512),
        low(shard_rows // 128 + 2, 2, 16, 512),
        low(shard_rows // 192 + 2, 2, 48, 256),
        low(shard_rows // 128 + 2, 2, 16, 512),
        low(32, 16, 128),
        low(24, 48, 256),
        low(32, 16, 512),
        low(16, 16, 512),
        low(32, 16, 256),
        low(24, 48, 256),
        low(16, 16, 512),
        low(2, 2, 3, 48, 256),
        low(2, 2, 4, 16, 512),
        low(2, 2, 2, 16, 512),
        low(2, 2, 4, 16, 256),
        low(2, 2, 3, 48, 256),
        low(2, 2, 2, 16, 512),
        low(6, 48, 256),
        low(8, 16, 512),
        low(4, 16, 512),
        low(8, 16, 256),
        low(6, 48, 256),
        low(4, 16, 512),
        low(4 * chips, 2, 16, 128),
        low(chips, 2, 48, 256),
        low(chips, 2, 16, 512),
        low(chips, 2, 16, 512),
        low(chips, 2, 16, 256),
        low(chips, 2, 48, 256),
        low(chips, 2, 16, 512),
        vm(32, 128),
        vm(192, 128),
        vm(128, 128),
        vm(128, 128),
        vm(64, 128),
        vm(192, 128),
        vm(128, 128),
        vm(784, 128),
        vm(784, 128),
        vm(REST_PART, 128),
        vm(REST_PART, 128),
        vm(REST_PART, 128),
        vm(REST_PART, 128),
        vm(TABLE_ROWS, 128),
        vm(TABLE_ROWS, 128),
        vm(TABLE_ROWS, 128),
        low(2, 3, 48, 256),
        low(2, 3, 48, 256),
        low(2, 3, 48, 256),
        low(2, 3, 48, 256),
        low(2, 4, 16, 512),
        low(2, 4, 16, 512),
        low(2, 2, 16, 512),
        low(2, 2, 16, 512),
        low(2, 2, 16, 512),
        low(2, 2, 16, 512),
        low(2, 4, 16, 256),
        low(2, 4, 16, 256),
        low(2, 16, 128),
        low(shard_rows // 32 + 2, 2, 16, 128),
        low(2, 48, 256),
        low(shard_rows // 192 + 2, 2, 48, 256),
        low(2, 16, 512),
        low(shard_rows // 128 + 2, 2, 16, 512),
        low(2, 16, 512),
        low(shard_rows // 128 + 2, 2, 16, 512),
        low(2, 48, 256),
        low(shard_rows // 192 + 2, 2, 48, 256),
        low(2, 16, 512),
        low(shard_rows // 128 + 2, 2, 16, 512),
        vm(shard_rows, 128),
        vm(4 * PX, 128),
        low(2, 4, PX, 128),
        vm(2, 4 * PX, 128),
        low(16, 16, 128),
        vm(16, 128),
        low(16, 128),
        low(min(shard_rows // 16 + 2, 16), 16, 128),
        low(32, 16, 128),
        vm(16, 128),
        low(16, 128),
        low(min(shard_rows // 16 + 2, 32), 16, 128),
        vm(512, 128),
        low(16, 16, 128),
        vm(16, 128),
        low(16, 128),
        low(min(shard_rows // 16 + 2, 16), 16, 128),
        low(32, 16, 128),
        vm(16, 128),
        low(16, 128),
        low(min(shard_rows // 16 + 2, 32), 16, 128),
        vm(512, 128),
        dma((PHASES,)),
        dma((PHASES, 2)),
        dma((19,)),
        dma((19,)),
        dma((2, 2)),
        dma((4,)),
        dma((2,)),
        dma((2,)),
        dma((2,)),
        dma((2,)),
        dma((2,)),
        dma((2,)),
        dma,
        dma,
        dma((2,)),
        dma((11,)),
        dma((11,)),
        dma((11,)),
        dma((11,)),
        dma((11, 4)),
        dma((11,)),
        dma((11, 2)),
        dma((11,)),
        dma((11,)),
        dma,
        dma,
        dma((4,)),
        dma((4,)),
        dma((11,)),
        dma((11, 2)),
        dma((shard_rows // 32 + 2,)),
        dma((shard_rows // 192 + 2,)),
        dma((shard_rows // 128 + 2,)),
        dma((shard_rows // 128 + 2,)),
        dma((shard_rows // 192 + 2,)),
        dma((shard_rows // 128 + 2,)),
        dma((11,)),
    ]
    sds = jax.ShapeDtypeStruct
    outs = (
        sds((2, PX, 256), BF16),
        sds((2, 4 * PX, 128), BF16),
        sds((shard_rows, 128), F32),
    )
    vmem = pl.BlockSpec(memory_space=pltpu.VMEM)
    smem = pl.BlockSpec(memory_space=pltpu.SMEM)
    return pl.pallas_call(
        make_kernel(n),
        out_shape=outs,
        in_specs=[smem if i == 2 else vmem for i in range(len(operands))],
        out_specs=[vmem] * len(outs),
        scratch_shapes=scratch,
        compiler_params=pltpu.CompilerParams(
            collective_id=0, has_side_effects=True, vmem_limit_bytes=60 << 20
        ),
    )(*operands)


def per_device(images, cotangent, res_codes, section_weights):
    n = lax.axis_size("dp")
    out_o, out_i, out_w = call_kernel(
        n,
        (
            images.reshape(2, 4 * PX, 128),
            cotangent.reshape(2, PX, 256),
            res_codes,
            section_weights.reshape(-1, 128),
        ),
    )
    block_out = out_o.reshape(2, SIDE, SIDE, 256)
    input_grad = out_i.reshape(images.shape)
    return block_out, input_grad, out_w.reshape(section_weights.shape)


def solution(mesh):
    return jax.shard_map(
        per_device,
        mesh=mesh,
        in_specs=(
            P("dp", None, None, "section"),
            P("dp", None, None, "section"),
            P("dp"),
            P("section", "dp"),
        ),
        out_specs=(
            P("dp", None, None, "section"),
            P("dp", None, None, "section"),
            P("section", "dp"),
        ),
        check_vma=False,
    )
```

```python
import jax
import jax.numpy as jnp
from jax import lax
from jax.experimental import pallas as pl
from jax.experimental.pallas import tpu as pltpu
from jax.sharding import PartitionSpec as P

CIN = 512
COUT = 1024
CMID = 256
CSQ = 128
SIDE = 16
PX = SIDE * SIDE
HALF = 128
WSLOTS = 1351680
EPS = 1e-05
HIGH = lax.Precision.HIGHEST
MESH = pl.DeviceIdType.MESH
F32 = jnp.float32
BF16 = jnp.bfloat16
PHASES = 14
ROWS = (
    (3, 0),
    (4, 0),
    (2, 2),
    (16, 0),
    (2, 0),
    (4, 0),
    (2, 2),
    (8, 0),
    (8, 0),
    (10, 2),
    (2, 0),
    (16, 0),
    (10, 2),
    (2, 0),
)


class Matrix:
    def __init__(self, index, row, start, blocks, pieces, rows, first, step, split="columns"):
        self.index = index
        self.row = row
        self.start = start
        self.blocks = blocks
        self.pieces = pieces
        self.rows = rows
        self.first = first
        self.step = step
        self.split = split
        self.flat = blocks * rows
        self.width = 128 * (blocks // 2 if split == "columns" else blocks)


IN0 = Matrix(0, 0, 0, 2, 8, 16, 0, 1)
MID0 = Matrix(1, 0, 1028, 4, 6, 48, 0, 1)
REST0 = Matrix(2, 0, 5636, 1, 8, 25, 0, 1, split="none")
SC0 = Matrix(3, 0, 6418, 8, 8, 16, 0, 1)
OUT1 = Matrix(4, 1, 0, 8, 4, 16, 1, 2)
IN1 = Matrix(5, 1, 2064, 2, 8, 16, 0, 1, split="rows")
MID2 = Matrix(6, 2, 0, 4, 6, 48, 2, 1)
REST2 = Matrix(7, 2, 4608, 1, 8, 25, 0, 1, split="none")
OUT3 = Matrix(8, 3, 0, 8, 4, 16, 0, 2)
SQ0 = Matrix(2, 0, 5644, 1, 4, 16, 0, 2, split="none")
EX0 = Matrix(9, 0, 5902, 1, 8, 16, 0, 1, split="none")
SQ2 = Matrix(7, 2, 4616, 1, 4, 16, 1, 2, split="none")
EX2 = Matrix(10, 2, 4874, 1, 8, 16, 0, 1, split="none")
CUT = (IN0, MID0, SC0, OUT1, MID2, OUT3)
USED = (10530, 4116, 5390, 2064)
REST_ROWS = 782
HOME_ROWS = 1152
REST_PART = 97
AT_SQ, AT_GSQ, AT_BSQ, AT_EX, AT_BEX = 8, 264, 265, 266, 778
TABLE = {
    (0, "g_in"): (0, 1024, 1),
    (0, "b_in"): (2, 1026, 1),
    (0, "g_mid"): (4, 5636, 2),
    (0, "b_mid"): (8, 5640, 2),
    (0, "g_sc"): (12, 10514, 4),
    (0, "b_sc"): (20, 10522, 4),
    (1, "g_out"): (34, 2048, 4),
    (1, "b_out"): (42, 2056, 4),
    (1, "g_in"): (50, 4112, 1),
    (1, "b_in"): (52, 4114, 1),
    (3, "g_out"): (54, 2048, 4),
    (3, "b_out"): (62, 2056, 4),
    (2, "g_mid"): (70, 4608, 2),
    (2, "b_mid"): (74, 4612, 2),
}
TABLE_ROWS = 84
LATE_ROWS = 12
SECTION_ROWS = {0: (0, 34), 1: (34, 20), 2: (70, 14), 3: (54, 16)}
AT_MID = {0: 4, 2: 70}
AT_SMALL = {0: 28, 2: 78}
RANGES = (
    (0, 1024, 4, 0),
    (0, 5636, 8, 4),
    (0, 10514, 16, 12),
    (0, 5900, 2, 28),
    (0, 6414, 4, 30),
    (1, 2048, 16, 34),
    (1, 4112, 4, 50),
    (2, 4608, 8, 70),
    (2, 4872, 2, 78),
    (2, 5386, 4, 80),
    (3, 2048, 16, 54),
)


def dot(a, b):
    return lax.dot_general(a, b, (((1,), (0,)), ((), ())), preferred_element_type=F32)


def dot_rt(a, b):
    return lax.dot_general(a, b, (((1,), (1,)), ((), ())), preferred_element_type=F32)


def dot_lt(a, b):
    return lax.dot_general(a, b, (((0,), (0,)), ((), ())), preferred_element_type=F32)


def dot_hi(a, b, dims=((1,), (0,))):
    return lax.dot_general(a, b, (dims, ((), ())), precision=HIGH, preferred_element_type=F32)


def sigmoid(v):
    return 0.5 + 0.5 * jnp.tanh(0.5 * v)


def fold8(x):
    return jnp.sum(x.reshape(x.shape[0] // 8, 8, x.shape[1]), axis=0)


def lanes(x, count):
    return jnp.concatenate([x] * count, axis=1) if count > 1 else x


def make_kernel(n):
    chips = n // 2
    shard_rows = WSLOTS // (128 * n)
    fill_rows = max(shard_rows + 34 * n, 96 * (n - 1), 100 * n, 8 * (4 * n - 1), 16 * (2 * n - 1))

    def kernel(
        img,
        cot,
        codes,
        shard,
        out_o,
        out_i,
        out_w,
        snd,
        rcv,
        side_t,
        u,
        um,
        pool,
        ctb,
        mref,
        z1,
        z2,
        zs,
        z3,
        z4,
        z5,
        z6,
        v3,
        cols1,
        cols2,
        rr1,
        rr2,
        a1,
        a2,
        y1,
        dv6,
        dbuf,
        spb,
        pz,
        pda,
        pdp,
        dz4,
        dz1,
        dz3,
        dzs,
        ep,
        dh,
        obuf,
        ibuf,
        sround,
        nought,
        fill,
        fill2,
        table,
        w_in0,
        w_mid0,
        w_sc,
        w_out1,
        w_in1,
        w_mid2,
        w_out3,
        ln_in0,
        ln_mid0,
        ln_sc,
        ln_out1,
        ln_in1,
        ln_mid2,
        ln_out3,
        st_in0,
        st_mid0,
        st_sc,
        st_out1,
        st_in1,
        st_mid2,
        st_out3,
        cu_in0,
        cu_mid0,
        cu_sc,
        cu_out1,
        cu_mid2,
        cu_out3,
        gw_in0,
        gw_mid0,
        gw_sc,
        gw_out1,
        gw_in1,
        gw_mid2,
        gw_out3,
        ga_mid0,
        ga_sc,
        ga_out1,
        ga_in1,
        ga_mid2,
        ga_out3,
        gp_mid0,
        gp_sc,
        gp_out1,
        gp_in1,
        gp_mid2,
        gp_out3,
        gb_in0,
        gb_mid0,
        gb_sc,
        gb_out1,
        gb_in1,
        gb_mid2,
        gb_out3,
        gf_in0,
        gf_mid0,
        gf_sc,
        gf_out1,
        gf_in1,
        gf_mid2,
        gf_out3,
        rg0,
        rg2,
        rl0,
        rl2,
        rf0,
        rf2,
        gvt,
        gvl,
        gvs,
        gd_mid0,
        gt_mid0,
        gd_mid2,
        gt_mid2,
        gd_sc,
        gt_sc,
        gd_out1,
        gt_out1,
        gd_out3,
        gt_out3,
        gd_in1,
        gt_in1,
        hb_in0,
        hi_in0,
        hb_mid0,
        hi_mid0,
        hb_sc,
        hi_sc,
        hb_out1,
        hi_out1,
        hb_mid2,
        hi_mid2,
        hb_out3,
        hi_out3,
        fill3,
        pixels,
        planes,
        merged,
        w_sq0,
        ln_sq0,
        st_sq0,
        cu_sq0,
        w_ex0,
        ln_ex0,
        st_ex0,
        cu_ex0,
        ex0,
        w_sq2,
        ln_sq2,
        st_sq2,
        cu_sq2,
        w_ex2,
        ln_ex2,
        st_ex2,
        cu_ex2,
        ex2,
        spb2,
        d1,
        d4,
        ssem,
        rsem,
        bs,
        br,
        img_s,
        img_r,
        ct_s,
        ct_r,
        oo_s,
        oo_r,
        oi_s,
        oi_r,
        h_s,
        t_s,
        t_r,
        h_r,
        a_s,
        c_r,
        f_s,
        q_r,
        ga_s,
        ga_r,
        gb_s,
        gb_r,
        gc_s,
        gc_r,
        v_s,
        v_r,
        gd_s,
        gd_r,
        hr_in0,
        hr_mid0,
        hr_sc,
        hr_out1,
        hr_mid2,
        hr_out3,
        hs_s,
    ):
        s = lax.axis_index("section")
        d = lax.axis_index("dp")
        c = d // 2
        k = d % 2
        m = s % 2
        g = (s // 2) * chips + c

        def peer(o, kk):
            gg = g ^ o
            return ((gg // chips) * 2 + m, 2 * (gg % chips) + kk)

        order = sorted(range(1, n), key=lambda o: (o % chips) + o // chips, reverse=True)

        nought[...] = jnp.zeros(nought.shape, F32)
        barrier = pltpu.get_barrier_semaphore()
        me = s * n + d
        beside_x = s + 1 - 2 * (s % 2)
        beside_y = lax.rem(s + 2, 4)

        def greet(i, _):
            e = lax.rem(me + i, 4 * n)
            pl.semaphore_signal(barrier, inc=1, device_id=(e // n, e % n), device_id_type=MESH)
            return 0

        lax.fori_loop(1, 4 * n, greet, 0)
        sround[...] = shard[...].astype(BF16).astype(F32)

        for slot in range(2):

            def widen(i, _):
                rows = pl.ds(pl.multiple_of(i * 128, 128), 128)
                pixels[rows, :] = img[slot, rows, :].astype(F32)
                return 0

            lax.fori_loop(0, 8, widen, 0)

            def split(r, _):
                for p in range(4):
                    at = (2 * r + p // 2) * 2 * SIDE + p % 2
                    x = pixels[pl.ds(at, SIDE, stride=2), :]
                    planes[slot, p, pl.ds(pl.multiple_of(r * SIDE, SIDE), SIDE), :] = x.astype(BF16)
                return 0

            lax.fori_loop(0, SIDE, split, 0)
        pl.semaphore_wait(barrier, 4 * n - 1)

        def to_twin(i, src, dst):
            return pltpu.make_async_remote_copy(
                src, dst, bs.at[i], br.at[i], device_id=(s, 2 * c + 1 - k), device_id_type=MESH
            )

        def move(src, dst, s_sem, r_sem, dev):
            own = (dev[0] == s) & (dev[1] == d)

            @pl.when(own)
            def _():
                pltpu.make_async_copy(src, dst, r_sem).start()

            @pl.when(jnp.logical_not(own))
            def _():
                pltpu.make_async_remote_copy(
                    src, dst, s_sem, r_sem, device_id=dev, device_id_type=MESH
                ).start()

        def end_move(src, s_sem, dev):
            own = (dev[0] == s) & (dev[1] == d)

            @pl.when(jnp.logical_not(own))
            def _():
                pltpu.make_async_copy(src, src, s_sem).wait()

        def is_self(dev):
            return (dev[0] == s) & (dev[1] == d)

        def move_rows(src, src_at, dst, dst_at, count, full, s_sem, r_sem, dev):
            def go(size, at):
                move(
                    src.at[pl.ds(src_at + at, size)],
                    dst.at[pl.ds(dst_at + at, size)],
                    s_sem,
                    r_sem,
                    dev,
                )

            def chunks(size, start, many):
                def one(i, _):
                    go(size, start + i * size)
                    return 0

                lax.fori_loop(0, many, one, 0)

            if full > 1:

                @pl.when(count == full)
                def _():
                    go(full, 0)

                @pl.when(count < full)
                def _():
                    if full > 16:
                        chunks(16, 0, count // 16)
                        chunks(1, (count // 16) * 16, count % 16)
                    else:
                        chunks(1, 0, count)

            else:
                chunks(1, 0, count)
            return jnp.where(is_self(dev), 0, count)

        def fill_up(src, dst, first, last, sem):
            def chunks(size, start, many):
                def one(i, _):
                    pltpu.make_async_copy(
                        src.at[pl.ds(0, size)], dst.at[pl.ds(start + i * size, size)], sem
                    ).start()
                    return 0

                lax.fori_loop(0, many, one, 0)

            count = last - first
            chunks(128, first, count // 128)
            chunks(16, first + (count // 128) * 128, count % 128 // 16)
            chunks(1, first + (count // 16) * 16, count % 16)

        used = jnp.where(
            s == 0, USED[0], jnp.where(s == 1, USED[1], jnp.where(s == 2, USED[2], USED[3]))
        )

        mine_from = d * shard_rows
        mine_to = mine_from + shard_rows

        def cut(mat, land, stage, base):
            if mat.split == "none":
                stage[...] = land[pl.ds(base, mat.flat), :].astype(BF16)
                return
            for j in range(mat.blocks):
                for h in range(2):
                    if mat.split == "rows":
                        x = land[pl.ds(base + h * mat.flat + j, mat.rows, stride=mat.blocks), :]
                        stage[h, j] = x.astype(BF16)
                    elif j // (mat.blocks // 2) == h:
                        x = land[pl.ds(base + j, mat.rows, stride=mat.blocks), :]
                        at = 128 * (j % (mat.blocks // 2))
                        stage[h, :, at : at + 128] = x.astype(BF16)

        def holds(mat):
            i = d - mat.first
            inside = (i >= 0) & (i < mat.step * mat.pieces)
            return inside & (i % mat.step == 0) if mat.step > 1 else inside

        def piece(mat):
            return s * mat.pieces + jnp.maximum(d - mat.first, 0) // mat.step

        def scatter_cut(mat, land, stage, ready, part=0, parts=1):
            first = jnp.maximum(mine_from - mat.start, 0) // mat.flat
            last = (jnp.maximum(mine_to - mat.start, 0) + mat.flat - 1) // mat.flat
            last = jnp.minimum(last, 4 * mat.pieces)

            def one(p, sent):
                start = mat.start + p * mat.flat
                lo = jnp.maximum(start, mine_from)
                count = jnp.minimum(start + mat.flat, mine_to) - lo
                dev = (p // mat.pieces, mat.first + mat.step * (p % mat.pieces))

                def in_one():
                    to = ready.at[p - first]
                    cut(mat, sround, to, lo - mine_from)
                    move(to, stage, h_s, h_r.at[mat.index], dev)
                    return jnp.where(is_self(dev), 0, mat.flat // 2)

                def in_rows():
                    return move_rows(
                        sround,
                        lo - mine_from,
                        land,
                        lo - start,
                        count,
                        mat.flat,
                        h_s,
                        h_r.at[mat.index],
                        dev,
                    )

                return sent + lax.cond(count == mat.flat, in_one, in_rows)

            step = (jnp.maximum(last - first, 0) + parts - 1) // parts
            begin = first + part * step
            end = jnp.minimum(last, begin + step)
            return lax.fori_loop(begin, end, one, jnp.int32(0))

        def stage_ready(mat, land, stage):
            start = mat.start + piece(mat) * mat.flat
            whole = start // shard_rows == (start + mat.flat - 1) // shard_rows

            @pl.when(whole)
            def _():
                full_wait(stage, h_r.at[mat.index])

            @pl.when(jnp.logical_not(whole))
            def _():
                full_wait(land, h_r.at[mat.index])
                cut(mat, land, stage, 0)

        def scatter_pieces(mat, land, part=0, parts=1):
            total = mat.pieces * 4 * (2 if mat.split == "rows" else 1)
            first = jnp.maximum(mine_from - mat.start, 0) // mat.flat
            last = (jnp.maximum(mine_to - mat.start, 0) + mat.flat - 1) // mat.flat

            def one(p, sent):
                start = mat.start + p * mat.flat
                lo = jnp.maximum(start, mine_from)
                count = jnp.minimum(start + mat.flat, mine_to) - lo
                h = p // (4 * mat.pieces)
                q = p % (4 * mat.pieces)
                dev = (q // mat.pieces, mat.first + mat.step * (q % mat.pieces))
                return sent + move_rows(
                    sround,
                    lo - mine_from,
                    land,
                    h * mat.flat + lo - start,
                    count,
                    mat.flat,
                    h_s,
                    h_r.at[mat.index],
                    dev,
                )

            last = jnp.minimum(last, total)
            step = (jnp.maximum(last - first, 0) + parts - 1) // parts
            begin = first + part * step
            end = jnp.minimum(last, begin + step)
            return lax.fori_loop(begin, end, one, jnp.int32(0))

        def scatter_table(start, rows, at):
            lo = jnp.maximum(start, mine_from)
            count = jnp.maximum(jnp.minimum(start + rows, mine_to) - lo, 0)

            def one(i, sent):
                e = lax.rem(d + i, n)
                return sent + move_rows(
                    sround,
                    lo - mine_from,
                    table,
                    at + lo - start,
                    count,
                    rows,
                    h_s,
                    t_r.at[0],
                    (s, e),
                )

            return lax.fori_loop(0, jnp.where(count > 0, n, 0), one, jnp.int32(0))

        def pass_table():
            for r, (at, many) in SECTION_ROWS.items():

                @pl.when(s == r)
                def _():
                    here = table.at[pl.ds(at, many)]
                    full_wait(here, t_r.at[0])
                    for i in range(1, 4):
                        pltpu.make_async_remote_copy(
                            here,
                            here,
                            t_s,
                            t_r.at[1],
                            device_id=(lax.rem(s + i, 4), d),
                            device_id_type=MESH,
                        ).start()

        def table_arrived():
            for r in range(4):
                rest = TABLE_ROWS - SECTION_ROWS.get(r, (0, 0))[1]

                @pl.when(s == r)
                def _():
                    full_wait(table.at[pl.ds(0, rest)], t_r.at[1])

        def end_table():
            for r, (_, many) in SECTION_ROWS.items():

                @pl.when(s == r)
                def _():
                    full_wait(fill.at[pl.ds(0, 3 * many)], t_s)

        def full_wait(ref, sem):
            pltpu.make_async_copy(ref, ref, sem).wait()

        def when_row(r, body):
            return lax.cond(s == r, body, lambda: jnp.int32(0))

        sent = when_row(
            0,
            lambda: scatter_cut(MID0, ln_mid0, st_mid0, cu_mid0) + scatter_cut(IN0, ln_in0, st_in0, cu_in0),
        )

        for slot in range(2):
            for kk in range(2):
                move(
                    planes.at[slot, pl.ds(2 * kk, 2)],
                    u.at[s, pl.ds(2 * kk, 2)],
                    img_s.at[slot, kk],
                    img_r.at[s],
                    (2 * k + slot, 2 * c + kk),
                )
        for slot in range(2):
            width = (SIDE - 2 * codes[slot]).astype(F32)
            side_t[k, slot] = jnp.full((8, 128), width, F32)
        side_copy = to_twin(0, side_t.at[k], side_t.at[k])
        side_copy.start()
        snd[...] = jnp.zeros(snd.shape, F32)

        def tables(r):
            count = jnp.int32(0)
            for row_of, start, rows, at in RANGES:
                if row_of == r:
                    count = count + scatter_table(start, rows, at)
            return count

        sent = sent + when_row(0, lambda: tables(0) + scatter_cut(SC0, ln_sc, st_sc, cu_sc))
        sent = sent + when_row(1, lambda: scatter_cut(OUT1, ln_out1, st_out1, cu_out1) + tables(1))
        sent = sent + when_row(2, lambda: tables(2))
        sent = sent + when_row(3, lambda: tables(3))

        def scatter_some(sent, part, parts):
            sent = sent + when_row(2, lambda: scatter_cut(MID2, ln_mid2, st_mid2, cu_mid2, part, parts))
            return sent + when_row(3, lambda: scatter_cut(OUT3, ln_out3, st_out3, cu_out3, part, parts))

        def scatter_early(sent):
            sent = sent + when_row(1, lambda: scatter_pieces(IN1, ln_in1))
            return scatter_some(sent, 1, 3)

        def scatter_late(sent):
            sent = scatter_some(sent, 2, 3)
            sent = sent + when_row(
                2,
                lambda: scatter_cut(SQ2, ln_sq2, st_sq2, cu_sq2)
                + scatter_cut(EX2, ln_ex2, st_ex2, cu_ex2),
            )
            fill_up(nought, fill, sent, fill_rows, h_s)

        sent = scatter_some(sent, 0, 3)
        sent = sent + when_row(
            0,
            lambda: scatter_cut(SQ0, ln_sq0, st_sq0, cu_sq0) + scatter_cut(EX0, ln_ex0, st_ex0, cu_ex0),
        )

        def spread(mat, land, stage, whole):
            @pl.when(holds(mat))
            def _():
                if mat.split == "rows":
                    full_wait(land, h_r.at[mat.index])
                    cut(mat, land, stage, 0)
                else:
                    stage_ready(mat, land, stage)
                p = piece(mat)

                def one(i, _):
                    e = lax.rem(d + i, n)
                    h = e % 2
                    dst = whole.at[:, p] if mat.split == "rows" else whole.at[p]
                    move(stage.at[h], dst, a_s.at[mat.index], c_r.at[mat.index], (s, e))
                    return 0

                lax.fori_loop(0, n, one, 0)

        def quarters(mat, whole, first, many, part=None):
            if part is None:
                span = pl.ds(first * mat.pieces, many * mat.pieces)
            else:
                half = mat.pieces // 2
                span = pl.ds(first * mat.pieces + part * half, half)
            return whole.at[:, span] if mat.split == "rows" else whole.at[span]

        def hand(mat, here, i, to):
            pltpu.make_async_remote_copy(
                here,
                here,
                f_s.at[mat.index],
                q_r.at[mat.index, i],
                device_id=(to, d),
                device_id_type=MESH,
            ).start()

        def pass_on(mat, whole):
            here = quarters(mat, whole, s, 1)
            full_wait(here, c_r.at[mat.index])
            hand(mat, here, 0, beside_x)
            hand(mat, here, 1, beside_y)

        def pass_all(mat, whole):
            here = quarters(mat, whole, s, 1)
            full_wait(here, c_r.at[mat.index])
            for i, to in enumerate((beside_x, beside_y, 3 - s)):
                hand(mat, here, i, to)

        def all_arrived(mat, whole):
            for i, q in enumerate((beside_x, beside_y, 3 - s)):
                full_wait(quarters(mat, whole, q, 1), q_r.at[mat.index, i])

        def pass_far(mat, whole):
            full_wait(quarters(mat, whole, beside_x, 1), q_r.at[mat.index, 0])
            hand(mat, quarters(mat, whole, beside_x, 1, 0), 2, beside_y)
            full_wait(quarters(mat, whole, beside_y, 1), q_r.at[mat.index, 1])
            hand(mat, quarters(mat, whole, beside_y, 1, 1), 3, beside_x)

        def arrived(mat, whole):
            far = 3 - s
            for i in range(2):
                full_wait(quarters(mat, whole, far, 1, i), q_r.at[mat.index, 2 + i])

        def end_spread(mat, whole):
            @pl.when(holds(mat))
            def _():
                rows = mat.rows * mat.width // 256
                full_wait(fill.at[pl.ds(0, (n - 1) * rows)], a_s.at[mat.index])

            full_wait(quarters(mat, whole, 0, 3), f_s.at[mat.index])

        def spread_small(mat, land, stage, whole):
            @pl.when(holds(mat))
            def _():
                stage_ready(mat, land, stage)
                p = piece(mat)

                def one(i, _):
                    e = lax.rem(s * chips + c + i, 4 * chips)
                    move(
                        stage,
                        whole.at[p],
                        a_s.at[mat.index],
                        c_r.at[mat.index],
                        (e // chips, 2 * (e % chips)),
                    )
                    return 0

                lax.fori_loop(0, 4 * chips, one, 0)

        def share_small(mat, whole, i):
            @pl.when(k == 0)
            def _():
                full_wait(whole, c_r.at[mat.index])
                to_twin(i, whole, whole).start()

        def small_arrived(whole, i):
            @pl.when(k == 1)
            def _():
                to_twin(i, whole, whole).wait_recv()

        def end_small(mat, whole, i):
            @pl.when(k == 0)
            def _():
                to_twin(i, whole, whole).wait_send()

            for kk in range(2):

                @pl.when(holds(mat) & (k == kk))
                def _():
                    rows = (4 * chips - 1 + kk) * mat.flat // 2
                    full_wait(fill.at[pl.ds(0, rows)], a_s.at[mat.index])

        @pl.when(holds(IN0))
        def _():
            stage_ready(IN0, ln_in0, st_in0)

            def one(i, _):
                e = lax.rem(me + i, 4 * n)
                h = e % 2
                move(
                    st_in0.at[h],
                    w_in0.at[h, s * 8 + d],
                    a_s.at[0],
                    c_r.at[0],
                    (e // n, e % n),
                )
                return 0

            lax.fori_loop(0, 4 * n, one, 0)

        def whole_rows():
            count = jnp.int32(0)
            for mat in CUT:
                low, high = whole_range(mat)
                count = count + jnp.where(s == mat.row, (high - low) * mat.flat, 0)
            return count

        def part_of(mat, ref, quarter, part):
            half = mat.pieces // 2
            return ref.at[pl.ds(quarter * mat.pieces + part * half, half)]

        def shed(mat, gw, land):
            for part, to in enumerate((beside_x, beside_y)):
                for i, quarter in enumerate((to, 3 - s)):
                    pltpu.make_async_remote_copy(
                        part_of(mat, gw, quarter, part),
                        land.at[part, i],
                        ga_s.at[mat.index],
                        ga_r.at[mat.index, part],
                        device_id=(to, d),
                        device_id_type=MESH,
                    ).start()

        def shed_mid(mat, gw, land, add, land3):
            half = mat.pieces // 2
            for part, to in enumerate((beside_y, beside_x)):
                full_wait(land.at[part], ga_r.at[mat.index, part])
                base = to * mat.pieces + part * half

                def one(i, _):
                    x = gw[base + i].astype(F32) + land[part, 1, i].astype(F32)
                    add[part, i] = x.astype(BF16)
                    return 0

                lax.fori_loop(0, half, one, 0)
                pltpu.make_async_remote_copy(
                    add.at[part],
                    land3.at[part],
                    gd_s.at[mat.index],
                    gd_r.at[mat.index, part],
                    device_id=(to, d),
                    device_id_type=MESH,
                ).start()

        def shed_more(mat, gw, land, land3, part_sum, land2):
            half = mat.pieces // 2
            for part in range(2):
                full_wait(land3.at[part], gd_r.at[mat.index, part])

                def one(j, _):
                    i = part * half + j
                    x = gw[s * mat.pieces + i].astype(F32) + land[part, 0, j].astype(F32)
                    part_sum[i] = (x + land3[part, j].astype(F32)).astype(BF16)
                    move(
                        part_sum.at[i],
                        land2.at[c, k],
                        gb_s.at[mat.index],
                        gb_r.at[mat.index],
                        (s, mat.first + mat.step * i),
                    )
                    return 0

                lax.fori_loop(0, half, one, 0)

        def home_rows(src, src_at, start, rows, limit, r, active):
            left = jnp.int32(0)
            for i in range((rows + shard_rows - 2) // shard_rows + 1):
                owner = start // shard_rows + i
                lo = jnp.maximum(start, owner * shard_rows)
                hi = jnp.minimum(jnp.minimum(start + rows, limit), (owner + 1) * shard_rows)
                count = jnp.where(active, jnp.maximum(hi - lo, 0), 0)
                owner = jnp.minimum(owner, n - 1)

                def go():
                    return move_rows(
                        src,
                        src_at + lo - start,
                        out_w,
                        lo - owner * shard_rows,
                        count,
                        rows,
                        gc_s,
                        gc_r,
                        (r, owner),
                    )

                left = left + lax.cond(count > 0, go, lambda: jnp.int32(0))
            return left

        def home(mat, land2, flat):
            @pl.when(holds(mat))
            def _():
                full_wait(land2, gb_r.at[mat.index])
                for h in range(2):
                    x = jnp.sum(land2[:, h].astype(F32), axis=0)
                    for j in range(mat.width // 128):
                        if mat.split == "rows":
                            at = h * mat.flat + j
                        else:
                            at = h * (mat.blocks // 2) + j
                        flat[pl.ds(at, mat.rows, stride=mat.blocks), :] = x[:, 128 * j : 128 * (j + 1)]

            p = piece(mat)
            left = home_rows(
                flat, 0, mat.start + p * mat.flat, mat.flat, USED[mat.row], mat.row, holds(mat)
            )
            if mat.split == "rows":
                p = p + 4 * mat.pieces
                left = left + home_rows(
                    flat,
                    mat.flat,
                    mat.start + p * mat.flat,
                    mat.flat,
                    USED[mat.row],
                    mat.row,
                    holds(mat),
                )
            return left

        def first_piece(mat, owner):
            return jnp.maximum(owner * shard_rows - mat.start, 0) // mat.flat

        def home_whole(mat):
            start = mat.start + piece(mat) * mat.flat
            return start, start // shard_rows == (start + mat.flat - 1) // shard_rows

        def home_cut(mat, land2, flat, ready, inbox, in_sem, turn=None):
            start, whole = home_whole(mat)
            owner = jnp.minimum(start // shard_rows, n - 1)
            held = holds(mat)
            if turn is not None:
                held = held & ((c < chips // 2) if turn == 0 else (c >= chips // 2))

            @pl.when(held)
            def _():
                full_wait(land2, gb_r.at[mat.index])

            @pl.when(held & whole)
            def _():
                for h in range(2):
                    ready[h] = jnp.sum(land2[:, h].astype(F32), axis=0).astype(BF16)
                slot = piece(mat) - first_piece(mat, owner)
                move(ready, inbox.at[slot], hs_s.at[mat.index], in_sem.at[slot], (mat.row, owner))

            @pl.when(held & jnp.logical_not(whole))
            def _():
                for h in range(2):
                    x = jnp.sum(land2[:, h].astype(F32), axis=0)
                    for j in range(mat.width // 128):
                        at = h * (mat.blocks // 2) + j
                        flat[pl.ds(at, mat.rows, stride=mat.blocks), :] = x[:, 128 * j : 128 * (j + 1)]

            return home_rows(
                flat,
                0,
                start,
                mat.flat,
                USED[mat.row],
                mat.row,
                held & jnp.logical_not(whole),
            )

        def end_home_cut(mat, ready):
            start, whole = home_whole(mat)
            away = (s != mat.row) | (d != start // shard_rows)

            @pl.when(holds(mat) & whole & away)
            def _():
                full_wait(ready, hs_s.at[mat.index])

        def whole_range(mat):
            low = (jnp.maximum(mine_from - mat.start, 0) + mat.flat - 1) // mat.flat
            high = jnp.minimum(jnp.maximum(mine_to - mat.start, 0) // mat.flat, 4 * mat.pieces)
            return low, jnp.maximum(high, low)

        def take(mat, inbox, in_sem):
            @pl.when(s == mat.row)
            def _():
                low, high = whole_range(mat)
                first = first_piece(mat, d)

                def one(p, _):
                    slot = p - first
                    full_wait(inbox.at[slot], in_sem.at[slot])
                    at = mat.start + p * mat.flat - mine_from
                    for h in range(2):
                        for j in range(mat.width // 128):
                            x = inbox[slot, h, :, 128 * j : 128 * (j + 1)].astype(F32)
                            row_at = at + h * (mat.blocks // 2) + j
                            out_w[pl.ds(row_at, mat.rows, stride=mat.blocks), :] = x
                    return 0

                lax.fori_loop(low, high, one, 0)

        def end_shed(mat, gw):
            full_wait(gw.at[pl.ds(0, 2 * mat.pieces)], ga_s.at[mat.index])
            full_wait(gw.at[pl.ds(0, mat.pieces)], gd_s.at[mat.index])

            @pl.when(holds(mat))
            def _():
                full_wait(gw.at[pl.ds(0, mat.pieces - 1)], gb_s.at[mat.index])

            @pl.when(jnp.logical_not(holds(mat)))
            def _():
                full_wait(gw.at[pl.ds(0, mat.pieces)], gb_s.at[mat.index])

        def rest_meet(i, mat, rg, land):
            @pl.when((s == mat.row) & (d < 8))
            def _():
                pltpu.make_async_remote_copy(
                    rg.at[pl.ds(AT_SQ + REST_PART * d, REST_PART)],
                    land,
                    v_s.at[i],
                    v_r.at[i],
                    device_id=(s + 1, d),
                    device_id_type=MESH,
                ).start()

        def rest_home(i, mat, rg, land, flat):
            active = (s == mat.row + 1) & (d < 8)
            at = AT_SQ + REST_PART * jnp.minimum(d, 7)

            @pl.when(active)
            def _():
                full_wait(land, v_r.at[i])
                flat[...] = rg[pl.ds(at, REST_PART), :] + land[...]

            return home_rows(
                flat, 0, mat.start + at, REST_PART, mat.start + REST_ROWS, mat.row, active
            )

        def table_meet(i, first, rows):
            @pl.when((s == 0) & (d < 2))
            def _():
                pltpu.make_async_remote_copy(
                    gvt.at[pl.ds(first, rows)],
                    gvl.at[pl.ds(first, rows)],
                    v_s.at[i],
                    v_r.at[i],
                    device_id=(s + 1, d),
                    device_id_type=MESH,
                ).start()

        def table_home(i, first, rows):
            active = (s == 1) & (d < 2)

            @pl.when(active)
            def _():
                span = pl.ds(first, rows)
                full_wait(gvl.at[span], v_r.at[i])
                gvs[first : first + rows, :] = gvt[first : first + rows, :] + gvl[first : first + rows, :]

            left = jnp.int32(0)
            for (r, _), (at, start, many) in TABLE.items():
                if first <= at < first + rows:
                    left = left + home_rows(
                        gvs,
                        at + many * k,
                        start + many * k,
                        many,
                        start + 2 * many,
                        r,
                        active,
                    )
            return left

        def put(ph, base, value):
            for j in range(value.shape[1] // 128):
                snd[ph, base + j : base + j + 1, :] = value[:, 128 * j : 128 * (j + 1)]

        def send(ph):
            mine, theirs = ROWS[ph]

            def to(o, kk, rows):
                pltpu.make_async_remote_copy(
                    snd.at[ph, pl.ds(0, rows)],
                    rcv.at[ph, k, o, pl.ds(0, rows)],
                    ssem.at[ph],
                    rsem.at[ph, k],
                    device_id=peer(o, kk),
                    device_id_type=MESH,
                ).start()
                return 0

            if n > 8:
                lax.fori_loop(1, n, lambda o, _: to(o, k, mine), 0)
                if theirs:
                    lax.fori_loop(0, n, lambda o, _: to(o, 1 - k, theirs), 0)
            else:
                for o in order:
                    to(o, k, mine)
                    if theirs:
                        to(o, 1 - k, theirs)
                if theirs:
                    to(0, 1 - k, theirs)
            rcv[ph, k, 0] = snd[ph]

        def receive(ph):
            mine, theirs = ROWS[ph]
            full_wait(rcv.at[ph, k, pl.ds(1, n - 1), pl.ds(0, mine)], rsem.at[ph, k])
            if theirs:
                full_wait(rcv.at[ph, 1 - k, :, pl.ds(0, theirs)], rsem.at[ph, 1 - k])

        def end_send(ph):
            mine, theirs = ROWS[ph]
            full_wait(fill.at[pl.ds(0, (n - 1) * mine + n * theirs)], ssem.at[ph])

        def totals(ph):
            return jnp.sum(rcv[ph, k, :, 0 : -(-ROWS[ph][0] // 8) * 8, :], axis=0)

        def row(total, base, width):
            return jnp.concatenate(
                [total[base + j : base + j + 1, :] for j in range(width // 128)], axis=1
            )

        def across(ph, h, base, width):
            return jnp.concatenate(
                [rcv[ph, h, :, base + j, :] for j in range(width // 128)], axis=1
            )

        def rows_of(ref, at, many):
            return jnp.concatenate([ref[pl.ds(at + j, 1), :] for j in range(many)], axis=1)

        def vrow(key):
            at, _, many = TABLE[key]
            return rows_of(table, at + many * k, many)

        def set_gvec(key, value):
            at, _, many = TABLE[key]
            for j in range(many):
                gvt[pl.ds(at + many * k + j, 1), :] = value[:, 128 * j : 128 * (j + 1)]

        def set_rows(ref, at, value):
            for j in range(value.shape[1] // 128):
                ref[at + j : at + j + 1, :] = value[:, 128 * j : 128 * (j + 1)]

        def mean_rstd(total, base, width, count):
            mu = row(total, base, width) / count
            second = row(total, base + width // 128, width) / count
            return mu, lax.rsqrt(jnp.maximum(second - mu * mu, 0.0) + EPS)

        gvt[...] = jnp.zeros(gvt.shape, F32)

        side_copy.wait()
        side_row = jnp.where(
            m == 0, side_t[s // 2, 0, 0:1, :], side_t[s // 2, 1, 0:1, :]
        )
        pixel = lax.broadcasted_iota(jnp.int32, (PX, 128), 0)
        prow = (pixel // SIDE).astype(F32)
        pcol = (pixel % SIDE).astype(F32)
        mref[...] = jnp.where((prow < side_row) & (pcol < side_row), 1.0, 0.0)
        inv_own = 1.0 / (side_row * side_row)

        spread(MID0, ln_mid0, st_mid0, w_mid0)
        for q in range(4):
            here = u.at[q, pl.ds(2 * k, 2)]
            pltpu.make_async_copy(here, here, img_r.at[q]).wait()
            pltpu.make_async_remote_copy(
                here,
                here,
                bs.at[10 + q],
                br.at[10 + q],
                device_id=(s, 2 * c + 1 - k),
                device_id_type=MESH,
            ).start()
        for q in range(4):
            here = u.at[q, pl.ds(2 * (1 - k), 2)]
            pltpu.make_async_copy(here, here, br.at[10 + q]).wait()

        def mask_block(b, _):
            r = pl.multiple_of(b * 32, 32)
            rows = pl.ds(r, 32)
            mask = mref[rows, :]
            for q in range(4):
                total = jnp.zeros((32, 128), F32)
                for p in range(4):
                    x = u[q, p, rows, :].astype(F32) * mask
                    um[p, rows, 128 * q : 128 * (q + 1)] = x.astype(BF16)
                    total = total + x
                pool[rows, 128 * q : 128 * (q + 1)] = (total * 0.25).astype(BF16)
            return 0

        lax.fori_loop(0, 8, mask_block, 0)
        pass_table()
        full_wait(w_in0.at[k], c_r.at[0])

        def z1_block(p, carry):
            z = dot(um[p], w_in0[k].reshape(CIN, 128))
            z1[p] = z
            return (carry[0] + fold8(z), carry[1] + fold8(z * z))

        zero8 = jnp.zeros((8, 128), F32)
        t0, t1 = lax.fori_loop(0, 4, z1_block, (zero8, zero8))
        put(0, 0, jnp.sum(t0, axis=0, keepdims=True))
        put(0, 1, jnp.sum(t1, axis=0, keepdims=True))
        put(0, 2, side_row)
        send(0)
        pass_on(MID0, w_mid0)
        sent = scatter_early(sent)
        pass_far(MID0, w_mid0)
        spread(SC0, ln_sc, st_sc, w_sc)
        spread(OUT1, ln_out1, st_out1, w_out1)
        table_arrived()
        receive(0)
        total = totals(0)
        sides = across(0, k, 2, 128)
        inv_area = 1.0 / (sides * sides)
        count1 = jnp.sum(sides * sides, axis=0, keepdims=True)
        counts = {w: lanes(count1, w // 128) for w in (128, 256, 512)}
        mu1, rs1 = mean_rstd(total, 0, 128, 4.0 * count1)
        lin1 = rs1 * vrow((0, "g_in"))
        off1 = vrow((0, "b_in")) - mu1 * lin1

        colpos = lax.broadcasted_iota(jnp.int32, (PX, 128), 0) % SIDE

        def shift_cols(x, by):
            moved = pltpu.roll(x, by % PX, 0)
            edge = 0 if by == 1 else SIDE - 1
            return jnp.where(colpos == edge, 0.0, moved)

        def store_tap(cols, di, dj, x, shift):
            at = 128 * (3 * di + dj)
            span = slice(at, at + 128)
            x = x.astype(BF16)
            if shift == 1:
                cols[0:SIDE, span] = jnp.zeros((SIDE, 128), BF16)
                cols[SIDE:PX, span] = x[0 : PX - SIDE]
            elif shift == -1:
                cols[PX - SIDE : PX, span] = jnp.zeros((SIDE, 128), BF16)
                cols[0 : PX - SIDE, span] = x[SIDE:PX]
            else:
                cols[:, span] = x

        def plane_taps(parity):
            return ((1, 0),) if parity == 0 else ((0, 1), (2, 0))

        for p in range(4):
            v = z1[p] * lin1 + off1
            h = v * sigmoid(v) * mref[...]
            for dj, cshift in plane_taps(p % 2):
                x = shift_cols(h, 1) if cshift else h
                for di, rshift in plane_taps(p // 2):
                    store_tap(cols1, di, dj, x, rshift)

        def conv_forward(ph, cols, w_mid, zref):
            z = dot(cols[...], w_mid[...].reshape(1152, 256))
            zref[...] = z
            zm = z * lanes(mref[...], 2)
            put(ph, 0, jnp.sum(zm, axis=0, keepdims=True))
            put(ph, 2, jnp.sum(zm * z, axis=0, keepdims=True))
            send(ph)

        def small(rest):
            _, w_sq, ex = rest
            w_ex = jnp.concatenate([ex[pl.ds(j, CSQ, stride=4), :] for j in range(4)], axis=1)
            return w_sq[...].reshape(CMID, CSQ).astype(F32), w_ex

        def attention_forward(ph, twin, total, at, rest, zref, rr, aref, beside):
            mu, rs = mean_rstd(total, 0, 256, counts[256])
            lin = rs * rows_of(table, at + 2 * k, 2)
            off = rows_of(table, at + 4 + 2 * k, 2) - mu * lin

            def block(b, acc):
                rows = pl.ds(pl.multiple_of(b * 64, 64), 64)
                v = zref[rows, :] * lin + off
                r = v * sigmoid(v) * lanes(mref[rows, :], 2)
                rr[k, rows, :] = r
                return acc + fold8(r)

            acc = lax.fori_loop(0, 4, block, jnp.zeros((8, 256), F32))
            pooled_own = jnp.sum(acc, axis=0, keepdims=True) * lanes(inv_own, 2)
            put(ph, 0, pooled_own)
            send(ph)
            swap = to_twin(twin, rr.at[k], rr.at[k])
            swap.start()
            beside()
            receive(ph)
            w_sq, w_ex = small(rest)
            pooled = across(ph, 0, 0, 256) + across(ph, 1, 0, 256)
            zq = dot_hi(pooled, w_sq)
            mq = jnp.mean(zq, axis=0, keepdims=True)
            vq = jnp.mean(zq * zq, axis=0, keepdims=True) - mq * mq
            rq = lax.rsqrt(jnp.maximum(vq, 0.0) + EPS)
            hq = (zq - mq) * rq
            nq = hq * rows_of(table, rest[0], 1) + rows_of(table, rest[0] + 1, 1)
            sgq = sigmoid(nq)
            qq = nq * sgq
            logits = dot_hi(qq, w_ex) + rows_of(table, rest[0] + 2, 4)
            diff = logits[:, 0:256] - logits[:, 256:512]
            sh0 = sigmoid(diff)
            sh1 = sigmoid(-diff)
            swap.wait()
            s0 = sh0[0:1, :]
            s1 = sh1[0:1, :]

            def mix(b, _):
                rows = pl.ds(pl.multiple_of(b * 64, 64), 64)
                aref[rows, :] = (s0 * rr[0, rows, :] + s1 * rr[1, rows, :]).astype(BF16)
                return 0

            lax.fori_loop(0, 4, mix, 0)
            return (mu, rs, lin, off), (pooled, rq, hq, nq, sgq, qq, sh0, sh1)

        def slope(v):
            sg = sigmoid(v)
            return sg * (1.0 + v * (1.0 - sg))

        def attention_slopes(ph, kept_mid, zref, sp_ref):
            mu, rs, lin, off = kept_mid

            def block(b, acc):
                rows = pl.ds(pl.multiple_of(b * 32, 32), 32)
                z = zref[rows, :]
                sp = slope(z * lin + off) * lanes(mref[rows, :], 2)
                sp_ref[rows, :] = sp
                return (acc[0] + fold8(sp), acc[1] + fold8(sp * ((z - mu) * rs)))

            sums = lax.fori_loop(0, 8, block, (jnp.zeros((8, 256), F32),) * 2)
            put(ph, 4, jnp.sum(sums[0], axis=0, keepdims=True))
            put(ph, 8, jnp.sum(sums[1], axis=0, keepdims=True))

        def attention_backward(
            ph, kept_mid, kept_q, rest, rg, zref, spb, rr, cols, mat, gw_mid, ga_mid, da, beside
        ):
            mu, rs, lin, off = kept_mid
            pooled, rq, hq, nq, sgq, qq, sh0, sh1 = kept_q

            def block(b, acc):
                rows = pl.ds(pl.multiple_of(b * 32, 32), 32)
                hat = (zref[rows, :] - mu) * rs
                grad = da(rows)
                t = grad * spb[rows, :]
                dbuf[rows, :] = grad
                r = rr[k, rows, :]
                return tuple(x + fold8(y) for x, y in zip(acc, (grad * r, t, t * hat)))

            acc = lax.fori_loop(0, 8, block, (jnp.zeros((8, 256), F32),) * 3)
            for j, x in zip((0, 2, 6), acc):
                put(ph, j, jnp.sum(x, axis=0, keepdims=True))
            send(ph)
            beside()
            receive(ph)
            ds0 = across(ph, 0, 0, 256)
            ds1 = across(ph, 1, 0, 256)
            mean = sh0 * ds0 + sh1 * ds1
            dl = jnp.concatenate([sh0 * (ds0 - mean), sh1 * (ds1 - mean)], axis=1)
            w_sq, w_ex = small(rest)
            set_rows(rg, AT_BEX, jnp.sum(dl, axis=0, keepdims=True))
            dq = dot_hi(dl, w_ex, ((1,), (1,)))
            dn = dq * sgq * (1.0 + nq * (1.0 - sgq))
            set_rows(rg, AT_GSQ, jnp.sum(dn * hq, axis=0, keepdims=True))
            set_rows(rg, AT_BSQ, jnp.sum(dn, axis=0, keepdims=True))
            dn = dn * rows_of(table, rest[0], 1)
            dzq = rq * (
                dn
                - jnp.mean(dn, axis=0, keepdims=True)
                - hq * jnp.mean(dn * hq, axis=0, keepdims=True)
            )
            dpool = dot_hi(dzq, w_sq, ((1,), (1,))) * lanes(inv_area, 2)
            share = jnp.where(k == 0, sh0, sh1)

            def both_sums(first, second):
                return jnp.sum(
                    share * across(ph, k, first, 256) + dpool * across(ph, k, second, 256),
                    axis=0,
                    keepdims=True,
                )

            sdv = both_sums(2, 4)
            sdh = both_sums(6, 8)
            set_gvec((mat.row, "b_mid"), sdv)
            set_gvec((mat.row, "g_mid"), sdh)
            own_share = share[0:1, :]
            own_pool = dpool[0:1, :]
            c1 = sdv / counts[256]
            c2 = sdh / counts[256]

            def block2(b, _):
                rows = pl.ds(pl.multiple_of(b * 32, 32), 32)
                hat = (zref[rows, :] - mu) * rs
                dv = (own_share * dbuf[rows, :] + own_pool) * spb[rows, :]
                dz = lin * (dv - c1 - hat * c2) * lanes(mref[rows, :], 2)
                rows_low[rows, :] = dz.astype(BF16)
                return 0

            rows_low = dz_low
            lax.fori_loop(0, 8, block2, 0)

            def rest():
                gw_mid[...] = dot_lt(cols[...], dz_low[...]).astype(BF16).reshape(24, 48, 256)
                shed(mat, gw_mid, ga_mid)
                g_ex = dot_hi(qq, dl, ((0,), (0,)))
                for j in range(4):
                    rg[pl.ds(AT_EX + j, CSQ, stride=4), :] = g_ex[:, 128 * j : 128 * (j + 1)]
                rg[AT_SQ : AT_SQ + CMID, :] = dot_hi(pooled, dzq, ((0,), (0,)))

            return rest

        dz_low = dz3.at[:, pl.ds(0, 256)]

        rest0 = (AT_SMALL[0], w_sq0, ex0)
        rest2 = (AT_SMALL[2], w_sq2, ex2)
        arrived(MID0, w_mid0)
        conv_forward(1, cols1, w_mid0, z2)
        spread_small(SQ0, ln_sq0, st_sq0, w_sq0)
        spread_small(EX0, ln_ex0, st_ex0, w_ex0)
        scatter_late(sent)
        pass_on(SC0, w_sc)
        pass_on(OUT1, w_out1)
        spread(IN1, ln_in1, st_in1, w_in1)
        receive(1)

        def short_forward():
            spread(MID2, ln_mid2, st_mid2, w_mid2)
            share_small(SQ0, w_sq0, 15)
            share_small(EX0, w_ex0, 17)
            pass_far(SC0, w_sc)
            pass_far(OUT1, w_out1)
            pass_all(IN1, w_in1)
            arrived(SC0, w_sc)
            z = dot(pool[...], w_sc[...].reshape(CIN, 512))
            zs[...] = z
            put(3, 8, jnp.sum(z, axis=0, keepdims=True))
            put(3, 12, jnp.sum(z * z, axis=0, keepdims=True))
            small_arrived(w_sq0, 15)
            small_arrived(w_ex0, 17)
            ex0[...] = w_ex0[...].reshape(512, 128).astype(F32)

        mid1, q1 = attention_forward(2, 2, totals(1), AT_MID[0], rest0, z2, rr1, a1, short_forward)
        arrived(OUT1, w_out1)

        def wide_forward(ph, aref, w, zref):
            z = dot(aref[...], w[...].reshape(CMID, 512))
            zref[...] = z
            put(ph, 0, jnp.sum(z, axis=0, keepdims=True))
            put(ph, 4, jnp.sum(z * z, axis=0, keepdims=True))
            send(ph)

        wide_forward(3, a1, w_out1, z3)
        pass_all(MID2, w_mid2)
        spread_small(SQ2, ln_sq2, st_sq2, w_sq2)
        spread_small(EX2, ln_ex2, st_ex2, w_ex2)
        receive(3)
        total = totals(3)
        mus, rss = mean_rstd(total, 8, 512, counts[512])
        lins = rss * vrow((0, "g_sc"))
        offs = vrow((0, "b_sc")) - mus * lins

        mu3, rs3 = mean_rstd(total, 0, 512, counts[512])
        lin3 = rs3 * vrow((1, "g_out"))
        off3 = vrow((1, "b_out")) - mu3 * lin3

        def y1_block(b, _):
            rows = pl.ds(pl.multiple_of(b * 32, 32), 32)
            short = (zs[rows, :] * lins + offs).astype(BF16).astype(F32)
            v = z3[rows, :] * lin3 + off3 + short
            v3[rows, :] = v
            y1[rows, :] = (v * sigmoid(v) * lanes(mref[rows, :], 4)).astype(BF16)
            return 0

        lax.fori_loop(0, 8, y1_block, 0)
        all_arrived(IN1, w_in1)
        pz[0] = dot(y1[...], w_in1[1 - k].reshape(512, 128))
        swap = to_twin(3, pz.at[0], pz.at[1])
        swap.start()
        z = dot(y1[...], w_in1[k].reshape(512, 128))
        swap.wait()
        z = z + pz[1]
        z4[...] = z
        put(4, 0, jnp.sum(z, axis=0, keepdims=True))
        put(4, 1, jnp.sum(z * z, axis=0, keepdims=True))
        send(4)
        spread(OUT3, ln_out3, st_out3, w_out3)
        receive(4)
        mu4, rs4 = mean_rstd(totals(4), 0, 128, count1)
        lin4 = rs4 * vrow((1, "g_in"))
        off4 = vrow((1, "b_in")) - mu4 * lin4
        v = z4[...] * lin4 + off4
        h = v * sigmoid(v) * mref[...]
        for dj in range(3):
            x = h if dj == 1 else shift_cols(h, 1 - dj)
            for di in range(3):
                store_tap(cols2, di, dj, x, 1 - di)

        all_arrived(MID2, w_mid2)
        conv_forward(5, cols2, w_mid2, z5)
        share_small(SQ2, w_sq2, 16)
        share_small(EX2, w_ex2, 18)
        pass_on(OUT3, w_out3)

        def slope3(b, _):
            rows = pl.ds(pl.multiple_of(b * 32, 32), 32)
            v3[rows, :] = slope(v3[rows, :]) * lanes(mref[rows, :], 4)
            return 0

        lax.fori_loop(0, 8, slope3, 0)
        receive(5)

        def last_weights():
            pass_far(OUT3, w_out3)
            small_arrived(w_sq2, 16)
            small_arrived(w_ex2, 18)
            ex2[...] = w_ex2[...].reshape(512, 128).astype(F32)
            for slot in range(2):
                move(
                    cot.at[slot],
                    ctb.at[lax.rem(s, 2)],
                    ct_s.at[slot],
                    ct_r.at[lax.rem(s, 2)],
                    (2 * k + slot, 2 * c + s // 2),
                )
            to_twin(14, w_in0.at[k], w_in0.at[k]).start()

        mid2, q2 = attention_forward(6, 4, totals(5), AT_MID[2], rest2, z5, rr2, a2, last_weights)
        arrived(OUT3, w_out3)
        wide_forward(7, a2, w_out3, z6)
        to_twin(14, w_in0.at[k], w_in0.at[k]).wait()
        for i in range(2):
            pltpu.make_async_copy(ctb.at[i], ctb.at[i], ct_r.at[i]).wait()
        attention_slopes(9, mid2, z5, spb2)
        d4[...] = slope(z4[...] * lin4 + off4) * mref[...]
        receive(7)
        mu6, rs6 = mean_rstd(totals(7), 0, 512, counts[512])
        lin6 = rs6 * vrow((3, "g_out"))
        off6 = vrow((3, "b_out")) - mu6 * lin6

        def out_block(b, acc):
            rows = pl.ds(pl.multiple_of(b * 32, 32), 32)
            z = z6[rows, :]
            mask = lanes(mref[rows, :], 4)
            v = z * lin6 + off6 + y1[rows, :].astype(F32)
            sg = sigmoid(v)
            y = (v * sg * mask).astype(BF16)
            obuf[0, rows, :] = y[:, 0:256]
            obuf[1, rows, :] = y[:, 256:512]
            ct = jnp.concatenate([ctb[0, rows, :], ctb[1, rows, :]], axis=1).astype(F32)
            dv = ct * (sg * (1.0 + v * (1.0 - sg)) * mask)
            dv6[rows, :] = dv
            return (acc[0] + fold8(dv), acc[1] + fold8(dv * ((z - mu6) * rs6)))

        zero512 = jnp.zeros((8, 512), F32)
        t0, t1 = lax.fori_loop(0, 8, out_block, (zero512, zero512))
        put(8, 0, jnp.sum(t0, axis=0, keepdims=True))
        put(8, 4, jnp.sum(t1, axis=0, keepdims=True))
        send(8)
        fill_up(nought, out_w, jnp.clip(used - d * shard_rows, 0, shard_rows), shard_rows, gc_r)
        fill_up(nought, fill3, 0, whole_rows(), gc_r)
        for j in range(2):
            move(
                obuf.at[j],
                out_o.at[lax.rem(s, 2)],
                oo_s.at[j],
                oo_r.at[lax.rem(s, 2)],
                (2 * k + j, 2 * c + s // 2),
            )
        for mat, whole in ((MID0, w_mid0), (SC0, w_sc), (OUT1, w_out1)):
            end_spread(mat, whole)
        end_small(SQ0, w_sq0, 15)
        end_small(EX0, w_ex0, 17)
        end_table()
        attention_slopes(12, mid1, z2, spb)

        def slope1(p, _):
            d1[p] = slope(z1[p] * lin1 + off1) * mref[...]
            return 0

        lax.fori_loop(0, 4, slope1, 0)
        receive(8)

        def wide_back(total, base, key_g, key_b, lin, mu, rs, zref, dvf, dst):
            sdv = row(total, base, 512)
            sdh = row(total, base + 4, 512)
            set_gvec(key_b, sdv)
            set_gvec(key_g, sdh)
            c1 = sdv / counts[512]
            c2 = sdh / counts[512]

            def block(b, _):
                rows = pl.ds(pl.multiple_of(b * 32, 32), 32)
                hat = (zref[rows, :] - mu) * rs
                dz = lin * (dvf(rows) - c1 - hat * c2) * lanes(mref[rows, :], 4)
                dst[rows, :] = dz.astype(BF16)
                return 0

            lax.fori_loop(0, 8, block, 0)

        wide_back(
            totals(8),
            0,
            (3, "g_out"),
            (3, "b_out"),
            lin6,
            mu6,
            rs6,
            z6,
            lambda rows: dv6[rows, :],
            dz3,
        )

        def attended_grad(twin, w, aref, mat, gw, land):
            pda[0] = dot_rt(dz3[...], w[...].reshape(CMID, 512))
            swap = to_twin(twin, pda.at[0], pda.at[1])
            swap.start()
            gw[...] = dot_lt(aref[...], dz3[...]).astype(BF16).reshape(16, 16, 512)
            shed(mat, gw, land)
            swap.wait()

        def summed_grad(rows):
            return (pda[0, rows, :] + pda[1, rows, :]).astype(BF16).astype(F32)

        attended_grad(5, w_out3, a2, OUT3, gw_out3, ga_out3)

        def beside9():
            for mat, whole in ((IN1, w_in1), (MID2, w_mid2), (OUT3, w_out3)):
                end_spread(mat, whole)
            end_small(SQ2, w_sq2, 16)
            end_small(EX2, w_ex2, 18)
            shed_mid(OUT3, gw_out3, ga_out3, gt_out3, gd_out3)

        grad_rest2 = attention_backward(
            9,
            mid2,
            q2,
            rest2,
            rg2,
            z5,
            spb2,
            rr2,
            cols2,
            MID2,
            gw_mid2,
            ga_mid2,
            summed_grad,
            beside9,
        )

        ep[...] = jnp.zeros(ep.shape, F32)
        for di in range(3):
            part = dot_rt(dz_low[...], w_mid2[8 * di : 8 * (di + 1)].reshape(384, 256))
            for dj in range(3):
                lo = SIDE * di
                ep[dj, lo : lo + PX, :] += part[:, 128 * dj : 128 * (dj + 1)]
        grad = ep[1, SIDE : SIDE + PX, :]
        grad = grad + shift_cols(ep[0, SIDE : SIDE + PX, :], -1)
        grad = grad + shift_cols(ep[2, SIDE : SIDE + PX, :], 1)
        grad = grad.astype(BF16).astype(F32)
        hat4 = (z4[...] - mu4) * rs4
        dv4 = grad * d4[...]
        dh[0] = dv4
        put(10, 0, jnp.sum(dv4, axis=0, keepdims=True))
        put(10, 1, jnp.sum(dv4 * hat4, axis=0, keepdims=True))
        send(10)
        grad_rest2()
        rest_meet(2, REST2, rg2, rl2)
        shed_more(OUT3, gw_out3, ga_out3, gd_out3, gp_out3, gb_out3)
        receive(10)
        total = totals(10)
        set_gvec((1, "b_in"), total[0:1, :])
        set_gvec((1, "g_in"), total[1:2, :])
        hat4 = (z4[...] - mu4) * rs4
        dz = lin4 * (dh[0] - total[0:1, :] / count1 - hat4 * (total[1:2, :] / count1)) * mref[...]
        dz4[k] = dz.astype(BF16)
        swap = to_twin(6, dz4.at[k], dz4.at[k])
        swap.start()
        swap.wait()

        def dy_block(b, acc):
            rows = pl.ds(pl.multiple_of(b * 64, 64), 64)
            dy = dot_rt(dz4[0, rows, :], w_in1[0].reshape(512, 128))
            dy = dy + dot_rt(dz4[1, rows, :], w_in1[1].reshape(512, 128))
            dy = dy + dv6[rows, :].astype(BF16).astype(F32)
            dv = dy * v3[rows, :]
            v3[rows, :] = dv
            low = dv.astype(BF16).astype(F32)
            hat = (z3[rows, :] - mu3) * rs3
            hats = (zs[rows, :] - mus) * rss
            return tuple(
                x + fold8(y) for x, y in zip(acc, (dv, dv * hat, low, low * hats))
            )

        acc = lax.fori_loop(0, 4, dy_block, (zero512,) * 4)
        for j, x in enumerate(acc):
            put(11, 4 * j, jnp.sum(x, axis=0, keepdims=True))
        send(11)
        both4 = jnp.concatenate([dz4[0], dz4[1]], axis=1)
        gw_in1[...] = dot_lt(y1[...], both4).astype(BF16).reshape(32, 16, 256)
        shed(IN1, gw_in1, ga_in1)
        shed_mid(MID2, gw_mid2, ga_mid2, gt_mid2, gd_mid2)
        left = rest_home(2, REST2, rg2, rl2, rf2)
        receive(11)
        total = totals(11)
        wide_back(
            total,
            0,
            (1, "g_out"),
            (1, "b_out"),
            lin3,
            mu3,
            rs3,
            z3,
            lambda rows: v3[rows, :],
            dz3,
        )
        wide_back(
            total,
            8,
            (0, "g_sc"),
            (0, "b_sc"),
            lins,
            mus,
            rss,
            zs,
            lambda rows: v3[rows, :].astype(BF16).astype(F32),
            dzs,
        )
        attended_grad(7, w_out1, a1, OUT1, gw_out1, ga_out1)

        def short_back():
            part = dot_rt(dzs[...], w_sc[...].reshape(CIN, 512))
            pdp[0] = jnp.where(k == 0, part[:, 256:512], part[:, 0:256])
            to_twin(8, pdp.at[0], pdp.at[1]).start()
            pdp[2] = jnp.where(k == 0, part[:, 0:256], part[:, 256:512])
            gw_sc[...] = dot_lt(pool[...], dzs[...]).astype(BF16).reshape(32, 16, 512)
            shed(SC0, gw_sc, ga_sc)
            table_meet(0, LATE_ROWS, TABLE_ROWS - LATE_ROWS)
            shed_mid(IN1, gw_in1, ga_in1, gt_in1, gd_in1)
            shed_mid(OUT1, gw_out1, ga_out1, gt_out1, gd_out1)
            shed_more(MID2, gw_mid2, ga_mid2, gd_mid2, gp_mid2, gb_mid2)

        grad_rest0 = attention_backward(
            12,
            mid1,
            q1,
            rest0,
            rg0,
            z2,
            spb,
            rr1,
            cols1,
            MID0,
            gw_mid0,
            ga_mid0,
            summed_grad,
            short_back,
        )

        for p in range(4):
            dh[p] = jnp.zeros((PX, 128), F32)
        for di in range(3):
            part = dot_rt(dz_low[...], w_mid0[8 * di : 8 * (di + 1)].reshape(384, 256))
            pr = 0 if di == 1 else 1
            for dj in range(3):
                x = part[:, 128 * dj : 128 * (dj + 1)]
                if dj == 0:
                    x = shift_cols(x, -1)
                p = 2 * pr + (0 if dj == 1 else 1)
                if di == 0:
                    dh[p, 0 : PX - SIDE, :] += x[SIDE:PX]
                else:
                    dh[p] += x

        def dv1_block(p, acc):
            z = z1[p]
            dv = dh[p] * d1[p]
            dh[p] = dv
            return (acc[0] + fold8(dv), acc[1] + fold8(dv * ((z - mu1) * rs1)))

        t0, t1 = lax.fori_loop(0, 4, dv1_block, (zero8, zero8))
        put(13, 0, jnp.sum(t0, axis=0, keepdims=True))
        put(13, 1, jnp.sum(t1, axis=0, keepdims=True))
        send(13)
        grad_rest0()
        rest_meet(1, REST0, rg0, rl0)
        shed_more(IN1, gw_in1, ga_in1, gd_in1, gp_in1, gb_in1)
        shed_more(OUT1, gw_out1, ga_out1, gd_out1, gp_out1, gb_out1)
        shed_mid(SC0, gw_sc, ga_sc, gt_sc, gd_sc)
        left = left + home_cut(OUT3, gb_out3, gf_out3, hb_out3, hi_out3, hr_out3)
        left = left + home_cut(MID2, gb_mid2, gf_mid2, hb_mid2, hi_mid2, hr_mid2, 0)
        left = left + table_home(0, LATE_ROWS, TABLE_ROWS - LATE_ROWS)
        receive(13)
        total = totals(13)
        set_gvec((0, "b_in"), total[0:1, :])
        set_gvec((0, "g_in"), total[1:2, :])
        table_meet(3, 0, LATE_ROWS)
        k1 = total[0:1, :] / (4.0 * count1)
        k2 = total[1:2, :] / (4.0 * count1)

        def dz1_block(p, _):
            hat = (z1[p] - mu1) * rs1
            dz1[k, p] = (lin1 * (dh[p] - k1 - hat * k2) * mref[...]).astype(BF16)
            return 0

        lax.fori_loop(0, 4, dz1_block, 0)
        swap = to_twin(9, dz1.at[k], dz1.at[k])
        swap.start()
        total = jnp.zeros((CIN, 128), F32)
        for p in range(4):
            total = total + dot_lt(um[p], dz1[k, p])
        gw_in0[...] = total.astype(BF16).reshape(32, 16, 128)

        def shed_in0(i, _):
            p = lax.rem(8 * s + i, 32)
            move(
                gw_in0.at[p],
                gb_in0.at[s * chips + c, k],
                gb_s.at[0],
                gb_r.at[0],
                (p // 8, p % 8),
            )
            return 0

        lax.fori_loop(0, 32, shed_in0, 0)
        shed_mid(MID0, gw_mid0, ga_mid0, gt_mid0, gd_mid0)
        shed_more(SC0, gw_sc, ga_sc, gd_sc, gp_sc, gb_sc)
        swap.wait()
        to_twin(8, pdp.at[0], pdp.at[1]).wait()

        def du_block(p, _):
            mine = pl.ds(16 * k, 16)
            grad = dot_rt(dz1[0, p], w_in0[0, mine].reshape(256, 128))
            grad = grad + dot_rt(dz1[1, p], w_in0[1, mine].reshape(256, 128))
            grad = (grad + 0.25 * (pdp[1] + pdp[2])) * lanes(mref[...], 2)
            for r in range(SIDE):
                at = (2 * r + p // 2) * 2 * SIDE + p % 2
                for j in range(2):
                    x = grad[SIDE * r : SIDE * (r + 1), 128 * j : 128 * (j + 1)]
                    merged[j, pl.ds(at, SIDE, stride=2), :] = x
            return 0

        lax.fori_loop(0, 4, du_block, 0)

        def narrow(i, _):
            rows = pl.ds(pl.multiple_of(i * 128, 128), 128)
            for j in range(2):
                ibuf[j, rows, :] = merged[j, rows, :].astype(BF16)
            return 0

        lax.fori_loop(0, 8, narrow, 0)
        for j in range(2):
            move(
                ibuf.at[j],
                out_i.at[lax.rem(s, 2)],
                oi_s.at[j],
                oi_r.at[lax.rem(s, 2)],
                (2 * k + j, 2 * c + s // 2),
            )

        shed_more(MID0, gw_mid0, ga_mid0, gd_mid0, gp_mid0, gb_mid0)
        left = left + home_cut(MID2, gb_mid2, gf_mid2, hb_mid2, hi_mid2, hr_mid2, 1)
        left = left + home(IN1, gb_in1, gf_in1)
        left = left + home_cut(OUT1, gb_out1, gf_out1, hb_out1, hi_out1, hr_out1)
        left = left + home_cut(SC0, gb_sc, gf_sc, hb_sc, hi_sc, hr_sc)
        left = left + rest_home(1, REST0, rg0, rl0, rf0)
        left = left + table_home(3, 0, LATE_ROWS)
        left = left + home_cut(IN0, gb_in0, gf_in0, hb_in0, hi_in0, hr_in0)
        left = left + home_cut(MID0, gb_mid0, gf_mid0, hb_mid0, hi_mid0, hr_mid0)

        fill_up(nought, fill2, left, HOME_ROWS, gc_s)

        for ph in range(PHASES):
            end_send(ph)
        for slot in range(2):
            for kk in range(2):
                end_move(
                    planes.at[slot, pl.ds(2 * kk, 2)],
                    img_s.at[slot, kk],
                    (2 * k + slot, 2 * c + kk),
                )
            end_move(cot.at[slot], ct_s.at[slot], (2 * k + slot, 2 * c + s // 2))
        for j in range(2):
            end_move(obuf.at[j], oo_s.at[j], (2 * k + j, 2 * c + s // 2))
        for q in range(4):
            full_wait(u.at[q, pl.ds(2 * k, 2)], bs.at[10 + q])
        full_wait(fill, h_s)
        for mat, gw in ((OUT1, gw_out1), (IN1, gw_in1), (MID2, gw_mid2), (OUT3, gw_out3)):
            end_shed(mat, gw)

        @pl.when(holds(IN0))
        def _():
            full_wait(fill.at[pl.ds(0, 8 * (4 * n - 1))], a_s.at[0])

        for i, mat, land in ((1, REST0, rl0), (2, REST2, rl2)):

            @pl.when((s == mat.row) & (d < 8))
            def _():
                full_wait(land, v_s.at[i])

        @pl.when((s == 0) & (d < 2))
        def _():
            full_wait(gvl.at[pl.ds(LATE_ROWS, TABLE_ROWS - LATE_ROWS)], v_s.at[0])
            full_wait(gvl.at[pl.ds(0, LATE_ROWS)], v_s.at[3])

        take(OUT3, hi_out3, hr_out3)
        take(MID2, hi_mid2, hr_mid2)
        take(OUT1, hi_out1, hr_out1)
        take(SC0, hi_sc, hr_sc)
        take(IN0, hi_in0, hr_in0)
        take(MID0, hi_mid0, hr_mid0)

        for mat, ready in (
            (IN0, hb_in0),
            (MID0, hb_mid0),
            (SC0, hb_sc),
            (OUT1, hb_out1),
            (MID2, hb_mid2),
            (OUT3, hb_out3),
        ):
            end_home_cut(mat, ready)
        for mat, gw in ((MID0, gw_mid0), (SC0, gw_sc)):
            end_shed(mat, gw)

        @pl.when(holds(IN0))
        def _():
            full_wait(gw_in0.at[pl.ds(0, 31)], gb_s.at[0])

        @pl.when(jnp.logical_not(holds(IN0)))
        def _():
            full_wait(gw_in0, gb_s.at[0])

        full_wait(fill2, gc_s)
        full_wait(out_w, gc_r)
        for slot in range(2):
            full_wait(out_o.at[slot], oo_r.at[slot])
            full_wait(out_i.at[slot], oi_r.at[slot])
        for j in range(2):
            end_move(ibuf.at[j], oi_s.at[j], (2 * k + j, 2 * c + s // 2))

    return kernel


def call_kernel(n, operands):
    chips = n // 2
    shard_rows = WSLOTS // (128 * n)
    fill_rows = max(shard_rows + 34 * n, 96 * (n - 1), 100 * n, 8 * (4 * n - 1), 16 * (2 * n - 1))

    def vm(*shape, dtype=F32):
        return pltpu.VMEM(shape, dtype)

    def low(*shape):
        return pltpu.VMEM(shape, BF16)

    dma = pltpu.SemaphoreType.DMA
    scratch = [
        vm(PHASES, 16, 128),
        vm(PHASES, 2, n, 16, 128),
        vm(2, 2, 8, 128),
        low(4, 4, PX, 128),
        low(4, PX, CIN),
        low(PX, CIN),
        low(2, PX, 256),
        vm(PX, 128),
        vm(4, PX, 128),
        vm(PX, 256),
        vm(PX, 512),
        vm(PX, 512),
        vm(PX, 128),
        vm(PX, 256),
        vm(PX, 512),
        vm(PX, 512),
        low(PX, 1152),
        low(PX, 1152),
        vm(2, PX, 256),
        vm(2, PX, 256),
        low(PX, 256),
        low(PX, 256),
        low(PX, 512),
        vm(PX, 512),
        vm(PX, 256),
        vm(PX, 256),
        vm(2, PX, 128),
        vm(2, PX, 256),
        vm(3, PX, 256),
        low(2, PX, 128),
        low(2, 4, PX, 128),
        low(PX, 512),
        low(PX, 512),
        vm(3, PX + 2 * SIDE, 128),
        vm(4, PX, 128),
        low(2, PX, 256),
        low(2, 4 * PX, 128),
        vm(shard_rows, 128),
        vm(128, 128),
        vm(fill_rows, 128),
        vm(HOME_ROWS, 128),
        vm(TABLE_ROWS, 128),
        low(2, 32, 16, 128),
        low(24, 48, 256),
        low(32, 16, 512),
        low(16, 16, 512),
        low(2, 32, 16, 128),
        low(24, 48, 256),
        low(16, 16, 512),
        vm(32, 128),
        vm(192, 128),
        vm(128, 128),
        vm(128, 128),
        vm(64, 128),
        vm(192, 128),
        vm(128, 128),
        low(2, 16, 128),
        low(2, 48, 256),
        low(2, 16, 512),
        low(2, 16, 512),
        low(2, 2, 16, 128),
        low(2, 48, 256),
        low(2, 16, 512),
        low(shard_rows // 32 + 2, 2, 16, 128),
        low(shard_rows // 192 + 2, 2, 48, 256),
        low(shard_rows // 128 + 2, 2, 16, 512),
        low(shard_rows // 128 + 2, 2, 16, 512),
        low(shard_rows // 192 + 2, 2, 48, 256),
        low(shard_rows // 128 + 2, 2, 16, 512),
        low(32, 16, 128),
        low(24, 48, 256),
        low(32, 16, 512),
        low(16, 16, 512),
        low(32, 16, 256),
        low(24, 48, 256),
        low(16, 16, 512),
        low(2, 2, 3, 48, 256),
        low(2, 2, 4, 16, 512),
        low(2, 2, 2, 16, 512),
        low(2, 2, 4, 16, 256),
        low(2, 2, 3, 48, 256),
        low(2, 2, 2, 16, 512),
        low(6, 48, 256),
        low(8, 16, 512),
        low(4, 16, 512),
        low(8, 16, 256),
        low(6, 48, 256),
        low(4, 16, 512),
        low(4 * chips, 2, 16, 128),
        low(chips, 2, 48, 256),
        low(chips, 2, 16, 512),
        low(chips, 2, 16, 512),
        low(chips, 2, 16, 256),
        low(chips, 2, 48, 256),
        low(chips, 2, 16, 512),
        vm(32, 128),
        vm(192, 128),
        vm(128, 128),
        vm(128, 128),
        vm(64, 128),
        vm(192, 128),
        vm(128, 128),
        vm(784, 128),
        vm(784, 128),
        vm(REST_PART, 128),
        vm(REST_PART, 128),
        vm(REST_PART, 128),
        vm(REST_PART, 128),
        vm(TABLE_ROWS, 128),
        vm(TABLE_ROWS, 128),
        vm(TABLE_ROWS, 128),
        low(2, 3, 48, 256),
        low(2, 3, 48, 256),
        low(2, 3, 48, 256),
        low(2, 3, 48, 256),
        low(2, 4, 16, 512),
        low(2, 4, 16, 512),
        low(2, 2, 16, 512),
        low(2, 2, 16, 512),
        low(2, 2, 16, 512),
        low(2, 2, 16, 512),
        low(2, 4, 16, 256),
        low(2, 4, 16, 256),
        low(2, 16, 128),
        low(shard_rows // 32 + 2, 2, 16, 128),
        low(2, 48, 256),
        low(shard_rows // 192 + 2, 2, 48, 256),
        low(2, 16, 512),
        low(shard_rows // 128 + 2, 2, 16, 512),
        low(2, 16, 512),
        low(shard_rows // 128 + 2, 2, 16, 512),
        low(2, 48, 256),
        low(shard_rows // 192 + 2, 2, 48, 256),
        low(2, 16, 512),
        low(shard_rows // 128 + 2, 2, 16, 512),
        vm(shard_rows, 128),
        vm(4 * PX, 128),
        low(2, 4, PX, 128),
        vm(2, 4 * PX, 128),
        low(16, 16, 128),
        vm(16, 128),
        low(16, 128),
        low(min(shard_rows // 16 + 2, 16), 16, 128),
        low(32, 16, 128),
        vm(16, 128),
        low(16, 128),
        low(min(shard_rows // 16 + 2, 32), 16, 128),
        vm(512, 128),
        low(16, 16, 128),
        vm(16, 128),
        low(16, 128),
        low(min(shard_rows // 16 + 2, 16), 16, 128),
        low(32, 16, 128),
        vm(16, 128),
        low(16, 128),
        low(min(shard_rows // 16 + 2, 32), 16, 128),
        vm(512, 128),
        vm(PX, 256),
        vm(4, PX, 128),
        vm(PX, 128),
        dma((PHASES,)),
        dma((PHASES, 2)),
        dma((19,)),
        dma((19,)),
        dma((2, 2)),
        dma((4,)),
        dma((2,)),
        dma((2,)),
        dma((2,)),
        dma((2,)),
        dma((2,)),
        dma((2,)),
        dma,
        dma,
        dma((2,)),
        dma((11,)),
        dma((11,)),
        dma((11,)),
        dma((11,)),
        dma((11, 4)),
        dma((11,)),
        dma((11, 2)),
        dma((11,)),
        dma((11,)),
        dma,
        dma,
        dma((4,)),
        dma((4,)),
        dma((11,)),
        dma((11, 2)),
        dma((shard_rows // 32 + 2,)),
        dma((shard_rows // 192 + 2,)),
        dma((shard_rows // 128 + 2,)),
        dma((shard_rows // 128 + 2,)),
        dma((shard_rows // 192 + 2,)),
        dma((shard_rows // 128 + 2,)),
        dma((11,)),
    ]
    sds = jax.ShapeDtypeStruct
    outs = (
        sds((2, PX, 256), BF16),
        sds((2, 4 * PX, 128), BF16),
        sds((shard_rows, 128), F32),
    )
    vmem = pl.BlockSpec(memory_space=pltpu.VMEM)
    smem = pl.BlockSpec(memory_space=pltpu.SMEM)
    return pl.pallas_call(
        make_kernel(n),
        out_shape=outs,
        in_specs=[smem if i == 2 else vmem for i in range(len(operands))],
        out_specs=[vmem] * len(outs),
        scratch_shapes=scratch,
        compiler_params=pltpu.CompilerParams(
            collective_id=0, has_side_effects=True, vmem_limit_bytes=60 << 20
        ),
    )(*operands)


def per_device(images, cotangent, res_codes, section_weights):
    n = lax.axis_size("dp")
    out_o, out_i, out_w = call_kernel(
        n,
        (
            images.reshape(2, 4 * PX, 128),
            cotangent.reshape(2, PX, 256),
            res_codes,
            section_weights.reshape(-1, 128),
        ),
    )
    block_out = out_o.reshape(2, SIDE, SIDE, 256)
    input_grad = out_i.reshape(images.shape)
    return block_out, input_grad, out_w.reshape(section_weights.shape)


def solution(mesh):
    return jax.shard_map(
        per_device,
        mesh=mesh,
        in_specs=(
            P("dp", None, None, "section"),
            P("dp", None, None, "section"),
            P("dp"),
            P("section", "dp"),
        ),
        out_specs=(
            P("dp", None, None, "section"),
            P("dp", None, None, "section"),
            P("section", "dp"),
        ),
        check_vma=False,
    )
```
